32 devices in a mesh: dp: 8 (over z, x), mp: 4 (over y, core).
Axes of the slice: x: 2, y: 2, z: 4, core: 2. Of those that a mesh axis runs over, the one named last changes fastest.
Arguments:
- tokens: bfloat16 [16384, 1024], P('dp', 'mp'), may hold values from -6 to 6
- w_qkv: bfloat16 [1024, 3, 1024], P('dp', None, 'mp'), may hold values from -0.1875 to 0.1875
- w_out: bfloat16 [1024, 1024], P('dp', 'mp'), may hold values from -0.1875 to 0.1875
- w_gate_up: bfloat16 [1024, 2, 4096], P('dp', None, 'mp'), may hold values from -0.1875 to 0.1875
- w_down: bfloat16 [1024, 4096], P('dp', 'mp'), may hold values from -0.09375 to 0.09375
- s_qk: float32 [64, 16], P(None, 'mp'), may hold values from 0.8 to 1.6
- alpha_attn: float32 [64, 16], P(None, 'mp'), may hold values from 0.15 to 0.6
- alpha_mlp: float32 [64, 16], P(None, 'mp'), may hold values from 0.15 to 0.6
- s_mlp: float32 [256, 2, 16], P(None, None, 'mp'), may hold values from 0.5 to 2
- doc_lengths: int32 [8, 4], P('dp'), may hold values from 0 to 2048, as said below
- grad_out: bfloat16 [16384, 1024], P('dp', 'mp'), may hold values from -6 to 6
Outputs:
- out: bfloat16 [16384, 1024], P('dp', 'mp')
- grad_in: float32 [16384, 1024], P('dp', 'mp')
- grad_w_qkv: float32 [1024, 3, 1024], P('dp', None, 'mp')
- grad_w_out: float32 [1024, 1024], P('dp', 'mp')
- grad_w_gate_up: float32 [1024, 2, 4096], P('dp', None, 'mp')
- grad_w_down: float32 [1024, 4096], P('dp', 'mp')
- grad_s_qk: float32 [64, 16], P('dp', 'mp')
- grad_alpha_attn: float32 [64, 16], P('dp', 'mp')
- grad_alpha_mlp: float32 [64, 16], P('dp', 'mp')
- grad_s_mlp: float32 [256, 2, 16], P('dp', None, 'mp')
The draws below stay inside these ranges and needn't reach their ends.
Inputs may be any that keep to these rules, and one draw needn't show every extreme that they name: `doc_lengths`: row r packs the sequences of the bucket on data group r: either one sequence of 2048 tokens followed by zeros, or 4 sequences of 512 tokens each. Every draw has buckets of both kinds; which buckets are long varies from seed to seed.
All inputs are finite; a program needn't handle non-finite values.
Results may differ from the reference program's by a relative error of at most 0.024.
Values may be sent and summed in bfloat16 or wider, within the bound.
A program may use at most 192 MiB of HBM per device.

```python
import math
import jax
import jax.numpy as jnp
from jax import lax

D = 1024
H = 16
DK = 64
FF = 4096
TOK_DEV = 2048
PIECES = 4
TOKENS = 16384
N_DP = 8


def draw_doc_lengths(key, part):
    key = jax.random.fold_in(key, 11)
    first_key, second_key = jax.random.split(key)
    long_count = jax.random.randint(first_key, (), 1, N_DP)
    order = jax.random.permutation(second_key, N_DP)
    is_long = order < long_count
    pieces_index = jnp.arange(PIECES, dtype=jnp.int32)
    long_row = jnp.where(pieces_index == 0, TOK_DEV, 0).astype(jnp.int32)
    short_row = jnp.full((PIECES,), TOK_DEV // PIECES, dtype=jnp.int32)
    return jnp.where(is_long[:, None], long_row[None, :], short_row[None, :]).astype(jnp.int32)


def level_of(stream_key, extent, cuts, low, top_value):
    def one(dim, shards_of):
        heights = jax.random.uniform(jax.random.fold_in(jax.random.fold_in(stream_key, 6), dim), (shards_of,), jnp.float32, low / len(cuts), top_value / len(cuts))
        return jnp.repeat(jnp.exp(heights), extent[dim] // shards_of).reshape((-1,) + (1,) * (len(extent) - dim - 1))

    level = one(*cuts[0])
    for cut in cuts[1:]:
        level = level * one(*cut)
    return level


def bell_draw(own_key, extent, width, reach, cuts=(), held_as=jnp.bfloat16):
    entries = jax.random.normal(own_key, extent, jnp.float32) * width
    if len(cuts) > 0:
        entries = level_of(own_key, extent, cuts, -0.22, 0.18) * entries
    return jnp.clip(entries, min=-reach, max=reach).astype(held_as)


def setup_inputs(seed: int = 0) -> dict:
    key_list = jax.random.split(jax.random.key(seed), 12)
    tokens = bell_draw(key_list[0], (TOKENS, D), 1.0, 6.0, ((0, 8), (1, 4)))
    w_qkv = bell_draw(key_list[1], (D, 3, D), D ** -0.5, 0.1875, ((0, 8), (2, 4)))
    w_out = bell_draw(key_list[2], (D, D), D ** -0.5, 0.1875, ((0, 8), (1, 4)))
    w_gate_up = bell_draw(key_list[3], (D, 2, FF), D ** -0.5, 0.1875, ((0, 8), (2, 4)))
    w_down = bell_draw(key_list[4], (D, FF), FF ** -0.5, 0.09375, ((0, 8), (1, 4)))
    s_qk = jnp.clip(jnp.exp(math.log(1.6) - 0.6931472 * jax.random.uniform(key_list[5], (DK, H), jnp.float32) ** level_of(key_list[5], (DK, H), ((1, 4),), -0.2, 0.2)), 0.8, 1.6)
    alpha_attn = jnp.clip(0.15 + 0.45000002 * jax.random.uniform(key_list[6], (DK, H), jnp.float32) ** level_of(key_list[6], (DK, H), ((1, 4),), -0.2, 0.2), 0.15, 0.6)
    alpha_mlp = jnp.clip(0.15 + 0.45000002 * jax.random.uniform(key_list[7], (DK, H), jnp.float32) ** level_of(key_list[7], (DK, H), ((1, 4),), -0.2, 0.2), 0.15, 0.6)
    s_mlp = jnp.clip(jnp.exp(math.log(2.0) - 1.3862944 * jax.random.uniform(key_list[8], (FF // H, 2, H), jnp.float32) ** level_of(key_list[8], (FF // H, 2, H), ((2, 4),), -0.2, 0.2)), 0.5, 2.0)
    doc_lengths = draw_doc_lengths(jax.random.fold_in(key_list[11], 71), 0)
    grad_out = bell_draw(key_list[10], (TOKENS, D), 1.0, 6.0, ((0, 8), (1, 4)))
    return {"tokens": tokens, "w_qkv": w_qkv, "w_out": w_out, "w_gate_up": w_gate_up, "w_down": w_down, "s_qk": s_qk, "alpha_attn": alpha_attn, "alpha_mlp": alpha_mlp, "s_mlp": s_mlp, "doc_lengths": doc_lengths, "grad_out": grad_out}


@jax.custom_vjp
def low(v):
    return lax.optimization_barrier(v.astype(jnp.bfloat16)).astype(jnp.float32)

@jax.custom_vjp
def low_back(v):
    return v

def low_keep(v):
    return (low(v), None)

def low_pass(kept, grad):
    return (grad,)

def back_keep(v):
    return (v, None)

def back_low(kept, grad):
    return (low(grad),)
low.defvjp(low_keep, low_pass)
low_back.defvjp(back_keep, back_low)
epsilon = 1e-06
theta_base = 10000.0
highest = lax.Precision.HIGHEST

def layout(lengths, token_count):
    starts = (jnp.cumsum(lengths) - lengths).astype(jnp.int32)
    place = jnp.arange(token_count, dtype=jnp.int32)
    doc_ids = lax.optimization_barrier(jnp.sum((place[:, None] >= starts[None, 1:]).astype(jnp.int32), axis=1))
    picked = (doc_ids[:, None] == jnp.arange(lengths.shape[0], dtype=jnp.int32)[None, :]).astype(jnp.int32)
    position = place - lax.optimization_barrier(jnp.sum(picked * starts[None, :], axis=1))
    return (doc_ids, position)

def angles(position):
    half_size = DK // 2
    frequency = theta_base ** (-(2.0 / DK) * jnp.arange(half_size, dtype=jnp.float32))
    angle_grid = position.astype(jnp.float32)[:, None] * frequency[None, :]
    return (jnp.cos(angle_grid)[:, None, :], jnp.sin(angle_grid)[:, None, :])

def rotate(values, cosine, sine_rows):
    half_size = values.shape[-1] // 2
    first_half = values[..., :half_size]
    second_half = values[..., half_size:]
    return jnp.concatenate([first_half * cosine - second_half * sine_rows, second_half * cosine + first_half * sine_rows], axis=-1)

def unit_rows(values):
    return values * lax.rsqrt(lax.optimization_barrier(jnp.sum(values * values, axis=-1, keepdims=True)) + epsilon)

def sphere(values):
    return values * lax.rsqrt(lax.optimization_barrier(jnp.mean(values * values, axis=-1, keepdims=True)) + epsilon)

def bucket_forward(values, lengths, params):
    w_qkv, w_out, w_gate_up, w_down, s_qk, alpha_attn, alpha_mlp, s_mlp = params
    token_count = values.shape[0]
    doc_ids, position = layout(lengths, token_count)
    place = jnp.arange(token_count, dtype=jnp.int32)
    allowed = (doc_ids[:, None] == doc_ids[None, :]) & (place[None, :] <= place[:, None])
    qkv = low_back(jnp.dot(values, w_qkv.reshape(D, 3 * D), precision=highest)).reshape(token_count, 3, H, DK)
    cosine, sine_rows = angles(position)
    q_hat = low(unit_rows(rotate(qkv[:, 0], cosine, sine_rows)) * s_qk.T)
    k_hat = low(unit_rows(rotate(qkv[:, 1], cosine, sine_rows)) * s_qk.T)
    v_hat = low(qkv[:, 2])

    def one_head(item):
        queries, keys_here, values_here = item
        scores = low_back(jnp.dot(queries, keys_here.T, precision=highest) * math.sqrt(DK))
        scores = jnp.where(allowed, scores, -jnp.inf)
        row_max = lax.optimization_barrier(jnp.max(scores, axis=1, keepdims=True))
        powers = jnp.exp(scores - row_max)
        attn_probs = low(powers / lax.optimization_barrier(jnp.sum(powers, axis=1, keepdims=True)))
        return low(low_back(jnp.dot(attn_probs, values_here, precision=highest)))
    attn_mix = lax.map(jax.checkpoint(one_head), (q_hat.transpose(1, 0, 2), k_hat.transpose(1, 0, 2), v_hat.transpose(1, 0, 2)))
    attn_mix = attn_mix.transpose(1, 0, 2).reshape(token_count, D)
    attn_unit = sphere(low_back(jnp.dot(attn_mix, w_out.T, precision=highest)))
    hidden = sphere(values + alpha_attn.T.reshape(D) * (attn_unit - values))
    gate_up = low_back(jnp.dot(low(hidden), w_gate_up.reshape(D, 2 * FF), precision=highest)).reshape(token_count, 2, FF)
    unit_scales = s_mlp.transpose(1, 2, 0).reshape(2, FF)
    mlp_act = low(gate_up[:, 0] * unit_scales[0] * jax.nn.silu(gate_up[:, 1] * unit_scales[1]))
    mlp_unit = sphere(low_back(jnp.dot(mlp_act, w_down.T, precision=highest)))
    return sphere(hidden + alpha_mlp.T.reshape(D) * (mlp_unit - hidden))

def reference(tokens, w_qkv, w_out, w_gate_up, w_down, s_qk, alpha_attn, alpha_mlp, s_mlp, doc_lengths, grad_out):
    inputs = tokens.astype(jnp.float32)
    weights = (w_qkv.astype(jnp.float32), w_out.astype(jnp.float32), w_gate_up.astype(jnp.float32), w_down.astype(jnp.float32), s_qk, alpha_attn, alpha_mlp, s_mlp)

    def forward(values, *params):

        def one_bucket(item):
            return bucket_forward(item[0], item[1], params)
        outputs = lax.map(jax.checkpoint(one_bucket), (values.reshape(N_DP, TOK_DEV, D), doc_lengths))
        return outputs.reshape(TOKENS, D)
    result, pullback = jax.vjp(forward, inputs, *weights)
    grads = pullback(grad_out.astype(jnp.float32))
    return (result.astype(jnp.bfloat16), grads[0], grads[1], grads[2], grads[3], grads[4], grads[5], grads[6], grads[7], grads[8])
```

```python
import math

import jax
import jax.numpy as jnp
from jax import lax
from jax.sharding import PartitionSpec as P
from jax.experimental import pallas as pl
from jax.experimental.pallas import tpu as pltpu

D = 1024
DK = 64


epsilon = 1e-06
theta_base = 10000.0


LC=math.sqrt(DK)*math.log2(math.e)
NEG=-1e30
def nt(a,b): return lax.dot_general(a,b,(((1,),(1,)),((),())),preferred_element_type=jnp.float32)
def nn(a,b): return jnp.dot(a,b,preferred_element_type=jnp.float32)
def head_mask(x,h):
    lane=lax.broadcasted_iota(jnp.int32,x.shape,1)
    return jnp.where((lane//DK)==(h%2), x, jnp.zeros_like(x))
def attn_fwd_block(i, TB, H, q_ref, k_ref, vT_ref, ob, acc):
    qs=pl.ds(pl.multiple_of(i*TB,TB),TB)
    qz=[head_mask(q_ref[qs,pl.ds((h//2)*128,128)],h) for h in range(H)]
    ones=jnp.ones((16,TB),jnp.bfloat16)
    def tile(h,ks,nk,qsub,bias,tri):
        p2=pl.ds((h//2)*128,128)
        sT=nt(k_ref[ks,p2], qsub)
        x=sT*LC
        if bias is not None: x=x+bias
        if tri:
            r=lax.broadcasted_iota(jnp.int32,x.shape,0); c=lax.broadcasted_iota(jnp.int32,x.shape,1)
            x=jnp.where(r<=c,x,NEG)
        p=jnp.exp2(x).astype(jnp.bfloat16)
        vx=jnp.concatenate([vT_ref[h*DK:(h+1)*DK,ks],jnp.ones((16,nk),jnp.bfloat16)],axis=0)
        return nn(vx,p)
    hb=TB//2
    k0=pl.ds(pl.multiple_of(i*TB,hb),hb); k1=pl.ds(pl.multiple_of(i*TB+hb,hb),hb)
    for h in range(H):
        a0=tile(h,k0,hb,qz[h],None,True)
        a1=tile(h,k1,hb,qz[h][hb:],None,True)
        acc[h,:,0:hb]=a0[:,0:hb]
        acc[h,:,hb:TB]=a0[:,hb:TB]+a1
    def body(j,_):
        ks=pl.ds(pl.multiple_of(j*TB,TB),TB)
        for h in range(H):
            acc[h]+=tile(h,ks,TB,qz[h],ob,False)
        return 0
    lax.fori_loop(0,i,body,0)
def fwd_kernel(ob_ref,q_ref,k_ref,vT_ref,o_ref,ll_ref,acc,oT):
    T,C=q_ref.shape; H=C//DK; TB=T//4
    ob=ob_ref[0]
    def body(i,_):
        attn_fwd_block(i,TB,H,q_ref,k_ref,vT_ref,ob,acc)
        qs=pl.ds(pl.multiple_of(i*TB,TB),TB)
        for h in range(H):
            l=acc[h,DK:DK+1,:]
            oT[h*DK:(h+1)*DK,:]=acc[h,0:DK,:]/l
            ll_ref[pl.ds(h,1),qs]=jnp.log2(l)
        o_ref[qs,:]=oT[...].T.astype(jnp.bfloat16)
        return 0
    lax.fori_loop(0,4,body,0)
def attn_fwd(ob,q,k,vT):
    T,C=q.shape; H=C//DK
    vm=pl.BlockSpec(memory_space=pltpu.VMEM)
    return pl.pallas_call(fwd_kernel,out_shape=[jax.ShapeDtypeStruct((T,C),jnp.bfloat16),jax.ShapeDtypeStruct((8,T),jnp.float32)],
      in_specs=[pl.BlockSpec(memory_space=pltpu.SMEM),vm,vm,vm],out_specs=[vm,vm],
      scratch_shapes=[pltpu.VMEM((H,DK+16,T//4),jnp.float32),pltpu.VMEM((C,T//4),jnp.float32)],
      compiler_params=pltpu.CompilerParams(vmem_limit_bytes=60*2**20))(ob,q,k,vT)
def attn_bwd_block(i,TB,H,q_ref,k_ref,v_ref,kT_ref,g_ref,ll_ref,dl_ref,ob,dqT,dk,dv):
    qs=pl.ds(pl.multiple_of(i*TB,TB),TB); hb=TB//2
    qz=[head_mask(q_ref[qs,pl.ds((h//2)*128,128)],h) for h in range(H)]
    gz=[head_mask(g_ref[qs,pl.ds((h//2)*128,128)],h) for h in range(H)]
    lr=[ll_ref[pl.ds(h,1),qs] for h in range(H)]
    dr=[dl_ref[pl.ds(h,1),qs] for h in range(H)]
    def tile(h,ks,qv,gv,lb,dd,tri):
        p2=pl.ds((h//2)*128,128)
        x=nt(k_ref[ks,p2],qv)*LC-lb
        dp=nt(v_ref[ks,p2],gv)
        if tri:
            r=lax.broadcasted_iota(jnp.int32,x.shape,0); c=lax.broadcasted_iota(jnp.int32,x.shape,1)
            x=jnp.where(r<=c,x,NEG)
        p=jnp.exp2(x)
        ds=(p*(dp-dd)).astype(jnp.bfloat16)
        dvp=nn(p.astype(jnp.bfloat16),gv)
        dkp=nn(ds,qv)
        dqp=nn(kT_ref[h*DK:(h+1)*DK,ks],ds)
        return dqp,dkp,dvp
    k0=pl.ds(pl.multiple_of(i*TB,hb),hb); k1=pl.ds(pl.multiple_of(i*TB+hb,hb),hb)
    for pr in range((H+1)//2):
        p2=pl.ds(pr*128,128)
        dk0=dv0=dk1=dv1=0
        for h in range(2*pr,min(2*pr+2,H)):
            a,b,c=tile(h,k0,qz[h],gz[h],lr[h],dr[h],True)
            a1,b1,c1=tile(h,k1,qz[h][hb:],gz[h][hb:],lr[h][:,hb:],dr[h][:,hb:],True)
            hs=slice(h*DK,(h+1)*DK)
            dqT[hs,0:hb]=a[:,0:hb]; dqT[hs,hb:TB]=a[:,hb:]+a1
            dk0+=b; dv0+=c; dk1+=b1; dv1+=c1
        dk[k0,p2]=dk0; dv[k0,p2]=dv0; dk[k1,p2]=dk1; dv[k1,p2]=dv1
    lo=[l-ob for l in lr]
    def body(j,_):
        ks=pl.ds(pl.multiple_of(j*TB,TB),TB)
        for pr in range((H+1)//2):
            p2=pl.ds(pr*128,128)
            dka=dva=0
            for h in range(2*pr,min(2*pr+2,H)):
                a,b,c=tile(h,ks,qz[h],gz[h],lo[h],dr[h],False)
                dqT[h*DK:(h+1)*DK,:]+=a
                dka+=b; dva+=c
            dk[ks,p2]+=dka; dv[ks,p2]+=dva
        return 0
    lax.fori_loop(0,i,body,0)
def bwd_kernel(ob_ref,q_ref,k_ref,v_ref,kT_ref,g_ref,ll_ref,dl_ref,dq_ref,dk_ref,dv_ref,dqT):
    T,C=q_ref.shape; H=C//DK; TB=T//4
    ob=ob_ref[0]
    def body(i,_):
        attn_bwd_block(i,TB,H,q_ref,k_ref,v_ref,kT_ref,g_ref,ll_ref,dl_ref,ob,dqT,dk_ref,dv_ref)
        dq_ref[pl.ds(pl.multiple_of(i*TB,TB),TB),:]=dqT[...].T*8.0
        return 0
    lax.fori_loop(0,4,body,0)
    dk_ref[...]=dk_ref[...]*8.0
def attn_bwd(ob,q,k,v,kT,g,ll,dl):
    T,C=q.shape; H=C//DK
    vm=pl.BlockSpec(memory_space=pltpu.VMEM)
    o=jax.ShapeDtypeStruct((T,C),jnp.float32)
    return pl.pallas_call(bwd_kernel,out_shape=[o,o,o],
      in_specs=[pl.BlockSpec(memory_space=pltpu.SMEM)]+[vm]*7,out_specs=[vm]*3,
      scratch_shapes=[pltpu.VMEM((C,T//4),jnp.float32)],
      compiler_params=pltpu.CompilerParams(vmem_limit_bytes=60*2**20))(ob,q,k,v,kT,g,ll,dl)


def layout(lengths, token_count):
    starts = jnp.cumsum(lengths) - lengths
    place = jnp.arange(token_count, dtype=jnp.int32)
    doc_ids = jnp.sum((place[:, None] >= starts[None, 1:]).astype(jnp.int32), axis=1)
    picked = (doc_ids[:, None] == jnp.arange(lengths.shape[0], dtype=jnp.int32)[None, :]).astype(
        jnp.int32
    )
    position = place - jnp.sum(picked * starts[None, :], axis=1)
    return (doc_ids, position)


def angles(position):
    half_size = DK // 2
    frequency = theta_base ** (-(2.0 / DK) * jnp.arange(half_size, dtype=jnp.float32))
    angle_grid = position.astype(jnp.float32)[:, None] * frequency[None, :]
    return (jnp.cos(angle_grid)[:, None, :], jnp.sin(angle_grid)[:, None, :])


def rotate(values, cosine, sine_rows):
    half_size = values.shape[-1] // 2
    first_half = values[..., :half_size]
    second_half = values[..., half_size:]
    return jnp.concatenate(
        [
            first_half * cosine - second_half * sine_rows,
            second_half * cosine + first_half * sine_rows,
        ],
        axis=-1,
    )


def rotate_back(grads, cosine, sine_rows):
    half_size = grads.shape[-1] // 2
    first_half = grads[..., :half_size]
    second_half = grads[..., half_size:]
    return jnp.concatenate(
        [
            first_half * cosine + second_half * sine_rows,
            second_half * cosine - first_half * sine_rows,
        ],
        axis=-1,
    )


def unit_back(grad_unit, unit, inverse):
    return inverse * (grad_unit - unit * jnp.sum(grad_unit * unit, axis=-1, keepdims=True))


def token_total(values):
    return lax.psum(jnp.sum(values, axis=1), "mp")


def sphere_scale(values):
    return lax.rsqrt(token_total(values * values)[:, None] / D + epsilon)


def sphere_back(grads, unit, scale):
    return scale * (grads - unit * token_total(grads * unit)[:, None] / D)


def widen(values):
    return lax.all_gather(values, "mp", axis=1, tiled=True)


def widen_grad(values):
    return lax.all_gather(values, "mp", axis=1, tiled=True)


def narrow(partial_value):
    return lax.psum_scatter(
        partial_value.astype(jnp.bfloat16), "mp", scatter_dimension=1, tiled=True
    ).astype(jnp.float32)


def narrow_grad(partial_value):
    return lax.psum_scatter(
        partial_value.astype(jnp.bfloat16), "mp", scatter_dimension=1, tiled=True
    ).astype(jnp.float32)


def contract_last(left, right):
    return lax.dot_general(
        left, right, (((1,), (1,)), ((), ())), preferred_element_type=jnp.float32
    )


def project(tokens_full, w_qkv_full, position, scale_qk):
    token_count = tokens_full.shape[0]
    local_heads = scale_qk.shape[0]
    qkv = jnp.dot(
        tokens_full, w_qkv_full.reshape(w_qkv_full.shape[0], -1), preferred_element_type=jnp.float32
    )
    qkv = qkv.reshape(token_count, 3, local_heads, DK)
    cosine, sine_rows = angles(position)
    turned_q = rotate(qkv[:, 0], cosine, sine_rows)
    turned_k = rotate(qkv[:, 1], cosine, sine_rows)
    inverse_q = lax.rsqrt(jnp.sum(turned_q * turned_q, axis=-1, keepdims=True) + epsilon)
    inverse_k = lax.rsqrt(jnp.sum(turned_k * turned_k, axis=-1, keepdims=True) + epsilon)
    unit_q = turned_q * inverse_q
    unit_k = turned_k * inverse_k
    q_hat = (unit_q * scale_qk).astype(jnp.bfloat16)
    k_hat = (unit_k * scale_qk).astype(jnp.bfloat16)
    v_hat = qkv[:, 2].astype(jnp.bfloat16)
    return (q_hat, k_hat, v_hat, (unit_q, inverse_q, unit_k, inverse_k))


def feed(hidden_full, w_gate_up_full, unit_scales):
    token_count = hidden_full.shape[0]
    gate_up = jnp.dot(
        hidden_full,
        w_gate_up_full.reshape(w_gate_up_full.shape[0], -1),
        preferred_element_type=jnp.float32,
    )
    gate_up = gate_up.reshape(token_count, 2, -1)
    up_part = gate_up[:, 0] * unit_scales[0]
    gate_part = gate_up[:, 1] * unit_scales[1]
    mlp_act = (up_part * jax.nn.silu(gate_part)).astype(jnp.bfloat16)
    return (gate_up, mlp_act)


def on_device(
    tokens,
    w_qkv,
    w_out,
    w_gate_up,
    w_down,
    s_qk,
    alpha_attn,
    alpha_mlp,
    s_mlp,
    doc_lengths,
    grad_out,
):
    token_count = tokens.shape[0]
    local_heads = s_qk.shape[1]
    doc_ids, position = layout(doc_lengths[0], token_count)
    scale_qk = s_qk.T
    keep_attn = alpha_attn.T.reshape(-1)
    keep_mlp = alpha_mlp.T.reshape(-1)
    unit_scales = s_mlp.transpose(1, 2, 0).reshape(2, -1)
    fwd_weights = (
        lax.all_gather(w_qkv, "dp", axis=0, tiled=True),
        lax.all_gather(w_out, "dp", axis=0, tiled=True),
        lax.all_gather(w_gate_up, "dp", axis=0, tiled=True),
        lax.all_gather(w_down, "dp", axis=0, tiled=True),
    )
    inputs = tokens.astype(jnp.float32)
    tokens_full = widen(tokens)
    q_hat, k_hat, v_hat, unit_parts = project(tokens_full, fwd_weights[0], position, scale_qk)
    q2, k2, v2 = (t.reshape(token_count, -1) for t in (q_hat, k_hat, v_hat))
    off_bias = jnp.where(doc_lengths[0, 0] == token_count, 0.0, NEG).astype(jnp.float32).reshape(1)
    attn_mix, log_total = attn_fwd(off_bias, q2, k2, v2.T)
    attn_branch = lax.psum_scatter(
        contract_last(attn_mix, fwd_weights[1]).astype(jnp.bfloat16),
        "mp",
        scatter_dimension=1,
        tiled=True,
    ).astype(jnp.float32)
    attn_scale = sphere_scale(attn_branch)
    attn_unit = attn_branch * attn_scale
    first_mix = inputs + keep_attn * (attn_unit - inputs)
    first_scale = sphere_scale(first_mix)
    hidden = first_mix * first_scale
    hidden_low = hidden.astype(jnp.bfloat16)
    hidden_full = widen(hidden_low)
    gate_up, mlp_act = feed(hidden_full, fwd_weights[2], unit_scales)
    mlp_branch = narrow(contract_last(mlp_act, fwd_weights[3]))
    mlp_scale = sphere_scale(mlp_branch)
    mlp_unit = mlp_branch * mlp_scale
    second_mix = hidden + keep_mlp * (mlp_unit - hidden)
    second_scale = sphere_scale(second_mix)
    result = second_mix * second_scale
    back_weights = fwd_weights
    tokens_back = tokens_full
    hidden_back = hidden_full
    cotangent = grad_out.astype(jnp.float32)
    grad_second = sphere_back(cotangent, result, second_scale)
    grad_keep_mlp = jnp.sum(grad_second * (mlp_unit - hidden), axis=0)
    grad_mlp_unit = grad_second * keep_mlp
    grad_hidden = grad_second * (1.0 - keep_mlp)
    grad_mlp_branch = sphere_back(grad_mlp_unit, mlp_unit, mlp_scale).astype(jnp.bfloat16)
    grad_mlp_full = widen_grad(grad_mlp_branch)
    grad_act = jnp.dot(grad_mlp_full, back_weights[3], preferred_element_type=jnp.float32)
    grad_w_down = jnp.einsum(
        "te,tf->ef", grad_mlp_full, mlp_act, preferred_element_type=jnp.float32
    )
    up_part = gate_up[:, 0] * unit_scales[0]
    gate_part = gate_up[:, 1] * unit_scales[1]
    gate_sigmoid = jax.nn.sigmoid(gate_part)
    grad_up = grad_act * gate_part * gate_sigmoid
    grad_gate = grad_act * up_part * gate_sigmoid * (1.0 + gate_part * (1.0 - gate_sigmoid))
    grad_scales = jnp.stack(
        [jnp.sum(grad_up * gate_up[:, 0], axis=0), jnp.sum(grad_gate * gate_up[:, 1], axis=0)]
    )
    grad_gate_up = jnp.stack([grad_up * unit_scales[0], grad_gate * unit_scales[1]], axis=1).astype(
        jnp.bfloat16
    )
    grad_w_gate_up = jnp.einsum(
        "td,tgf->dgf", hidden_back, grad_gate_up, preferred_element_type=jnp.float32
    )
    gate_up_rows = back_weights[2].reshape(back_weights[2].shape[0], -1)
    grad_hidden = grad_hidden + narrow_grad(
        contract_last(grad_gate_up.reshape(token_count, -1), gate_up_rows)
    )
    scale_rows = grad_scales.reshape(2, local_heads, -1).transpose(2, 0, 1)
    keep_mlp_rows = grad_keep_mlp.reshape(local_heads, -1).T
    grad_first = sphere_back(grad_hidden, hidden, first_scale)
    grad_keep_attn = jnp.sum(grad_first * (attn_unit - inputs), axis=0)
    grad_attn_unit = grad_first * keep_attn
    grad_inputs = grad_first * (1.0 - keep_attn)
    grad_attn_branch = sphere_back(grad_attn_unit, attn_unit, attn_scale).astype(jnp.bfloat16)
    grad_attn_full = widen_grad(grad_attn_branch)
    grad_mix = jnp.dot(grad_attn_full, back_weights[1], preferred_element_type=jnp.float32).astype(
        jnp.bfloat16
    )
    grad_w_out = jnp.einsum(
        "te,tf->ef", grad_attn_full, attn_mix, preferred_element_type=jnp.float32
    )
    row_dot = jnp.sum(
        (grad_mix.astype(jnp.float32) * attn_mix.astype(jnp.float32)).reshape(
            token_count, local_heads, DK
        ),
        axis=2,
    ).T
    row_dot = jnp.pad(row_dot, ((0, 8 - local_heads), (0, 0)))
    grad_queries, grad_keys, grad_values = (
        t.reshape(q_hat.shape)
        for t in attn_bwd(off_bias, q2, k2, v2, k2.T, grad_mix, log_total, row_dot)
    )
    unit_q, inverse_q, unit_k, inverse_k = unit_parts
    grad_scale_qk = jnp.sum(grad_queries * unit_q + grad_keys * unit_k, axis=0)
    cosine, sine_rows = angles(position)
    grad_q = rotate_back(unit_back(grad_queries * scale_qk, unit_q, inverse_q), cosine, sine_rows)
    grad_k = rotate_back(unit_back(grad_keys * scale_qk, unit_k, inverse_k), cosine, sine_rows)
    grad_qkv = (
        jnp.stack([grad_q, grad_k, grad_values], axis=1)
        .reshape(token_count, -1)
        .astype(jnp.bfloat16)
    )
    qkv_rows = back_weights[0].reshape(back_weights[0].shape[0], -1)
    grad_w_qkv = jnp.einsum(
        "td,tc->dc", tokens_back, grad_qkv, preferred_element_type=jnp.float32
    ).reshape(back_weights[0].shape)
    grad_inputs = grad_inputs + narrow_grad(contract_last(grad_qkv, qkv_rows))
    keep_attn_rows = grad_keep_attn.reshape(local_heads, -1).T
    scale_qk_rows = grad_scale_qk.T
    summed = (
        lax.psum_scatter(
            grad_w_qkv.astype(jnp.bfloat16), "dp", scatter_dimension=0, tiled=True
        ).astype(jnp.float32),
        lax.psum_scatter(
            grad_w_out.astype(jnp.bfloat16), "dp", scatter_dimension=0, tiled=True
        ).astype(jnp.float32),
        lax.psum_scatter(
            grad_w_gate_up.astype(jnp.bfloat16), "dp", scatter_dimension=0, tiled=True
        ).astype(jnp.float32),
        lax.psum_scatter(
            grad_w_down.astype(jnp.bfloat16), "dp", scatter_dimension=0, tiled=True
        ).astype(jnp.float32),
        lax.psum_scatter(
            scale_qk_rows.astype(jnp.bfloat16), "dp", scatter_dimension=0, tiled=True
        ).astype(jnp.float32),
        lax.psum_scatter(
            keep_attn_rows.astype(jnp.bfloat16), "dp", scatter_dimension=0, tiled=True
        ).astype(jnp.float32),
        lax.psum_scatter(
            keep_mlp_rows.astype(jnp.bfloat16), "dp", scatter_dimension=0, tiled=True
        ).astype(jnp.float32),
        lax.psum_scatter(
            scale_rows.astype(jnp.bfloat16), "dp", scatter_dimension=0, tiled=True
        ).astype(jnp.float32),
    )
    return (
        result.astype(jnp.bfloat16),
        grad_inputs,
        summed[0],
        summed[1],
        summed[2],
        summed[3],
        summed[4],
        summed[5],
        summed[6],
        summed[7],
    )


def solution(mesh):
    placed = (
        P("dp", "mp"),
        P("dp", None, "mp"),
        P("dp", "mp"),
        P("dp", None, "mp"),
        P("dp", "mp"),
        P(None, "mp"),
        P(None, "mp"),
        P(None, "mp"),
        P(None, None, "mp"),
        P("dp", None),
        P("dp", "mp"),
    )
    return jax.shard_map(
        on_device,
        mesh=mesh,
        in_specs=placed,
        out_specs=(
            P("dp", "mp"),
            P("dp", "mp"),
            P("dp", None, "mp"),
            P("dp", "mp"),
            P("dp", None, "mp"),
            P("dp", "mp"),
            P("dp", "mp"),
            P("dp", "mp"),
            P("dp", "mp"),
            P("dp", None, "mp"),
        ),
        check_vma=False,
    )
```

```python
import functools
import math

import jax
import jax.numpy as jnp
from jax import lax
from jax.experimental import pallas as pl
from jax.experimental.pallas import tpu as pltpu
from jax.sharding import PartitionSpec as P

DK = 64
epsilon = 1e-06
theta_base = 10000.0


def layout(lengths, token_count):
    starts = jnp.cumsum(lengths) - lengths
    place = jnp.arange(token_count, dtype=jnp.int32)
    doc_ids = jnp.sum((place[:, None] >= starts[None, 1:]).astype(jnp.int32), axis=1)
    picked = (doc_ids[:, None] == jnp.arange(lengths.shape[0], dtype=jnp.int32)[None, :]).astype(
        jnp.int32
    )
    position = place - jnp.sum(picked * starts[None, :], axis=1)
    return (doc_ids, position)


def rotate_back(grads, cosine, sine_rows):
    half_size = grads.shape[-1] // 2
    first_half = grads[..., :half_size]
    second_half = grads[..., half_size:]
    return jnp.concatenate(
        [
            first_half * cosine + second_half * sine_rows,
            second_half * cosine - first_half * sine_rows,
        ],
        axis=-1,
    )


def unit_back(grad_unit, unit, inverse):
    return inverse * (grad_unit - unit * jnp.sum(grad_unit * unit, axis=-1, keepdims=True))


LC=math.sqrt(DK)*math.log2(math.e)
NEG=-1e30
def nt(a,b): return lax.dot_general(a,b,(((1,),(1,)),((),())),preferred_element_type=jnp.float32)
def nn(a,b): return jnp.dot(a,b,preferred_element_type=jnp.float32)
def head_mask(x,h):
    lane=lax.broadcasted_iota(jnp.int32,x.shape,1)
    return jnp.where((lane//DK)==(h%2), x, jnp.zeros_like(x))
def attn_fwd_block(i, TB, H, q_ref, q0, k_ref, k0c, vT_ref, ob, acc):
    qs=pl.ds(pl.multiple_of(i*TB,TB),TB)
    qz=[head_mask(q_ref[qs,pl.ds(q0+(h//2)*128,128)],h) for h in range(H)]
    def tile(h,ks,nk,qsub,bias,tri):
        sT=nt(k_ref[ks,pl.ds(k0c+(h//2)*128,128)], qsub)
        x=sT*LC
        if bias is not None: x=x+bias
        if tri:
            r=lax.broadcasted_iota(jnp.int32,x.shape,0); c=lax.broadcasted_iota(jnp.int32,x.shape,1)
            x=jnp.where(r<=c,x,NEG)
        p=jnp.exp2(x).astype(jnp.bfloat16)
        vx=jnp.concatenate([vT_ref[h*DK:(h+1)*DK,ks],jnp.ones((16,nk),jnp.bfloat16)],axis=0)
        return nn(vx,p)
    hb=TB//2
    k0=pl.ds(pl.multiple_of(i*TB,hb),hb); k1=pl.ds(pl.multiple_of(i*TB+hb,hb),hb)
    for h in range(H):
        a0=tile(h,k0,hb,qz[h],None,True)
        a1=tile(h,k1,hb,qz[h][hb:],None,True)
        acc[h,:,0:hb]=a0[:,0:hb]
        acc[h,:,hb:TB]=a0[:,hb:TB]+a1
    def body(j,_):
        ks=pl.ds(pl.multiple_of(j*TB,TB),TB)
        for h in range(H):
            acc[h]+=tile(h,ks,TB,qz[h],ob,False)
        return 0
    lax.fori_loop(0,i,body,0)
def attn_bwd_block(i,TB,H,q_ref,k_ref,v_ref,kT_ref,g_ref,ll_ref,dl_ref,ob,dqT,dk,dv):
    qs=pl.ds(pl.multiple_of(i*TB,TB),TB); hb=TB//2
    qz=[head_mask(q_ref[qs,pl.ds((h//2)*128,128)],h) for h in range(H)]
    gz=[head_mask(g_ref[qs,pl.ds((h//2)*128,128)],h) for h in range(H)]
    lr=[ll_ref[pl.ds(h,1),qs] for h in range(H)]
    dr=[dl_ref[pl.ds(h,1),qs] for h in range(H)]
    def tile(h,ks,qv,gv,lb,dd,tri):
        p2=pl.ds((h//2)*128,128)
        x=nt(k_ref[ks,p2],qv)*LC-lb
        dp=nt(v_ref[ks,p2],gv)
        if tri:
            r=lax.broadcasted_iota(jnp.int32,x.shape,0); c=lax.broadcasted_iota(jnp.int32,x.shape,1)
            x=jnp.where(r<=c,x,NEG)
        p=jnp.exp2(x)
        ds=(p*(dp-dd)).astype(jnp.bfloat16)
        dvp=nn(p.astype(jnp.bfloat16),gv)
        dkp=nn(ds,qv)
        dqp=nn(kT_ref[h*DK:(h+1)*DK,ks],ds)
        return dqp,dkp,dvp
    k0=pl.ds(pl.multiple_of(i*TB,hb),hb); k1=pl.ds(pl.multiple_of(i*TB+hb,hb),hb)
    for pr in range((H+1)//2):
        p2=pl.ds(pr*128,128)
        dk0=dv0=dk1=dv1=0
        for h in range(2*pr,min(2*pr+2,H)):
            a,b,c=tile(h,k0,qz[h],gz[h],lr[h],dr[h],True)
            a1,b1,c1=tile(h,k1,qz[h][hb:],gz[h][hb:],lr[h][:,hb:],dr[h][:,hb:],True)
            hs=slice(h*DK,(h+1)*DK)
            dqT[hs,0:hb]=a[:,0:hb]; dqT[hs,hb:TB]=a[:,hb:]+a1
            dk0+=b; dv0+=c; dk1+=b1; dv1+=c1
        dk[k0,p2]=dk0; dv[k0,p2]=dv0; dk[k1,p2]=dk1; dv[k1,p2]=dv1
    lo=[l-ob for l in lr]
    def body(j,_):
        ks=pl.ds(pl.multiple_of(j*TB,TB),TB)
        for pr in range((H+1)//2):
            p2=pl.ds(pr*128,128)
            dka=dva=0
            for h in range(2*pr,min(2*pr+2,H)):
                a,b,c=tile(h,ks,qz[h],gz[h],lo[h],dr[h],False)
                dqT[h*DK:(h+1)*DK,:]+=a
                dka+=b; dva+=c
            dk[ks,p2]+=dka; dv[ks,p2]+=dva
        return 0
    lax.fori_loop(0,i,body,0)
def bwd_kernel(ob_ref,q_ref,k_ref,v_ref,kT_ref,g_ref,ll_ref,dl_ref,dq_ref,dk_ref,dv_ref,dqT):
    T,C=q_ref.shape; H=C//DK; TB=T//4
    ob=ob_ref[0]
    def body(i,_):
        attn_bwd_block(i,TB,H,q_ref,k_ref,v_ref,kT_ref,g_ref,ll_ref,dl_ref,ob,dqT,dk_ref,dv_ref)
        dq_ref[pl.ds(pl.multiple_of(i*TB,TB),TB),:]=dqT[...].T*8.0
        return 0
    lax.fori_loop(0,4,body,0)
    dk_ref[...]=dk_ref[...]*8.0
def attn_bwd(ob,q,k,v,kT,g,ll,dl):
    T,C=q.shape; H=C//DK
    vm=pl.BlockSpec(memory_space=pltpu.VMEM)
    o=jax.ShapeDtypeStruct((T,C),jnp.float32)
    return pl.pallas_call(bwd_kernel,out_shape=[o,o,o],
      in_specs=[pl.BlockSpec(memory_space=pltpu.SMEM)]+[vm]*7,out_specs=[vm]*3,
      scratch_shapes=[pltpu.VMEM((C,T//4),jnp.float32)],
      compiler_params=pltpu.CompilerParams(vmem_limit_bytes=60*2**20))(ob,q,k,v,kT,g,ll,dl)


MESH = pl.DeviceIdType.MESH
F32, BF = jnp.float32, jnp.bfloat16


class Sizes:
    def __init__(self, mesh_shape, T, C, CF, F, pieces):
        self.mp, self.dp = mesh_shape["mp"], mesh_shape["dp"]
        self.ny = self.mp // 2
        self.A = 4 if self.dp % 4 == 0 else 1
        self.B = self.dp // self.A
        self.T, self.C, self.CF, self.F = T, C, CF, F
        self.D = CF * self.mp
        self.H = C // DK
        self.nc = pieces
        self.TB = T // pieces
        self.TH = self.TB // 2
        self.R = self.D // self.dp


def place():
    return lax.axis_index("dp"), lax.axis_index("mp")


def remote(src, dst, ss, rs, dev):
    return pltpu.make_async_remote_copy(
        src, dst, send_sem=ss, recv_sem=rs, device_id=dev, device_id_type=MESH
    )


def local(src, dst, sem):
    return pltpu.make_async_copy(src, dst, sem)


def rows_at(start, size):
    return pl.ds(pl.multiple_of(start, size), size)


def loop(n, fn):
    def body(i, carry):
        fn(i)
        return carry

    lax.fori_loop(0, n, body, 0)


def fold(x):
    return jnp.sum(x.reshape(x.shape[0] // 8, 8, x.shape[1]), axis=0)


def mean_sq(x, D):
    return lax.rsqrt(jnp.sum(x * x, axis=1, keepdims=True) * (1.0 / D) + epsilon)


def split_dot(x, ones):
    hi = x.astype(BF)
    return nn(hi, ones) + nn((x - hi.astype(F32)).astype(BF), ones)


def head_ones():
    i = lax.broadcasted_iota(jnp.int32, (128, 128), 0) // DK
    j = lax.broadcasted_iota(jnp.int32, (128, 128), 1) // DK
    return jnp.where(i == j, 1.0, 0.0).astype(BF)


def turn(x, cosine, sine, sign):
    lane = lax.broadcasted_iota(jnp.int32, x.shape, 1)
    first = (lane % DK) < DK // 2
    other = jnp.where(first, -pltpu.roll(x, 128 - DK // 2, 1), pltpu.roll(x, DK // 2, 1))
    return x * cosine + sign * other * sine


def front(
    z,
    ob_ref, tokens, gout, wq, wo, wg, wd, alpha, cos, sin, sq, sml,
    out, q_o, k_o, v_o, qr_o, kr_o, attn_o, ll_o, tokf, gba_o, gres_o, wqf, wof, gwd_o, gwg_o, ga_o, gs_o, goh,
    tokv, wqv, wov, wgv, wdv, gml, act, gu, gba, vT, rot, attn, ll, acc, oT,
    sy1, ry1, sy2, ry2, sy3, ry3, rc, sc, own, tokh, ghid, gst, fst, wst, alv, gacc, gsacc,
    tok_s, tok_r, w_s, w_r, al_s, al_r, go_s, go_r, ex_s, ex_r, y_s, y_r, hc_s, hc_r, out_s, out_r, lsem,
):
    T, C, CF, F, D, H = z.T, z.C, z.CF, z.F, z.D, z.H
    nc, TB, TH, R, A, B, ny, mp = z.nc, z.TB, z.TH, z.R, z.A, z.B, z.ny, z.mp
    d, m = place()
    a, b = d // B, d % B
    y, core = m // 2, m % 2
    mate = 1 - core
    peer = (d, y * 2 + mate)

    def ypeer(k, cc):
        return (d, ((y + k) % ny) * 2 + cc)

    zpeer = lambda k: (((a + k) % A) * B + b, m)
    xpeer = lambda k: (a * B + (b + k) % B, m)
    others = [peer] + [ypeer(k, cc) for k in range(1, ny) for cc in (core, mate)]
    everyone = others + [zpeer(k) for k in range(1, A)] + [xpeer(k) for k in range(1, B)]
    bar = pltpu.get_barrier_semaphore()
    for dev in everyone:
        pl.semaphore_signal(bar, 1, device_id=dev, device_id_type=MESH)
    pl.semaphore_wait(bar, len(everyone))

    ob = ob_ref[0]
    feat = lambda mm: pl.ds(pl.multiple_of(mm * CF, CF), CF)
    mine = feat(m)


    def tok_own(c, i, dev):
        r = rows_at(c * TB, TB)
        return remote(tokens.at[r], tokv.at[r, mine], tok_s.at[c, i], tok_r.at[c, i], dev)

    def tok_got(c, i, mm):
        r = rows_at(c * TB, TB)
        return remote(tokv.at[r, feat(mm)], tokv.at[r, feat(mm)], tok_s.at[c, i], tok_r.at[c, i], peer)

    def start_tok(i):
        c = nc - 1 - i
        for k in range(1, ny):
            tok_own(c, k, ypeer(k, core)).start()
        tok_own(c, 0, peer).start()

    weights = [(wq, wqv), (wo, wov), (wg, wgv), (wd, wdv)]

    def shard(aa, bb):
        return rows_at((aa * B + bb) * R, R)

    def w_z(w, k):
        src, dst = weights[w]
        return remote(src, dst.at[shard(a, b)], w_s.at[w, k - 1], w_r.at[w, k - 1], zpeer(k))

    def w_z_got(w, k):
        src, dst = weights[w]
        return remote(src, dst.at[shard((a - k + A) % A, b)], w_s.at[w, k - 1], w_r.at[w, k - 1], zpeer(k))

    def w_x(w, ks, kb):
        src, dst = weights[w]
        i = A - 1 + ks * (B - 1) + kb - 1
        r = shard((a - ks + A) % A, b)
        return remote(src if ks == 0 else dst.at[r], dst.at[r], w_s.at[w, i], w_r.at[w, i], xpeer(kb))

    def w_x_got(w, ks, kb):
        src, dst = weights[w]
        i = A - 1 + ks * (B - 1) + kb - 1
        r = shard((a - ks + A) % A, (b - kb + B) % B)
        return remote(src, dst.at[r], w_s.at[w, i], w_r.at[w, i], xpeer(kb))

    def w_local(w):
        src, dst = weights[w]
        return local(src, dst.at[shard(a, b)], lsem.at[w])

    def w_start(w):
        for k in range(1, A):
            w_z(w, k).start()
        for kb in range(1, B):
            w_x(w, 0, kb).start()
        w_local(w).start()

    def w_forward(w):
        for k in range(1, A):
            w_z_got(w, k).wait_recv()
            for kb in range(1, B):
                w_x(w, k, kb).start()

    def w_finish(w):
        for ks in range(A):
            for kb in range(1, B):
                w_x_got(w, ks, kb).wait_recv()
        for k in range(1, A):
            w_z(w, k).wait_send()
        for ks in range(A):
            for kb in range(1, B):
                w_x(w, ks, kb).wait_send()
        w_local(w).wait()

    w_start(0)
    loop(nc, start_tok)
    tok_local = local(tokens, tokv.at[:, mine], lsem.at[4])
    tok_local.start()
    al_local = local(alpha, alv.at[:, mine], lsem.at[5])
    al_local.start()
    al_copies = [
        remote(alpha, alv.at[:, mine], al_s.at[i], al_r.at[i], dev) for i, dev in enumerate(others)
    ]
    for cp in al_copies:
        cp.start()
    w_start(1)

    def pass_tok(i):
        c = nc - 1 - i
        for k in range(1, ny):
            src = ((y - k + ny) % ny) * 2 + core
            tok_got(c, k, src).wait_recv()
            tok_got(c, ny + k - 1, src).start()

    half_way = nc // 2
    loop(half_way, pass_tok)
    w_forward(0)
    w_start(2)
    loop(nc - half_way, lambda i: pass_tok(i + half_way))

    def end_tok(i):
        c = nc - 1 - i
        tok_got(c, 0, y * 2 + mate).wait_recv()
        for k in range(1, ny):
            src = ((y - k + ny) % ny) * 2 + mate
            tok_got(c, ny + k - 1, src).wait_recv()

    loop(nc, end_tok)

    def tok_sent(i):
        c = nc - 1 - i
        tok_own(c, 0, peer).wait_send()
        for k in range(1, ny):
            tok_own(c, k, ypeer(k, core)).wait_send()
            tok_got(c, ny + k - 1, ((y - k + ny) % ny) * 2 + core).wait_send()

    loop(nc, tok_sent)
    tok_local.wait()
    w_forward(1)
    w_finish(0)
    w_start(3)

    go4 = gout

    def go_copy(i, dev, cc):
        return remote(go4.at[:, cc], goh.at[:, :, mine], go_s.at[i], go_r.at[i], dev)

    go_copies = [go_copy(0, peer, mate)]
    i = 1
    for k in range(1, ny):
        for cc in (core, mate):
            go_copies.append(go_copy(i, ypeer(k, cc), cc))
            i += 1
    go_local = local(go4.at[:, core], goh.at[:, :, mine], lsem.at[6])
    go_local.start()
    for cp in go_copies:
        cp.start()

    ones = head_ones()
    mask_q = gml

    def project_rows(i):
        r = rows_at(i * TB, TB)
        x = tokv[r, :]
        cs, sn = cos[r, :], sin[r, :]
        for part in range(2):
            for pr in range(C // 128):
                cols = slice(part * C + pr * 128, part * C + pr * 128 + 128)
                t = turn(nn(x, wqv[:, cols]), cs, sn, 1.0)
                rot[part, r, pr * 128 : pr * 128 + 128] = t.astype(BF)
                inv = lax.rsqrt(split_dot(t * t, ones) + epsilon)
                mask_q[r, cols] = (t * inv * sq[:, pr * 128 : pr * 128 + 128]).astype(BF)
        v = nn(x, wqv[:, 2 * C : 3 * C])
        mask_q[r, 2 * C : 3 * C] = v.astype(BF)
        vT[:, r] = v.T.astype(BF)

    loop(nc, project_rows)
    save_tok = local(tokv, tokf, lsem.at[4])
    save_tok.start()
    saves = [
        local(mask_q.at[:, 0:C], q_o, lsem.at[7]),
        local(mask_q.at[:, C : 2 * C], k_o, lsem.at[8]),
        local(mask_q.at[:, 2 * C : 3 * C], v_o, lsem.at[9]),
        local(rot.at[0], qr_o, lsem.at[10]),
        local(rot.at[1], kr_o, lsem.at[11]),
        local(wqv, wqf, lsem.at[12]),
    ]
    for cp in saves:
        cp.start()
    w_finish(1)

    def exchange(e, c, part, sy, ry):
        mate_rows = c * TB + mate * TH
        own_rows = c * TB + core * TH
        NJ = 256

        def give(j):
            cols = rows_at(j * NJ, NJ)
            sc[:, cols] = part(rows_at(mate_rows, TH), cols).astype(BF)

        loop(D // NJ, give)
        cp = remote(sc, rc.at[c], ex_s.at[e, c], ex_r.at[e, c], peer)
        cp.start()

        def keep(j):
            cols = rows_at(j * NJ, NJ)
            own[:, cols] = part(rows_at(own_rows, TH), cols)

        loop(D // NJ, keep)
        cp.wait()

        def add(t):
            r = rows_at(t * 32, 32)
            sy[c, r, :] = (own[r, :] + rc[c, r, :].astype(F32)).astype(BF)

        loop(TH // 32, add)
        for k in range(1, ny):
            remote(
                sy.at[c], ry.at[k - 1, c], y_s.at[e, c, k - 1], y_r.at[e, c, k - 1], ypeer(k, core)
            ).start()

    def landed(e, c, sy, ry):
        for k in range(1, ny):
            remote(
                sy.at[c], ry.at[k - 1, c], y_s.at[e, c, k - 1], y_r.at[e, c, k - 1], ypeer(k, core)
            ).wait()

    def total(c, r, sy, ry):
        t = sy[c, r, :].astype(F32)
        for k in range(ny - 1):
            t = t + ry[k, c, r, :].astype(F32)
        return t

    def share(e, c, buf):
        own_rows = rows_at(c * TB + core * TH, TH)
        return remote(buf.at[own_rows], buf.at[own_rows], hc_s.at[e, c], hc_r.at[e, c], peer)

    def attend_chunk(i):
        c = nc - 1 - i
        attn_fwd_block(c, TB, H, mask_q, 0, mask_q, C, vT, ob, acc)
        r = rows_at(c * TB, TB)
        for h in range(H):
            l = acc[h, DK : DK + 1, :]
            oT[h * DK : (h + 1) * DK, :] = acc[h, 0:DK, :] / l
            ll[pl.ds(h, 1), r] = jnp.log2(l)
        attn[r, :] = oT[...].T.astype(BF)

        def part(rr, cols):
            return nt(attn[rr, :], wov[cols, :])

        @pl.when(i == 0)
        def _():
            save_tok.wait()

        exchange(0, c, part, sy1, ry1)

    ll[...] = jnp.zeros_like(ll)
    loop(nc, attend_chunk)
    save_attn = local(attn, attn_o, lsem.at[13])
    save_attn.start()
    save_ll = local(ll, ll_o, lsem.at[14])
    save_ll.start()
    save_wo = local(wov, wof, lsem.at[15])
    save_wo.start()
    for cp in saves:
        cp.wait()
    al_local.wait()
    for cp in al_copies:
        cp.wait()
    w_forward(2)
    w_forward(3)
    w_finish(2)
    w_finish(3)

    RT = 32
    gacc[...] = jnp.zeros_like(gacc)
    gsacc[...] = jnp.zeros_like(gsacc)

    def feed_chunk(i):
        c = nc - 1 - i
        landed(0, c, sy1, ry1)
        base = c * TB + core * TH

        def rows(t):
            r = rows_at(t * RT, RT)
            g = rows_at(base + t * RT, RT)
            br = total(c, r, sy1, ry1)
            xb = tokv[g, :]
            tokh[c, r, :] = xb
            x = xb.astype(F32)
            ha = br * mean_sq(br, D)
            mix = x + alv[0:1, :] * (ha - x)
            tokv[g, :] = (mix * mean_sq(mix, D)).astype(BF)

        loop(TH // RT, rows)
        cp = share(0, c, tokv)
        cp.start()
        cp.wait()
        r = rows_at(c * TB, TB)

        def units(n):
            cu, cv = rows_at(n * 256, 256), rows_at(F + n * 256, 256)
            x = tokv[r, :]
            u = nn(x, wgv[:, cu])
            v = nn(x, wgv[:, cv])
            gu[r, cu] = u.astype(BF)
            gu[r, cv] = v.astype(BF)
            us = u * sml[0:1, cu]
            vs = v * sml[1:2, cu]
            act[r, cu] = (us * vs * jax.nn.sigmoid(vs)).astype(BF)

        loop(F // 256, units)
        exchange(1, c, lambda rr, cols: nt(act[rr, :], wdv[cols, :]), sy2, ry2)

    loop(nc, feed_chunk)
    go_local.wait()
    for cp in go_copies:
        cp.wait()

    def back_chunk(i):
        c = nc - 1 - i
        lg = local(goh.at[c], gst, lsem.at[6])
        lg.start()
        lg.wait()
        landed(1, c, sy2, ry2)
        base = c * TB + core * TH

        def rows(t):
            r = rows_at(t * RT, RT)
            g = rows_at(base + t * RT, RT)
            am = alv[1:2, :]
            bm = total(c, r, sy2, ry2)
            h = tokv[g, :].astype(F32)
            rm = mean_sq(bm, D)
            hm = bm * rm
            diff = hm - h
            mix = h + am * diff
            r2 = mean_sq(mix, D)
            fin = mix * r2
            fst[r, :] = fin.astype(BF)
            go = gst[r, :].astype(F32)
            gm = r2 * (go - fin * (jnp.sum(go * fin, axis=1, keepdims=True) * (1.0 / D)))
            gacc[8:16, :] += fold(gm * diff)
            gh = am * gm
            ghid[c, r, :] = (gm - gh).astype(BF)
            gb = rm * (gh - hm * (jnp.sum(gh * hm, axis=1, keepdims=True) * (1.0 / D)))
            gml[g, :] = gb.astype(BF)

        loop(TH // RT, rows)
        cp = share(1, c, gml)
        cp.start()
        og = rows_at(base, TH)
        o_here = local(fst.at[:, mine], out.at[og], lsem.at[6])
        o_here.start()
        o_there = remote(
            fst.at[:, feat(y * 2 + mate)], out.at[og], out_s.at[c], out_r.at[c], peer
        )
        o_there.start()
        cp.wait()
        r = rows_at(c * TB, TB)

        def units(n):
            cu, cv = rows_at(n * 256, 256), rows_at(F + n * 256, 256)
            ga = nn(gml[r, :], wdv[:, cu])
            u = gu[r, cu].astype(F32)
            v = gu[r, cv].astype(F32)
            su, sv = sml[0:1, cu], sml[1:2, cu]
            us, vs = u * su, v * sv
            sg = jax.nn.sigmoid(vs)
            g_u = ga * (vs * sg)
            g_v = ga * us * sg * (1.0 + vs * (1.0 - sg))
            gsacc[0:8, cu] += fold(g_u * u)
            gsacc[8:16, cu] += fold(g_v * v)
            gu[r, cu] = (g_u * su).astype(BF)
            gu[r, cv] = (g_v * sv).astype(BF)

        loop(F // 256, units)
        exchange(2, c, lambda rr, cols: nt(gu[rr, :], wgv[cols, :]), sy3, ry3)
        o_here.wait()
        o_there.wait()

    loop(nc, back_chunk)

    RA = D // A

    def grad_tile(t):
        cols = rows_at(t * RA, RA)
        lhs = gml[:, cols]
        wst[:, 0:F] = lax.dot_general(
            lhs, act[...], (((0,), (0,)), ((), ())), preferred_element_type=F32
        ).astype(BF)
        cp = local(wst.at[:, 0:F], gwd_o.at[cols], lsem.at[6])
        cp.start()
        cp.wait()
        lhs = tokv[:, cols]
        wst[:, 0:F] = lax.dot_general(
            lhs, gu[:, 0:F], (((0,), (0,)), ((), ())), preferred_element_type=F32
        ).astype(BF)
        wst[:, F : 2 * F] = lax.dot_general(
            lhs, gu[:, F : 2 * F], (((0,), (0,)), ((), ())), preferred_element_type=F32
        ).astype(BF)
        cp = local(wst, gwg_o.at[cols], lsem.at[6])
        cp.start()
        cp.wait()

    loop(A, grad_tile)

    def attn_grad_chunk(i):
        c = nc - 1 - i
        landed(2, c, sy3, ry3)
        base = c * TB + core * TH

        def rows(t):
            r = rows_at(t * RT, RT)
            g = rows_at(base + t * RT, RT)
            aa = alv[0:1, :]
            br = total(c, r, sy1, ry1)
            x = tokh[c, r, :].astype(F32)
            ra = mean_sq(br, D)
            ha = br * ra
            diff = ha - x
            mix = x + aa * diff
            r1 = mean_sq(mix, D)
            hid = mix * r1
            gh = ghid[c, r, :].astype(F32) + total(c, r, sy3, ry3)
            gm = r1 * (gh - hid * (jnp.sum(gh * hid, axis=1, keepdims=True) * (1.0 / D)))
            gacc[0:8, :] += fold(gm * diff)
            gt = aa * gm
            ghid[c, r, :] = (gm - gt).astype(BF)
            gb = ra * (gt - ha * (jnp.sum(gt * ha, axis=1, keepdims=True) * (1.0 / D)))
            gba[g, :] = gb.astype(BF)

        loop(TH // RT, rows)
        cp = share(2, c, gba)
        cp.start()
        cp.wait()

    loop(nc, attn_grad_chunk)
    ends = [
        local(gba, gba_o, lsem.at[0]),
        local(ghid, gres_o, lsem.at[1]),
        local(gacc, ga_o, lsem.at[2]),
        local(gsacc, gs_o, lsem.at[3]),
    ]
    for cp in ends:
        cp.start()
    for cp in ends + [save_attn, save_ll, save_wo]:
        cp.wait()


def run_front(z, off_bias, tokens, gout, wq, wo, wg, wd, alpha, cos, sin, sq, sml):
    T, C, CF, F, D, H = z.T, z.C, z.CF, z.F, z.D, z.H
    nc, TB, TH, R, A, B, ny, mp = z.nc, z.TB, z.TH, z.R, z.A, z.B, z.ny, z.mp
    S = jax.ShapeDtypeStruct
    hbm = pl.BlockSpec(memory_space=pltpu.HBM)
    vm = pl.BlockSpec(memory_space=pltpu.VMEM)
    outs = [
        S((T, CF), BF), S((T, C), BF), S((T, C), BF), S((T, C), BF), S((T, C), BF), S((T, C), BF),
        S((T, C), BF), S((8, T), F32), S((T, D), BF), S((T, D), BF), S((nc, TH, D), BF),
        S((D, 3 * C), BF), S((D, C), BF), S((D, F), BF), S((D, 2 * F), BF), S((16, D), F32),
        S((16, F), F32), S((nc, TH, D), BF),
    ]
    V = pltpu.VMEM
    scratch = [
        V((T, D), BF), V((D, 3 * C), BF), V((D, C), BF), V((D, 2 * F), BF), V((D, F), BF),
        V((T, D), BF), V((T, F), BF), V((T, 2 * F), BF), V((T, D), BF), V((C, T), BF),
        V((2, T, C), BF), V((T, C), BF), V((8, T), F32), V((H, DK + 16, TB), F32), V((C, TB), F32),
    ]
    for _ in range(3):
        scratch += [V((nc, TH, D), BF), V((ny - 1, nc, TH, D), BF)]
    scratch += [
        V((nc, TH, D), BF), V((TH, D), BF), V((TH, D), F32), V((nc, TH, D), BF), V((nc, TH, D), BF),
        V((TH, D), BF), V((TH, D), BF), V((D // A, 2 * F), BF), V((8, D), F32), V((16, D), F32), V((16, F), F32),
    ]
    sem = pltpu.SemaphoreType.DMA
    nw = A - 1 + A * (B - 1)
    for shape in (
        (nc, 2 * ny - 1), (4, nw), (mp - 1,), (mp - 1,), (3, nc), (3, nc, ny - 1), (3, nc), (nc,),
    ):
        scratch += [sem(shape), sem(shape)]
    scratch += [sem((16,))]
    return pl.pallas_call(
        functools.partial(front, z),
        out_shape=outs,
        in_specs=[pl.BlockSpec(memory_space=pltpu.SMEM)] + [hbm] * 7 + [vm] * 4,
        out_specs=[hbm] * len(outs),
        scratch_shapes=scratch,
        compiler_params=pltpu.CompilerParams(
            collective_id=0, has_side_effects=True, vmem_limit_bytes=63 * 2**20
        ),
        name="front",
    )(off_bias, tokens, gout.reshape(nc, 2, TH, CF), wq, wo, wg, wd, alpha, cos, sin, sq, sml)


def tables(position):
    half = DK // 2
    frequency = theta_base ** (-(2.0 / DK) * jnp.arange(half, dtype=jnp.float32))
    grid = position.astype(jnp.float32)[:, None] * frequency[None, :]
    return jnp.cos(grid), jnp.sin(grid)


def on_device(
    sizes,
    tokens,
    w_qkv,
    w_out,
    w_gate_up,
    w_down,
    s_qk,
    alpha_attn,
    alpha_mlp,
    s_mlp,
    doc_lengths,
    grad_out,
):
    T, CF = tokens.shape
    H = s_qk.shape[1]
    C = H * DK
    F = w_down.shape[1]
    z = Sizes(sizes, T, C, CF, F, doc_lengths.shape[1])
    D, R = z.D, z.R
    doc_ids, position = layout(doc_lengths[0], T)
    cos, sin = tables(position)
    scale = s_qk.T.reshape(1, C)
    sml = s_mlp.transpose(1, 2, 0).reshape(2, F)
    alpha = jnp.pad(
        jnp.stack([alpha_attn.T.reshape(-1), alpha_mlp.T.reshape(-1)]), ((0, 6), (0, 0))
    )
    off_bias = jnp.where(doc_lengths[0, 0] == T, 0.0, NEG).astype(F32).reshape(1)
    (out, q, k, v, qr, kr, attn, ll, tokf, gba, gres, wqf, wof, gwd, gwg, ga, gs, _) = run_front(
        z, off_bias, tokens, grad_out, w_qkv.reshape(R, 3 * C), w_out, w_gate_up.reshape(R, 2 * F),
        w_down, alpha, jnp.tile(cos, (1, 4)), jnp.tile(sin, (1, 4)), scale, sml,
    )
    d, m = place()
    grad_mix = jnp.dot(gba, wof, preferred_element_type=F32).astype(BF)
    grad_w_out = jnp.einsum("te,tf->ef", gba, attn, preferred_element_type=F32)
    row_dot = jnp.sum(
        (grad_mix.astype(F32) * attn.astype(F32)).reshape(T, H, DK), axis=2
    ).T
    row_dot = jnp.pad(row_dot, ((0, 8 - H), (0, 0)))
    grads = attn_bwd(off_bias, q, k, v, k.T, grad_mix, ll, row_dot)
    grad_queries, grad_keys, grad_values = (t.reshape(T, H, DK) for t in grads)

    def unit(turned):
        t = turned.astype(F32).reshape(T, H, DK)
        inv = lax.rsqrt(jnp.sum(t * t, axis=-1, keepdims=True) + epsilon)
        return t * inv, inv

    unit_q, inverse_q = unit(qr)
    unit_k, inverse_k = unit(kr)
    scale_qk = s_qk.T
    grad_scale_qk = jnp.sum(grad_queries * unit_q + grad_keys * unit_k, axis=0)
    cosine, sine = cos[:, None, :], sin[:, None, :]
    grad_q = rotate_back(unit_back(grad_queries * scale_qk, unit_q, inverse_q), cosine, sine)
    grad_k = rotate_back(unit_back(grad_keys * scale_qk, unit_k, inverse_k), cosine, sine)
    grad_qkv = jnp.stack([grad_q, grad_k, grad_values], axis=1).reshape(T, -1).astype(BF)
    grad_w_qkv = jnp.einsum("td,tc->dc", tokf, grad_qkv, preferred_element_type=F32)
    partial = nt(grad_qkv, wqf).reshape(z.nc, 2, z.TH, D)
    half = (jnp.arange(2) == m % 2)[None, :, None, None]
    chip = (jnp.arange(D) // (2 * CF) == m // 2)[None, None, None, :]
    partial = partial + jnp.where(half & chip, gres.astype(F32)[:, None], 0.0)
    grad_in = lax.psum_scatter(
        partial.reshape(T, D).astype(BF), "mp", scatter_dimension=1, tiled=True
    ).astype(F32)
    ga = lax.psum(ga.reshape(2, 8, D).sum(1), ("dp", "mp")) * (1.0 / z.ny)
    ga = lax.dynamic_slice_in_dim(ga, m * CF, CF, 1).reshape(2, H, DK).transpose(0, 2, 1)
    ga = lax.dynamic_slice_in_dim(ga, d * (DK // z.dp), DK // z.dp, 1)
    sums = lax.psum((gs.reshape(2, 8, F).sum(1), grad_scale_qk), "dp")
    gs = sums[0].reshape(2, H, F // H).transpose(2, 0, 1)
    gs = lax.dynamic_slice_in_dim(gs, d * (F // H // z.dp), F // H // z.dp, 0)
    gsq = lax.dynamic_slice_in_dim(sums[1].T, d * (DK // z.dp), DK // z.dp, 0)

    def over_dp(g):
        return lax.psum_scatter(g.astype(BF), "dp", scatter_dimension=0, tiled=True).astype(F32)

    return (
        out,
        grad_in,
        over_dp(grad_w_qkv).reshape(R, 3, C),
        over_dp(grad_w_out),
        over_dp(gwg).reshape(R, 2, F),
        over_dp(gwd),
        gsq,
        ga[0],
        ga[1],
        gs,
    )


def solution(mesh):
    placed = (
        P("dp", "mp"),
        P("dp", None, "mp"),
        P("dp", "mp"),
        P("dp", None, "mp"),
        P("dp", "mp"),
        P(None, "mp"),
        P(None, "mp"),
        P(None, "mp"),
        P(None, None, "mp"),
        P("dp", None),
        P("dp", "mp"),
    )
    return jax.shard_map(
        functools.partial(on_device, dict(mesh.shape)),
        mesh=mesh,
        in_specs=placed,
        out_specs=(
            P("dp", "mp"),
            P("dp", "mp"),
            P("dp", None, "mp"),
            P("dp", "mp"),
            P("dp", None, "mp"),
            P("dp", "mp"),
            P("dp", "mp"),
            P("dp", "mp"),
            P("dp", "mp"),
            P("dp", None, "mp"),
        ),
        check_vma=False,
    )
```

```python
import functools
import math

import jax
import jax.numpy as jnp
from jax import lax
from jax.experimental import pallas as pl
from jax.experimental.pallas import tpu as pltpu
from jax.sharding import PartitionSpec as P

DK = 64
epsilon = 1e-06
theta_base = 10000.0


def layout(lengths, token_count):
    starts = jnp.cumsum(lengths) - lengths
    place = jnp.arange(token_count, dtype=jnp.int32)
    doc_ids = jnp.sum((place[:, None] >= starts[None, 1:]).astype(jnp.int32), axis=1)
    picked = (doc_ids[:, None] == jnp.arange(lengths.shape[0], dtype=jnp.int32)[None, :]).astype(
        jnp.int32
    )
    position = place - jnp.sum(picked * starts[None, :], axis=1)
    return (doc_ids, position)


LC=math.sqrt(DK)*math.log2(math.e)
NEG=-1e30
def nt(a,b): return lax.dot_general(a,b,(((1,),(1,)),((),())),preferred_element_type=jnp.float32)
def nn(a,b): return jnp.dot(a,b,preferred_element_type=jnp.float32)
def head_mask(x,h):
    lane=lax.broadcasted_iota(jnp.int32,x.shape,1)
    return jnp.where((lane//DK)==(h%2), x, jnp.zeros_like(x))
def attn_fwd_block(i, TB, H, q_ref, q0, k_ref, k0c, vT_ref, ob, acc):
    qs=pl.ds(pl.multiple_of(i*TB,TB),TB)
    qz=[head_mask(q_ref[qs,pl.ds(q0+(h//2)*128,128)],h) for h in range(H)]
    def tile(h,ks,nk,qsub,bias,tri):
        sT=nt(k_ref[ks,pl.ds(k0c+(h//2)*128,128)], qsub)
        x=sT*LC
        if bias is not None: x=x+bias
        if tri:
            r=lax.broadcasted_iota(jnp.int32,x.shape,0); c=lax.broadcasted_iota(jnp.int32,x.shape,1)
            x=jnp.where(r<=c,x,NEG)
        p=jnp.exp2(x).astype(jnp.bfloat16)
        vx=jnp.concatenate([vT_ref[h*DK:(h+1)*DK,ks],jnp.ones((16,nk),jnp.bfloat16)],axis=0)
        return nn(vx,p)
    hb=TB//2
    k0=pl.ds(pl.multiple_of(i*TB,hb),hb); k1=pl.ds(pl.multiple_of(i*TB+hb,hb),hb)
    for h in range(H):
        a0=tile(h,k0,hb,qz[h],None,True)
        a1=tile(h,k1,hb,qz[h][hb:],None,True)
        acc[h,:,0:hb]=a0[:,0:hb]
        acc[h,:,hb:TB]=a0[:,hb:TB]+a1
    def body(j,_):
        ks=pl.ds(pl.multiple_of(j*TB,TB),TB)
        for h in range(H):
            acc[h]+=tile(h,ks,TB,qz[h],ob,False)
        return 0
    lax.fori_loop(0,i,body,0)
def attn_bwd_block(i,TB,H,q_ref,k_ref,v_ref,kT_ref,g_ref,ll_ref,dl_ref,ob,dqT,dk,dv):
    qs=pl.ds(pl.multiple_of(i*TB,TB),TB); hb=TB//2
    qz=[head_mask(q_ref[qs,pl.ds((h//2)*128,128)],h) for h in range(H)]
    gz=[head_mask(g_ref[qs,pl.ds((h//2)*128,128)],h) for h in range(H)]
    lr=[ll_ref[pl.ds(h,1),qs] for h in range(H)]
    dr=[dl_ref[pl.ds(h,1),qs] for h in range(H)]
    def tile(h,ks,qv,gv,lb,dd,tri):
        p2=pl.ds((h//2)*128,128)
        x=nt(k_ref[ks,p2],qv)*LC-lb
        dp=nt(v_ref[ks,p2],gv)
        if tri:
            r=lax.broadcasted_iota(jnp.int32,x.shape,0); c=lax.broadcasted_iota(jnp.int32,x.shape,1)
            x=jnp.where(r<=c,x,NEG)
        p=jnp.exp2(x)
        ds=(p*(dp-dd)).astype(jnp.bfloat16)
        dvp=nn(p.astype(jnp.bfloat16),gv)
        dkp=nn(ds,qv)
        dqp=nn(kT_ref[h*DK:(h+1)*DK,ks],ds)
        return dqp,dkp,dvp
    k0=pl.ds(pl.multiple_of(i*TB,hb),hb); k1=pl.ds(pl.multiple_of(i*TB+hb,hb),hb)
    for pr in range((H+1)//2):
        p2=pl.ds(pr*128,128)
        dk0=dv0=dk1=dv1=0
        for h in range(2*pr,min(2*pr+2,H)):
            a,b,c=tile(h,k0,qz[h],gz[h],lr[h],dr[h],True)
            a1,b1,c1=tile(h,k1,qz[h][hb:],gz[h][hb:],lr[h][:,hb:],dr[h][:,hb:],True)
            hs=slice(h*DK,(h+1)*DK)
            dqT[hs,0:hb]=a[:,0:hb]; dqT[hs,hb:TB]=a[:,hb:]+a1
            dk0+=b; dv0+=c; dk1+=b1; dv1+=c1
        dk[k0,p2]+=dk0; dv[k0,p2]+=dv0; dk[k1,p2]+=dk1; dv[k1,p2]+=dv1
    lo=[l-ob for l in lr]
    def body(j,_):
        ks=pl.ds(pl.multiple_of(j*TB,TB),TB)
        for pr in range((H+1)//2):
            p2=pl.ds(pr*128,128)
            dka=dva=0
            for h in range(2*pr,min(2*pr+2,H)):
                a,b,c=tile(h,ks,qz[h],gz[h],lo[h],dr[h],False)
                dqT[h*DK:(h+1)*DK,:]+=a
                dka+=b; dva+=c
            dk[ks,p2]+=dka; dv[ks,p2]+=dva
        return 0
    lax.fori_loop(0,i,body,0)


MESH = pl.DeviceIdType.MESH
F32, BF = jnp.float32, jnp.bfloat16


class Sizes:
    def __init__(self, mesh_shape, T, C, CF, F, pieces):
        self.mp, self.dp = mesh_shape["mp"], mesh_shape["dp"]
        self.ny = self.mp // 2
        self.A = 4 if self.dp % 4 == 0 else 1
        self.B = self.dp // self.A
        self.T, self.C, self.CF, self.F = T, C, CF, F
        self.D = CF * self.mp
        self.H = C // DK
        self.nc = pieces
        self.TB = T // pieces
        self.TH = self.TB // 2
        self.R = self.D // self.dp


def place():
    return lax.axis_index("dp"), lax.axis_index("mp")


def remote(src, dst, ss, rs, dev):
    return pltpu.make_async_remote_copy(
        src, dst, send_sem=ss, recv_sem=rs, device_id=dev, device_id_type=MESH
    )


def local(src, dst, sem):
    return pltpu.make_async_copy(src, dst, sem)


def rows_at(start, size):
    return pl.ds(pl.multiple_of(start, size), size)


def loop(n, fn):
    def body(i, carry):
        fn(i)
        return carry

    lax.fori_loop(0, n, body, 0)


def fold(x):
    return jnp.sum(x.reshape(x.shape[0] // 8, 8, x.shape[1]), axis=0)


def mean_sq(x, D):
    return lax.rsqrt(jnp.sum(x * x, axis=1, keepdims=True) * (1.0 / D) + epsilon)


def split_dot(x, ones):
    hi = x.astype(BF)
    return nn(hi, ones) + nn((x - hi.astype(F32)).astype(BF), ones)


def head_ones():
    i = lax.broadcasted_iota(jnp.int32, (128, 128), 0) // DK
    j = lax.broadcasted_iota(jnp.int32, (128, 128), 1) // DK
    return jnp.where(i == j, 1.0, 0.0).astype(BF)


def turn(x, cosine, sine, sign):
    lane = lax.broadcasted_iota(jnp.int32, x.shape, 1)
    first = (lane % DK) < DK // 2
    other = jnp.where(first, -pltpu.roll(x, 128 - DK // 2, 1), pltpu.roll(x, DK // 2, 1))
    return x * cosine + sign * other * sine


def front(
    z,
    ob_ref, tokens, gout, wq, wo, wg, wd, alpha, cos, sin, sq, sml,
    out, q_o, k_o, v_o, qr_o, kr_o, attn_o, ll_o, tokf, gba_o, gres_o, wqf, wof, gwd_o, gwg_o, ga_o, gs_o, goh,
    tokv, wqv, wov, wgv, wdv, gml, act, gu, gba, vT, rot, attn, ll, acc, oT,
    sy1, ry1, sy2, ry2, sy3, ry3, rc, sc, own, tokh, ghid, gst, fst, wst, alv, gacc, gsacc,
    tok_s, tok_r, w_s, w_r, al_s, al_r, go_s, go_r, ex_s, ex_r, y_s, y_r, hc_s, hc_r, out_s, out_r, lsem,
):
    T, C, CF, F, D, H = z.T, z.C, z.CF, z.F, z.D, z.H
    nc, TB, TH, R, A, B, ny, mp = z.nc, z.TB, z.TH, z.R, z.A, z.B, z.ny, z.mp
    d, m = place()
    a, b = d // B, d % B
    y, core = m // 2, m % 2
    mate = 1 - core
    peer = (d, y * 2 + mate)

    def ypeer(k, cc):
        return (d, ((y + k) % ny) * 2 + cc)

    zpeer = lambda k: (((a + k) % A) * B + b, m)
    xpeer = lambda k: (a * B + (b + k) % B, m)
    others = [peer] + [ypeer(k, cc) for k in range(1, ny) for cc in (core, mate)]
    everyone = others + [zpeer(k) for k in range(1, A)] + [xpeer(k) for k in range(1, B)]
    bar = pltpu.get_barrier_semaphore()
    for dev in everyone:
        pl.semaphore_signal(bar, 1, device_id=dev, device_id_type=MESH)
    pl.semaphore_wait(bar, len(everyone))

    ob = ob_ref[0]
    feat = lambda mm: pl.ds(pl.multiple_of(mm * CF, CF), CF)
    mine = feat(m)


    def tok_own(c, i, dev):
        r = rows_at(c * TB, TB)
        return remote(tokens.at[r], tokv.at[r, mine], tok_s.at[c, i], tok_r.at[c, i], dev)

    def tok_got(c, i, mm):
        r = rows_at(c * TB, TB)
        return remote(tokv.at[r, feat(mm)], tokv.at[r, feat(mm)], tok_s.at[c, i], tok_r.at[c, i], peer)

    def start_tok(i):
        c = nc - 1 - i
        for k in range(1, ny):
            tok_own(c, k, ypeer(k, core)).start()
        tok_own(c, 0, peer).start()

    weights = [(wq, wqv), (wo, wov), (wg, wgv), (wd, wdv)]

    def shard(aa, bb):
        return rows_at((aa * B + bb) * R, R)

    def w_z(w, k):
        src, dst = weights[w]
        return remote(src, dst.at[shard(a, b)], w_s.at[w, k - 1], w_r.at[w, k - 1], zpeer(k))

    def w_z_got(w, k):
        src, dst = weights[w]
        return remote(src, dst.at[shard((a - k + A) % A, b)], w_s.at[w, k - 1], w_r.at[w, k - 1], zpeer(k))

    def w_x(w, ks, kb):
        src, dst = weights[w]
        i = A - 1 + ks * (B - 1) + kb - 1
        r = shard((a - ks + A) % A, b)
        return remote(src if ks == 0 else dst.at[r], dst.at[r], w_s.at[w, i], w_r.at[w, i], xpeer(kb))

    def w_x_got(w, ks, kb):
        src, dst = weights[w]
        i = A - 1 + ks * (B - 1) + kb - 1
        r = shard((a - ks + A) % A, (b - kb + B) % B)
        return remote(src, dst.at[r], w_s.at[w, i], w_r.at[w, i], xpeer(kb))

    def w_local(w):
        src, dst = weights[w]
        return local(src, dst.at[shard(a, b)], lsem.at[w])

    def w_start(w):
        for k in range(1, A):
            w_z(w, k).start()
        for kb in range(1, B):
            w_x(w, 0, kb).start()
        w_local(w).start()

    def w_forward(w):
        for k in range(1, A):
            w_z_got(w, k).wait_recv()
            for kb in range(1, B):
                w_x(w, k, kb).start()

    def w_finish(w):
        for ks in range(A):
            for kb in range(1, B):
                w_x_got(w, ks, kb).wait_recv()
        for k in range(1, A):
            w_z(w, k).wait_send()
        for ks in range(A):
            for kb in range(1, B):
                w_x(w, ks, kb).wait_send()
        w_local(w).wait()

    w_start(0)
    loop(nc, start_tok)
    tok_local = local(tokens, tokv.at[:, mine], lsem.at[4])
    tok_local.start()
    al_local = local(alpha, alv.at[:, mine], lsem.at[5])
    al_local.start()
    al_copies = [
        remote(alpha, alv.at[:, mine], al_s.at[i], al_r.at[i], dev) for i, dev in enumerate(others)
    ]
    for cp in al_copies:
        cp.start()
    w_start(1)

    def pass_tok(i):
        c = nc - 1 - i
        for k in range(1, ny):
            src = ((y - k + ny) % ny) * 2 + core
            tok_got(c, k, src).wait_recv()
            tok_got(c, ny + k - 1, src).start()

    half_way = nc // 2
    loop(half_way, pass_tok)
    w_forward(0)
    w_start(2)
    loop(nc - half_way, lambda i: pass_tok(i + half_way))

    def end_tok(i):
        c = nc - 1 - i
        tok_got(c, 0, y * 2 + mate).wait_recv()
        for k in range(1, ny):
            src = ((y - k + ny) % ny) * 2 + mate
            tok_got(c, ny + k - 1, src).wait_recv()

    loop(nc, end_tok)

    def tok_sent(i):
        c = nc - 1 - i
        tok_own(c, 0, peer).wait_send()
        for k in range(1, ny):
            tok_own(c, k, ypeer(k, core)).wait_send()
            tok_got(c, ny + k - 1, ((y - k + ny) % ny) * 2 + core).wait_send()

    loop(nc, tok_sent)
    tok_local.wait()
    w_forward(1)
    w_finish(0)
    w_start(3)

    go4 = gout

    def go_copy(i, dev, cc):
        return remote(go4.at[:, cc], goh.at[:, :, mine], go_s.at[i], go_r.at[i], dev)

    go_copies = [go_copy(0, peer, mate)]
    i = 1
    for k in range(1, ny):
        for cc in (core, mate):
            go_copies.append(go_copy(i, ypeer(k, cc), cc))
            i += 1
    go_local = local(go4.at[:, core], goh.at[:, :, mine], lsem.at[6])
    go_local.start()
    for cp in go_copies:
        cp.start()

    ones = head_ones()
    mask_q = gml

    def project_rows(i):
        r = rows_at(i * TB, TB)
        x = tokv[r, :]
        cs, sn = cos[r, :], sin[r, :]
        for part in range(2):
            for pr in range(C // 128):
                cols = slice(part * C + pr * 128, part * C + pr * 128 + 128)
                t = turn(nn(x, wqv[:, cols]), cs, sn, 1.0)
                rot[part, r, pr * 128 : pr * 128 + 128] = t.astype(BF)
                inv = lax.rsqrt(split_dot(t * t, ones) + epsilon)
                mask_q[r, cols] = (t * inv * sq[:, pr * 128 : pr * 128 + 128]).astype(BF)
        v = nn(x, wqv[:, 2 * C : 3 * C])
        mask_q[r, 2 * C : 3 * C] = v.astype(BF)
        vT[:, r] = v.T.astype(BF)

    loop(nc, project_rows)
    save_tok = local(tokv, tokf, lsem.at[4])
    save_tok.start()
    saves = [
        local(mask_q.at[:, 0:C], q_o, lsem.at[7]),
        local(mask_q.at[:, C : 2 * C], k_o, lsem.at[8]),
        local(mask_q.at[:, 2 * C : 3 * C], v_o, lsem.at[9]),
        local(rot.at[0], qr_o, lsem.at[10]),
        local(rot.at[1], kr_o, lsem.at[11]),
        local(wqv, wqf, lsem.at[12]),
    ]
    for cp in saves:
        cp.start()
    w_finish(1)

    def exchange(e, c, part, sy, ry):
        mate_rows = c * TB + mate * TH
        own_rows = c * TB + core * TH
        NJ = 256

        def give(j):
            cols = rows_at(j * NJ, NJ)
            sc[:, cols] = part(rows_at(mate_rows, TH), cols).astype(BF)

        loop(D // NJ, give)
        cp = remote(sc, rc.at[c], ex_s.at[e, c], ex_r.at[e, c], peer)
        cp.start()

        def keep(j):
            cols = rows_at(j * NJ, NJ)
            own[:, cols] = part(rows_at(own_rows, TH), cols)

        loop(D // NJ, keep)
        cp.wait()

        def add(t):
            r = rows_at(t * 32, 32)
            sy[c, r, :] = (own[r, :] + rc[c, r, :].astype(F32)).astype(BF)

        loop(TH // 32, add)
        for k in range(1, ny):
            remote(
                sy.at[c], ry.at[k - 1, c], y_s.at[e, c, k - 1], y_r.at[e, c, k - 1], ypeer(k, core)
            ).start()

    def landed(e, c, sy, ry):
        for k in range(1, ny):
            remote(
                sy.at[c], ry.at[k - 1, c], y_s.at[e, c, k - 1], y_r.at[e, c, k - 1], ypeer(k, core)
            ).wait()

    def total(c, r, sy, ry):
        t = sy[c, r, :].astype(F32)
        for k in range(ny - 1):
            t = t + ry[k, c, r, :].astype(F32)
        return t

    def share(e, c, buf):
        own_rows = rows_at(c * TB + core * TH, TH)
        return remote(buf.at[own_rows], buf.at[own_rows], hc_s.at[e, c], hc_r.at[e, c], peer)

    def attend_chunk(i):
        c = nc - 1 - i
        attn_fwd_block(c, TB, H, mask_q, 0, mask_q, C, vT, ob, acc)
        r = rows_at(c * TB, TB)
        for h in range(H):
            l = acc[h, DK : DK + 1, :]
            oT[h * DK : (h + 1) * DK, :] = acc[h, 0:DK, :] / l
            ll[pl.ds(h, 1), r] = jnp.log2(l)
        attn[r, :] = oT[...].T.astype(BF)

        def part(rr, cols):
            return nt(attn[rr, :], wov[cols, :])

        @pl.when(i == 0)
        def _():
            save_tok.wait()

        exchange(0, c, part, sy1, ry1)

    ll[...] = jnp.zeros_like(ll)
    loop(nc, attend_chunk)
    save_attn = local(attn, attn_o, lsem.at[13])
    save_attn.start()
    save_ll = local(ll, ll_o, lsem.at[14])
    save_ll.start()
    save_wo = local(wov, wof, lsem.at[15])
    save_wo.start()
    for cp in saves:
        cp.wait()
    al_local.wait()
    for cp in al_copies:
        cp.wait()
    w_forward(2)
    w_forward(3)
    w_finish(2)
    w_finish(3)

    RT = 32
    gacc[...] = jnp.zeros_like(gacc)
    gsacc[...] = jnp.zeros_like(gsacc)

    def feed_chunk(i):
        c = nc - 1 - i
        landed(0, c, sy1, ry1)
        base = c * TB + core * TH

        def rows(t):
            r = rows_at(t * RT, RT)
            g = rows_at(base + t * RT, RT)
            br = total(c, r, sy1, ry1)
            xb = tokv[g, :]
            tokh[c, r, :] = xb
            x = xb.astype(F32)
            ha = br * mean_sq(br, D)
            mix = x + alv[0:1, :] * (ha - x)
            tokv[g, :] = (mix * mean_sq(mix, D)).astype(BF)

        loop(TH // RT, rows)
        cp = share(0, c, tokv)
        cp.start()
        cp.wait()
        r = rows_at(c * TB, TB)

        def units(n):
            cu, cv = rows_at(n * 256, 256), rows_at(F + n * 256, 256)
            x = tokv[r, :]
            u = nn(x, wgv[:, cu])
            v = nn(x, wgv[:, cv])
            gu[r, cu] = u.astype(BF)
            gu[r, cv] = v.astype(BF)
            us = u * sml[0:1, cu]
            vs = v * sml[1:2, cu]
            act[r, cu] = (us * vs * jax.nn.sigmoid(vs)).astype(BF)

        loop(F // 256, units)
        exchange(1, c, lambda rr, cols: nt(act[rr, :], wdv[cols, :]), sy2, ry2)

    loop(nc, feed_chunk)
    go_local.wait()
    for cp in go_copies:
        cp.wait()

    def back_chunk(i):
        c = nc - 1 - i
        lg = local(goh.at[c], gst, lsem.at[6])
        lg.start()
        lg.wait()
        landed(1, c, sy2, ry2)
        base = c * TB + core * TH

        def rows(t):
            r = rows_at(t * RT, RT)
            g = rows_at(base + t * RT, RT)
            am = alv[1:2, :]
            bm = total(c, r, sy2, ry2)
            h = tokv[g, :].astype(F32)
            rm = mean_sq(bm, D)
            hm = bm * rm
            diff = hm - h
            mix = h + am * diff
            r2 = mean_sq(mix, D)
            fin = mix * r2
            fst[r, :] = fin.astype(BF)
            go = gst[r, :].astype(F32)
            gm = r2 * (go - fin * (jnp.sum(go * fin, axis=1, keepdims=True) * (1.0 / D)))
            gacc[8:16, :] += fold(gm * diff)
            gh = am * gm
            ghid[c, r, :] = (gm - gh).astype(BF)
            gb = rm * (gh - hm * (jnp.sum(gh * hm, axis=1, keepdims=True) * (1.0 / D)))
            gml[g, :] = gb.astype(BF)

        loop(TH // RT, rows)
        cp = share(1, c, gml)
        cp.start()
        og = rows_at(base, TH)
        o_here = local(fst.at[:, mine], out.at[og], lsem.at[6])
        o_here.start()
        o_there = remote(
            fst.at[:, feat(y * 2 + mate)], out.at[og], out_s.at[c], out_r.at[c], peer
        )
        o_there.start()
        cp.wait()
        r = rows_at(c * TB, TB)

        def units(n):
            cu, cv = rows_at(n * 256, 256), rows_at(F + n * 256, 256)
            ga = nn(gml[r, :], wdv[:, cu])
            u = gu[r, cu].astype(F32)
            v = gu[r, cv].astype(F32)
            su, sv = sml[0:1, cu], sml[1:2, cu]
            us, vs = u * su, v * sv
            sg = jax.nn.sigmoid(vs)
            g_u = ga * (vs * sg)
            g_v = ga * us * sg * (1.0 + vs * (1.0 - sg))
            gsacc[0:8, cu] += fold(g_u * u)
            gsacc[8:16, cu] += fold(g_v * v)
            gu[r, cu] = (g_u * su).astype(BF)
            gu[r, cv] = (g_v * sv).astype(BF)

        loop(F // 256, units)
        exchange(2, c, lambda rr, cols: nt(gu[rr, :], wgv[cols, :]), sy3, ry3)
        o_here.wait()
        o_there.wait()

    loop(nc, back_chunk)

    RA = D // A

    def grad_tile(t):
        cols = rows_at(t * RA, RA)
        lhs = gml[:, cols]
        wst[:, 0:F] = lax.dot_general(
            lhs, act[...], (((0,), (0,)), ((), ())), preferred_element_type=F32
        ).astype(BF)
        cp = local(wst.at[:, 0:F], gwd_o.at[cols], lsem.at[6])
        cp.start()
        cp.wait()
        lhs = tokv[:, cols]
        wst[:, 0:F] = lax.dot_general(
            lhs, gu[:, 0:F], (((0,), (0,)), ((), ())), preferred_element_type=F32
        ).astype(BF)
        wst[:, F : 2 * F] = lax.dot_general(
            lhs, gu[:, F : 2 * F], (((0,), (0,)), ((), ())), preferred_element_type=F32
        ).astype(BF)
        cp = local(wst, gwg_o.at[cols], lsem.at[6])
        cp.start()
        cp.wait()

    loop(A, grad_tile)

    def attn_grad_chunk(i):
        c = nc - 1 - i
        landed(2, c, sy3, ry3)
        base = c * TB + core * TH

        def rows(t):
            r = rows_at(t * RT, RT)
            g = rows_at(base + t * RT, RT)
            aa = alv[0:1, :]
            br = total(c, r, sy1, ry1)
            x = tokh[c, r, :].astype(F32)
            ra = mean_sq(br, D)
            ha = br * ra
            diff = ha - x
            mix = x + aa * diff
            r1 = mean_sq(mix, D)
            hid = mix * r1
            gh = ghid[c, r, :].astype(F32) + total(c, r, sy3, ry3)
            gm = r1 * (gh - hid * (jnp.sum(gh * hid, axis=1, keepdims=True) * (1.0 / D)))
            gacc[0:8, :] += fold(gm * diff)
            gt = aa * gm
            ghid[c, r, :] = (gm - gt).astype(BF)
            gb = ra * (gt - ha * (jnp.sum(gt * ha, axis=1, keepdims=True) * (1.0 / D)))
            gba[g, :] = gb.astype(BF)

        loop(TH // RT, rows)
        cp = share(2, c, gba)
        cp.start()
        cp.wait()

    loop(nc, attn_grad_chunk)
    ends = [
        local(gba, gba_o, lsem.at[0]),
        local(ghid, gres_o, lsem.at[1]),
        local(gacc, ga_o, lsem.at[2]),
        local(gsacc, gs_o, lsem.at[3]),
    ]
    for cp in ends:
        cp.start()
    for cp in ends + [save_attn, save_ll, save_wo]:
        cp.wait()


def run_front(z, off_bias, tokens, gout, wq, wo, wg, wd, alpha, cos, sin, sq, sml):
    T, C, CF, F, D, H = z.T, z.C, z.CF, z.F, z.D, z.H
    nc, TB, TH, R, A, B, ny, mp = z.nc, z.TB, z.TH, z.R, z.A, z.B, z.ny, z.mp
    S = jax.ShapeDtypeStruct
    hbm = pl.BlockSpec(memory_space=pltpu.HBM)
    vm = pl.BlockSpec(memory_space=pltpu.VMEM)
    outs = [
        S((T, CF), BF), S((T, C), BF), S((T, C), BF), S((T, C), BF), S((T, C), BF), S((T, C), BF),
        S((T, C), BF), S((8, T), F32), S((T, D), BF), S((T, D), BF), S((nc, TH, D), BF),
        S((D, 3 * C), BF), S((D, C), BF), S((D, F), BF), S((D, 2 * F), BF), S((16, D), F32),
        S((16, F), F32), S((nc, TH, D), BF),
    ]
    V = pltpu.VMEM
    scratch = [
        V((T, D), BF), V((D, 3 * C), BF), V((D, C), BF), V((D, 2 * F), BF), V((D, F), BF),
        V((T, D), BF), V((T, F), BF), V((T, 2 * F), BF), V((T, D), BF), V((C, T), BF),
        V((2, T, C), BF), V((T, C), BF), V((8, T), F32), V((H, DK + 16, TB), F32), V((C, TB), F32),
    ]
    for _ in range(3):
        scratch += [V((nc, TH, D), BF), V((ny - 1, nc, TH, D), BF)]
    scratch += [
        V((nc, TH, D), BF), V((TH, D), BF), V((TH, D), F32), V((nc, TH, D), BF), V((nc, TH, D), BF),
        V((TH, D), BF), V((TH, D), BF), V((D // A, 2 * F), BF), V((8, D), F32), V((16, D), F32), V((16, F), F32),
    ]
    sem = pltpu.SemaphoreType.DMA
    nw = A - 1 + A * (B - 1)
    for shape in (
        (nc, 2 * ny - 1), (4, nw), (mp - 1,), (mp - 1,), (3, nc), (3, nc, ny - 1), (3, nc), (nc,),
    ):
        scratch += [sem(shape), sem(shape)]
    scratch += [sem((16,))]
    return pl.pallas_call(
        functools.partial(front, z),
        out_shape=outs,
        in_specs=[pl.BlockSpec(memory_space=pltpu.SMEM)] + [hbm] * 7 + [vm] * 4,
        out_specs=[hbm] * len(outs),
        scratch_shapes=scratch,
        compiler_params=pltpu.CompilerParams(
            collective_id=0, has_side_effects=True, vmem_limit_bytes=63 * 2**20
        ),
        name="front",
    )(off_bias, tokens, gout.reshape(nc, 2, TH, CF), wq, wo, wg, wd, alpha, cos, sin, sq, sml)


def back(
    z,
    ob_ref, q_h, k_h, v_h, qr_h, kr_h, attn_h, ll_h, tok_h, gba_h, gres_h, wq_h, wo_h, gwd_h, gwg_h, ga_h, gs_h,
    cos, sin, sq,
    gin_o, owq, owo, owg, owd, vec_o,
    qv, kv, vv, kT, rot, attn, ll, dl, wqv, wov, gba, tok, gres, gm, dk, dv, dqT, gqkv, gsq,
    own_d, own_g0, own_g1, gwo, gwq,
    r1_d, r1_g0, r1_g1, r1_o, r1_q, s2_d, s2_g0, s2_g1, s2_o, s2_q, r2_d, r2_g0, r2_g1, r2_o, r2_q,
    f_d, f_g, f_o, f_q,
    sc2, rc2, ow, sy, ry, gin, gal, gar, gsl, vec, rv1, rv2,
    x_s, x_r, z_s, z_r, c_s, c_r, y_s, y_r, m_s, m_r, lsem,
):
    T, C, CF, F, D, H = z.T, z.C, z.CF, z.F, z.D, z.H
    nc, TB, TH, R, A, B, ny = z.nc, z.TB, z.TH, z.R, z.A, z.B, z.ny
    d, m = place()
    a, b = d // B, d % B
    y, core = m // 2, m % 2
    mate = 1 - core
    peer = (d, y * 2 + mate)
    ypeer = lambda k: (d, ((y + k) % ny) * 2 + core)
    zpeer = lambda k: (((a + k) % A) * B + b, m)
    xpeer = lambda k: (a * B + (b + k) % B, m)
    everyone = (
        [peer]
        + [ypeer(k) for k in range(1, ny)]
        + [zpeer(k) for k in range(1, A)]
        + [xpeer(k) for k in range(1, B)]
    )
    bar = pltpu.get_barrier_semaphore()
    for dev in everyone:
        pl.semaphore_signal(bar, 1, device_id=dev, device_id_type=MESH)
    pl.semaphore_wait(bar, len(everyone))
    feat = lambda mm: pl.ds(pl.multiple_of(mm * CF, CF), CF)
    ob = ob_ref[0]

    lo, hi = slice(0, F), slice(F, 2 * F)
    pieces = [
        (lambda bb: gwd_h.at[:, bb], own_d, r1_d, s2_d, r2_d, f_d, owd),
        (lambda bb: gwg_h.at[:, bb, :, lo], own_g0, r1_g0, s2_g0, r2_g0, f_g.at[:, lo], None),
        (lambda bb: gwg_h.at[:, bb, :, hi], own_g1, r1_g1, s2_g1, r2_g1, f_g.at[:, hi], owg),
        (lambda bb: gwo.at[:, bb], None, r1_o, s2_o, r2_o, f_o, owo),
        (lambda bb: gwq.at[:, bb], None, r1_q, s2_q, r2_q, f_q, owq),
    ]

    def x_copy(p, k):
        blocks, r1 = pieces[p][0], pieces[p][2]
        return remote(
            blocks((b + k) % B), r1.at[k - 1], x_s.at[p, k - 1], x_r.at[p, k - 1], xpeer(k)
        )

    def own_copy(p):
        return local(pieces[p][0](b), pieces[p][1], lsem.at[p])

    def rs_start(p):
        for k in range(1, B):
            x_copy(p, k).start()
        if pieces[p][1] is not None:
            own_copy(p).start()

    def z_copy(p, k):
        s2, r2 = pieces[p][3], pieces[p][4]
        return remote(s2.at[(a + k) % A], r2.at[k - 1], z_s.at[p, k - 1], z_r.at[p, k - 1], zpeer(k))

    def rs_middle(p):
        blocks, mine, r1, s2 = pieces[p][:4]
        if mine is not None:
            own_copy(p).wait()
        for k in range(1, B):
            x_copy(p, k).wait()
        for k in list(range(1, A)) + [0]:
            aa = (a + k) % A

            def add(t):
                r = rows_at(t * 16, 16)
                src = mine[aa, r, :] if mine is not None else blocks(b)[aa, r, :]
                total = src.astype(F32)
                for kk in range(B - 1):
                    total = total + r1[kk, aa, r, :].astype(F32)
                s2[aa, r, :] = total.astype(BF)

            loop(R // 16, add)
            if k:
                z_copy(p, k).start()

    def rs_end(p):
        s2, r2, res = pieces[p][3:6]
        for k in range(1, A):
            z_copy(p, k).wait()

        def add(t):
            r = rows_at(t * 16, 16)
            total = s2[a, r, :].astype(F32)
            for kk in range(A - 1):
                total = total + r2[kk, r, :].astype(F32)
            res[r, :] = total

        loop(R // 16, add)

    rs_start(0)
    rs_start(1)
    rs_start(2)
    ga_there = remote(
        ga_h.at[:, feat(y * 2 + mate)], gar, m_s.at[0], m_r.at[0], peer
    )
    ga_there.start()
    loads = [
        local(s, t, lsem.at[5 + i])
        for i, (s, t) in enumerate(
            [
                (q_h, qv), (k_h, kv), (wo_h, wov), (gba_h, gba), (v_h, vv), (attn_h, attn), (ll_h, ll),
                (qr_h, rot.at[0]), (kr_h, rot.at[1]), (wq_h, wqv), (gres_h, gres),
                (ga_h.at[:, feat(m)], gal), (gs_h, gsl), (tok_h, tok),
            ]
        )
    ]
    for cp in loads:
        cp.start()
    dk[...] = jnp.zeros_like(dk)
    dv[...] = jnp.zeros_like(dv)
    gsq[...] = jnp.zeros_like(gsq)
    for cp in loads[:7]:
        cp.wait()

    def turn_keys(i):
        r = rows_at(i * TB, TB)
        kT[:, r] = kv[r, :].astype(F32).T.astype(BF)

    loop(nc, turn_keys)
    ones = head_ones()
    heads = lax.broadcasted_iota(jnp.int32, (8, C), 0)
    lanes = lax.broadcasted_iota(jnp.int32, (8, C), 1) // DK
    pick = jnp.where(heads == lanes, 1.0, 0.0).astype(BF)
    for cp in loads[7:]:
        cp.wait()

    def gin_copy(c):
        return remote(sc2.at[c], rc2.at[c], c_s.at[c], c_r.at[c], peer)

    def y_copy(c, k):
        return remote(sy.at[c, k - 1], ry.at[k - 1, c], y_s.at[c, k - 1], y_r.at[c, k - 1], ypeer(k))

    def chunk(i):
        c = nc - 1 - i
        r = rows_at(c * TB, TB)
        g = nn(gba[r, :], wov[...]).astype(BF)
        gm[r, :] = g
        prod = g.astype(F32) * attn[r, :].astype(F32)
        ph = prod.astype(BF)
        dl[:, r] = nt(pick, ph) + nt(pick, (prod - ph.astype(F32)).astype(BF))
        attn_bwd_block(c, TB, H, qv, kv, vv, kT, gm, ll, dl, ob, dqT, dk, dv)
        cs, sn = cos[r, :], sin[r, :]
        for part in range(2):
            for pr in range(C // 128):
                cols = slice(pr * 128, pr * 128 + 128)
                if part == 0:
                    gh = dqT[cols, :].T * 8.0
                else:
                    gh = dk[r, cols] * 8.0
                t = rot[part, r, cols].astype(F32)
                inv = lax.rsqrt(split_dot(t * t, ones) + epsilon)
                un = t * inv
                gsq[:, cols] += fold(gh * un)
                gh = gh * sq[:, cols]
                gr = inv * (gh - un * split_dot(gh * un, ones))
                gqkv[r, part * C + pr * 128 : part * C + pr * 128 + 128] = turn(gr, cs, sn, -1.0).astype(BF)
        gqkv[r, 2 * C : 3 * C] = dv[r, :].astype(BF)

        def product(hsel, k, cc):
            rr = rows_at(c * TB + hsel * TH, TH)
            cols = feat(((y + k) % ny) * 2 + cc)
            t = nt(gqkv[rr, :], wqv[cols, :])
            if k == 0:
                t = t + jnp.where(hsel == core, 1.0, 0.0) * gres[c, :, cols].astype(F32)
            return t

        for k in range(ny):
            for hs in range(2):
                sc2[c, k, hs * TH : (hs + 1) * TH, :] = product(hs, k, mate).astype(BF)
        gin_copy(c).start()
        for k in range(ny):
            for hs in range(2):
                ow[k, hs * TH : (hs + 1) * TH, :] = product(hs, k, core)
        gin_copy(c).wait()
        gin[r, :] = ow[0] + rc2[c, 0].astype(F32)
        for k in range(1, ny):
            sy[c, k - 1] = (ow[k] + rc2[c, k].astype(F32)).astype(BF)
            y_copy(c, k).start()

        @pl.when(i == 1)
        def _():
            rs_middle(0)

    loop(nc, chunk)

    def out_tile(t):
        cols = rows_at(t * B * R, B * R)
        g = lax.dot_general(
            gba[:, cols], attn[...], (((0,), (0,)), ((), ())), preferred_element_type=F32
        )
        gwo[t] = g.astype(BF).reshape(B, R, C)

    loop(A, out_tile)
    rs_start(3)

    def qkv_tile(t):
        cols = rows_at(t * B * R, B * R)
        g = lax.dot_general(
            tok[:, cols], gqkv[...], (((0,), (0,)), ((), ())), preferred_element_type=F32
        )
        gwq[t] = g.astype(BF).reshape(B, R, 3 * C)

    loop(A, qkv_tile)
    rs_start(4)
    W = vec.shape[1]
    ga_there.wait()
    vec[...] = jnp.zeros_like(vec)
    gt = gal[...] + gar[...]
    vec[0:1, 0:F] = jnp.sum(gsl[0:8, :], axis=0, keepdims=True)
    vec[1:2, 0:F] = jnp.sum(gsl[8:16, :], axis=0, keepdims=True)
    vec[2:3, 0:CF] = jnp.sum(gt[0:8], axis=0, keepdims=True)
    vec[3:4, 0:CF] = jnp.sum(gt[8:16], axis=0, keepdims=True)
    vec[4:5, 0:C] = jnp.sum(gsq[...], axis=0, keepdims=True)
    vx = [remote(vec, rv1.at[k - 1], m_s.at[k], m_r.at[k], xpeer(k)) for k in range(1, B)]
    for cp in vx:
        cp.start()
    rs_middle(1)
    for cp in vx:
        cp.wait()
    t = vec[...]
    for k in range(B - 1):
        t = t + rv1[k]
    vec[...] = t
    vz = [
        remote(vec, rv2.at[k - 1], m_s.at[B - 1 + k], m_r.at[B - 1 + k], zpeer(k)) for k in range(1, A)
    ]
    for cp in vz:
        cp.start()
    rs_middle(2)
    rs_end(0)
    ends = [local(f_d, owd, lsem.at[0])]
    ends[0].start()

    def gin_end(i):
        c = nc - 1 - i
        r = rows_at(c * TB, TB)
        for k in range(1, ny):
            y_copy(c, k).wait()
            gin[r, :] += ry[k - 1, c].astype(F32)

    loop(nc, gin_end)
    ends.append(local(gin, gin_o, lsem.at[1]))
    ends[-1].start()
    rs_middle(3)
    rs_middle(4)
    rs_end(1)
    rs_end(2)
    ends.append(local(f_g, owg, lsem.at[2]))
    ends[-1].start()
    for cp in vz:
        cp.wait()
    t = vec[...]
    for k in range(A - 1):
        t = t + rv2[k]
    vec[...] = t
    ends.append(local(vec, vec_o, lsem.at[3]))
    ends[-1].start()
    rs_end(3)
    ends.append(local(f_o, owo, lsem.at[4]))
    ends[-1].start()
    rs_end(4)
    ends.append(local(f_q, owq, lsem.at[5]))
    ends[-1].start()
    for cp in ends:
        cp.wait()


def run_back(z, off_bias, q, k, v, qr, kr, attn, ll, tokf, gba, gres, wqf, wof, gwd, gwg, ga, gs, cos, sin, sq):
    T, C, CF, F, D, H = z.T, z.C, z.CF, z.F, z.D, z.H
    nc, TB, TH, R, A, B, ny = z.nc, z.TB, z.TH, z.R, z.A, z.B, z.ny
    S = jax.ShapeDtypeStruct
    V = pltpu.VMEM
    hbm = pl.BlockSpec(memory_space=pltpu.HBM)
    vm = pl.BlockSpec(memory_space=pltpu.VMEM)
    W = max(F, CF, C)
    outs = [
        S((T, CF), F32), S((R, 3 * C), F32), S((R, C), F32), S((R, 2 * F), F32), S((R, F), F32), S((8, W), F32),
    ]
    cols = (F, F, F, C, 3 * C)
    scratch = [
        V((T, C), BF), V((T, C), BF), V((T, C), BF), V((C, T), BF), V((2, T, C), BF), V((T, C), BF),
        V((8, T), F32), V((8, T), F32), V((D, 3 * C), BF), V((D, C), BF), V((T, D), BF), V((T, D), BF),
        V((nc, TH, D), BF), V((T, C), BF), V((T, C), F32), V((T, C), F32), V((C, TB), F32),
        V((T, 3 * C), BF), V((8, C), F32),
        V((A, R, F), BF), V((A, R, F), BF), V((A, R, F), BF), V((A, B, R, C), BF), V((A, B, R, 3 * C), BF),
    ]
    scratch += [V((B - 1, A, R, w), BF) for w in cols]
    scratch += [V((A, R, w), BF) for w in cols]
    scratch += [V((A - 1, R, w), BF) for w in cols]
    scratch += [V((R, F), F32), V((R, 2 * F), F32), V((R, C), F32), V((R, 3 * C), F32)]
    scratch += [
        V((nc, ny, TB, CF), BF), V((nc, ny, TB, CF), BF), V((ny, TB, CF), F32), V((nc, ny - 1, TB, CF), BF),
        V((ny - 1, nc, TB, CF), BF), V((T, CF), F32), V((16, CF), F32), V((16, CF), F32), V((16, F), F32),
        V((8, W), F32), V((B - 1, 8, W), F32), V((A - 1, 8, W), F32),
    ]
    sem = pltpu.SemaphoreType.DMA
    for shape in ((5, B - 1), (5, A - 1), (nc,), (nc, ny - 1), (A + B - 1,)):
        scratch += [sem(shape), sem(shape)]
    scratch += [sem((20,))]
    return pl.pallas_call(
        functools.partial(back, z),
        out_shape=outs,
        in_specs=[pl.BlockSpec(memory_space=pltpu.SMEM)] + [hbm] * 16 + [vm] * 3,
        out_specs=[hbm] * len(outs),
        scratch_shapes=scratch,
        compiler_params=pltpu.CompilerParams(
            collective_id=1, has_side_effects=True, vmem_limit_bytes=63 * 2**20
        ),
        name="back",
    )(
        off_bias, q, k, v, qr, kr, attn, ll, tokf, gba, gres, wqf, wof, gwd.reshape(A, B, R, F),
        gwg.reshape(A, B, R, 2 * F), ga, gs, cos, sin, sq,
    )


def tables(position):
    half = DK // 2
    frequency = theta_base ** (-(2.0 / DK) * jnp.arange(half, dtype=jnp.float32))
    grid = position.astype(jnp.float32)[:, None] * frequency[None, :]
    return jnp.cos(grid), jnp.sin(grid)


def on_device(
    sizes,
    tokens,
    w_qkv,
    w_out,
    w_gate_up,
    w_down,
    s_qk,
    alpha_attn,
    alpha_mlp,
    s_mlp,
    doc_lengths,
    grad_out,
):
    T, CF = tokens.shape
    H = s_qk.shape[1]
    C = H * DK
    F = w_down.shape[1]
    z = Sizes(sizes, T, C, CF, F, doc_lengths.shape[1])
    D, R = z.D, z.R
    doc_ids, position = layout(doc_lengths[0], T)
    cos, sin = tables(position)
    scale = s_qk.T.reshape(1, C)
    sml = s_mlp.transpose(1, 2, 0).reshape(2, F)
    alpha = jnp.pad(
        jnp.stack([alpha_attn.T.reshape(-1), alpha_mlp.T.reshape(-1)]), ((0, 6), (0, 0))
    )
    off_bias = jnp.where(doc_lengths[0, 0] == T, 0.0, NEG).astype(F32).reshape(1)
    cos, sin = jnp.tile(cos, (1, 4)), jnp.tile(sin, (1, 4))
    (out, q, k, v, qr, kr, attn, ll, tokf, gba, gres, wqf, wof, gwd, gwg, ga, gs, _) = run_front(
        z, off_bias, tokens, grad_out, w_qkv.reshape(R, 3 * C), w_out, w_gate_up.reshape(R, 2 * F),
        w_down, alpha, cos, sin, scale, sml,
    )
    grad_in, gw_qkv, gw_out, gw_gu, gw_down, vec = run_back(
        z, off_bias, q, k, v, qr, kr, attn, ll, tokf, gba, gres, wqf, wof, gwd, gwg, ga, gs, cos, sin, scale
    )
    d, m = place()

    def channel_rows(v, per_head):
        n = per_head // z.dp
        return lax.dynamic_slice_in_dim(v.reshape(H, per_head).T, d * n, n, 0)

    gs = jnp.stack([channel_rows(vec[i, 0:F], F // H) for i in range(2)], axis=1)
    return (
        out,
        grad_in,
        gw_qkv.reshape(R, 3, C),
        gw_out,
        gw_gu.reshape(R, 2, F),
        gw_down,
        channel_rows(vec[4, 0:C], DK),
        channel_rows(vec[2, 0:CF], DK),
        channel_rows(vec[3, 0:CF], DK),
        gs,
    )


def solution(mesh):
    placed = (
        P("dp", "mp"),
        P("dp", None, "mp"),
        P("dp", "mp"),
        P("dp", None, "mp"),
        P("dp", "mp"),
        P(None, "mp"),
        P(None, "mp"),
        P(None, "mp"),
        P(None, None, "mp"),
        P("dp", None),
        P("dp", "mp"),
    )
    return jax.shard_map(
        functools.partial(on_device, dict(mesh.shape)),
        mesh=mesh,
        in_specs=placed,
        out_specs=(
            P("dp", "mp"),
            P("dp", "mp"),
            P("dp", None, "mp"),
            P("dp", "mp"),
            P("dp", None, "mp"),
            P("dp", "mp"),
            P("dp", "mp"),
            P("dp", "mp"),
            P("dp", "mp"),
            P("dp", None, "mp"),
        ),
        check_vma=False,
    )
```

```python
import functools
import math

import jax
import jax.numpy as jnp
from jax import lax
from jax.experimental import pallas as pl
from jax.experimental.pallas import tpu as pltpu
from jax.sharding import PartitionSpec as P

DK = 64
epsilon = 1e-06
theta_base = 10000.0


def layout(lengths, token_count):
    starts = jnp.cumsum(lengths) - lengths
    place = jnp.arange(token_count, dtype=jnp.int32)
    doc_ids = jnp.sum((place[:, None] >= starts[None, 1:]).astype(jnp.int32), axis=1)
    picked = (doc_ids[:, None] == jnp.arange(lengths.shape[0], dtype=jnp.int32)[None, :]).astype(
        jnp.int32
    )
    position = place - jnp.sum(picked * starts[None, :], axis=1)
    return (doc_ids, position)


LC=math.sqrt(DK)*math.log2(math.e)
NEG=-1e30
def nt(a,b): return lax.dot_general(a,b,(((1,),(1,)),((),())),preferred_element_type=jnp.float32)
def nn(a,b): return jnp.dot(a,b,preferred_element_type=jnp.float32)
def head_mask(x,h):
    lane=lax.broadcasted_iota(jnp.int32,x.shape,1)
    return jnp.where((lane//DK)==(h%2), x, jnp.zeros_like(x))
def attn_fwd_block(i, TB, H, ref, C, live, acc):
    hb=TB//2
    qs=pl.ds(pl.multiple_of(i*TB,TB),TB)
    def vx(h,ks):
        v=ref[ks,pl.ds(2*C+(h//2)*128,128)]
        lane=lax.broadcasted_iota(jnp.int32,v.shape,1)
        return jnp.where((lane//DK)==(h%2),v,jnp.ones_like(v))
    def tile(h,qsl,ks,tri):
        p2=pl.ds((h//2)*128,128)
        x=nt(ref[qsl,p2],head_mask(ref[ks,pl.ds(C+(h//2)*128,128)],h))
        if tri:
            r=lax.broadcasted_iota(jnp.int32,x.shape,0); c=lax.broadcasted_iota(jnp.int32,x.shape,1)
            x=jnp.where(c<=r,x,NEG)
        p=jnp.exp2(x*LC).astype(jnp.bfloat16)
        return nn(p,vx(h,ks))
    k0=pl.ds(pl.multiple_of(i*TB,hb),hb); k1=pl.ds(pl.multiple_of(i*TB+hb,hb),hb)
    for h in range(H):
        a0=tile(h,qs,k0,True)
        a1=tile(h,k1,k1,True)
        acc[h,0:hb]=a0[0:hb]; acc[h,hb:TB]=a0[hb:TB]+a1
    def body(j,_):
        ks=pl.ds(pl.multiple_of(j*TB,TB),TB)
        for h in range(H):
            acc[h]+=live*tile(h,qs,ks,False)
        return 0
    lax.fori_loop(0,i,body,0)
def tdot(a,b): return lax.dot_general(a,b,(((0,),(0,)),((),())),preferred_element_type=jnp.float32)
def attn_bwd_block(i,TB,H,q_ref,k_ref,v_ref,g_ref,ll_ref,dl_ref,ob,dq,dk,dv):
    qs=pl.ds(pl.multiple_of(i*TB,TB),TB); hb=TB//2
    qz=[head_mask(q_ref[qs,pl.ds((h//2)*128,128)],h) for h in range(H)]
    gz=[head_mask(g_ref[qs,pl.ds((h//2)*128,128)],h) for h in range(H)]
    lr=[ll_ref[pl.ds(h,1),qs] for h in range(H)]
    dr=[dl_ref[pl.ds(h,1),qs] for h in range(H)]
    def tile(h,ks,qv,gv,lb,dd,tri):
        p2=pl.ds((h//2)*128,128)
        x=nt(k_ref[ks,p2],qv)*LC-lb
        dp=nt(v_ref[ks,p2],gv)
        if tri:
            r=lax.broadcasted_iota(jnp.int32,x.shape,0); c=lax.broadcasted_iota(jnp.int32,x.shape,1)
            x=jnp.where(r<=c,x,NEG)
        p=jnp.exp2(x)
        ds=(p*(dp-dd)).astype(jnp.bfloat16)
        dvp=nn(p.astype(jnp.bfloat16),gv)
        dkp=nn(ds,qv)
        dqp=tdot(ds,head_mask(k_ref[ks,p2],h))
        return dqp,dkp,dvp
    k0=pl.ds(pl.multiple_of(i*TB,hb),hb); k1=pl.ds(pl.multiple_of(i*TB+hb,hb),hb)
    for pr in range((H+1)//2):
        p2=pl.ds(pr*128,128)
        dk0=dv0=dk1=dv1=0; q0=q1=0
        for h in range(2*pr,min(2*pr+2,H)):
            a,b,c=tile(h,k0,qz[h],gz[h],lr[h],dr[h],True)
            a1,b1,c1=tile(h,k1,qz[h][hb:],gz[h][hb:],lr[h][:,hb:],dr[h][:,hb:],True)
            q0+=a[0:hb]; q1+=a[hb:]+a1
            dk0+=b; dv0+=c; dk1+=b1; dv1+=c1
        dq[0:hb,p2]=q0; dq[hb:TB,p2]=q1
        dk[k0,p2]+=dk0; dv[k0,p2]+=dv0; dk[k1,p2]+=dk1; dv[k1,p2]+=dv1
    lo=[l-ob for l in lr]
    def body(j,_):
        ks=pl.ds(pl.multiple_of(j*TB,TB),TB)
        for pr in range((H+1)//2):
            p2=pl.ds(pr*128,128)
            dka=dva=dqa=0
            for h in range(2*pr,min(2*pr+2,H)):
                a,b,c=tile(h,ks,qz[h],gz[h],lo[h],dr[h],False)
                dqa+=a; dka+=b; dva+=c
            dq[:,p2]+=dqa
            dk[ks,p2]+=dka; dv[ks,p2]+=dva
        return 0
    lax.fori_loop(0,i,body,0)


MESH = pl.DeviceIdType.MESH
F32, BF = jnp.float32, jnp.bfloat16


class Sizes:
    def __init__(self, mesh_shape, T, C, CF, F, pieces):
        self.mp, self.dp = mesh_shape["mp"], mesh_shape["dp"]
        self.ny = self.mp // 2
        self.A = 4 if self.dp % 4 == 0 else 1
        self.B = self.dp // self.A
        self.T, self.C, self.CF, self.F = T, C, CF, F
        self.D = CF * self.mp
        self.H = C // DK
        self.nc = pieces
        self.TB = T // pieces
        self.TH = self.TB // 2
        self.R = self.D // self.dp


def place():
    return lax.axis_index("dp"), lax.axis_index("mp")


def remote(src, dst, ss, rs, dev):
    return pltpu.make_async_remote_copy(
        src, dst, send_sem=ss, recv_sem=rs, device_id=dev, device_id_type=MESH
    )


def local(src, dst, sem):
    return pltpu.make_async_copy(src, dst, sem)


def rows_at(start, size):
    return pl.ds(pl.multiple_of(start, size), size)


def loop(n, fn):
    def body(i, carry):
        fn(i)
        return carry

    lax.fori_loop(0, n, body, 0)


def fold(x):
    return jnp.sum(x.reshape(x.shape[0] // 8, 8, x.shape[1]), axis=0)


def mean_sq(x, D):
    return lax.rsqrt(jnp.sum(x * x, axis=1, keepdims=True) * (1.0 / D) + epsilon)


def split_dot(x, ones):
    hi = x.astype(BF)
    return nn(hi, ones) + nn((x - hi.astype(F32)).astype(BF), ones)


def head_ones(width):
    i = lax.broadcasted_iota(jnp.int32, (width, width), 0) // DK
    j = lax.broadcasted_iota(jnp.int32, (width, width), 1) // DK
    return jnp.where(i == j, 1.0, 0.0).astype(BF)


def turn(x, cosine, sine, sign):
    lane = lax.broadcasted_iota(jnp.int32, x.shape, 1)
    first = (lane % DK) < DK // 2
    other = jnp.where(first, -pltpu.roll(x, x.shape[1] - DK // 2, 1), pltpu.roll(x, DK // 2, 1))
    return x * cosine + sign * other * sine


def front(
    z,
    ob_ref, tokens, gout, wq, wo, wg, wd, alpha, cos, sin, sq, sml,
    out, q_o, k_o, v_o, qr_o, kr_o, attn_o, ll_o, tokf, gba_o, gres_o, wqf, wof, gwd_o, gwg_o, ga_o, gs_o, goh,
    tokv, wqv, wov, wgv, wdv, gml, act, gu, gba, rot, attn, ll, acc,
    sy1, ry1, sy2, ry2, sy3, ry3, rc, sc, tokh, ghid, gst, fst, wst, alv, gacc, gsacc,
    tok_s, tok_r, w_s, w_r, x_s, x_r, al_s, al_r, go_s, go_r, ex_s, ex_r, y_s, y_r, hc_s, hc_r, out_s, out_r, lsem,
):
    T, C, CF, F, D, H = z.T, z.C, z.CF, z.F, z.D, z.H
    nc, TB, TH, R, A, B, ny, mp = z.nc, z.TB, z.TH, z.R, z.A, z.B, z.ny, z.mp
    d, m = place()
    a, b = d // B, d % B
    y, core = m // 2, m % 2
    mate = 1 - core
    peer = (d, y * 2 + mate)

    def ypeer(k, cc):
        return (d, ((y + k) % ny) * 2 + cc)

    zpeer = lambda k: (((a + k) % A) * B + b, m)
    xpeer = lambda k: (a * B + (b + k) % B, m)
    others = [peer] + [ypeer(k, cc) for k in range(1, ny) for cc in (core, mate)]
    everyone = others + [zpeer(k) for k in range(1, A)] + [xpeer(k) for k in range(1, B)]
    bar = pltpu.get_barrier_semaphore()
    for dev in everyone:
        pl.semaphore_signal(bar, 1, device_id=dev, device_id_type=MESH)
    pl.semaphore_wait(bar, len(everyone))

    live = ob_ref[0]
    feat = lambda mm: pl.ds(pl.multiple_of(mm * CF, CF), CF)
    mine = feat(m)


    def tok_own(c, i, dev):
        r = rows_at(c * TB, TB)
        return remote(tokens.at[r], tokv.at[r, mine], tok_s.at[c, i], tok_r.at[c, i], dev)

    def tok_got(c, i, mm):
        r = rows_at(c * TB, TB)
        return remote(tokv.at[r, feat(mm)], tokv.at[r, feat(mm)], tok_s.at[c, i], tok_r.at[c, i], peer)

    def start_tok(i):
        c = nc - 1 - i
        for k in range(1, ny):
            tok_own(c, k, ypeer(k, core)).start()
        tok_own(c, 0, peer).start()

    weights = [(wq, wqv), (wo, wov), (wg, wgv), (wd, wdv)]

    def shard(aa, bb):
        return rows_at((aa * B + bb) * R, R)

    def column(st):
        return (b - st + B) % B

    def z_moves(w, st, h):
        src, dst = weights[w]
        moves = []
        for way, step in ((0, 1), (1, -1)):
            aa = a - step * (h - 1)
            ok = (a + step >= 0) & (a + step < A) & (aa >= 0) & (aa < A)
            moves.append((way, step, jnp.clip(aa, 0, A - 1), ok))
        return src, dst, moves

    def z_copy(w, st, h, way, step, aa):
        src, dst = weights[w]
        r = shard(aa, column(st))
        source = src if (h == 1 and st == 0) else dst.at[r]
        to = jnp.clip(a + step, 0, A - 1) * B + b
        return remote(source, dst.at[r], w_s.at[w, st, way, h - 1], w_r.at[w, st, way, h - 1], (to, m))

    def z_hop(w, st, h):
        if h >= A:
            return
        for way, step, aa, ok in z_moves(w, st, h)[2]:

            @pl.when(ok)
            def _():
                z_copy(w, st, h, way, step, aa).start()

    def z_sent(w, st, h):
        for way, step, aa, ok in z_moves(w, st, h)[2]:

            @pl.when(ok)
            def _():
                z_copy(w, st, h, way, step, aa).wait_send()

    def z_wait(w, st, h, forward=False):
        if h >= A:
            return
        for way, step in ((0, 1), (1, -1)):
            aa = a - step * h

            @pl.when((aa >= 0) & (aa < A))
            def _():
                z_copy(w, st, h, way, step, jnp.clip(aa, 0, A - 1)).wait_recv()
                if forward:
                    x_send(w, aa)

    def x_copy(w, aa, k, own=False):
        src, dst = weights[w]
        r = shard(aa, b)
        return remote(
            src if own else dst.at[r], dst.at[r], x_s.at[w, aa, k - 1], x_r.at[w, aa, k - 1], xpeer(k)
        )

    def x_send(w, aa, own=False):
        for k in range(1, B):
            x_copy(w, aa, k, own).start()

    def x_wait(w, aa):
        src, dst = weights[w]
        for k in range(1, B):
            r = shard(aa, (b - k + B) % B)
            remote(src, dst.at[r], x_s.at[w, aa, k - 1], x_r.at[w, aa, k - 1], xpeer(k)).wait_recv()

    def w_local(w):
        src, dst = weights[w]
        return local(src, dst.at[shard(a, b)], lsem.at[w])

    def w_start(w):
        z_hop(w, 0, 1)
        x_send(w, a, own=True)
        w_local(w).start()

    def w_next(w, st, h, forward=True):
        z_wait(w, st, h, forward)
        z_hop(w, st, h + 1)

    def w_ready(w):
        for aa in range(A):
            x_wait(w, aa)
        w_local(w).wait()

    def w_sent(w, forward):
        for st in range(1 if forward else B):
            for h in range(1, A):
                z_sent(w, st, h)
        for k in range(1, B):
            for aa in range(A) if forward else [a]:
                x_copy(w, aa, k).wait_send()

    w_start(0)
    loop(nc, start_tok)
    w_start(1)
    tok_local = local(tokens, tokv.at[:, mine], lsem.at[4])
    tok_local.start()
    al_local = local(alpha, alv.at[:, mine], lsem.at[5])
    al_local.start()
    al_copies = [
        remote(alpha, alv.at[:, mine], al_s.at[i], al_r.at[i], dev) for i, dev in enumerate(others)
    ]
    for cp in al_copies:
        cp.start()

    def pass_tok(i):
        c = nc - 1 - i
        for k in range(1, ny):
            src = ((y - k + ny) % ny) * 2 + core
            tok_got(c, k, src).wait_recv()
            tok_got(c, ny + k - 1, src).start()

    w_next(0, 0, 1)
    w_start(2)
    w_next(1, 0, 1)
    w_next(0, 0, 2)
    w_next(1, 0, 2)
    pass_tok(0)
    w_next(0, 0, 3)
    w_next(1, 0, 3)
    w_start(3)
    loop(nc - 1, lambda i: pass_tok(i + 1))

    def end_tok(i):
        c = nc - 1 - i
        tok_got(c, 0, y * 2 + mate).wait_recv()
        for k in range(1, ny):
            src = ((y - k + ny) % ny) * 2 + mate
            tok_got(c, ny + k - 1, src).wait_recv()

    loop(nc, end_tok)

    def tok_sent(i):
        c = nc - 1 - i
        tok_own(c, 0, peer).wait_send()
        for k in range(1, ny):
            tok_own(c, k, ypeer(k, core)).wait_send()
            tok_got(c, ny + k - 1, ((y - k + ny) % ny) * 2 + core).wait_send()

    loop(nc, tok_sent)
    tok_local.wait()
    w_next(2, 0, 1, False)
    w_ready(0)

    go4 = gout

    def go_copy(i, dev, cc):
        return remote(go4.at[:, cc], goh.at[:, :, mine], go_s.at[i], go_r.at[i], dev)

    go_copies = [go_copy(0, peer, mate)]
    i = 1
    for k in range(1, ny):
        for cc in (core, mate):
            go_copies.append(go_copy(i, ypeer(k, cc), cc))
            i += 1
    go_local = local(go4.at[:, core], goh.at[:, :, mine], lsem.at[6])
    go_local.start()
    for cp in go_copies:
        cp.start()

    ones = head_ones(C)
    qkvv = gml

    def project_rows(i):
        r = rows_at(i * TB, TB)
        x = tokv[r, :]
        cs = jnp.concatenate([cos[r, :]] * (C // 128), axis=1)
        sn = jnp.concatenate([sin[r, :]] * (C // 128), axis=1)
        for part in range(2):
            cols = slice(part * C, part * C + C)
            t = turn(nn(x, wqv[:, cols]), cs, sn, 1.0)
            rot[part, r, :] = t.astype(BF)
            inv = lax.rsqrt(split_dot(t * t, ones) + epsilon)
            qkvv[r, cols] = (t * inv * sq[...]).astype(BF)
        qkvv[r, 2 * C : 3 * C] = nn(x, wqv[:, 2 * C : 3 * C]).astype(BF)

    loop(nc, project_rows)
    save_tok = local(tokv, tokf, lsem.at[4])
    save_tok.start()
    saves = [
        local(qkvv.at[:, 0:C], q_o, lsem.at[7]),
        local(qkvv.at[:, C : 2 * C], k_o, lsem.at[8]),
        local(qkvv.at[:, 2 * C : 3 * C], v_o, lsem.at[9]),
        local(rot.at[0], qr_o, lsem.at[10]),
        local(rot.at[1], kr_o, lsem.at[11]),
        local(wqv, wqf, lsem.at[12]),
    ]
    for cp in saves:
        cp.start()
    w_ready(1)
    w_next(2, 0, 2, False)
    x_wait(2, a)
    for st in range(1, B):
        z_hop(2, st, 1)
    w_next(3, 0, 1)

    RT = 64
    NG = 2
    GW = D // NG

    def y_copy(e, c, k, n, sy, ry):
        cols = slice(n * GW, n * GW + GW)
        return remote(
            sy.at[c, :, cols], ry.at[k - 1, c, :, cols], y_s.at[e, c, k - 1, n], y_r.at[e, c, k - 1, n],
            ypeer(k, core),
        )

    def exchange(e, c, part, sy, ry):
        r = rows_at(c * TB, TB)
        theirs, ours = rows_at(mate * TH, TH), rows_at(core * TH, TH)
        copies = []
        for n in range(NG):
            cols = slice(n * GW, n * GW + GW)
            sc[:, cols] = part(r, cols).astype(BF)
            cp = remote(
                sc.at[theirs, cols], rc.at[c, :, cols], ex_s.at[e, c, n], ex_r.at[e, c, n], peer
            )
            cp.start()
            copies.append(cp)
        for n in range(NG):
            cols = slice(n * GW, n * GW + GW)
            copies[n].wait()
            sy[c, :, cols] = (sc[ours, cols].astype(F32) + rc[c, :, cols].astype(F32)).astype(BF)
            for k in range(1, ny):
                y_copy(e, c, k, n, sy, ry).start()

    def landed(e, c, sy, ry):
        for k in range(1, ny):
            for n in range(NG):
                y_copy(e, c, k, n, sy, ry).wait()

    def total(c, r, sy, ry):
        t = sy[c, r, :].astype(F32)
        for k in range(ny - 1):
            t = t + ry[k, c, r, :].astype(F32)
        return t

    NS = 2
    SH = TH // NS

    def share(e, c, n, buf):
        r = rows_at(c * TB + core * TH + n * SH, SH)
        return remote(buf.at[r], buf.at[r], hc_s.at[e, c, n], hc_r.at[e, c, n], peer)

    def rows_then_share(e, c, rows, buf):
        for n in range(NS):
            loop(SH // RT, lambda t: rows(n * (SH // RT) + t))
            share(e, c, n, buf).start()

    def shared(e, c, buf):
        for n in range(NS):
            share(e, c, n, buf).wait()

    def attend_chunk(i):
        c = nc - 1 - i
        attn_fwd_block(c, TB, H, qkvv, C, live, acc)
        r = rows_at(c * TB, TB)
        for pr in range(C // 128):
            both = []
            for h in (2 * pr, 2 * pr + 1):
                t = acc[h]
                both.append(t / pltpu.roll(t, DK, 1))
                row = DK if h % 2 == 0 else 0
                ll[pl.ds(h, 1), r] = jnp.log2(t).T[row : row + 1]
            lane = lax.broadcasted_iota(jnp.int32, (TB, 128), 1)
            attn[r, pr * 128 : pr * 128 + 128] = jnp.where(lane < DK, both[0], both[1]).astype(BF)

        def part(rr, cols):
            return nt(attn[rr, :], wov[cols, :])

        @pl.when(i == 0)
        def _():
            save_tok.wait()

        exchange(0, c, part, sy1, ry1)

        @pl.when(i == 0)
        def _():
            w_next(2, 0, 3, False)
            for st in range(1, B):
                w_next(2, st, 1, False)
            w_next(3, 0, 2)

        @pl.when(i == 1)
        def _():
            for st in range(1, B):
                w_next(2, st, 2, False)
            w_next(3, 0, 3)


    ll[...] = jnp.zeros_like(ll)
    loop(nc, attend_chunk)
    save_attn = local(attn, attn_o, lsem.at[13])
    save_attn.start()
    save_ll = local(ll, ll_o, lsem.at[14])
    save_ll.start()
    save_wo = local(wov, wof, lsem.at[15])
    save_wo.start()
    for cp in saves:
        cp.wait()
    al_local.wait()
    for cp in al_copies:
        cp.wait()
    for st in range(1, B):
        w_next(2, st, 3, False)
    w_local(2).wait()

    gacc[...] = jnp.zeros_like(gacc)
    gsacc[...] = jnp.zeros_like(gsacc)

    def feed_chunk(i):
        c = nc - 1 - i
        landed(0, c, sy1, ry1)
        base = c * TB + core * TH

        def rows(t):
            r = rows_at(t * RT, RT)
            g = rows_at(base + t * RT, RT)
            br = total(c, r, sy1, ry1)
            xb = tokv[g, :]
            tokh[c, r, :] = xb
            x = xb.astype(F32)
            ha = br * mean_sq(br, D)
            mix = x + alv[0:1, :] * (ha - x)
            tokv[g, :] = (mix * mean_sq(mix, D)).astype(BF)

        rows_then_share(0, c, rows, tokv)
        shared(0, c, tokv)
        r = rows_at(c * TB, TB)

        def units(n):
            cu, cv = rows_at(n * 256, 256), rows_at(F + n * 256, 256)
            x = tokv[r, :]
            u = nn(x, wgv[:, cu])
            v = nn(x, wgv[:, cv])
            gu[r, cu] = u.astype(BF)
            gu[r, cv] = v.astype(BF)
            us = u * sml[0:1, cu]
            vs = v * sml[1:2, cu]
            act[r, cu] = (us * vs * jax.nn.sigmoid(vs)).astype(BF)

        loop(F // 256, units)

        @pl.when(i == 0)
        def _():
            w_ready(3)

        exchange(1, c, lambda rr, cols: nt(act[rr, :], wdv[cols, :]), sy2, ry2)

    loop(nc, feed_chunk)
    go_local.wait()
    for cp in go_copies:
        cp.wait()

    def back_chunk(i):
        c = nc - 1 - i
        lg = local(goh.at[c], gst, lsem.at[6])
        lg.start()
        lg.wait()
        landed(1, c, sy2, ry2)
        base = c * TB + core * TH

        def rows(t):
            r = rows_at(t * RT, RT)
            g = rows_at(base + t * RT, RT)
            am = alv[1:2, :]
            bm = total(c, r, sy2, ry2)
            h = tokv[g, :].astype(F32)
            rm = mean_sq(bm, D)
            hm = bm * rm
            diff = hm - h
            mix = h + am * diff
            r2 = mean_sq(mix, D)
            fin = mix * r2
            fst[r, :] = fin.astype(BF)
            go = gst[r, :].astype(F32)
            gm = r2 * (go - fin * (jnp.sum(go * fin, axis=1, keepdims=True) * (1.0 / D)))
            gacc[8:16, :] += fold(gm * diff)
            gh = am * gm
            ghid[c, r, :] = (gm - gh).astype(BF)
            gb = rm * (gh - hm * (jnp.sum(gh * hm, axis=1, keepdims=True) * (1.0 / D)))
            gml[g, :] = gb.astype(BF)

        rows_then_share(1, c, rows, gml)
        og = rows_at(base, TH)
        o_here = local(fst.at[:, mine], out.at[og], lsem.at[6])
        o_here.start()
        o_there = remote(
            fst.at[:, feat(y * 2 + mate)], out.at[og], out_s.at[c], out_r.at[c], peer
        )
        o_there.start()
        shared(1, c, gml)
        r = rows_at(c * TB, TB)

        def units(n):
            cu, cv = rows_at(n * 256, 256), rows_at(F + n * 256, 256)
            ga = nn(gml[r, :], wdv[:, cu])
            u = gu[r, cu].astype(F32)
            v = gu[r, cv].astype(F32)
            su, sv = sml[0:1, cu], sml[1:2, cu]
            us, vs = u * su, v * sv
            sg = jax.nn.sigmoid(vs)
            si = vs * sg
            g_u = ga * si
            g_v = ga * us * (sg + si - si * sg)
            gsacc[0:8, cu] += fold(g_u * u)
            gsacc[8:16, cu] += fold(g_v * v)
            gu[r, cu] = (g_u * su).astype(BF)
            gu[r, cv] = (g_v * sv).astype(BF)

        loop(F // 256, units)
        exchange(2, c, lambda rr, cols: nt(gu[rr, :], wgv[cols, :]), sy3, ry3)
        o_here.wait()
        o_there.wait()

    loop(nc, back_chunk)

    RA = D // A

    def grad_tile(t):
        cols = rows_at(t * RA, RA)
        lhs = gml[:, cols]
        wst[:, 0:F] = lax.dot_general(
            lhs, act[...], (((0,), (0,)), ((), ())), preferred_element_type=F32
        ).astype(BF)
        cp = local(wst.at[:, 0:F], gwd_o.at[cols], lsem.at[6])
        cp.start()
        cp.wait()
        lhs = tokv[:, cols]
        wst[:, 0:F] = lax.dot_general(
            lhs, gu[:, 0:F], (((0,), (0,)), ((), ())), preferred_element_type=F32
        ).astype(BF)
        wst[:, F : 2 * F] = lax.dot_general(
            lhs, gu[:, F : 2 * F], (((0,), (0,)), ((), ())), preferred_element_type=F32
        ).astype(BF)
        cp = local(wst, gwg_o.at[cols], lsem.at[6])
        cp.start()
        cp.wait()

    loop(A, grad_tile)

    def attn_grad_chunk(i):
        c = nc - 1 - i
        landed(2, c, sy3, ry3)
        base = c * TB + core * TH

        def rows(t):
            r = rows_at(t * RT, RT)
            g = rows_at(base + t * RT, RT)
            aa = alv[0:1, :]
            br = total(c, r, sy1, ry1)
            x = tokh[c, r, :].astype(F32)
            ra = mean_sq(br, D)
            ha = br * ra
            diff = ha - x
            mix = x + aa * diff
            r1 = mean_sq(mix, D)
            hid = mix * r1
            gh = ghid[c, r, :].astype(F32) + total(c, r, sy3, ry3)
            gm = r1 * (gh - hid * (jnp.sum(gh * hid, axis=1, keepdims=True) * (1.0 / D)))
            gacc[0:8, :] += fold(gm * diff)
            gt = aa * gm
            ghid[c, r, :] = (gm - gt).astype(BF)
            gb = ra * (gt - ha * (jnp.sum(gt * ha, axis=1, keepdims=True) * (1.0 / D)))
            gba[g, :] = gb.astype(BF)

        rows_then_share(2, c, rows, gba)
        shared(2, c, gba)

    loop(nc, attn_grad_chunk)
    ends = [
        local(gba, gba_o, lsem.at[0]),
        local(ghid, gres_o, lsem.at[1]),
        local(gacc, ga_o, lsem.at[2]),
        local(gsacc, gs_o, lsem.at[3]),
    ]
    for cp in ends:
        cp.start()
    for w in range(4):
        w_sent(w, w != 2)
    for cp in ends + [save_attn, save_ll, save_wo]:
        cp.wait()


def run_front(z, off_bias, tokens, gout, wq, wo, wg, wd, alpha, cos, sin, sq, sml):
    T, C, CF, F, D, H = z.T, z.C, z.CF, z.F, z.D, z.H
    nc, TB, TH, R, A, B, ny, mp = z.nc, z.TB, z.TH, z.R, z.A, z.B, z.ny, z.mp
    S = jax.ShapeDtypeStruct
    hbm = pl.BlockSpec(memory_space=pltpu.HBM)
    vm = pl.BlockSpec(memory_space=pltpu.VMEM)
    outs = [
        S((T, CF), BF), S((T, C), BF), S((T, C), BF), S((T, C), BF), S((T, C), BF), S((T, C), BF),
        S((T, C), BF), S((8, T), F32), S((T, D), BF), S((T, D), BF), S((nc, TH, D), BF),
        S((D, 3 * C), BF), S((D, C), BF), S((D, F), BF), S((D, 2 * F), BF), S((16, D), F32),
        S((16, F), F32), S((nc, TH, D), BF),
    ]
    V = pltpu.VMEM
    scratch = [
        V((T, D), BF), V((D, 3 * C), BF), V((D, C), BF), V((D, 2 * F), BF), V((D, F), BF),
        V((T, D), BF), V((T, F), BF), V((T, 2 * F), BF), V((T, D), BF),
        V((2, T, C), BF), V((T, C), BF), V((8, T), F32), V((H, TB, 128), F32),
    ]
    for _ in range(3):
        scratch += [V((nc, TH, D), BF), V((ny - 1, nc, TH, D), BF)]
    scratch += [
        V((nc, TH, D), BF), V((TB, D), BF), V((nc, TH, D), BF), V((nc, TH, D), BF),
        V((TH, D), BF), V((TH, D), BF), V((D // A, 2 * F), BF), V((8, D), F32), V((16, D), F32), V((16, F), F32),
    ]
    sem = pltpu.SemaphoreType.DMA
    for shape in (
        (nc, 2 * ny - 1), (4, B, 2, max(A - 1, 1)), (4, A, max(B - 1, 1)), (mp - 1,), (mp - 1,), (3, nc, 2),
        (3, nc, ny - 1, 2), (3, nc, 2), (nc,),
    ):
        scratch += [sem(shape), sem(shape)]
    scratch += [sem((16,))]
    return pl.pallas_call(
        functools.partial(front, z),
        out_shape=outs,
        in_specs=[pl.BlockSpec(memory_space=pltpu.SMEM)] + [hbm] * 7 + [vm] * 4,
        out_specs=[hbm] * len(outs),
        scratch_shapes=scratch,
        compiler_params=pltpu.CompilerParams(
            collective_id=0, has_side_effects=True, vmem_limit_bytes=63 * 2**20
        ),
        name="front",
    )(off_bias, tokens, gout.reshape(nc, 2, TH, CF), wq, wo, wg, wd, alpha, cos, sin, sq, sml)


def back(
    z,
    ob_ref, q_h, k_h, v_h, qr_h, kr_h, attn_h, ll_h, tok_h, gba_h, gres_h, wq_h, wo_h, gwd_h, gwg_h, ga_h, gs_h,
    cos, sin, sq,
    gin_o, owq, owo, owg, owd, vec_o,
    qv, kv, vv, rot, attn, ll, dl, wqv, wov, gba, tok, gres, gm, dk, dv, dq, gqkv, gsq,
    own_d, own_g0, own_g1, gwo, gwq,
    r1_d, r1_g0, r1_g1, r1_o, r1_q, s2_d, s2_g0, s2_g1, s2_o, s2_q, r2_d, r2_g0, r2_g1, r2_o, r2_q,
    f_d, f_g, f_o, f_q,
    sc2, rc2, ow, sy, ry, gin, gal, gar, gsl, vec, rv1, rv2,
    x_s, x_r, z_s, z_r, c_s, c_r, y_s, y_r, m_s, m_r, lsem,
):
    T, C, CF, F, D, H = z.T, z.C, z.CF, z.F, z.D, z.H
    nc, TB, TH, R, A, B, ny = z.nc, z.TB, z.TH, z.R, z.A, z.B, z.ny
    d, m = place()
    a, b = d // B, d % B
    y, core = m // 2, m % 2
    mate = 1 - core
    peer = (d, y * 2 + mate)
    ypeer = lambda k: (d, ((y + k) % ny) * 2 + core)
    zpeer = lambda k: (((a + k) % A) * B + b, m)
    xpeer = lambda k: (a * B + (b + k) % B, m)
    everyone = (
        [peer]
        + [ypeer(k) for k in range(1, ny)]
        + [zpeer(k) for k in range(1, A)]
        + [xpeer(k) for k in range(1, B)]
    )
    bar = pltpu.get_barrier_semaphore()
    for dev in everyone:
        pl.semaphore_signal(bar, 1, device_id=dev, device_id_type=MESH)
    pl.semaphore_wait(bar, len(everyone))
    feat = lambda mm: pl.ds(pl.multiple_of(mm * CF, CF), CF)
    ob = ob_ref[0]

    lo, hi = slice(0, F), slice(F, 2 * F)
    pieces = [
        (lambda bb: gwd_h.at[:, bb], own_d, r1_d, s2_d, r2_d, f_d, owd),
        (lambda bb: gwg_h.at[:, bb, :, lo], own_g0, r1_g0, s2_g0, r2_g0, f_g.at[:, lo], None),
        (lambda bb: gwg_h.at[:, bb, :, hi], own_g1, r1_g1, s2_g1, r2_g1, f_g.at[:, hi], owg),
        (lambda bb: gwo.at[:, bb], None, r1_o, s2_o, r2_o, f_o, owo),
        (lambda bb: gwq.at[:, bb], None, r1_q, s2_q, r2_q, f_q, owq),
    ]

    def x_copy(p, k):
        blocks, r1 = pieces[p][0], pieces[p][2]
        return remote(
            blocks((b + k) % B), r1.at[k - 1], x_s.at[p, k - 1], x_r.at[p, k - 1], xpeer(k)
        )

    def own_copy(p):
        return local(pieces[p][0](b), pieces[p][1], lsem.at[p])

    def rs_start(p):
        for k in range(1, B):
            x_copy(p, k).start()
        if pieces[p][1] is not None:
            own_copy(p).start()

    def z_copy(p, k):
        s2, r2 = pieces[p][3], pieces[p][4]
        return remote(s2.at[(a + k) % A], r2.at[k - 1], z_s.at[p, k - 1], z_r.at[p, k - 1], zpeer(k))

    def rs_middle(p):
        blocks, mine, r1, s2 = pieces[p][:4]
        if mine is not None:
            own_copy(p).wait()
        for k in range(1, B):
            x_copy(p, k).wait()
        for k in list(range(1, A)) + [0]:
            aa = (a + k) % A

            def add(t):
                r = rows_at(t * 16, 16)
                src = mine[aa, r, :] if mine is not None else blocks(b)[aa, r, :]
                total = src.astype(F32)
                for kk in range(B - 1):
                    total = total + r1[kk, aa, r, :].astype(F32)
                s2[aa, r, :] = total.astype(BF)

            loop(R // 16, add)
            if k:
                z_copy(p, k).start()

    def rs_end(p):
        s2, r2, res = pieces[p][3:6]
        for k in range(1, A):
            z_copy(p, k).wait()

        def add(t):
            r = rows_at(t * 16, 16)
            total = s2[a, r, :].astype(F32)
            for kk in range(A - 1):
                total = total + r2[kk, r, :].astype(F32)
            res[r, :] = total

        loop(R // 16, add)

    rs_start(0)
    rs_start(1)
    rs_start(2)
    ga_there = remote(
        ga_h.at[:, feat(y * 2 + mate)], gar, m_s.at[0], m_r.at[0], peer
    )
    ga_there.start()
    loads = [
        local(s, t, lsem.at[5 + i])
        for i, (s, t) in enumerate(
            [
                (q_h, qv), (k_h, kv), (wo_h, wov), (gba_h, gba), (v_h, vv), (attn_h, attn), (ll_h, ll),
                (qr_h, rot.at[0]), (kr_h, rot.at[1]), (wq_h, wqv), (gres_h, gres),
                (ga_h.at[:, feat(m)], gal), (gs_h, gsl), (tok_h, tok),
            ]
        )
    ]
    for cp in loads:
        cp.start()
    dk[...] = jnp.zeros_like(dk)
    dv[...] = jnp.zeros_like(dv)
    gsq[...] = jnp.zeros_like(gsq)
    for cp in loads[:7]:
        cp.wait()

    ones = head_ones(C)
    heads = lax.broadcasted_iota(jnp.int32, (8, C), 0)
    lanes = lax.broadcasted_iota(jnp.int32, (8, C), 1) // DK
    pick = jnp.where(heads == lanes, 1.0, 0.0).astype(BF)
    for cp in loads[7:]:
        cp.wait()

    def gin_copy(c):
        return remote(sc2.at[c], rc2.at[c], c_s.at[c], c_r.at[c], peer)

    def y_copy(c, k):
        return remote(sy.at[c, k - 1], ry.at[k - 1, c], y_s.at[c, k - 1], y_r.at[c, k - 1], ypeer(k))

    def chunk(i):
        c = nc - 1 - i
        r = rows_at(c * TB, TB)
        g = nn(gba[r, :], wov[...]).astype(BF)
        gm[r, :] = g
        prod = g.astype(F32) * attn[r, :].astype(F32)
        ph = prod.astype(BF)
        dl[:, r] = nt(pick, ph) + nt(pick, (prod - ph.astype(F32)).astype(BF))
        attn_bwd_block(c, TB, H, qv, kv, vv, gm, ll, dl, ob, dq, dk, dv)
        cs = jnp.concatenate([cos[r, :]] * (C // 128), axis=1)
        sn = jnp.concatenate([sin[r, :]] * (C // 128), axis=1)
        for part in range(2):
            gh = (dq[...] if part == 0 else dk[r, :]) * 8.0
            t = rot[part, r, :].astype(F32)
            inv = lax.rsqrt(split_dot(t * t, ones) + epsilon)
            un = t * inv
            gsq[...] += fold(gh * un)
            gh = gh * sq[...]
            gr = inv * (gh - un * split_dot(gh * un, ones))
            gqkv[r, part * C : part * C + C] = turn(gr, cs, sn, -1.0).astype(BF)
        gqkv[r, 2 * C : 3 * C] = dv[r, :].astype(BF)

        def product(hsel, k, cc):
            rr = rows_at(c * TB + hsel * TH, TH)
            cols = feat(((y + k) % ny) * 2 + cc)
            t = nt(gqkv[rr, :], wqv[cols, :])
            if k == 0:
                t = t + jnp.where(hsel == core, 1.0, 0.0) * gres[c, :, cols].astype(F32)
            return t

        for k in range(ny):
            for hs in range(2):
                sc2[c, k, hs * TH : (hs + 1) * TH, :] = product(hs, k, mate).astype(BF)
        gin_copy(c).start()
        for k in range(ny):
            for hs in range(2):
                ow[k, hs * TH : (hs + 1) * TH, :] = product(hs, k, core)
        gin_copy(c).wait()
        gin[r, :] = ow[0] + rc2[c, 0].astype(F32)
        for k in range(1, ny):
            sy[c, k - 1] = (ow[k] + rc2[c, k].astype(F32)).astype(BF)
            y_copy(c, k).start()

        @pl.when(i == 1)
        def _():
            rs_middle(0)

    loop(nc, chunk)

    def out_tile(t):
        cols = rows_at(t * B * R, B * R)
        g = lax.dot_general(
            gba[:, cols], attn[...], (((0,), (0,)), ((), ())), preferred_element_type=F32
        )
        gwo[t] = g.astype(BF).reshape(B, R, C)

    loop(A, out_tile)
    rs_start(3)

    def qkv_tile(t):
        cols = rows_at(t * B * R, B * R)
        g = lax.dot_general(
            tok[:, cols], gqkv[...], (((0,), (0,)), ((), ())), preferred_element_type=F32
        )
        gwq[t] = g.astype(BF).reshape(B, R, 3 * C)

    loop(A, qkv_tile)
    rs_start(4)
    W = vec.shape[1]
    ga_there.wait()
    vec[...] = jnp.zeros_like(vec)
    gt = gal[...] + gar[...]
    vec[0:1, 0:F] = jnp.sum(gsl[0:8, :], axis=0, keepdims=True)
    vec[1:2, 0:F] = jnp.sum(gsl[8:16, :], axis=0, keepdims=True)
    vec[2:3, 0:CF] = jnp.sum(gt[0:8], axis=0, keepdims=True)
    vec[3:4, 0:CF] = jnp.sum(gt[8:16], axis=0, keepdims=True)
    vec[4:5, 0:C] = jnp.sum(gsq[...], axis=0, keepdims=True)
    vx = [remote(vec, rv1.at[k - 1], m_s.at[k], m_r.at[k], xpeer(k)) for k in range(1, B)]
    for cp in vx:
        cp.start()
    rs_middle(1)
    for cp in vx:
        cp.wait()
    t = vec[...]
    for k in range(B - 1):
        t = t + rv1[k]
    vec[...] = t
    vz = [
        remote(vec, rv2.at[k - 1], m_s.at[B - 1 + k], m_r.at[B - 1 + k], zpeer(k)) for k in range(1, A)
    ]
    for cp in vz:
        cp.start()
    rs_middle(2)
    rs_end(0)
    ends = [local(f_d, owd, lsem.at[0])]
    ends[0].start()

    def gin_end(i):
        c = nc - 1 - i
        r = rows_at(c * TB, TB)
        for k in range(1, ny):
            y_copy(c, k).wait()
            gin[r, :] += ry[k - 1, c].astype(F32)

    loop(nc, gin_end)
    ends.append(local(gin, gin_o, lsem.at[1]))
    ends[-1].start()
    rs_middle(3)
    rs_middle(4)
    rs_end(1)
    rs_end(2)
    ends.append(local(f_g, owg, lsem.at[2]))
    ends[-1].start()
    for cp in vz:
        cp.wait()
    t = vec[...]
    for k in range(A - 1):
        t = t + rv2[k]
    vec[...] = t
    ends.append(local(vec, vec_o, lsem.at[3]))
    ends[-1].start()
    rs_end(3)
    ends.append(local(f_o, owo, lsem.at[4]))
    ends[-1].start()
    rs_end(4)
    ends.append(local(f_q, owq, lsem.at[5]))
    ends[-1].start()
    for cp in ends:
        cp.wait()


def run_back(z, off_bias, q, k, v, qr, kr, attn, ll, tokf, gba, gres, wqf, wof, gwd, gwg, ga, gs, cos, sin, sq):
    T, C, CF, F, D, H = z.T, z.C, z.CF, z.F, z.D, z.H
    nc, TB, TH, R, A, B, ny = z.nc, z.TB, z.TH, z.R, z.A, z.B, z.ny
    S = jax.ShapeDtypeStruct
    V = pltpu.VMEM
    hbm = pl.BlockSpec(memory_space=pltpu.HBM)
    vm = pl.BlockSpec(memory_space=pltpu.VMEM)
    W = max(F, CF, C)
    outs = [
        S((T, CF), F32), S((R, 3 * C), F32), S((R, C), F32), S((R, 2 * F), F32), S((R, F), F32), S((8, W), F32),
    ]
    cols = (F, F, F, C, 3 * C)
    scratch = [
        V((T, C), BF), V((T, C), BF), V((T, C), BF), V((2, T, C), BF), V((T, C), BF),
        V((8, T), F32), V((8, T), F32), V((D, 3 * C), BF), V((D, C), BF), V((T, D), BF), V((T, D), BF),
        V((nc, TH, D), BF), V((T, C), BF), V((T, C), F32), V((T, C), F32), V((TB, C), F32),
        V((T, 3 * C), BF), V((8, C), F32),
        V((A, R, F), BF), V((A, R, F), BF), V((A, R, F), BF), V((A, B, R, C), BF), V((A, B, R, 3 * C), BF),
    ]
    scratch += [V((B - 1, A, R, w), BF) for w in cols]
    scratch += [V((A, R, w), BF) for w in cols]
    scratch += [V((A - 1, R, w), BF) for w in cols]
    scratch += [V((R, F), F32), V((R, 2 * F), F32), V((R, C), F32), V((R, 3 * C), F32)]
    scratch += [
        V((nc, ny, TB, CF), BF), V((nc, ny, TB, CF), BF), V((ny, TB, CF), F32), V((nc, ny - 1, TB, CF), BF),
        V((ny - 1, nc, TB, CF), BF), V((T, CF), F32), V((16, CF), F32), V((16, CF), F32), V((16, F), F32),
        V((8, W), F32), V((B - 1, 8, W), F32), V((A - 1, 8, W), F32),
    ]
    sem = pltpu.SemaphoreType.DMA
    for shape in ((5, B - 1), (5, A - 1), (nc,), (nc, ny - 1), (A + B - 1,)):
        scratch += [sem(shape), sem(shape)]
    scratch += [sem((20,))]
    return pl.pallas_call(
        functools.partial(back, z),
        out_shape=outs,
        in_specs=[pl.BlockSpec(memory_space=pltpu.SMEM)] + [hbm] * 16 + [vm] * 3,
        out_specs=[hbm] * len(outs),
        scratch_shapes=scratch,
        compiler_params=pltpu.CompilerParams(
            collective_id=1, has_side_effects=True, vmem_limit_bytes=63 * 2**20
        ),
        name="back",
    )(
        off_bias, q, k, v, qr, kr, attn, ll, tokf, gba, gres, wqf, wof, gwd.reshape(A, B, R, F),
        gwg.reshape(A, B, R, 2 * F), ga, gs, cos, sin, sq,
    )


def tables(position):
    half = DK // 2
    frequency = theta_base ** (-(2.0 / DK) * jnp.arange(half, dtype=jnp.float32))
    grid = position.astype(jnp.float32)[:, None] * frequency[None, :]
    return jnp.cos(grid), jnp.sin(grid)


def on_device(
    sizes,
    tokens,
    w_qkv,
    w_out,
    w_gate_up,
    w_down,
    s_qk,
    alpha_attn,
    alpha_mlp,
    s_mlp,
    doc_lengths,
    grad_out,
):
    T, CF = tokens.shape
    H = s_qk.shape[1]
    C = H * DK
    F = w_down.shape[1]
    z = Sizes(sizes, T, C, CF, F, doc_lengths.shape[1])
    D, R = z.D, z.R
    doc_ids, position = layout(doc_lengths[0], T)
    cos, sin = tables(position)
    scale = s_qk.T.reshape(1, C)
    sml = s_mlp.transpose(1, 2, 0).reshape(2, F)
    alpha = jnp.pad(
        jnp.stack([alpha_attn.T.reshape(-1), alpha_mlp.T.reshape(-1)]), ((0, 6), (0, 0))
    )
    whole = doc_lengths[0, 0] == T
    off_bias = jnp.where(whole, 0.0, NEG).astype(F32).reshape(1)
    live = whole.astype(F32).reshape(1)
    cos, sin = jnp.tile(cos, (1, 4)), jnp.tile(sin, (1, 4))
    (out, q, k, v, qr, kr, attn, ll, tokf, gba, gres, wqf, wof, gwd, gwg, ga, gs, _) = run_front(
        z, live, tokens, grad_out, w_qkv.reshape(R, 3 * C), w_out, w_gate_up.reshape(R, 2 * F),
        w_down, alpha, cos, sin, scale, sml,
    )
    grad_in, gw_qkv, gw_out, gw_gu, gw_down, vec = run_back(
        z, off_bias, q, k, v, qr, kr, attn, ll, tokf, gba, gres, wqf, wof, gwd, gwg, ga, gs, cos, sin, scale
    )
    d, m = place()

    def channel_rows(v, per_head):
        n = per_head // z.dp
        return lax.dynamic_slice_in_dim(v.reshape(H, per_head).T, d * n, n, 0)

    gs = jnp.stack([channel_rows(vec[i, 0:F], F // H) for i in range(2)], axis=1)
    return (
        out,
        grad_in,
        gw_qkv.reshape(R, 3, C),
        gw_out,
        gw_gu.reshape(R, 2, F),
        gw_down,
        channel_rows(vec[4, 0:C], DK),
        channel_rows(vec[2, 0:CF], DK),
        channel_rows(vec[3, 0:CF], DK),
        gs,
    )


def solution(mesh):
    placed = (
        P("dp", "mp"),
        P("dp", None, "mp"),
        P("dp", "mp"),
        P("dp", None, "mp"),
        P("dp", "mp"),
        P(None, "mp"),
        P(None, "mp"),
        P(None, "mp"),
        P(None, None, "mp"),
        P("dp", None),
        P("dp", "mp"),
    )
    return jax.shard_map(
        functools.partial(on_device, dict(mesh.shape)),
        mesh=mesh,
        in_specs=placed,
        out_specs=(
            P("dp", "mp"),
            P("dp", "mp"),
            P("dp", None, "mp"),
            P("dp", "mp"),
            P("dp", None, "mp"),
            P("dp", "mp"),
            P("dp", "mp"),
            P("dp", "mp"),
            P("dp", "mp"),
            P("dp", None, "mp"),
        ),
        check_vma=False,
    )
```

```python
import functools
import math

import jax
import jax.numpy as jnp
from jax import lax
from jax.experimental import pallas as pl
from jax.experimental.pallas import tpu as pltpu
from jax.sharding import PartitionSpec as P

DK = 64
epsilon = 1e-06
theta_base = 10000.0


def layout(lengths, token_count):
    starts = jnp.cumsum(lengths) - lengths
    place = jnp.arange(token_count, dtype=jnp.int32)
    doc_ids = jnp.sum((place[:, None] >= starts[None, 1:]).astype(jnp.int32), axis=1)
    picked = (doc_ids[:, None] == jnp.arange(lengths.shape[0], dtype=jnp.int32)[None, :]).astype(
        jnp.int32
    )
    position = place - jnp.sum(picked * starts[None, :], axis=1)
    return (doc_ids, position)


LC=math.sqrt(DK)*math.log2(math.e)
NEG=-1e30
def nt(a,b): return lax.dot_general(a,b,(((1,),(1,)),((),())),preferred_element_type=jnp.float32)
def nn(a,b): return jnp.dot(a,b,preferred_element_type=jnp.float32)
def head_mask(x,h):
    lane=lax.broadcasted_iota(jnp.int32,x.shape,1)
    return jnp.where((lane//DK)==(h%2), x, jnp.zeros_like(x))
def attn_fwd_block(i, TB, H, ref, C, live, acc):
    hb=TB//2
    qs=pl.ds(pl.multiple_of(i*TB,TB),TB)
    def vx(h,ks):
        v=ref[ks,pl.ds(2*C+(h//2)*128,128)]
        lane=lax.broadcasted_iota(jnp.int32,v.shape,1)
        return jnp.where((lane//DK)==(h%2),v,jnp.ones_like(v))
    def tile(h,qsl,ks,tri):
        p2=pl.ds((h//2)*128,128)
        x=nt(ref[qsl,p2],head_mask(ref[ks,pl.ds(C+(h//2)*128,128)],h))
        if tri:
            r=lax.broadcasted_iota(jnp.int32,x.shape,0); c=lax.broadcasted_iota(jnp.int32,x.shape,1)
            x=jnp.where(c<=r,x,NEG)
        p=jnp.exp2(x*LC).astype(jnp.bfloat16)
        return nn(p,vx(h,ks))
    k0=pl.ds(pl.multiple_of(i*TB,hb),hb); k1=pl.ds(pl.multiple_of(i*TB+hb,hb),hb)
    for h in range(H):
        a0=tile(h,qs,k0,True)
        a1=tile(h,k1,k1,True)
        acc[h,0:hb]=a0[0:hb]; acc[h,hb:TB]=a0[hb:TB]+a1
    def body(j,_):
        ks=pl.ds(pl.multiple_of(j*TB,TB),TB)
        for h in range(H):
            acc[h]+=live*tile(h,qs,ks,False)
        return 0
    lax.fori_loop(0,i,body,0)
def tdot(a,b): return lax.dot_general(a,b,(((0,),(0,)),((),())),preferred_element_type=jnp.float32)
def attn_bwd_block(i,TB,H,q_ref,k_ref,v_ref,g_ref,ll_ref,dl_ref,ob,dq,dk,dv):
    qs=pl.ds(pl.multiple_of(i*TB,TB),TB); hb=TB//2
    qz=[head_mask(q_ref[qs,pl.ds((h//2)*128,128)],h) for h in range(H)]
    gz=[head_mask(g_ref[qs,pl.ds((h//2)*128,128)],h) for h in range(H)]
    lr=[ll_ref[pl.ds(h,1),qs] for h in range(H)]
    dr=[dl_ref[pl.ds(h,1),qs] for h in range(H)]
    def tile(h,ks,qv,gv,lb,dd,tri):
        p2=pl.ds((h//2)*128,128)
        x=nt(k_ref[ks,p2],qv)*LC-lb
        dp=nt(v_ref[ks,p2],gv)
        if tri:
            r=lax.broadcasted_iota(jnp.int32,x.shape,0); c=lax.broadcasted_iota(jnp.int32,x.shape,1)
            x=jnp.where(r<=c,x,NEG)
        p=jnp.exp2(x)
        ds=(p*(dp-dd)).astype(jnp.bfloat16)
        dvp=nn(p.astype(jnp.bfloat16),gv)
        dkp=nn(ds,qv)
        dqp=tdot(ds,head_mask(k_ref[ks,p2],h))
        return dqp,dkp,dvp
    k0=pl.ds(pl.multiple_of(i*TB,hb),hb); k1=pl.ds(pl.multiple_of(i*TB+hb,hb),hb)
    for pr in range((H+1)//2):
        p2=pl.ds(pr*128,128)
        dk0=dv0=dk1=dv1=0; q0=q1=0
        for h in range(2*pr,min(2*pr+2,H)):
            a,b,c=tile(h,k0,qz[h],gz[h],lr[h],dr[h],True)
            a1,b1,c1=tile(h,k1,qz[h][hb:],gz[h][hb:],lr[h][:,hb:],dr[h][:,hb:],True)
            q0+=a[0:hb]; q1+=a[hb:]+a1
            dk0+=b; dv0+=c; dk1+=b1; dv1+=c1
        dq[0:hb,p2]=q0; dq[hb:TB,p2]=q1
        dk[k0,p2]+=dk0; dv[k0,p2]+=dv0; dk[k1,p2]+=dk1; dv[k1,p2]+=dv1
    lo=[l-ob for l in lr]
    def body(j,_):
        ks=pl.ds(pl.multiple_of(j*TB,TB),TB)
        for pr in range((H+1)//2):
            p2=pl.ds(pr*128,128)
            dka=dva=dqa=0
            for h in range(2*pr,min(2*pr+2,H)):
                a,b,c=tile(h,ks,qz[h],gz[h],lo[h],dr[h],False)
                dqa+=a; dka+=b; dva+=c
            dq[:,p2]+=dqa
            dk[ks,p2]+=dka; dv[ks,p2]+=dva
        return 0
    lax.fori_loop(0,i,body,0)


MESH = pl.DeviceIdType.MESH
F32, BF = jnp.float32, jnp.bfloat16


class Sizes:
    def __init__(self, mesh_shape, T, C, CF, F, pieces):
        self.mp, self.dp = mesh_shape["mp"], mesh_shape["dp"]
        self.ny = self.mp // 2
        self.A = 4 if self.dp % 4 == 0 else 1
        self.B = self.dp // self.A
        self.T, self.C, self.CF, self.F = T, C, CF, F
        self.D = CF * self.mp
        self.H = C // DK
        self.nc = pieces
        self.TB = T // pieces
        self.TH = self.TB // 2
        self.R = self.D // self.dp


def place():
    return lax.axis_index("dp"), lax.axis_index("mp")


def remote(src, dst, ss, rs, dev):
    return pltpu.make_async_remote_copy(
        src, dst, send_sem=ss, recv_sem=rs, device_id=dev, device_id_type=MESH
    )


def local(src, dst, sem):
    return pltpu.make_async_copy(src, dst, sem)


def rows_at(start, size):
    return pl.ds(pl.multiple_of(start, size), size)


def loop(n, fn):
    def body(i, carry):
        fn(i)
        return carry

    lax.fori_loop(0, n, body, 0)


def fold(x):
    return jnp.sum(x.reshape(x.shape[0] // 8, 8, x.shape[1]), axis=0)


def mean_sq(x, D):
    return lax.rsqrt(jnp.sum(x * x, axis=1, keepdims=True) * (1.0 / D) + epsilon)


def split_dot(x, ones):
    hi = x.astype(BF)
    return nn(hi, ones) + nn((x - hi.astype(F32)).astype(BF), ones)


def head_ones(width):
    i = lax.broadcasted_iota(jnp.int32, (width, width), 0) // DK
    j = lax.broadcasted_iota(jnp.int32, (width, width), 1) // DK
    return jnp.where(i == j, 1.0, 0.0).astype(BF)


def turn(x, cosine, sine, sign):
    lane = lax.broadcasted_iota(jnp.int32, x.shape, 1)
    first = (lane % DK) < DK // 2
    other = jnp.where(first, -pltpu.roll(x, x.shape[1] - DK // 2, 1), pltpu.roll(x, DK // 2, 1))
    return x * cosine + sign * other * sine


def front(
    z,
    ob_ref, tokens, gout, wqo, wg, wd, alpha, cos, sin, sq, sml,
    out, q_o, k_o, v_o, qr_o, kr_o, attn_o, ll_o, tokf, gba_o, gres_o, wqof, gwd_o, gwg_o, r1_o, ga_o, gs_o, goh,
    tokv, wqov, wgv, wdv, gml, act, gu, gba, rot, attn, ll, acc,
    sy1, ry1, sy2, ry2, sy3, ry3, rc, sc, tokh, ghid, gst, fst, wst, alv, gacc, gsacc,
    tok_s, tok_r, w_s, w_r, x_s, x_r, al_s, al_r, go_s, go_r, ex_s, ex_r, y_s, y_r, hc_s, hc_r, out_s, out_r, r1_s, r1_r, lsem,
):
    T, C, CF, F, D, H = z.T, z.C, z.CF, z.F, z.D, z.H
    nc, TB, TH, R, A, B, ny, mp = z.nc, z.TB, z.TH, z.R, z.A, z.B, z.ny, z.mp
    d, m = place()
    a, b = d // B, d % B
    y, core = m // 2, m % 2
    mate = 1 - core
    peer = (d, y * 2 + mate)

    def ypeer(k, cc):
        return (d, ((y + k) % ny) * 2 + cc)

    zpeer = lambda k: (((a + k) % A) * B + b, m)
    xpeer = lambda k: (a * B + (b + k) % B, m)
    others = [peer] + [ypeer(k, cc) for k in range(1, ny) for cc in (core, mate)]
    everyone = others + [zpeer(k) for k in range(1, A)] + [xpeer(k) for k in range(1, B)]
    bar = pltpu.get_barrier_semaphore()
    for dev in everyone:
        pl.semaphore_signal(bar, 1, device_id=dev, device_id_type=MESH)
    pl.semaphore_wait(bar, len(everyone))

    live = ob_ref[0]
    feat = lambda mm: pl.ds(pl.multiple_of(mm * CF, CF), CF)
    mine = feat(m)


    def tok_own(c, i, dev):
        r = rows_at(c * TB, TB)
        return remote(tokens.at[r], tokv.at[r, mine], tok_s.at[c, i], tok_r.at[c, i], dev)

    def tok_got(c, i, mm):
        r = rows_at(c * TB, TB)
        return remote(tokv.at[r, feat(mm)], tokv.at[r, feat(mm)], tok_s.at[c, i], tok_r.at[c, i], peer)

    def start_tok(i):
        c = nc - 1 - i
        for k in range(1, ny):
            tok_own(c, k, ypeer(k, core)).start()
        tok_own(c, 0, peer).start()

    lo, hi = slice(0, F), slice(F, 2 * F)
    dl, dh = slice(0, F // 2), slice(F // 2, F)
    weights = [
        (wqo, wqov),
        (wg.at[:, lo], wgv.at[:, lo]),
        (wg.at[:, hi], wgv.at[:, hi]),
        (wd.at[:, dl], wdv.at[:, dl]),
        (wd.at[:, dh], wdv.at[:, dh]),
    ]

    def shard(aa, bb):
        return rows_at((aa * B + bb) * R, R)

    def column(st):
        return (b - st + B) % B

    def z_moves(w, st, h):
        src, dst = weights[w]
        moves = []
        for way, step in ((0, 1), (1, -1)):
            aa = a - step * (h - 1)
            ok = (a + step >= 0) & (a + step < A) & (aa >= 0) & (aa < A)
            moves.append((way, step, jnp.clip(aa, 0, A - 1), ok))
        return src, dst, moves

    def z_copy(w, st, h, way, step, aa):
        src, dst = weights[w]
        r = shard(aa, column(st))
        source = src if (h == 1 and st == 0) else dst.at[r]
        to = jnp.clip(a + step, 0, A - 1) * B + b
        return remote(source, dst.at[r], w_s.at[w, st, way, h - 1], w_r.at[w, st, way, h - 1], (to, m))

    def z_hop(w, st, h):
        if h >= A:
            return
        for way, step, aa, ok in z_moves(w, st, h)[2]:

            @pl.when(ok)
            def _():
                z_copy(w, st, h, way, step, aa).start()

    def z_sent(w, st, h):
        for way, step, aa, ok in z_moves(w, st, h)[2]:

            @pl.when(ok)
            def _():
                z_copy(w, st, h, way, step, aa).wait_send()

    def z_wait(w, st, h, forward=False):
        if h >= A:
            return
        for way, step in ((0, 1), (1, -1)):
            aa = a - step * h

            @pl.when((aa >= 0) & (aa < A))
            def _():
                z_copy(w, st, h, way, step, jnp.clip(aa, 0, A - 1)).wait_recv()
                if forward:
                    x_send(w, aa)

    def x_copy(w, aa, k, own=False):
        src, dst = weights[w]
        r = shard(aa, b)
        return remote(
            src if own else dst.at[r], dst.at[r], x_s.at[w, aa, k - 1], x_r.at[w, aa, k - 1], xpeer(k)
        )

    def x_send(w, aa, own=False):
        for k in range(1, B):
            x_copy(w, aa, k, own).start()

    def x_wait(w, aa):
        src, dst = weights[w]
        for k in range(1, B):
            r = shard(aa, (b - k + B) % B)
            remote(src, dst.at[r], x_s.at[w, aa, k - 1], x_r.at[w, aa, k - 1], xpeer(k)).wait_recv()

    def w_local(w):
        src, dst = weights[w]
        return local(src, dst.at[shard(a, b)], lsem.at[16 + w])

    def w_start(w):
        z_hop(w, 0, 1)
        x_send(w, a, own=True)
        w_local(w).start()

    def w_next(w, st, h, forward=True):
        z_wait(w, st, h, forward)
        z_hop(w, st, h + 1)

    def w_ready(w):
        for aa in range(A):
            x_wait(w, aa)
        w_local(w).wait()

    def w_sent(w, forward):
        for st in range(1 if forward else B):
            for h in range(1, A):
                z_sent(w, st, h)
        for k in range(1, B):
            for aa in range(A) if forward else [a]:
                x_copy(w, aa, k).wait_send()

    w_start(0)
    loop(nc, start_tok)
    x_send(4, a, own=True)
    w_local(4).start()
    tok_local = local(tokens, tokv.at[:, mine], lsem.at[4])
    tok_local.start()
    al_local = local(alpha, alv.at[:, mine], lsem.at[5])
    al_local.start()
    al_copies = [
        remote(alpha, alv.at[:, mine], al_s.at[i], al_r.at[i], dev) for i, dev in enumerate(others)
    ]
    for cp in al_copies:
        cp.start()

    def pass_tok(i):
        c = nc - 1 - i
        for k in range(1, ny):
            src = ((y - k + ny) % ny) * 2 + core
            tok_got(c, k, src).wait_recv()
            tok_got(c, ny + k - 1, src).start()

    w_next(0, 0, 1)
    pass_tok(0)
    w_next(0, 0, 2)
    pass_tok(1)
    w_next(0, 0, 3)
    w_start(1)
    w_start(2)
    loop(nc - 2, lambda i: pass_tok(i + 2))

    def end_tok(i):
        c = nc - 1 - i
        tok_got(c, 0, y * 2 + mate).wait_recv()
        for k in range(1, ny):
            src = ((y - k + ny) % ny) * 2 + mate
            tok_got(c, ny + k - 1, src).wait_recv()

    loop(nc, end_tok)

    def tok_sent(i):
        c = nc - 1 - i
        tok_own(c, 0, peer).wait_send()
        for k in range(1, ny):
            tok_own(c, k, ypeer(k, core)).wait_send()
            tok_got(c, ny + k - 1, ((y - k + ny) % ny) * 2 + core).wait_send()

    loop(nc, tok_sent)
    tok_local.wait()
    w_ready(0)

    go4 = gout

    def go_copy(i, dev, cc):
        return remote(go4.at[:, cc], goh.at[:, :, mine], go_s.at[i], go_r.at[i], dev)

    go_copies = [go_copy(0, peer, mate)]
    i = 1
    for k in range(1, ny):
        for cc in (core, mate):
            go_copies.append(go_copy(i, ypeer(k, cc), cc))
            i += 1
    go_local = local(go4.at[:, core], goh.at[:, :, mine], lsem.at[6])
    go_local.start()
    for cp in go_copies:
        cp.start()

    ones = head_ones(C)
    qkvv = gml

    def project_rows(i):
        r = rows_at(i * TB, TB)
        x = tokv[r, :]
        cs = jnp.concatenate([cos[r, :]] * (C // 128), axis=1)
        sn = jnp.concatenate([sin[r, :]] * (C // 128), axis=1)
        for part in range(2):
            cols = slice(part * C, part * C + C)
            t = turn(nn(x, wqov[:, cols]), cs, sn, 1.0)
            rot[part, r, :] = t.astype(BF)
            inv = lax.rsqrt(split_dot(t * t, ones) + epsilon)
            qkvv[r, cols] = (t * inv * sq[...]).astype(BF)
        qkvv[r, 2 * C : 3 * C] = nn(x, wqov[:, 2 * C : 3 * C]).astype(BF)

        @pl.when(i == 0)
        def _():
            w_next(1, 0, 1)

        @pl.when(i == 1)
        def _():
            w_next(2, 0, 1)

        @pl.when(i == 2)
        def _():
            w_next(1, 0, 2)

    loop(nc, project_rows)
    save_tok = local(tokv, tokf, lsem.at[4])
    save_tok.start()
    saves = [
        local(qkvv.at[:, 0:C], q_o, lsem.at[7]),
        local(qkvv.at[:, C : 2 * C], k_o, lsem.at[8]),
        local(qkvv.at[:, 2 * C : 3 * C], v_o, lsem.at[9]),
        local(rot.at[0], qr_o, lsem.at[10]),
        local(rot.at[1], kr_o, lsem.at[11]),
        local(wqov, wqof, lsem.at[12]),
    ]
    for cp in saves:
        cp.start()

    RT = 64
    NG = 2
    GW = D // NG

    def y_copy(e, c, k, n, sy, ry):
        cols = slice(n * GW, n * GW + GW)
        return remote(
            sy.at[c, :, cols], ry.at[k - 1, c, :, cols], y_s.at[e, c, k - 1, n], y_r.at[e, c, k - 1, n],
            ypeer(k, core),
        )

    def exchange(e, c, part, sy, ry):
        r = rows_at(c * TB, TB)
        theirs, ours = rows_at(mate * TH, TH), rows_at(core * TH, TH)
        copies = []
        for n in range(NG):
            cols = slice(n * GW, n * GW + GW)
            sc[:, cols] = part(r, cols).astype(BF)
            cp = remote(
                sc.at[theirs, cols], rc.at[c, :, cols], ex_s.at[e, c, n], ex_r.at[e, c, n], peer
            )
            cp.start()
            copies.append(cp)
        for n in range(NG):
            cols = slice(n * GW, n * GW + GW)
            copies[n].wait()
            sy[c, :, cols] = (sc[ours, cols].astype(F32) + rc[c, :, cols].astype(F32)).astype(BF)
            for k in range(1, ny):
                y_copy(e, c, k, n, sy, ry).start()

    def landed(e, c, sy, ry):
        for k in range(1, ny):
            for n in range(NG):
                y_copy(e, c, k, n, sy, ry).wait()

    def total(c, r, sy, ry):
        t = sy[c, r, :].astype(F32)
        for k in range(ny - 1):
            t = t + ry[k, c, r, :].astype(F32)
        return t

    NS = 2
    SH = TH // NS

    def share(e, c, n, buf):
        r = rows_at(c * TB + core * TH + n * SH, SH)
        return remote(buf.at[r], buf.at[r], hc_s.at[e, c, n], hc_r.at[e, c, n], peer)

    def rows_then_share(e, c, rows, buf):
        for n in range(NS):
            loop(SH // RT, lambda t: rows(n * (SH // RT) + t))
            share(e, c, n, buf).start()

    def shared(e, c, buf):
        for n in range(NS):
            share(e, c, n, buf).wait()

    def attend_chunk(i):
        c = nc - 1 - i
        attn_fwd_block(c, TB, H, qkvv, C, live, acc)
        r = rows_at(c * TB, TB)
        for pr in range(C // 128):
            both = []
            for h in (2 * pr, 2 * pr + 1):
                t = acc[h]
                both.append(t / pltpu.roll(t, DK, 1))
                row = DK if h % 2 == 0 else 0
                ll[pl.ds(h, 1), r] = jnp.log2(t).T[row : row + 1]
            lane = lax.broadcasted_iota(jnp.int32, (TB, 128), 1)
            attn[r, pr * 128 : pr * 128 + 128] = jnp.where(lane < DK, both[0], both[1]).astype(BF)

        def part(rr, cols):
            return nt(attn[rr, :], wqov[cols, 3 * C : 4 * C])

        @pl.when(i == 0)
        def _():
            save_tok.wait()

        exchange(0, c, part, sy1, ry1)

        @pl.when(i == 0)
        def _():
            w_next(2, 0, 2)
            w_next(1, 0, 3)
            w_start(3)
            z_hop(4, 0, 1)
            x_wait(4, a)
            for st in range(1, B):
                z_hop(4, st, 1)

        @pl.when(i == 1)
        def _():
            w_next(2, 0, 3)
            w_next(3, 0, 1)

        @pl.when(i == 2)
        def _():
            for st in range(B):
                w_next(4, st, 1, False)

        @pl.when(i == 3)
        def _():
            w_next(3, 0, 2)
            for st in range(B):
                w_next(4, st, 2, False)

    ll[...] = jnp.zeros_like(ll)
    loop(nc, attend_chunk)
    save_attn = local(attn, attn_o, lsem.at[13])
    save_attn.start()
    save_ll = local(ll, ll_o, lsem.at[14])
    save_ll.start()
    for cp in saves:
        cp.wait()
    al_local.wait()
    for cp in al_copies:
        cp.wait()
    w_ready(1)
    w_ready(2)

    gacc[...] = jnp.zeros_like(gacc)
    gsacc[...] = jnp.zeros_like(gsacc)

    def feed_chunk(i):
        c = nc - 1 - i
        landed(0, c, sy1, ry1)
        base = c * TB + core * TH

        def rows(t):
            r = rows_at(t * RT, RT)
            g = rows_at(base + t * RT, RT)
            br = total(c, r, sy1, ry1)
            xb = tokv[g, :]
            tokh[c, r, :] = xb
            x = xb.astype(F32)
            ha = br * mean_sq(br, D)
            mix = x + alv[0:1, :] * (ha - x)
            tokv[g, :] = (mix * mean_sq(mix, D)).astype(BF)

        rows_then_share(0, c, rows, tokv)
        shared(0, c, tokv)
        r = rows_at(c * TB, TB)

        def units(n):
            cu, cv = rows_at(n * 256, 256), rows_at(F + n * 256, 256)
            x = tokv[r, :]
            u = nn(x, wgv[:, cu])
            v = nn(x, wgv[:, cv])
            gu[r, cu] = u.astype(BF)
            gu[r, cv] = v.astype(BF)
            us = u * sml[0:1, cu]
            vs = v * sml[1:2, cu]
            act[r, cu] = (us * vs * jax.nn.sigmoid(vs)).astype(BF)

        loop(F // 256, units)

        @pl.when(i == 0)
        def _():
            w_next(3, 0, 3)

        @pl.when(i == 1)
        def _():
            for st in range(B):
                w_next(4, st, 3, False)

    loop(nc, feed_chunk)
    w_ready(3)
    w_local(4).wait()

    def down_chunk(i):
        c = nc - 1 - i
        exchange(1, c, lambda rr, cols: nt(act[rr, :], wdv[cols, :]), sy2, ry2)

    loop(nc, down_chunk)
    go_local.wait()
    for cp in go_copies:
        cp.wait()

    def back_chunk(i):
        c = nc - 1 - i
        lg = local(goh.at[c], gst, lsem.at[6])
        lg.start()
        lg.wait()
        landed(1, c, sy2, ry2)
        base = c * TB + core * TH

        def rows(t):
            r = rows_at(t * RT, RT)
            g = rows_at(base + t * RT, RT)
            am = alv[1:2, :]
            bm = total(c, r, sy2, ry2)
            h = tokv[g, :].astype(F32)
            rm = mean_sq(bm, D)
            hm = bm * rm
            diff = hm - h
            mix = h + am * diff
            r2 = mean_sq(mix, D)
            fin = mix * r2
            fst[r, :] = fin.astype(BF)
            go = gst[r, :].astype(F32)
            gm = r2 * (go - fin * (jnp.sum(go * fin, axis=1, keepdims=True) * (1.0 / D)))
            gacc[8:16, :] += fold(gm * diff)
            gh = am * gm
            ghid[c, r, :] = (gm - gh).astype(BF)
            gb = rm * (gh - hm * (jnp.sum(gh * hm, axis=1, keepdims=True) * (1.0 / D)))
            gml[g, :] = gb.astype(BF)

        rows_then_share(1, c, rows, gml)
        og = rows_at(base, TH)
        o_here = local(fst.at[:, mine], out.at[og], lsem.at[6])
        o_here.start()
        o_there = remote(
            fst.at[:, feat(y * 2 + mate)], out.at[og], out_s.at[c], out_r.at[c], peer
        )
        o_there.start()
        shared(1, c, gml)
        r = rows_at(c * TB, TB)

        def units(n):
            cu, cv = rows_at(n * 256, 256), rows_at(F + n * 256, 256)
            ga = nn(gml[r, :], wdv[:, cu])
            u = gu[r, cu].astype(F32)
            v = gu[r, cv].astype(F32)
            su, sv = sml[0:1, cu], sml[1:2, cu]
            us, vs = u * su, v * sv
            sg = jax.nn.sigmoid(vs)
            si = vs * sg
            g_u = ga * si
            g_v = ga * us * (sg + si - si * sg)
            gsacc[0:8, cu] += fold(g_u * u)
            gsacc[8:16, cu] += fold(g_v * v)
            gu[r, cu] = (g_u * su).astype(BF)
            gu[r, cv] = (g_v * sv).astype(BF)

        loop(F // 256, units)
        exchange(2, c, lambda rr, cols: nt(gu[rr, :], wgv[cols, :]), sy3, ry3)
        o_here.wait()
        o_there.wait()

    loop(nc, back_chunk)

    RA = D // A

    def down_tile(t):
        cols = rows_at(t * RA, RA)
        wst[:, :, 0:F] = tdot(gml[:, cols], act[...]).astype(BF).reshape(B, R, F)
        cp = local(wst.at[:, :, 0:F], gwd_o.at[t], lsem.at[6])
        cp.start()
        cp.wait()

    loop(A, down_tile)
    r1_copies = [
        remote(gwd_o.at[:, (b + k) % B], r1_o.at[k - 1], r1_s.at[k - 1], r1_r.at[k - 1], xpeer(k))
        for k in range(1, B)
    ]
    for cp in r1_copies:
        cp.start()

    def up_tile(t):
        cols = rows_at(t * RA, RA)
        lhs = tokv[:, cols]
        wst[:, :, 0:F] = tdot(lhs, gu[:, 0:F]).astype(BF).reshape(B, R, F)
        wst[:, :, F : 2 * F] = tdot(lhs, gu[:, F : 2 * F]).astype(BF).reshape(B, R, F)
        cp = local(wst, gwg_o.at[t], lsem.at[6])
        cp.start()
        cp.wait()

    loop(A, up_tile)

    def attn_grad_chunk(i):
        c = nc - 1 - i
        landed(2, c, sy3, ry3)
        base = c * TB + core * TH

        def rows(t):
            r = rows_at(t * RT, RT)
            g = rows_at(base + t * RT, RT)
            aa = alv[0:1, :]
            br = total(c, r, sy1, ry1)
            x = tokh[c, r, :].astype(F32)
            ra = mean_sq(br, D)
            ha = br * ra
            diff = ha - x
            mix = x + aa * diff
            r1 = mean_sq(mix, D)
            hid = mix * r1
            gh = ghid[c, r, :].astype(F32) + total(c, r, sy3, ry3)
            gm = r1 * (gh - hid * (jnp.sum(gh * hid, axis=1, keepdims=True) * (1.0 / D)))
            gacc[0:8, :] += fold(gm * diff)
            gt = aa * gm
            ghid[c, r, :] = (gm - gt).astype(BF)
            gb = ra * (gt - ha * (jnp.sum(gt * ha, axis=1, keepdims=True) * (1.0 / D)))
            gba[g, :] = gb.astype(BF)

        rows_then_share(2, c, rows, gba)
        shared(2, c, gba)

    loop(nc, attn_grad_chunk)
    ends = [
        local(gba, gba_o, lsem.at[0]),
        local(ghid, gres_o, lsem.at[1]),
        local(gacc, ga_o, lsem.at[2]),
        local(gsacc, gs_o, lsem.at[3]),
    ]
    for cp in ends:
        cp.start()
    for w in range(5):
        w_sent(w, w != 4)
    for cp in ends + [save_attn, save_ll] + r1_copies:
        cp.wait()


def run_front(z, off_bias, tokens, gout, wqo, wg, wd, alpha, cos, sin, sq, sml):
    T, C, CF, F, D, H = z.T, z.C, z.CF, z.F, z.D, z.H
    nc, TB, TH, R, A, B, ny, mp = z.nc, z.TB, z.TH, z.R, z.A, z.B, z.ny, z.mp
    S = jax.ShapeDtypeStruct
    hbm = pl.BlockSpec(memory_space=pltpu.HBM)
    vm = pl.BlockSpec(memory_space=pltpu.VMEM)
    outs = [
        S((T, CF), BF), S((T, C), BF), S((T, C), BF), S((T, C), BF), S((T, C), BF), S((T, C), BF),
        S((T, C), BF), S((8, T), F32), S((T, D), BF), S((T, D), BF), S((nc, TH, D), BF),
        S((D, 4 * C), BF), S((A, B, R, F), BF), S((A, B, R, 2 * F), BF),
        S((B - 1, A, R, F), BF), S((16, D), F32),
        S((16, F), F32), S((nc, TH, D), BF),
    ]
    V = pltpu.VMEM
    scratch = [
        V((T, D), BF), V((D, 4 * C), BF), V((D, 2 * F), BF), V((D, F), BF),
        V((T, D), BF), V((T, F), BF), V((T, 2 * F), BF), V((T, D), BF),
        V((2, T, C), BF), V((T, C), BF), V((8, T), F32), V((H, TB, 128), F32),
    ]
    for _ in range(3):
        scratch += [V((nc, TH, D), BF), V((ny - 1, nc, TH, D), BF)]
    scratch += [
        V((nc, TH, D), BF), V((TB, D), BF), V((nc, TH, D), BF), V((nc, TH, D), BF),
        V((TH, D), BF), V((TH, D), BF), V((B, R, 2 * F), BF), V((8, D), F32), V((16, D), F32), V((16, F), F32),
    ]
    sem = pltpu.SemaphoreType.DMA
    for shape in (
        (nc, 2 * ny - 1), (5, B, 2, max(A - 1, 1)), (5, A, max(B - 1, 1)), (mp - 1,), (mp - 1,), (3, nc, 2),
        (3, nc, ny - 1, 2), (3, nc, 2), (nc,), (B - 1,),
    ):
        scratch += [sem(shape), sem(shape)]
    scratch += [sem((21,))]
    return pl.pallas_call(
        functools.partial(front, z),
        out_shape=outs,
        in_specs=[pl.BlockSpec(memory_space=pltpu.SMEM)] + [hbm] * 6 + [vm] * 4,
        out_specs=[hbm] * len(outs),
        scratch_shapes=scratch,
        compiler_params=pltpu.CompilerParams(
            collective_id=0, has_side_effects=True, vmem_limit_bytes=63 * 2**20
        ),
        name="front",
    )(off_bias, tokens, gout.reshape(nc, 2, TH, CF), wqo, wg, wd, alpha, cos, sin, sq, sml)


def back(
    z,
    ob_ref, q_h, k_h, v_h, qr_h, kr_h, attn_h, ll_h, tok_h, gba_h, gres_h, wqo_h, gwd_h, gwg_h, r1_h, ga_h, gs_h,
    cos, sin, sq,
    gin_o, owq, owo, owg, owd, vec_o,
    qv, kv, vv, rot, attn, ll, dl, wqov, gba, tok, gres, gm, dk, dv, dq, gqkv, gsq,
    own_d, own_g, gqo, r1_d, r1_g, r1_q, s2_d, s2_g, s2_q, r2_d, r2_g, r2_q, f_d, f_g, f_q,
    sc2, rc2, ow, sy, ry, gin, gal, gar, gsl, vec, rv1, rv2,
    x_s, x_r, z_s, z_r, c_s, c_r, y_s, y_r, m_s, m_r, lsem,
):
    T, C, CF, F, D, H = z.T, z.C, z.CF, z.F, z.D, z.H
    nc, TB, TH, R, A, B, ny = z.nc, z.TB, z.TH, z.R, z.A, z.B, z.ny
    d, m = place()
    a, b = d // B, d % B
    y, core = m // 2, m % 2
    mate = 1 - core
    peer = (d, y * 2 + mate)
    ypeer = lambda k: (d, ((y + k) % ny) * 2 + core)
    zpeer = lambda k: (((a + k) % A) * B + b, m)
    xpeer = lambda k: (a * B + (b + k) % B, m)
    everyone = (
        [peer]
        + [ypeer(k) for k in range(1, ny)]
        + [zpeer(k) for k in range(1, A)]
        + [xpeer(k) for k in range(1, B)]
    )
    bar = pltpu.get_barrier_semaphore()
    for dev in everyone:
        pl.semaphore_signal(bar, 1, device_id=dev, device_id_type=MESH)
    pl.semaphore_wait(bar, len(everyone))
    feat = lambda mm: pl.ds(pl.multiple_of(mm * CF, CF), CF)
    ob = ob_ref[0]

    pieces = []
    for src, mine, r1, s2, r2, res, width, parts in (
        (gwd_h, own_d, r1_d, s2_d, r2_d, f_d, F, 2),
        (gwg_h, own_g, r1_g, s2_g, r2_g, f_g, 2 * F, 4),
        (gqo, None, r1_q, s2_q, r2_q, f_q, 4 * C, 2),
    ):
        for n in range(parts):
            cols = slice(n * width // parts, (n + 1) * width // parts)
            pieces.append(
                (
                    (lambda bb, src=src, cols=cols: src.at[:, bb, :, cols]),
                    None if mine is None else mine.at[:, :, cols],
                    r1.at[:, :, :, cols],
                    s2.at[:, :, cols],
                    r2.at[:, :, cols],
                    res.at[:, cols],
                )
            )

    def x_copy(p, k):
        blocks, r1 = pieces[p][0], pieces[p][2]
        return remote(
            blocks((b + k) % B), r1.at[k - 1], x_s.at[p, k - 1], x_r.at[p, k - 1], xpeer(k)
        )

    def own_copy(p):
        return local(pieces[p][0](b), pieces[p][1], lsem.at[p])

    def rs_start(p):
        for k in range(1, B):
            x_copy(p, k).start()

    def z_copy(p, k):
        s2, r2 = pieces[p][3], pieces[p][4]
        return remote(s2.at[(a + k) % A], r2.at[k - 1], z_s.at[p, k - 1], z_r.at[p, k - 1], zpeer(k))

    def rs_middle(p):
        blocks, mine, r1, s2 = pieces[p][:4]
        if p >= 2:
            for k in range(1, B):
                x_copy(p, k).wait()
        for k in list(range(1, A)) + [0]:
            aa = (a + k) % A

            def add(t):
                r = rows_at(t * 16, 16)
                src = mine[aa, r, :] if mine is not None else blocks(b)[aa, r, :]
                total = src.astype(F32)
                for kk in range(B - 1):
                    total = total + r1[kk, aa, r, :].astype(F32)
                s2[aa, r, :] = total.astype(BF)

            loop(R // 16, add)
            if k:
                z_copy(p, k).start()

    def rs_end(p):
        s2, r2, res = pieces[p][3:6]
        for k in range(1, A):
            z_copy(p, k).wait()

        def add(t):
            r = rows_at(t * 16, 16)
            total = s2[a, r, :].astype(F32)
            for kk in range(A - 1):
                total = total + r2[kk, r, :].astype(F32)
            res[r, :] = total

        loop(R // 16, add)

    rs_start(2)
    early = [
        local(r1_h, r1_d, lsem.at[0]),
        local(gwd_h.at[:, b], own_d, lsem.at[1]),
        local(gwg_h.at[:, b], own_g, lsem.at[2]),
    ]
    for cp in early:
        cp.start()
    ga_there = remote(
        ga_h.at[:, feat(y * 2 + mate)], gar, m_s.at[0], m_r.at[0], peer
    )
    ga_there.start()
    loads = [
        local(s, t, lsem.at[5 + i])
        for i, (s, t) in enumerate(
            [
                (q_h, qv), (k_h, kv), (wqo_h, wqov), (gba_h, gba), (v_h, vv), (attn_h, attn), (ll_h, ll),
                (qr_h, rot.at[0]), (kr_h, rot.at[1]), (gres_h, gres),
                (ga_h.at[:, feat(m)], gal), (gs_h, gsl), (tok_h, tok),
            ]
        )
    ]
    for cp in loads:
        cp.start()
    dk[...] = jnp.zeros_like(dk)
    dv[...] = jnp.zeros_like(dv)
    gsq[...] = jnp.zeros_like(gsq)
    for cp in early:
        cp.wait()
    rs_middle(0)
    rs_middle(1)
    rs_start(3)
    for cp in loads[:7]:
        cp.wait()

    ones = head_ones(C)
    heads = lax.broadcasted_iota(jnp.int32, (8, C), 0)
    lanes = lax.broadcasted_iota(jnp.int32, (8, C), 1) // DK
    pick = jnp.where(heads == lanes, 1.0, 0.0).astype(BF)
    for cp in loads[7:]:
        cp.wait()

    def gin_copy(c):
        return remote(sc2.at[c], rc2.at[c], c_s.at[c], c_r.at[c], peer)

    def y_copy(c, k):
        return remote(sy.at[c, k - 1], ry.at[k - 1, c], y_s.at[c, k - 1], y_r.at[c, k - 1], ypeer(k))

    def chunk(i):
        c = nc - 1 - i
        r = rows_at(c * TB, TB)
        g = nn(gba[r, :], wqov[:, 3 * C : 4 * C]).astype(BF)
        gm[r, :] = g
        prod = g.astype(F32) * attn[r, :].astype(F32)
        ph = prod.astype(BF)
        dl[:, r] = nt(pick, ph) + nt(pick, (prod - ph.astype(F32)).astype(BF))
        attn_bwd_block(c, TB, H, qv, kv, vv, gm, ll, dl, ob, dq, dk, dv)

        @pl.when(i == 0)
        def _():
            rs_middle(2)
            rs_start(4)

        @pl.when(i == 1)
        def _():
            rs_middle(3)
            rs_start(5)

        @pl.when(i == 2)
        def _():
            rs_middle(4)

        cs = jnp.concatenate([cos[r, :]] * (C // 128), axis=1)
        sn = jnp.concatenate([sin[r, :]] * (C // 128), axis=1)
        for part in range(2):
            gh = (dq[...] if part == 0 else dk[r, :]) * 8.0
            t = rot[part, r, :].astype(F32)
            inv = lax.rsqrt(split_dot(t * t, ones) + epsilon)
            un = t * inv
            gsq[...] += fold(gh * un)
            gh = gh * sq[...]
            gr = inv * (gh - un * split_dot(gh * un, ones))
            gqkv[r, part * C : part * C + C] = turn(gr, cs, sn, -1.0).astype(BF)
        gqkv[r, 2 * C : 3 * C] = dv[r, :].astype(BF)

        def product(hsel, k, cc):
            rr = rows_at(c * TB + hsel * TH, TH)
            cols = feat(((y + k) % ny) * 2 + cc)
            t = nt(gqkv[rr, :], wqov[cols, 0 : 3 * C])
            if k == 0:
                t = t + jnp.where(hsel == core, 1.0, 0.0) * gres[c, :, cols].astype(F32)
            return t

        for k in range(ny):
            for hs in range(2):
                sc2[c, k, hs * TH : (hs + 1) * TH, :] = product(hs, k, mate).astype(BF)
        gin_copy(c).start()
        for k in range(ny):
            for hs in range(2):
                ow[k, hs * TH : (hs + 1) * TH, :] = product(hs, k, core)
        gin_copy(c).wait()
        gin[r, :] = ow[0] + rc2[c, 0].astype(F32)
        for k in range(1, ny):
            sy[c, k - 1] = (ow[k] + rc2[c, k].astype(F32)).astype(BF)
            y_copy(c, k).start()

    loop(nc, chunk)

    def tile(t):
        cols = rows_at(t * B * R, B * R)
        g = tdot(tok[:, cols], gqkv[...]).astype(BF)
        gqo[t, :, :, 0 : 3 * C] = g.reshape(B, R, 3 * C)
        g = tdot(gba[:, cols], attn[...]).astype(BF)
        gqo[t, :, :, 3 * C : 4 * C] = g.reshape(B, R, C)

    loop(A, tile)
    rs_start(6)
    rs_middle(5)
    rs_start(7)
    W = vec.shape[1]
    ga_there.wait()
    vec[...] = jnp.zeros_like(vec)
    gt = gal[...] + gar[...]
    vec[0:1, 0:F] = jnp.sum(gsl[0:8, :], axis=0, keepdims=True)
    vec[1:2, 0:F] = jnp.sum(gsl[8:16, :], axis=0, keepdims=True)
    vec[2:3, 0:CF] = jnp.sum(gt[0:8], axis=0, keepdims=True)
    vec[3:4, 0:CF] = jnp.sum(gt[8:16], axis=0, keepdims=True)
    vec[4:5, 0:C] = jnp.sum(gsq[...], axis=0, keepdims=True)
    vx = [remote(vec, rv1.at[k - 1], m_s.at[k], m_r.at[k], xpeer(k)) for k in range(1, B)]
    for cp in vx:
        cp.start()
    rs_end(0)
    rs_end(1)
    ends = [local(f_d, owd, lsem.at[0])]
    ends[0].start()
    for cp in vx:
        cp.wait()
    t = vec[...]
    for k in range(B - 1):
        t = t + rv1[k]
    vec[...] = t
    vz = [
        remote(vec, rv2.at[k - 1], m_s.at[B - 1 + k], m_r.at[B - 1 + k], zpeer(k)) for k in range(1, A)
    ]
    for cp in vz:
        cp.start()
    def gin_end(i):
        c = nc - 1 - i
        r = rows_at(c * TB, TB)
        for k in range(1, ny):
            y_copy(c, k).wait()
            gin[r, :] += ry[k - 1, c].astype(F32)

    loop(nc, gin_end)
    ends.append(local(gin, gin_o, lsem.at[1]))
    ends[-1].start()
    rs_end(2)
    rs_end(3)
    rs_end(4)
    rs_middle(6)
    rs_end(5)
    ends.append(local(f_g, owg, lsem.at[2]))
    ends[-1].start()
    rs_middle(7)
    for cp in vz:
        cp.wait()
    t = vec[...]
    for k in range(A - 1):
        t = t + rv2[k]
    vec[...] = t
    ends.append(local(vec, vec_o, lsem.at[3]))
    ends[-1].start()
    rs_end(6)
    rs_end(7)
    ends.append(local(f_q.at[:, 0 : 3 * C], owq, lsem.at[4]))
    ends[-1].start()
    ends.append(local(f_q.at[:, 3 * C : 4 * C], owo, lsem.at[5]))
    ends[-1].start()
    for cp in ends:
        cp.wait()


def run_back(z, off_bias, q, k, v, qr, kr, attn, ll, tokf, gba, gres, wqof, gwd, gwg, r1, ga, gs, cos, sin, sq):
    T, C, CF, F, D, H = z.T, z.C, z.CF, z.F, z.D, z.H
    nc, TB, TH, R, A, B, ny = z.nc, z.TB, z.TH, z.R, z.A, z.B, z.ny
    S = jax.ShapeDtypeStruct
    V = pltpu.VMEM
    hbm = pl.BlockSpec(memory_space=pltpu.HBM)
    vm = pl.BlockSpec(memory_space=pltpu.VMEM)
    W = max(F, CF, C)
    outs = [
        S((T, CF), F32), S((R, 3 * C), F32), S((R, C), F32), S((R, 2 * F), F32), S((R, F), F32), S((8, W), F32),
    ]
    cols = (F, 2 * F, 4 * C)
    scratch = [
        V((T, C), BF), V((T, C), BF), V((T, C), BF), V((2, T, C), BF), V((T, C), BF),
        V((8, T), F32), V((8, T), F32), V((D, 4 * C), BF), V((T, D), BF), V((T, D), BF),
        V((nc, TH, D), BF), V((T, C), BF), V((T, C), F32), V((T, C), F32), V((TB, C), F32),
        V((T, 3 * C), BF), V((8, C), F32),
        V((A, R, F), BF), V((A, R, 2 * F), BF), V((A, B, R, 4 * C), BF),
    ]
    scratch += [V((B - 1, A, R, w), BF) for w in cols]
    scratch += [V((A, R, w), BF) for w in cols]
    scratch += [V((A - 1, R, w), BF) for w in cols]
    scratch += [V((R, F), F32), V((R, 2 * F), F32), V((R, 4 * C), F32)]
    scratch += [
        V((nc, ny, TB, CF), BF), V((nc, ny, TB, CF), BF), V((ny, TB, CF), F32), V((nc, ny - 1, TB, CF), BF),
        V((ny - 1, nc, TB, CF), BF), V((T, CF), F32), V((16, CF), F32), V((16, CF), F32), V((16, F), F32),
        V((8, W), F32), V((B - 1, 8, W), F32), V((A - 1, 8, W), F32),
    ]
    sem = pltpu.SemaphoreType.DMA
    for shape in ((8, B - 1), (8, A - 1), (nc,), (nc, ny - 1), (A + B - 1,)):
        scratch += [sem(shape), sem(shape)]
    scratch += [sem((20,))]
    return pl.pallas_call(
        functools.partial(back, z),
        out_shape=outs,
        in_specs=[pl.BlockSpec(memory_space=pltpu.SMEM)] + [hbm] * 16 + [vm] * 3,
        out_specs=[hbm] * len(outs),
        scratch_shapes=scratch,
        compiler_params=pltpu.CompilerParams(
            collective_id=1, has_side_effects=True, vmem_limit_bytes=63 * 2**20
        ),
        name="back",
    )(
        off_bias, q, k, v, qr, kr, attn, ll, tokf, gba, gres, wqof, gwd,
        gwg, r1, ga, gs, cos, sin, sq,
    )


def tables(position):
    half = DK // 2
    frequency = theta_base ** (-(2.0 / DK) * jnp.arange(half, dtype=jnp.float32))
    grid = position.astype(jnp.float32)[:, None] * frequency[None, :]
    return jnp.cos(grid), jnp.sin(grid)


def on_device(
    sizes,
    tokens,
    w_qkv,
    w_out,
    w_gate_up,
    w_down,
    s_qk,
    alpha_attn,
    alpha_mlp,
    s_mlp,
    doc_lengths,
    grad_out,
):
    T, CF = tokens.shape
    H = s_qk.shape[1]
    C = H * DK
    F = w_down.shape[1]
    z = Sizes(sizes, T, C, CF, F, doc_lengths.shape[1])
    D, R = z.D, z.R
    doc_ids, position = layout(doc_lengths[0], T)
    cos, sin = tables(position)
    scale = s_qk.T.reshape(1, C)
    sml = s_mlp.transpose(1, 2, 0).reshape(2, F)
    alpha = jnp.pad(
        jnp.stack([alpha_attn.T.reshape(-1), alpha_mlp.T.reshape(-1)]), ((0, 6), (0, 0))
    )
    whole = doc_lengths[0, 0] == T
    off_bias = jnp.where(whole, 0.0, NEG).astype(F32).reshape(1)
    live = whole.astype(F32).reshape(1)
    cos, sin = jnp.tile(cos, (1, 4)), jnp.tile(sin, (1, 4))
    (out, q, k, v, qr, kr, attn, ll, tokf, gba, gres, wqof, gwd, gwg, r1, ga, gs, _) = run_front(
        z, live, tokens, grad_out, jnp.concatenate([w_qkv.reshape(R, 3 * C), w_out], axis=1), w_gate_up.reshape(R, 2 * F),
        w_down, alpha, cos, sin, scale, sml,
    )
    grad_in, gw_qkv, gw_out, gw_gu, gw_down, vec = run_back(
        z, off_bias, q, k, v, qr, kr, attn, ll, tokf, gba, gres, wqof, gwd, gwg, r1, ga, gs, cos, sin, scale
    )
    d, m = place()

    def channel_rows(v, per_head):
        n = per_head // z.dp
        return lax.dynamic_slice_in_dim(v.reshape(H, per_head).T, d * n, n, 0)

    gs = jnp.stack([channel_rows(vec[i, 0:F], F // H) for i in range(2)], axis=1)
    return (
        out,
        grad_in,
        gw_qkv.reshape(R, 3, C),
        gw_out,
        gw_gu.reshape(R, 2, F),
        gw_down,
        channel_rows(vec[4, 0:C], DK),
        channel_rows(vec[2, 0:CF], DK),
        channel_rows(vec[3, 0:CF], DK),
        gs,
    )


def solution(mesh):
    placed = (
        P("dp", "mp"),
        P("dp", None, "mp"),
        P("dp", "mp"),
        P("dp", None, "mp"),
        P("dp", "mp"),
        P(None, "mp"),
        P(None, "mp"),
        P(None, "mp"),
        P(None, None, "mp"),
        P("dp", None),
        P("dp", "mp"),
    )
    return jax.shard_map(
        functools.partial(on_device, dict(mesh.shape)),
        mesh=mesh,
        in_specs=placed,
        out_specs=(
            P("dp", "mp"),
            P("dp", "mp"),
            P("dp", None, "mp"),
            P("dp", "mp"),
            P("dp", None, "mp"),
            P("dp", "mp"),
            P("dp", "mp"),
            P("dp", "mp"),
            P("dp", "mp"),
            P("dp", None, "mp"),
        ),
        check_vma=False,
    )
```

```python
import functools
import math

import jax
import jax.numpy as jnp
from jax import lax
from jax.experimental import pallas as pl
from jax.experimental.pallas import tpu as pltpu
from jax.sharding import PartitionSpec as P

DK = 64
epsilon = 1e-06
theta_base = 10000.0


def layout(lengths, token_count):
    starts = jnp.cumsum(lengths) - lengths
    place = jnp.arange(token_count, dtype=jnp.int32)
    doc_ids = jnp.sum((place[:, None] >= starts[None, 1:]).astype(jnp.int32), axis=1)
    picked = (doc_ids[:, None] == jnp.arange(lengths.shape[0], dtype=jnp.int32)[None, :]).astype(
        jnp.int32
    )
    position = place - jnp.sum(picked * starts[None, :], axis=1)
    return (doc_ids, position)


LC=math.sqrt(DK)*math.log2(math.e)
NEG=-1e30
def nt(a,b): return lax.dot_general(a,b,(((1,),(1,)),((),())),preferred_element_type=jnp.float32)
def nn(a,b): return jnp.dot(a,b,preferred_element_type=jnp.float32)
def head_mask(x,h):
    lane=lax.broadcasted_iota(jnp.int32,x.shape,1)
    return jnp.where((lane//DK)==(h%2), x, jnp.zeros_like(x))
def attn_fwd_block(i, TB, H, ref, C, live, acc):
    hb=TB//2
    qs=pl.ds(pl.multiple_of(i*TB,TB),TB)
    def vx(h,ks):
        v=ref[ks,pl.ds(2*C+(h//2)*128,128)]
        lane=lax.broadcasted_iota(jnp.int32,v.shape,1)
        return jnp.where((lane//DK)==(h%2),v,jnp.ones_like(v))
    def tile(h,qsl,ks,tri):
        p2=pl.ds((h//2)*128,128)
        x=nt(ref[qsl,p2],head_mask(ref[ks,pl.ds(C+(h//2)*128,128)],h))
        if tri:
            r=lax.broadcasted_iota(jnp.int32,x.shape,0); c=lax.broadcasted_iota(jnp.int32,x.shape,1)
            x=jnp.where(c<=r,x,NEG)
        p=jnp.exp2(x*LC).astype(jnp.bfloat16)
        return nn(p,vx(h,ks))
    k0=pl.ds(pl.multiple_of(i*TB,hb),hb); k1=pl.ds(pl.multiple_of(i*TB+hb,hb),hb)
    for h in range(H):
        a0=tile(h,qs,k0,True)
        a1=tile(h,k1,k1,True)
        acc[h,0:hb]=a0[0:hb]; acc[h,hb:TB]=a0[hb:TB]+a1
    def body(j,_):
        ks=pl.ds(pl.multiple_of(j*TB,TB),TB)
        for h in range(H):
            acc[h]+=live*tile(h,qs,ks,False)
        return 0
    lax.fori_loop(0,i,body,0)
def tdot(a,b): return lax.dot_general(a,b,(((0,),(0,)),((),())),preferred_element_type=jnp.float32)
def attn_bwd_block(i,TB,H,q_ref,k_ref,v_ref,g_ref,ll_ref,dl_ref,ob,dq,dk,dv):
    qs=pl.ds(pl.multiple_of(i*TB,TB),TB); hb=TB//2
    qz=[head_mask(q_ref[qs,pl.ds((h//2)*128,128)],h) for h in range(H)]
    gz=[head_mask(g_ref[qs,pl.ds((h//2)*128,128)],h) for h in range(H)]
    lr=[ll_ref[pl.ds(h,1),qs] for h in range(H)]
    dr=[dl_ref[pl.ds(h,1),qs] for h in range(H)]
    def tile(h,ks,qv,gv,lb,dd,tri):
        p2=pl.ds((h//2)*128,128)
        x=nt(k_ref[ks,p2],qv)*LC-lb
        dp=nt(v_ref[ks,p2],gv)
        if tri:
            r=lax.broadcasted_iota(jnp.int32,x.shape,0); c=lax.broadcasted_iota(jnp.int32,x.shape,1)
            x=jnp.where(r<=c,x,NEG)
        p=jnp.exp2(x)
        ds=(p*(dp-dd)).astype(jnp.bfloat16)
        dvp=nn(p.astype(jnp.bfloat16),gv)
        dkp=nn(ds,qv)
        dqp=tdot(ds,head_mask(k_ref[ks,p2],h))
        return dqp,dkp,dvp
    k0=pl.ds(pl.multiple_of(i*TB,hb),hb); k1=pl.ds(pl.multiple_of(i*TB+hb,hb),hb)
    for pr in range((H+1)//2):
        p2=pl.ds(pr*128,128)
        dk0=dv0=dk1=dv1=0; q0=q1=0
        for h in range(2*pr,min(2*pr+2,H)):
            a,b,c=tile(h,k0,qz[h],gz[h],lr[h],dr[h],True)
            a1,b1,c1=tile(h,k1,qz[h][hb:],gz[h][hb:],lr[h][:,hb:],dr[h][:,hb:],True)
            q0+=a[0:hb]; q1+=a[hb:]+a1
            dk0+=b; dv0+=c; dk1+=b1; dv1+=c1
        dq[0:hb,p2]=q0; dq[hb:TB,p2]=q1
        dk[k0,p2]+=dk0; dv[k0,p2]+=dv0; dk[k1,p2]+=dk1; dv[k1,p2]+=dv1
    lo=[l-ob for l in lr]
    def body(j,_):
        ks=pl.ds(pl.multiple_of(j*TB,TB),TB)
        for pr in range((H+1)//2):
            p2=pl.ds(pr*128,128)
            dka=dva=dqa=0
            for h in range(2*pr,min(2*pr+2,H)):
                a,b,c=tile(h,ks,qz[h],gz[h],lo[h],dr[h],False)
                dqa+=a; dka+=b; dva+=c
            dq[:,p2]+=dqa
            dk[ks,p2]+=dka; dv[ks,p2]+=dva
        return 0
    lax.fori_loop(0,i,body,0)


MESH = pl.DeviceIdType.MESH
F32, BF = jnp.float32, jnp.bfloat16


class Sizes:
    def __init__(self, mesh_shape, T, C, CF, F, pieces):
        self.mp, self.dp = mesh_shape["mp"], mesh_shape["dp"]
        self.ny = self.mp // 2
        self.A = 4 if self.dp % 4 == 0 else 1
        self.B = self.dp // self.A
        self.T, self.C, self.CF, self.F = T, C, CF, F
        self.D = CF * self.mp
        self.H = C // DK
        self.nc = pieces
        self.TB = T // pieces
        self.TH = self.TB // 2
        self.R = self.D // self.dp


def place():
    return lax.axis_index("dp"), lax.axis_index("mp")


def remote(src, dst, ss, rs, dev):
    return pltpu.make_async_remote_copy(
        src, dst, send_sem=ss, recv_sem=rs, device_id=dev, device_id_type=MESH
    )


def local(src, dst, sem):
    return pltpu.make_async_copy(src, dst, sem)


def rows_at(start, size):
    return pl.ds(pl.multiple_of(start, size), size)


def loop(n, fn):
    def body(i, carry):
        fn(i)
        return carry

    lax.fori_loop(0, n, body, 0)


def fold(x):
    return jnp.sum(x.reshape(x.shape[0] // 8, 8, x.shape[1]), axis=0)


def mean_sq(x, D):
    return lax.rsqrt(jnp.sum(x * x, axis=1, keepdims=True) * (1.0 / D) + epsilon)


def split_dot(x, ones):
    hi = x.astype(BF)
    return nn(hi, ones) + nn((x - hi.astype(F32)).astype(BF), ones)


def head_ones(width):
    i = lax.broadcasted_iota(jnp.int32, (width, width), 0) // DK
    j = lax.broadcasted_iota(jnp.int32, (width, width), 1) // DK
    return jnp.where(i == j, 1.0, 0.0).astype(BF)


def turn(x, cosine, sine, sign):
    lane = lax.broadcasted_iota(jnp.int32, x.shape, 1)
    first = (lane % DK) < DK // 2
    other = jnp.where(first, -pltpu.roll(x, x.shape[1] - DK // 2, 1), pltpu.roll(x, DK // 2, 1))
    return x * cosine + sign * other * sine


def layer(
    z,
    live_ref, tokens, gout, wqo, wg, wd, alpha, table, sq, sml,
    out, gin_o, owq, owo, owg, owd, vec_o,
    qkv_h, rot_h, tokf, goh, gwd_h, gwg_h, gqo_h, r1d_h, r1g_h, r1q_h, r2d_h, r2g_h, r2q_h,
    tokv, wqov, wgv, wdv, gml, act, gu, gba, attn, ll, dl, acc, dk, dv, dq, fstage,
    sy1, ry1, sy2, ry2, ry3, rc, sc, ghid, gst, fst, wst, alv, gacc, gsacc, gsq, gar, vec, rv1, rv2,
    tok_s, tok_r, w_s, w_r, x_s, x_r, al_s, al_r, go_s, go_r, ex_s, ex_r, y_s, y_r, hc_s, hc_r, out_s, out_r,
    p_s, p_r, q_s, q_r, c_s, c_r, yg_s, yg_r, m_s, m_r, lsem, rsem,
):
    T, C, CF, F, D, H = z.T, z.C, z.CF, z.F, z.D, z.H
    nc, TB, TH, R, A, B, ny, mp = z.nc, z.TB, z.TH, z.R, z.A, z.B, z.ny, z.mp
    d, m = place()
    a, b = d // B, d % B
    y, core = m // 2, m % 2
    mate = 1 - core
    peer = (d, y * 2 + mate)

    def ypeer(k, cc):
        return (d, ((y + k) % ny) * 2 + cc)

    zpeer = lambda k: (((a + k) % A) * B + b, m)
    xpeer = lambda k: (a * B + (b + k) % B, m)
    others = [peer] + [ypeer(k, cc) for k in range(1, ny) for cc in (core, mate)]
    everyone = others + [zpeer(k) for k in range(1, A)] + [xpeer(k) for k in range(1, B)]
    bar = pltpu.get_barrier_semaphore()
    for dev in everyone:
        pl.semaphore_signal(bar, 1, device_id=dev, device_id_type=MESH)
    pl.semaphore_wait(bar, len(everyone))

    live = live_ref[0]
    off_bias = jnp.where(live > 0.5, 0.0, NEG)
    feat = lambda mm: pl.ds(pl.multiple_of(mm * CF, CF), CF)
    mine = feat(m)


    def tok_own(c, i, dev):
        r = rows_at(c * TB, TB)
        return remote(tokens.at[r], tokv.at[r, mine], tok_s.at[c, i], tok_r.at[c, i], dev)

    def tok_got(c, i, mm):
        r = rows_at(c * TB, TB)
        return remote(tokv.at[r, feat(mm)], tokv.at[r, feat(mm)], tok_s.at[c, i], tok_r.at[c, i], peer)

    def start_tok(i):
        c = nc - 1 - i
        for k in range(1, ny):
            tok_own(c, k, ypeer(k, core)).start()
        tok_own(c, 0, peer).start()

    lo, hi = slice(0, F), slice(F, 2 * F)
    dlo, dhi = slice(0, F // 2), slice(F // 2, F)
    weights = [
        (wqo, wqov),
        (wg.at[:, lo], wgv.at[:, lo]),
        (wg.at[:, hi], wgv.at[:, hi]),
        (wd.at[:, dlo], wdv.at[:, dlo]),
        (wd.at[:, dhi], wdv.at[:, dhi]),
    ]

    def shard(aa, bb):
        return rows_at((aa * B + bb) * R, R)

    def column(st):
        return (b - st + B) % B

    def z_moves(w, st, h):
        src, dst = weights[w]
        moves = []
        for way, step in ((0, 1), (1, -1)):
            aa = a - step * (h - 1)
            ok = (a + step >= 0) & (a + step < A) & (aa >= 0) & (aa < A)
            moves.append((way, step, jnp.clip(aa, 0, A - 1), ok))
        return src, dst, moves

    def z_copy(w, st, h, way, step, aa):
        src, dst = weights[w]
        r = shard(aa, column(st))
        source = src if (h == 1 and st == 0) else dst.at[r]
        to = jnp.clip(a + step, 0, A - 1) * B + b
        return remote(source, dst.at[r], w_s.at[w, st, way, h - 1], w_r.at[w, st, way, h - 1], (to, m))

    def z_hop(w, st, h):
        if h >= A:
            return
        for way, step, aa, ok in z_moves(w, st, h)[2]:

            @pl.when(ok)
            def _():
                z_copy(w, st, h, way, step, aa).start()

    def z_sent(w, st, h):
        for way, step, aa, ok in z_moves(w, st, h)[2]:

            @pl.when(ok)
            def _():
                z_copy(w, st, h, way, step, aa).wait_send()

    def z_wait(w, st, h, forward=False):
        if h >= A:
            return
        for way, step in ((0, 1), (1, -1)):
            aa = a - step * h

            @pl.when((aa >= 0) & (aa < A))
            def _():
                z_copy(w, st, h, way, step, jnp.clip(aa, 0, A - 1)).wait_recv()
                if forward:
                    x_send(w, aa)

    def x_copy(w, aa, k, own=False):
        src, dst = weights[w]
        r = shard(aa, b)
        return remote(
            src if own else dst.at[r], dst.at[r], x_s.at[w, aa, k - 1], x_r.at[w, aa, k - 1], xpeer(k)
        )

    def x_send(w, aa, own=False):
        for k in range(1, B):
            x_copy(w, aa, k, own).start()

    def x_wait(w, aa):
        src, dst = weights[w]
        for k in range(1, B):
            r = shard(aa, (b - k + B) % B)
            remote(src, dst.at[r], x_s.at[w, aa, k - 1], x_r.at[w, aa, k - 1], xpeer(k)).wait_recv()

    def w_local(w):
        src, dst = weights[w]
        return local(src, dst.at[shard(a, b)], lsem.at[16 + w])

    def w_start(w):
        z_hop(w, 0, 1)
        x_send(w, a, own=True)
        w_local(w).start()

    def w_next(w, st, h, forward=True):
        z_wait(w, st, h, forward)
        z_hop(w, st, h + 1)

    def w_ready(w):
        for aa in range(A):
            x_wait(w, aa)
        w_local(w).wait()

    def w_sent(w, forward):
        for st in range(1 if forward else B):
            for h in range(1, A):
                z_sent(w, st, h)
        for k in range(1, B):
            for aa in range(A) if forward else [a]:
                x_copy(w, aa, k).wait_send()

    w_start(0)
    loop(nc, start_tok)
    x_send(4, a, own=True)
    w_local(4).start()
    tok_local = local(tokens, tokv.at[:, mine], lsem.at[4])
    tok_local.start()
    al_local = local(alpha, alv.at[:, mine], lsem.at[5])
    al_local.start()
    al_copies = [
        remote(alpha, alv.at[:, mine], al_s.at[i], al_r.at[i], dev) for i, dev in enumerate(others)
    ]
    for cp in al_copies:
        cp.start()

    def pass_tok(i):
        c = nc - 1 - i
        for k in range(1, ny):
            src = ((y - k + ny) % ny) * 2 + core
            tok_got(c, k, src).wait_recv()
            tok_got(c, ny + k - 1, src).start()

    w_next(0, 0, 1)
    pass_tok(0)
    w_next(0, 0, 2)
    pass_tok(1)
    w_next(0, 0, 3)
    w_start(1)
    w_start(2)
    loop(nc - 2, lambda i: pass_tok(i + 2))

    def end_tok(i):
        c = nc - 1 - i
        tok_got(c, 0, y * 2 + mate).wait_recv()
        for k in range(1, ny):
            src = ((y - k + ny) % ny) * 2 + mate
            tok_got(c, ny + k - 1, src).wait_recv()

    loop(nc, end_tok)

    def tok_sent(i):
        c = nc - 1 - i
        tok_own(c, 0, peer).wait_send()
        for k in range(1, ny):
            tok_own(c, k, ypeer(k, core)).wait_send()
            tok_got(c, ny + k - 1, ((y - k + ny) % ny) * 2 + core).wait_send()

    loop(nc, tok_sent)
    tok_local.wait()
    w_ready(0)

    go4 = gout

    def go_copy(i, dev, cc):
        return remote(go4.at[:, cc], goh.at[:, :, mine], go_s.at[i], go_r.at[i], dev)

    go_copies = [go_copy(0, peer, mate)]
    i = 1
    for k in range(1, ny):
        for cc in (core, mate):
            go_copies.append(go_copy(i, ypeer(k, cc), cc))
            i += 1
    go_local = local(go4.at[:, core], goh.at[:, :, mine], lsem.at[6])
    go_local.start()
    for cp in go_copies:
        cp.start()

    ones = head_ones(C)
    qkvv = gml

    def angles_of(r):
        t = table[r, :]
        u = pltpu.roll(t, DK, 1)
        first = lax.broadcasted_iota(jnp.int32, t.shape, 1) < DK
        cs, sn = jnp.where(first, t, u), jnp.where(first, u, t)
        return jnp.concatenate([cs] * (C // 128), axis=1), jnp.concatenate([sn] * (C // 128), axis=1)

    def project_rows(i):
        r = rows_at(i * TB, TB)
        x = tokv[r, :]
        cs, sn = angles_of(r)
        for part in range(2):
            cols = slice(part * C, part * C + C)
            t = turn(nn(x, wqov[:, cols]), cs, sn, 1.0)
            act[r, cols] = t.astype(BF)
            inv = lax.rsqrt(split_dot(t * t, ones) + epsilon)
            qkvv[r, cols] = (t * inv * sq[...]).astype(BF)
        qkvv[r, 2 * C : 3 * C] = nn(x, wqov[:, 2 * C : 3 * C]).astype(BF)

        @pl.when(i == 0)
        def _():
            w_next(1, 0, 1)

        @pl.when(i == 1)
        def _():
            w_next(2, 0, 1)

        @pl.when(i == 2)
        def _():
            w_next(1, 0, 2)

    loop(nc, project_rows)
    save_tok = local(tokv, tokf, lsem.at[4])
    save_tok.start()
    saves = [
        local(qkvv.at[:, 0 : 3 * C], qkv_h, lsem.at[7]),
        local(act.at[:, 0 : 2 * C], rot_h, lsem.at[8]),
    ]
    for cp in saves:
        cp.start()

    RT = 64
    NG = 2
    GW = D // NG

    def y_copy(e, c, k, n, sy, ry):
        cols = slice(n * GW, n * GW + GW)
        return remote(
            sy.at[c, :, cols], ry.at[k - 1, c, :, cols], y_s.at[e, c, k - 1, n], y_r.at[e, c, k - 1, n],
            ypeer(k, core),
        )

    def exchange(e, c, part, sy, ry):
        r = rows_at(c * TB, TB)
        theirs, ours = rows_at(mate * TH, TH), rows_at(core * TH, TH)
        copies = []
        for n in range(NG):
            cols = slice(n * GW, n * GW + GW)
            sc[:, cols] = part(r, cols).astype(BF)
            cp = remote(
                sc.at[theirs, cols], rc.at[c, :, cols], ex_s.at[e, c, n], ex_r.at[e, c, n], peer
            )
            cp.start()
            copies.append(cp)
        for n in range(NG):
            cols = slice(n * GW, n * GW + GW)
            copies[n].wait()
            sy[c, :, cols] = (sc[ours, cols].astype(F32) + rc[c, :, cols].astype(F32)).astype(BF)
            for k in range(1, ny):
                y_copy(e, c, k, n, sy, ry).start()

    def landed(e, c, sy, ry):
        for k in range(1, ny):
            for n in range(NG):
                y_copy(e, c, k, n, sy, ry).wait()

    def total(c, r, sy, ry):
        t = sy[c, r, :].astype(F32)
        for k in range(ny - 1):
            t = t + ry[k, c, r, :].astype(F32)
        return t

    NS = 2
    SH = TH // NS

    def share(e, c, n, buf):
        r = rows_at(c * TB + core * TH + n * SH, SH)
        return remote(buf.at[r], buf.at[r], hc_s.at[e, c, n], hc_r.at[e, c, n], peer)

    def rows_then_share(e, c, rows, buf):
        for n in range(NS):
            loop(SH // RT, lambda t: rows(n * (SH // RT) + t))
            share(e, c, n, buf).start()

    def shared(e, c, buf):
        for n in range(NS):
            share(e, c, n, buf).wait()

    def attend_chunk(i):
        c = nc - 1 - i
        attn_fwd_block(c, TB, H, qkvv, C, live, acc)
        r = rows_at(c * TB, TB)
        for pr in range(C // 128):
            both = []
            for h in (2 * pr, 2 * pr + 1):
                t = acc[h]
                both.append(t / pltpu.roll(t, DK, 1))
                row = DK if h % 2 == 0 else 0
                ll[pl.ds(h, 1), r] = jnp.log2(t).T[row : row + 1]
            lane = lax.broadcasted_iota(jnp.int32, (TB, 128), 1)
            attn[r, pr * 128 : pr * 128 + 128] = jnp.where(lane < DK, both[0], both[1]).astype(BF)

        def part(rr, cols):
            return nt(attn[rr, :], wqov[cols, 3 * C : 4 * C])

        @pl.when(i == 0)
        def _():
            save_tok.wait()

        exchange(0, c, part, sy1, ry1)

        @pl.when(i == 0)
        def _():
            w_next(2, 0, 2)
            w_next(1, 0, 3)
            w_start(3)
            z_hop(4, 0, 1)
            x_wait(4, a)
            for st in range(1, B):
                z_hop(4, st, 1)

        @pl.when(i == 1)
        def _():
            w_next(2, 0, 3)
            w_next(3, 0, 1)

        @pl.when(i == 2)
        def _():
            for st in range(B):
                w_next(4, st, 1, False)

        @pl.when(i == 3)
        def _():
            w_next(3, 0, 2)
            for st in range(B):
                w_next(4, st, 2, False)

    ll[...] = jnp.zeros_like(ll)
    loop(nc, attend_chunk)
    for cp in saves:
        cp.wait()
    al_local.wait()
    for cp in al_copies:
        cp.wait()
    w_ready(1)
    w_ready(2)

    gacc[...] = jnp.zeros_like(gacc)
    gsacc[...] = jnp.zeros_like(gsacc)

    def feed_chunk(i):
        c = nc - 1 - i
        landed(0, c, sy1, ry1)
        base = c * TB + core * TH

        def rows(t):
            r = rows_at(t * RT, RT)
            g = rows_at(base + t * RT, RT)
            br = total(c, r, sy1, ry1)
            xb = tokv[g, :]
            x = xb.astype(F32)
            ha = br * mean_sq(br, D)
            mix = x + alv[0:1, :] * (ha - x)
            tokv[g, :] = (mix * mean_sq(mix, D)).astype(BF)

        rows_then_share(0, c, rows, tokv)
        shared(0, c, tokv)
        r = rows_at(c * TB, TB)

        def units(n):
            cu, cv = rows_at(n * 256, 256), rows_at(F + n * 256, 256)
            x = tokv[r, :]
            u = nn(x, wgv[:, cu])
            v = nn(x, wgv[:, cv])
            gu[r, cu] = u.astype(BF)
            gu[r, cv] = v.astype(BF)
            us = u * sml[0:1, cu]
            vs = v * sml[1:2, cu]
            act[r, cu] = (us * vs * jax.nn.sigmoid(vs)).astype(BF)

        loop(F // 256, units)

        @pl.when(i == 0)
        def _():
            w_next(3, 0, 3)

        @pl.when(i == 1)
        def _():
            for st in range(B):
                w_next(4, st, 3, False)

    loop(nc, feed_chunk)
    w_ready(3)
    w_local(4).wait()

    def down_chunk(i):
        c = nc - 1 - i
        exchange(1, c, lambda rr, cols: nt(act[rr, :], wdv[cols, :]), sy2, ry2)

    loop(nc, down_chunk)
    go_local.wait()
    for cp in go_copies:
        cp.wait()

    def back_chunk(i):
        c = nc - 1 - i
        lg = local(goh.at[c], gst, lsem.at[6])
        lg.start()
        lg.wait()
        landed(1, c, sy2, ry2)
        base = c * TB + core * TH

        def rows(t):
            r = rows_at(t * RT, RT)
            g = rows_at(base + t * RT, RT)
            am = alv[1:2, :]
            bm = total(c, r, sy2, ry2)
            h = tokv[g, :].astype(F32)
            rm = mean_sq(bm, D)
            hm = bm * rm
            diff = hm - h
            mix = h + am * diff
            r2 = mean_sq(mix, D)
            fin = mix * r2
            fst[r, :] = fin.astype(BF)
            go = gst[r, :].astype(F32)
            gm = r2 * (go - fin * (jnp.sum(go * fin, axis=1, keepdims=True) * (1.0 / D)))
            gacc[8:16, :] += fold(gm * diff)
            gh = am * gm
            ghid[c, r, :] = (gm - gh).astype(BF)
            gb = rm * (gh - hm * (jnp.sum(gh * hm, axis=1, keepdims=True) * (1.0 / D)))
            gml[g, :] = gb.astype(BF)

        rows_then_share(1, c, rows, gml)
        og = rows_at(base, TH)
        o_here = local(fst.at[:, mine], out.at[og], lsem.at[6])
        o_here.start()
        o_there = remote(
            fst.at[:, feat(y * 2 + mate)], out.at[og], out_s.at[c], out_r.at[c], peer
        )
        o_there.start()
        shared(1, c, gml)
        r = rows_at(c * TB, TB)

        def units(n):
            cu, cv = rows_at(n * 256, 256), rows_at(F + n * 256, 256)
            ga = nn(gml[r, :], wdv[:, cu])
            u = gu[r, cu].astype(F32)
            v = gu[r, cv].astype(F32)
            su, sv = sml[0:1, cu], sml[1:2, cu]
            us, vs = u * su, v * sv
            sg = jax.nn.sigmoid(vs)
            si = vs * sg
            g_u = ga * si
            g_v = ga * us * (sg + si - si * sg)
            gsacc[0:8, cu] += fold(g_u * u)
            gsacc[8:16, cu] += fold(g_v * v)
            gu[r, cu] = (g_u * su).astype(BF)
            gu[r, cv] = (g_v * sv).astype(BF)

        loop(F // 256, units)
        exchange(2, c, lambda rr, cols: nt(gu[rr, :], wgv[cols, :]), sy2, ry3)
        o_here.wait()
        o_there.wait()

    loop(nc, back_chunk)

    RA, AR, w = D // A, A * R, F // 2
    pieces = []
    for src, r1, r2, cuts in (
        (gwd_h, r1d_h, r2d_h, (0, w, 2 * w)),
        (gwg_h, r1g_h, r2g_h, (0, w, 2 * w, 3 * w, 4 * w)),
        (gqo_h, r1q_h, r2q_h, (0, 2 * C, 3 * C, 4 * C)),
    ):
        for n in range(len(cuts) - 1):
            pieces.append((src, r1, r2, slice(cuts[n], cuts[n + 1])))
    lanes_of = (0, 1, 3, 0, 1, 3, 1, 3, 0)

    def px_copy(p, k):
        src, r1, _, cols = pieces[p]
        return remote(
            src.at[(b + k) % B, :, cols], r1.at[k - 1, :, cols], p_s.at[p, k - 1], p_r.at[p, k - 1], xpeer(k)
        )

    def rs_start(p):
        for k in range(1, B):
            px_copy(p, k).start()

    def slot(p):
        cols = pieces[p][3]
        return slice(lanes_of[p] * w, lanes_of[p] * w + cols.stop - cols.start)

    def sums(p, aa):
        return gu.at[pl.ds(pl.multiple_of(D + aa * R, R), R), slot(p)]

    def pz_copy(p, k):
        _, _, r2, cols = pieces[p]
        return remote(
            sums(p, (a + k) % A), r2.at[k - 1, :, cols], q_s.at[p, k - 1], q_r.at[p, k - 1], zpeer(k)
        )

    def own_load(p):
        src, _, _, cols = pieces[p]
        return local(src.at[b, :, cols], gu.at[0:AR, slot(p)], rsem.at[lanes_of[p], 0])

    def first_load(p, k):
        _, r1, _, cols = pieces[p]
        return local(
            r1.at[k - 1, :, cols], gu.at[k * AR : (k + 1) * AR, slot(p)], rsem.at[lanes_of[p], k]
        )

    def rs_load(p):
        own_load(p).start()
        for k in range(1, B):
            px_copy(p, k).wait()
            first_load(p, k).start()

    def rs_add(p):
        own_load(p).wait()
        for k in range(1, B):
            first_load(p, k).wait()
        for k in list(range(1, A)) + [0]:
            aa = (a + k) % A
            t = gu[rows_at(aa * R, R), slot(p)].astype(F32)
            for kk in range(1, B):
                t = t + gu[pl.ds(pl.multiple_of(kk * AR + aa * R, R), R), slot(p)].astype(F32)
            gu[pl.ds(pl.multiple_of(D + aa * R, R), R), slot(p)] = t.astype(BF)
            if k:
                pz_copy(p, k).start()

    def second_load(p, k):
        _, _, r2, cols = pieces[p]
        return local(
            r2.at[k - 1, :, cols], gu.at[D + AR + (k - 1) * R : D + AR + k * R, slot(p)], rsem.at[lanes_of[p], B + k]
        )

    def end_load(p):
        for k in range(1, A):
            pz_copy(p, k).wait()
            second_load(p, k).start()

    def rs_end(p, res):
        for k in range(1, A):
            second_load(p, k).wait()
        width = pieces[p][3].stop - pieces[p][3].start
        t = gu[pl.ds(pl.multiple_of(D + a * R, R), R), slot(p)].astype(F32)
        for k in range(1, A):
            t = t + gu[D + AR + (k - 1) * R : D + AR + k * R, slot(p)].astype(F32)
        fstage[:, 0:width] = t
        cp = local(fstage.at[:, 0:width], res, lsem.at[0])
        cp.start()
        cp.wait()

    def rs_finish(p):
        if p < 2:
            res = owd.at[:, p * w : p * w + w]
        elif p < 6:
            res = owg.at[:, (p - 2) * w : (p - 1) * w]
        elif p == 6:
            res = owq.at[:, 0 : 2 * C]
        elif p == 7:
            res = owq.at[:, 2 * C : 3 * C]
        else:
            res = owo
        rs_end(p, res)

    def tile_out(half, dst, t):
        src = wst.at[:, :, half * F : half * F + F]
        return local(src, dst.at[:, rows_at(t * R, R), half * F : half * F + F], lsem.at[1 + half])

    def down_out(half, t):
        src = wst.at[:, :, half * F : half * F + F]
        return local(src, gwd_h.at[:, rows_at(t * R, R)], lsem.at[1 + half])

    def down_tile(t):
        for half in range(2):
            tt = 2 * t + half

            @pl.when(t > 0)
            def _():
                down_out(half, tt).wait()

            cols = rows_at(tt * RA, RA)
            wst[:, :, half * F : half * F + F] = tdot(gml[:, cols], act[...]).astype(BF).reshape(B, R, F)
            down_out(half, tt).start()

    lt_first = local(tokf.at[rows_at((nc - 1) * TB + core * TH, TH)], gst, lsem.at[6])
    lt_first.start()
    loop(A // 2, down_tile)
    for half in range(2):
        down_out(half, 0).wait()
    rs_start(0)

    def up_tile(t):
        cols = rows_at(t * RA, RA)
        lhs = tokv[:, cols]
        for half in range(2):

            @pl.when(t > 0)
            def _():
                tile_out(half, gwg_h, t).wait()

            wst[:, :, half * F : half * F + F] = (
                tdot(lhs, gu[:, half * F : half * F + F]).astype(BF).reshape(B, R, F)
            )
            tile_out(half, gwg_h, t).start()

        @pl.when(t == A // 2)
        def _():
            rs_start(1)

    loop(A, up_tile)
    for half in range(2):
        tile_out(half, gwg_h, 0).wait()
    rs_start(2)
    rs_start(3)
    rs_load(0)
    qv, kv, vv = gml.at[:, 0:C], gml.at[:, C : 2 * C], gml.at[:, 2 * C : 3 * C]
    gv = gml.at[:, 3 * C : 4 * C]
    rot0 = 2 * w
    loads = [
        local(qkv_h, gml.at[:, 0 : 3 * C], lsem.at[7]),
        local(rot_h, gu.at[:, rot0 : rot0 + 2 * C], lsem.at[8]),
        local(tokf, tokv, lsem.at[9]),
    ]
    for cp in loads:
        cp.start()
    dk[...] = jnp.zeros_like(dk)
    dv[...] = jnp.zeros_like(dv)
    gsq[...] = jnp.zeros_like(gsq)
    heads = lax.broadcasted_iota(jnp.int32, (8, C), 0)
    lanes = lax.broadcasted_iota(jnp.int32, (8, C), 1) // DK
    pick = jnp.where(heads == lanes, 1.0, 0.0).astype(BF)
    for cp in loads[:2]:
        cp.wait()
    NY = ny * CF

    def gin_copy(c, hs):
        return remote(
            sc.at[hs * TH : (hs + 1) * TH, 0:NY], rc.at[c, :, hs * NY : (hs + 1) * NY], c_s.at[c, hs],
            c_r.at[c, hs], peer,
        )

    def gin_y(c, k, hs):
        src = slice((hs * (ny - 1) + k - 1) * CF, (hs * (ny - 1) + k) * CF)
        dst = slice(hs * CF, hs * CF + CF)
        return remote(
            sy2.at[c, :, src], ry2.at[k - 1, c, :, dst], yg_s.at[c, k - 1, hs], yg_r.at[c, k - 1, hs],
            ypeer(k, core),
        )

    n128 = CF // 128

    def gin_take(c):
        for hs in range(2):
            gin_copy(c, hs).wait()
            for k in range(ny):
                for q in range(n128):
                    col = hs * NY + k * CF + q * 128
                    t = acc[k * n128 + q, hs * TH : (hs + 1) * TH, :] + rc[c, :, col : col + 128].astype(F32)
                    if k == 0:
                        dk[rows_at(c * TB + hs * TH, TH), q * 128 : q * 128 + 128] = t
                    else:
                        col = (hs * (ny - 1) + k - 1) * CF + q * 128
                        sy2[c, :, col : col + 128] = t.astype(BF)
            for k in range(1, ny):
                gin_y(c, k, hs).start()

    def out_tiles():
        def o_tile(t):
            cols = rows_at(t * RA, RA)
            wst[:, :, 0:C] = tdot(gba[:, cols], attn[...]).astype(BF).reshape(B, R, C)
            cp = local(wst.at[:, :, 0:C], gqo_h.at[:, rows_at(t * R, R), 3 * C : 4 * C], lsem.at[1])
            cp.start()
            cp.wait()

        loop(A, o_tile)

    def kept_rows(c):
        return local(tokf.at[rows_at(c * TB + core * TH, TH)], gst, lsem.at[6])

    def branch_rows(c):
        base = c * TB + core * TH
        landed(2, c, sy2, ry3)
        kept_rows(c).wait()

        def rows(t):
            r = rows_at(t * RT, RT)
            g = rows_at(base + t * RT, RT)
            aa = alv[0:1, :]
            br = total(c, r, sy1, ry1)
            x = gst[r, :].astype(F32)
            ra = mean_sq(br, D)
            ha = br * ra
            diff = ha - x
            mix = x + aa * diff
            r1 = mean_sq(mix, D)
            hid = mix * r1
            gh = ghid[c, r, :].astype(F32) + total(c, r, sy2, ry3)
            gm = r1 * (gh - hid * (jnp.sum(gh * hid, axis=1, keepdims=True) * (1.0 / D)))
            gacc[0:8, :] += fold(gm * diff)
            gt = aa * gm
            ghid[c, r, :] = (gm - gt).astype(BF)
            gb = ra * (gt - ha * (jnp.sum(gt * ha, axis=1, keepdims=True) * (1.0 / D)))
            gba[g, :] = gb.astype(BF)

        rows_then_share(2, c, rows, gba)

        @pl.when(c > 0)
        def _():
            kept_rows(jnp.maximum(c - 1, 0)).start()

    branch_rows(nc - 1)
    rs_add(0)

    def attn_grad_chunk(i):
        c = nc - 1 - i
        shared(2, c, gba)

        @pl.when(c > 0)
        def _():
            branch_rows(jnp.maximum(c - 1, 0))

        r = rows_at(c * TB, TB)
        g = nn(gba[r, :], wqov[:, 3 * C : 4 * C]).astype(BF)
        gv[r, :] = g
        prod = g.astype(F32) * attn[r, :].astype(F32)
        ph = prod.astype(BF)
        dl[:, r] = nt(pick, ph) + nt(pick, (prod - ph.astype(F32)).astype(BF))
        attn_bwd_block(c, TB, H, qv, kv, vv, gv, ll, dl, off_bias, dq, dk, dv)

        @pl.when(i == 0)
        def _():
            rs_load(1)
            rs_start(4)

        @pl.when(i == 1)
        def _():
            rs_load(2)
            end_load(0)

        @pl.when(i == 2)
        def _():
            rs_load(3)
            end_load(1)

        @pl.when(i == nc - 1)
        def _():
            rs_finish(2)
            rs_load(5)
            out_tiles()
            rs_start(8)

        cs, sn = angles_of(r)
        for part in range(2):
            gh = (dq[...] if part == 0 else dk[r, :]) * 8.0
            t = gu[r, rot0 + part * C : rot0 + part * C + C].astype(F32)
            inv = lax.rsqrt(split_dot(t * t, ones) + epsilon)
            un = t * inv
            gsq[...] += fold(gh * un)
            gh = gh * sq[...]
            gr = inv * (gh - un * split_dot(gh * un, ones))
            act[r, part * C : part * C + C] = turn(gr, cs, sn, -1.0).astype(BF)
        act[r, 2 * C : 3 * C] = dv[r, :].astype(BF)

        def product(hsel, k, cc):
            rr = rows_at(c * TB + hsel * TH, TH)
            cols = feat(((y + k) % ny) * 2 + cc)
            t = nt(act[rr, 0 : 3 * C], wqov[cols, 0 : 3 * C])
            if k == 0:
                t = t + jnp.where(hsel == core, 1.0, 0.0) * ghid[c, :, cols].astype(F32)
            return t

        @pl.when(i > 0)
        def _():
            gin_take(jnp.minimum(c + 1, nc - 1))

        for hs in range(2):
            for k in range(ny):
                sc[hs * TH : (hs + 1) * TH, k * CF : (k + 1) * CF] = product(hs, k, mate).astype(BF)
            gin_copy(c, hs).start()
        for hs in range(2):
            for k in range(ny):
                t = product(hs, k, core)
                for q in range(n128):
                    acc[k * n128 + q, hs * TH : (hs + 1) * TH, :] = t[:, q * 128 : q * 128 + 128]

        @pl.when(i == 0)
        def _():
            rs_add(1)
            rs_start(5)

        @pl.when(i == 1)
        def _():
            rs_add(2)
            rs_finish(0)

        @pl.when(i == 2)
        def _():
            rs_add(3)
            rs_finish(1)
            rs_load(4)
            end_load(2)

        @pl.when(i == nc - 1)
        def _():
            rs_add(4)
            rs_add(5)
            end_load(3)

    loop(nc, attn_grad_chunk)
    ga_there = remote(gacc.at[:, feat(y * 2 + mate)], gar, m_s.at[0], m_r.at[0], peer)
    ga_there.start()
    loads[2].wait()

    def q_out(half, t):
        src = wst.at[:, :, half * F : half * F + 2 * C]
        return local(src, gqo_h.at[:, rows_at(t * R, R), 0 : 2 * C], lsem.at[1 + half])

    def q_tile(t):
        for half in range(2):
            tt = 2 * t + half

            @pl.when(t > 0)
            def _():
                q_out(half, tt).wait()

            g = tdot(tokv[:, rows_at(tt * RA, RA)], act[:, 0 : 2 * C]).astype(BF)
            wst[:, :, half * F : half * F + 2 * C] = g.reshape(B, R, 2 * C)
            q_out(half, tt).start()

    loop(A // 2, q_tile)
    for half in range(2):
        q_out(half, 0).wait()
    rs_start(6)

    def v_out(half, t):
        src = wst.at[:, :, half * F : half * F + C]
        return local(src, gqo_h.at[:, rows_at(t * R, R), 2 * C : 3 * C], lsem.at[1 + half])

    def v_tile(t):
        for half in range(2):
            tt = 2 * t + half

            @pl.when(t > 0)
            def _():
                v_out(half, tt).wait()

            g = tdot(tokv[:, rows_at(tt * RA, RA)], act[:, 2 * C : 3 * C]).astype(BF)
            wst[:, :, half * F : half * F + C] = g.reshape(B, R, C)
            v_out(half, tt).start()

    loop(A // 2, v_tile)
    for half in range(2):
        v_out(half, 0).wait()
    rs_start(7)
    gin_take(0)
    ga_there.wait()
    vec[...] = jnp.zeros_like(vec)
    gt = gacc[:, mine] + gar[...]
    vec[0:1, 0:F] = jnp.sum(gsacc[0:8, :], axis=0, keepdims=True)
    vec[1:2, 0:F] = jnp.sum(gsacc[8:16, :], axis=0, keepdims=True)
    vec[2:3, 0:CF] = jnp.sum(gt[0:8], axis=0, keepdims=True)
    vec[3:4, 0:CF] = jnp.sum(gt[8:16], axis=0, keepdims=True)
    vec[4:5, 0:C] = jnp.sum(gsq[...], axis=0, keepdims=True)
    vx = [remote(vec, rv1.at[k - 1], m_s.at[k], m_r.at[k], xpeer(k)) for k in range(1, B)]
    for cp in vx:
        cp.start()
    rs_finish(3)
    rs_load(8)
    end_load(4)
    for cp in vx:
        cp.wait()
    t = vec[...]
    for k in range(B - 1):
        t = t + rv1[k]
    vec[...] = t
    vz = [
        remote(vec, rv2.at[k - 1], m_s.at[B - 1 + k], m_r.at[B - 1 + k], zpeer(k)) for k in range(1, A)
    ]
    for cp in vz:
        cp.start()

    rs_add(8)
    rs_finish(4)
    end_load(5)

    def gin_end(i):
        c = nc - 1 - i
        for hs in range(2):
            rr = rows_at(c * TB + hs * TH, TH)
            for k in range(1, ny):
                gin_y(c, k, hs).wait()
                dk[rr, :] += ry2[k - 1, c, :, hs * CF : hs * CF + CF].astype(F32)

    loop(nc, gin_end)
    ends = [local(dk, gin_o, lsem.at[10])]
    ends[-1].start()
    rs_finish(5)
    rs_load(6)
    rs_add(6)
    rs_load(7)
    rs_add(7)
    end_load(8)
    for cp in vz:
        cp.wait()
    t = vec[...]
    for k in range(A - 1):
        t = t + rv2[k]
    vec[...] = t
    ends.append(local(vec, vec_o, lsem.at[11]))
    ends[-1].start()
    for p in range(5):
        w_sent(p, p != 4)
    rs_finish(8)
    end_load(6)
    rs_finish(6)
    end_load(7)
    rs_finish(7)
    for cp in ends:
        cp.wait()


def run_layer(z, live, tokens, gout, wqo, wg, wd, alpha, table, sq, sml):
    T, C, CF, F, D, H = z.T, z.C, z.CF, z.F, z.D, z.H
    nc, TB, TH, R, A, B, ny, mp = z.nc, z.TB, z.TH, z.R, z.A, z.B, z.ny, z.mp
    S = jax.ShapeDtypeStruct
    hbm = pl.BlockSpec(memory_space=pltpu.HBM)
    vm = pl.BlockSpec(memory_space=pltpu.VMEM)
    W = max(F, CF, C)
    AR = A * R
    outs = [
        S((T, CF), BF), S((T, CF), F32), S((R, 3 * C), F32), S((R, C), F32), S((R, 2 * F), F32), S((R, F), F32),
        S((8, W), F32),
        S((T, 3 * C), BF), S((T, 2 * C), BF), S((T, D), BF), S((nc, TH, D), BF),
    ]
    widths = (F, 2 * F, 4 * C)
    outs += [S((B, AR, n), BF) for n in widths]
    outs += [S((max(B - 1, 1), AR, n), BF) for n in widths]
    outs += [S((max(A - 1, 1), R, n), BF) for n in widths]
    V = pltpu.VMEM
    scratch = [
        V((T, D), BF), V((D, 4 * C), BF), V((D, 2 * F), BF), V((D, F), BF),
        V((T, D), BF), V((T, F), BF), V((T, 2 * F), BF), V((T, D), BF),
        V((T, C), BF), V((8, T), F32), V((8, T), F32), V((max(H, ny * CF // 128), TB, 128), F32),
        V((T, C), F32), V((T, C), F32), V((TB, C), F32), V((R, F // 2), F32),
    ]
    for _ in range(2):
        scratch += [V((nc, TH, D), BF), V((ny - 1, nc, TH, D), BF)]
    scratch += [
        V((ny - 1, nc, TH, D), BF), V((nc, TH, D), BF), V((TB, D), BF), V((nc, TH, D), BF), V((TH, D), BF), V((TH, D), BF),
        V((B, R, 2 * F), BF), V((8, D), F32), V((16, D), F32), V((16, F), F32), V((8, C), F32), V((16, CF), F32),
        V((8, W), F32), V((max(B - 1, 1), 8, W), F32), V((max(A - 1, 1), 8, W), F32),
    ]
    sem = pltpu.SemaphoreType.DMA
    for shape in (
        (nc, 2 * ny - 1), (5, B, 2, max(A - 1, 1)), (5, A, max(B - 1, 1)), (mp - 1,), (mp - 1,), (3, nc, 2),
        (3, nc, ny - 1, 2), (3, nc, 2), (nc,), (9, max(B - 1, 1)), (9, max(A - 1, 1)), (nc, 2), (nc, ny - 1, 2),
        (A + B - 1,),
    ):
        scratch += [sem(shape), sem(shape)]
    scratch += [sem((21,)), sem((4, A + B))]
    return pl.pallas_call(
        functools.partial(layer, z),
        out_shape=outs,
        in_specs=[pl.BlockSpec(memory_space=pltpu.SMEM)] + [hbm] * 6 + [vm] * 3,
        out_specs=[hbm] * len(outs),
        scratch_shapes=scratch,
        compiler_params=pltpu.CompilerParams(
            collective_id=0, has_side_effects=True, vmem_limit_bytes=64 * 2**20 - 2**19
        ),
        name="layer",
    )(live, tokens, gout.reshape(nc, 2, TH, CF), wqo, wg, wd, alpha, table, sq, sml)


def tables(position):
    half = DK // 2
    frequency = theta_base ** (-(2.0 / DK) * jnp.arange(half, dtype=jnp.float32))
    grid = position.astype(jnp.float32)[:, None] * frequency[None, :]
    return jnp.cos(grid), jnp.sin(grid)


def on_device(
    sizes,
    tokens,
    w_qkv,
    w_out,
    w_gate_up,
    w_down,
    s_qk,
    alpha_attn,
    alpha_mlp,
    s_mlp,
    doc_lengths,
    grad_out,
):
    T, CF = tokens.shape
    H = s_qk.shape[1]
    C = H * DK
    F = w_down.shape[1]
    z = Sizes(sizes, T, C, CF, F, doc_lengths.shape[1])
    D, R = z.D, z.R
    doc_ids, position = layout(doc_lengths[0], T)
    cos, sin = tables(position)
    table = jnp.concatenate([cos, cos, sin, sin], axis=1)
    scale = s_qk.T.reshape(1, C)
    sml = s_mlp.transpose(1, 2, 0).reshape(2, F)
    alpha = jnp.pad(
        jnp.stack([alpha_attn.T.reshape(-1), alpha_mlp.T.reshape(-1)]), ((0, 6), (0, 0))
    )
    whole = doc_lengths[0, 0] == T
    live = whole.astype(F32).reshape(1)
    (out, grad_in, gw_qkv, gw_out, gw_gu, gw_down, vec) = run_layer(
        z, live, tokens, grad_out, jnp.concatenate([w_qkv.reshape(R, 3 * C), w_out], axis=1),
        w_gate_up.reshape(R, 2 * F), w_down, alpha, table, scale, sml,
    )[:7]
    d, m = place()

    def channel_rows(v, per_head):
        n = per_head // z.dp
        return lax.dynamic_slice_in_dim(v.reshape(H, per_head).T, d * n, n, 0)

    gs = jnp.stack([channel_rows(vec[i, 0:F], F // H) for i in range(2)], axis=1)
    return (
        out,
        grad_in,
        gw_qkv.reshape(R, 3, C),
        gw_out,
        gw_gu.reshape(R, 2, F),
        gw_down,
        channel_rows(vec[4, 0:C], DK),
        channel_rows(vec[2, 0:CF], DK),
        channel_rows(vec[3, 0:CF], DK),
        gs,
    )


def solution(mesh):
    placed = (
        P("dp", "mp"),
        P("dp", None, "mp"),
        P("dp", "mp"),
        P("dp", None, "mp"),
        P("dp", "mp"),
        P(None, "mp"),
        P(None, "mp"),
        P(None, "mp"),
        P(None, None, "mp"),
        P("dp", None),
        P("dp", "mp"),
    )
    return jax.shard_map(
        functools.partial(on_device, dict(mesh.shape)),
        mesh=mesh,
        in_specs=placed,
        out_specs=(
            P("dp", "mp"),
            P("dp", "mp"),
            P("dp", None, "mp"),
            P("dp", "mp"),
            P("dp", None, "mp"),
            P("dp", "mp"),
            P("dp", "mp"),
            P("dp", "mp"),
            P("dp", "mp"),
            P("dp", None, "mp"),
        ),
        check_vma=False,
    )
```

```python
import functools
import math

import jax
import jax.numpy as jnp
import numpy as np
from jax import lax
from jax.experimental import pallas as pl
from jax.experimental.pallas import tpu as pltpu
from jax.sharding import PartitionSpec as P

DK = 64
epsilon = 1e-06
theta_base = 10000.0


LC=math.sqrt(DK)*math.log2(math.e)
NEG=-1e30
def nt(a,b): return lax.dot_general(a,b,(((1,),(1,)),((),())),preferred_element_type=jnp.float32)
def nn(a,b): return jnp.dot(a,b,preferred_element_type=jnp.float32)
def head_mask(x,h):
    lane=lax.broadcasted_iota(jnp.int32,x.shape,1)
    return jnp.where((lane//DK)==(h%2), x, jnp.zeros_like(x))
def attn_fwd_block(i, TB, H, ref, C, live, acc):
    hb=TB//2
    qs=pl.ds(pl.multiple_of(i*TB,TB),TB)
    def vx(h,ks):
        v=ref[ks,pl.ds(2*C+(h//2)*128,128)]
        lane=lax.broadcasted_iota(jnp.int32,v.shape,1)
        return jnp.where((lane//DK)==(h%2),v,jnp.ones_like(v))
    def tile(h,qsl,ks,tri):
        p2=pl.ds((h//2)*128,128)
        x=nt(ref[qsl,p2],head_mask(ref[ks,pl.ds(C+(h//2)*128,128)],h))
        if tri:
            r=lax.broadcasted_iota(jnp.int32,x.shape,0); c=lax.broadcasted_iota(jnp.int32,x.shape,1)
            x=jnp.where(c<=r,x,NEG)
        p=jnp.exp2(x*LC).astype(jnp.bfloat16)
        return nn(p,vx(h,ks))
    k0=pl.ds(pl.multiple_of(i*TB,hb),hb); k1=pl.ds(pl.multiple_of(i*TB+hb,hb),hb)
    for h in range(H):
        a0=tile(h,qs,k0,True)
        a1=tile(h,k1,k1,True)
        acc[h,0:hb]=a0[0:hb]; acc[h,hb:TB]=a0[hb:TB]+a1
    def body(j,_):
        ks=pl.ds(pl.multiple_of(j*TB,TB),TB)
        for h in range(H):
            acc[h]+=live*tile(h,qs,ks,False)
        return 0
    lax.fori_loop(0,i,body,0)
def tdot(a,b): return lax.dot_general(a,b,(((0,),(0,)),((),())),preferred_element_type=jnp.float32)
def attn_bwd_block(i,TB,H,q_ref,k_ref,v_ref,g_ref,ll_ref,dl_ref,ob,dq,dk,dv):
    qs=pl.ds(pl.multiple_of(i*TB,TB),TB); hb=TB//2
    qz=[head_mask(q_ref[qs,pl.ds((h//2)*128,128)],h) for h in range(H)]
    gz=[head_mask(g_ref[qs,pl.ds((h//2)*128,128)],h) for h in range(H)]
    lr=[ll_ref[pl.ds(h,1),qs] for h in range(H)]
    dr=[dl_ref[pl.ds(h,1),qs] for h in range(H)]
    def tile(h,ks,qv,gv,lb,dd,tri):
        p2=pl.ds((h//2)*128,128)
        x=nt(k_ref[ks,p2],qv)*LC-lb
        dp=nt(v_ref[ks,p2],gv)
        if tri:
            r=lax.broadcasted_iota(jnp.int32,x.shape,0); c=lax.broadcasted_iota(jnp.int32,x.shape,1)
            x=jnp.where(r<=c,x,NEG)
        p=jnp.exp2(x)
        ds=(p*(dp-dd)).astype(jnp.bfloat16)
        dvp=nn(p.astype(jnp.bfloat16),gv)
        dkp=nn(ds,qv)
        dqp=tdot(ds,head_mask(k_ref[ks,p2],h))
        return dqp,dkp,dvp
    k0=pl.ds(pl.multiple_of(i*TB,hb),hb); k1=pl.ds(pl.multiple_of(i*TB+hb,hb),hb)
    for pr in range((H+1)//2):
        p2=pl.ds(pr*128,128)
        dk0=dv0=dk1=dv1=0; q0=q1=0
        for h in range(2*pr,min(2*pr+2,H)):
            a,b,c=tile(h,k0,qz[h],gz[h],lr[h],dr[h],True)
            a1,b1,c1=tile(h,k1,qz[h][hb:],gz[h][hb:],lr[h][:,hb:],dr[h][:,hb:],True)
            q0+=a[0:hb]; q1+=a[hb:]+a1
            dk0+=b; dv0+=c; dk1+=b1; dv1+=c1
        dq[0:hb,p2]=q0; dq[hb:TB,p2]=q1
        dk[k0,p2]+=dk0; dv[k0,p2]+=dv0; dk[k1,p2]+=dk1; dv[k1,p2]+=dv1
    lo=[l-ob for l in lr]
    def body(j,_):
        ks=pl.ds(pl.multiple_of(j*TB,TB),TB)
        for pr in range((H+1)//2):
            p2=pl.ds(pr*128,128)
            dka=dva=dqa=0
            for h in range(2*pr,min(2*pr+2,H)):
                a,b,c=tile(h,ks,qz[h],gz[h],lo[h],dr[h],False)
                dqa+=a; dka+=b; dva+=c
            dq[:,p2]+=dqa
            dk[ks,p2]+=dka; dv[ks,p2]+=dva
        return 0
    lax.fori_loop(0,i,body,0)


MESH = pl.DeviceIdType.MESH
F32, BF = jnp.float32, jnp.bfloat16


class Sizes:
    def __init__(self, mesh_shape, T, C, CF, F, pieces):
        self.mp, self.dp = mesh_shape["mp"], mesh_shape["dp"]
        self.ny = self.mp // 2
        self.A = 4 if self.dp % 4 == 0 else 1
        self.B = self.dp // self.A
        self.T, self.C, self.CF, self.F = T, C, CF, F
        self.D = CF * self.mp
        self.H = C // DK
        self.nc = pieces
        self.TB = T // pieces
        self.TH = self.TB // 2
        self.R = self.D // self.dp


def place():
    return lax.axis_index("dp"), lax.axis_index("mp")


def remote(src, dst, ss, rs, dev):
    return pltpu.make_async_remote_copy(
        src, dst, send_sem=ss, recv_sem=rs, device_id=dev, device_id_type=MESH
    )


def local(src, dst, sem):
    return pltpu.make_async_copy(src, dst, sem)


def rows_at(start, size):
    return pl.ds(pl.multiple_of(start, size), size)


def loop(n, fn):
    def body(i, carry):
        fn(i)
        return carry

    lax.fori_loop(0, n, body, 0)


def fold(x):
    return jnp.sum(x.reshape(x.shape[0] // 8, 8, x.shape[1]), axis=0)


def mean_sq(x, D):
    return lax.rsqrt(jnp.sum(x * x, axis=1, keepdims=True) * (1.0 / D) + epsilon)


def split_dot(x, ones):
    hi = x.astype(BF)
    return nn(hi, ones) + nn((x - hi.astype(F32)).astype(BF), ones)


def head_ones(width):
    i = lax.broadcasted_iota(jnp.int32, (width, width), 0) // DK
    j = lax.broadcasted_iota(jnp.int32, (width, width), 1) // DK
    return jnp.where(i == j, 1.0, 0.0).astype(BF)


def turn(x, cosine, sine, sign):
    lane = lax.broadcasted_iota(jnp.int32, x.shape, 1)
    first = (lane % DK) < DK // 2
    other = jnp.where(first, -pltpu.roll(x, x.shape[1] - DK // 2, 1), pltpu.roll(x, DK // 2, 1))
    return x * cosine + sign * other * sine


def layer(
    z,
    live_ref, tokens, gout, wqo, wg, wd, alpha, table, sq, sml,
    out, gin_o, owq, owo, owg, owd, vec_o,
    qkv_h, rot_h, tokf, goh, gwd_h, gwg_h, gqo_h, r1d_h, r1g_h, r1q_h, r2d_h, r2g_h, r2q_h,
    tokv, wqov, wgv, wdv, gml, act, gu, gba, attn, ll, dl, acc, dk, dv, dq, fstage,
    sy1, ry1, sy2, ry2, ry3, rc, sc, ghid, gst, fst, wst, alv, gacc, gsacc, gsq, gar, vec, rv1, rv2,
    tok_s, tok_r, w_s, w_r, x_s, x_r, al_s, al_r, go_s, go_r, ex_s, ex_r, y_s, y_r, hc_s, hc_r, out_s, out_r,
    p_s, p_r, q_s, q_r, c_s, c_r, yg_s, yg_r, m_s, m_r, lsem, rsem,
):
    T, C, CF, F, D, H = z.T, z.C, z.CF, z.F, z.D, z.H
    nc, TB, TH, R, A, B, ny, mp = z.nc, z.TB, z.TH, z.R, z.A, z.B, z.ny, z.mp
    d, m = place()
    a, b = d // B, d % B
    y, core = m // 2, m % 2
    mate = 1 - core
    peer = (d, y * 2 + mate)

    def ypeer(k, cc):
        return (d, ((y + k) % ny) * 2 + cc)

    zpeer = lambda k: (((a + k) % A) * B + b, m)
    xpeer = lambda k: (a * B + (b + k) % B, m)
    others = [peer] + [ypeer(k, cc) for k in range(1, ny) for cc in (core, mate)]
    everyone = others + [zpeer(k) for k in range(1, A)] + [xpeer(k) for k in range(1, B)]
    bar = pltpu.get_barrier_semaphore()
    for dev in everyone:
        pl.semaphore_signal(bar, 1, device_id=dev, device_id_type=MESH)
    pl.semaphore_wait(bar, len(everyone))

    live = live_ref[0]
    off_bias = jnp.where(live > 0.5, 0.0, NEG)
    feat = lambda mm: pl.ds(pl.multiple_of(mm * CF, CF), CF)
    mine = feat(m)


    def tok_own(c, i, dev):
        r = rows_at(c * TB, TB)
        return remote(tokens.at[r], tokv.at[r, mine], tok_s.at[c, i], tok_r.at[c, i], dev)

    def tok_got(c, i, mm):
        r = rows_at(c * TB, TB)
        return remote(tokv.at[r, feat(mm)], tokv.at[r, feat(mm)], tok_s.at[c, i], tok_r.at[c, i], peer)

    def start_tok(i):
        c = nc - 1 - i
        for k in range(1, ny):
            tok_own(c, k, ypeer(k, core)).start()
        tok_own(c, 0, peer).start()

    lo, hi = slice(0, F), slice(F, 2 * F)
    dlo, dhi = slice(0, F // 2), slice(F // 2, F)
    weights = [
        (wqo, wqov),
        (wg.at[:, lo], wgv.at[:, lo]),
        (wg.at[:, hi], wgv.at[:, hi]),
        (wd.at[:, dlo], wdv.at[:, dlo]),
        (wd.at[:, dhi], wdv.at[:, dhi]),
    ]

    def shard(aa, bb):
        return rows_at((aa * B + bb) * R, R)

    def column(st):
        return (b - st + B) % B

    def z_moves(w, st, h):
        src, dst = weights[w]
        moves = []
        for way, step in ((0, 1), (1, -1)):
            aa = a - step * (h - 1)
            ok = (a + step >= 0) & (a + step < A) & (aa >= 0) & (aa < A)
            moves.append((way, step, jnp.clip(aa, 0, A - 1), ok))
        return src, dst, moves

    def z_copy(w, st, h, way, step, aa):
        src, dst = weights[w]
        r = shard(aa, column(st))
        source = src if (h == 1 and st == 0) else dst.at[r]
        to = jnp.clip(a + step, 0, A - 1) * B + b
        return remote(source, dst.at[r], w_s.at[w, st, way, h - 1], w_r.at[w, st, way, h - 1], (to, m))

    def z_hop(w, st, h):
        if h >= A:
            return
        for way, step, aa, ok in z_moves(w, st, h)[2]:

            @pl.when(ok)
            def _():
                z_copy(w, st, h, way, step, aa).start()

    def z_sent(w, st, h):
        for way, step, aa, ok in z_moves(w, st, h)[2]:

            @pl.when(ok)
            def _():
                z_copy(w, st, h, way, step, aa).wait_send()

    def z_wait(w, st, h, forward=False):
        if h >= A:
            return
        for way, step in ((0, 1), (1, -1)):
            aa = a - step * h

            @pl.when((aa >= 0) & (aa < A))
            def _():
                z_copy(w, st, h, way, step, jnp.clip(aa, 0, A - 1)).wait_recv()
                if forward:
                    x_send(w, aa)

    def x_copy(w, aa, k, own=False):
        src, dst = weights[w]
        r = shard(aa, b)
        return remote(
            src if own else dst.at[r], dst.at[r], x_s.at[w, aa, k - 1], x_r.at[w, aa, k - 1], xpeer(k)
        )

    def x_send(w, aa, own=False):
        for k in range(1, B):
            x_copy(w, aa, k, own).start()

    def x_wait(w, aa):
        src, dst = weights[w]
        for k in range(1, B):
            r = shard(aa, (b - k + B) % B)
            remote(src, dst.at[r], x_s.at[w, aa, k - 1], x_r.at[w, aa, k - 1], xpeer(k)).wait_recv()

    def w_local(w):
        src, dst = weights[w]
        return local(src, dst.at[shard(a, b)], lsem.at[16 + w])

    def w_start(w):
        z_hop(w, 0, 1)
        x_send(w, a, own=True)
        w_local(w).start()

    def w_next(w, st, h, forward=True):
        z_wait(w, st, h, forward)
        z_hop(w, st, h + 1)

    def w_ready(w):
        for aa in range(A):
            x_wait(w, aa)
        w_local(w).wait()

    def w_sent(w, forward):
        for st in range(1 if forward else B):
            for h in range(1, A):
                z_sent(w, st, h)
        for k in range(1, B):
            for aa in range(A) if forward else [a]:
                x_copy(w, aa, k).wait_send()

    w_start(0)
    loop(nc, start_tok)
    x_send(4, a, own=True)
    w_local(4).start()
    tok_local = local(tokens, tokv.at[:, mine], lsem.at[4])
    tok_local.start()
    al_local = local(alpha, alv.at[:, mine], lsem.at[5])
    al_local.start()
    al_copies = [
        remote(alpha, alv.at[:, mine], al_s.at[i], al_r.at[i], dev) for i, dev in enumerate(others)
    ]
    for cp in al_copies:
        cp.start()

    def pass_tok(i):
        c = nc - 1 - i
        for k in range(1, ny):
            src = ((y - k + ny) % ny) * 2 + core
            tok_got(c, k, src).wait_recv()
            tok_got(c, ny + k - 1, src).start()

    w_next(0, 0, 1)
    pass_tok(0)
    w_next(0, 0, 2)
    pass_tok(1)
    w_next(0, 0, 3)
    w_start(1)
    w_start(2)
    loop(nc - 2, lambda i: pass_tok(i + 2))

    go4 = gout

    def go_copy(i, dev, cc):
        return remote(go4.at[:, cc], goh.at[:, :, mine], go_s.at[i], go_r.at[i], dev)

    go_copies = [go_copy(0, peer, mate)]
    i = 1
    for k in range(1, ny):
        for cc in (core, mate):
            go_copies.append(go_copy(i, ypeer(k, cc), cc))
            i += 1
    go_local = local(go4.at[:, core], goh.at[:, :, mine], lsem.at[6])
    go_local.start()
    for cp in go_copies:
        cp.start()

    def end_tok(i):
        c = nc - 1 - i
        tok_got(c, 0, y * 2 + mate).wait_recv()
        for k in range(1, ny):
            src = ((y - k + ny) % ny) * 2 + mate
            tok_got(c, ny + k - 1, src).wait_recv()

    loop(nc, end_tok)

    def tok_sent(i):
        c = nc - 1 - i
        tok_own(c, 0, peer).wait_send()
        for k in range(1, ny):
            tok_own(c, k, ypeer(k, core)).wait_send()
            tok_got(c, ny + k - 1, ((y - k + ny) % ny) * 2 + core).wait_send()

    loop(nc, tok_sent)
    tok_local.wait()
    w_ready(0)

    ones = head_ones(C)
    qkvv = gml

    def angles_of(r):
        t = jnp.where(live > 0.5, table[r, :], table[0:TB, :])
        u = pltpu.roll(t, DK, 1)
        first = lax.broadcasted_iota(jnp.int32, t.shape, 1) < DK
        cs, sn = jnp.where(first, t, u), jnp.where(first, u, t)
        return jnp.concatenate([cs] * (C // 128), axis=1), jnp.concatenate([sn] * (C // 128), axis=1)

    def project_rows(i):
        r = rows_at(i * TB, TB)
        x = tokv[r, :]
        cs, sn = angles_of(r)
        for part in range(2):
            cols = slice(part * C, part * C + C)
            t = turn(nn(x, wqov[:, cols]), cs, sn, 1.0)
            act[r, cols] = t.astype(BF)
            inv = lax.rsqrt(split_dot(t * t, ones) + epsilon)
            qkvv[r, cols] = (t * inv * sq[...]).astype(BF)
        qkvv[r, 2 * C : 3 * C] = nn(x, wqov[:, 2 * C : 3 * C]).astype(BF)

        @pl.when(i == 1)
        def _():
            w_next(1, 0, 1)
            w_next(2, 0, 1)

    loop(nc, project_rows)
    save_tok = local(tokv, tokf, lsem.at[4])
    save_tok.start()
    saves = [
        local(qkvv.at[:, 0 : 3 * C], qkv_h, lsem.at[7]),
        local(act.at[:, 0 : 2 * C], rot_h, lsem.at[8]),
    ]
    for cp in saves:
        cp.start()

    RT = 64
    NG = 2
    GW = D // NG

    def y_copy(e, c, k, n, sy, ry):
        cols = slice(n * GW, n * GW + GW)
        return remote(
            sy.at[c, :, cols], ry.at[k - 1, c, :, cols], y_s.at[e, c, k - 1, n], y_r.at[e, c, k - 1, n],
            ypeer(k, core),
        )

    def exchange(e, c, part, sy, ry):
        r = rows_at(c * TB, TB)
        theirs, ours = rows_at(mate * TH, TH), rows_at(core * TH, TH)
        copies = []
        for n in range(NG):
            cols = slice(n * GW, n * GW + GW)
            sc[:, cols] = part(r, cols).astype(BF)
            cp = remote(
                sc.at[theirs, cols], rc.at[c, :, cols], ex_s.at[e, c, n], ex_r.at[e, c, n], peer
            )
            cp.start()
            copies.append(cp)
        for n in range(NG):
            cols = slice(n * GW, n * GW + GW)
            copies[n].wait()
            sy[c, :, cols] = (sc[ours, cols].astype(F32) + rc[c, :, cols].astype(F32)).astype(BF)
            for k in range(1, ny):
                y_copy(e, c, k, n, sy, ry).start()

    def landed(e, c, sy, ry):
        for k in range(1, ny):
            for n in range(NG):
                y_copy(e, c, k, n, sy, ry).wait()

    def total(c, r, sy, ry):
        t = sy[c, r, :].astype(F32)
        for k in range(ny - 1):
            t = t + ry[k, c, r, :].astype(F32)
        return t

    NS = 2
    SH = TH // NS

    def share(e, c, n, buf):
        r = rows_at(c * TB + core * TH + n * SH, SH)
        return remote(buf.at[r], buf.at[r], hc_s.at[e, c, n], hc_r.at[e, c, n], peer)

    def rows_then_share(e, c, rows, buf):
        for n in range(NS):
            loop(SH // RT, lambda t: rows(n * (SH // RT) + t))
            share(e, c, n, buf).start()

    def shared(e, c, buf):
        for n in range(NS):
            share(e, c, n, buf).wait()

    def attend_chunk(i):
        c = nc - 1 - i
        attn_fwd_block(c, TB, H, qkvv, C, live, acc)
        r = rows_at(c * TB, TB)
        for pr in range(C // 128):
            both = []
            for h in (2 * pr, 2 * pr + 1):
                t = acc[h]
                both.append(t / pltpu.roll(t, DK, 1))
                row = DK if h % 2 == 0 else 0
                ll[pl.ds(h, 1), r] = jnp.log2(t).T[row : row + 1]
            lane = lax.broadcasted_iota(jnp.int32, (TB, 128), 1)
            attn[r, pr * 128 : pr * 128 + 128] = jnp.where(lane < DK, both[0], both[1]).astype(BF)

        def part(rr, cols):
            return nt(attn[rr, :], wqov[cols, 3 * C : 4 * C])

        @pl.when(i == 0)
        def _():
            save_tok.wait()

        exchange(0, c, part, sy1, ry1)

        @pl.when(i == 0)
        def _():
            w_next(1, 0, 2)
            w_next(2, 0, 2)
            w_start(3)
            z_hop(4, 0, 1)
            x_wait(4, a)
            for st in range(1, B):
                z_hop(4, st, 1)

        @pl.when(i == 2)
        def _():
            w_next(1, 0, 3)
            w_next(2, 0, 3)

        @pl.when(i == 3)
        def _():
            w_next(3, 0, 1)
            for st in range(B):
                w_next(4, st, 1, False)

    ll[...] = jnp.zeros_like(ll)
    loop(nc, attend_chunk)
    for cp in saves:
        cp.wait()
    al_local.wait()
    for cp in al_copies:
        cp.wait()
    w_ready(1)
    w_ready(2)

    gacc[...] = jnp.zeros_like(gacc)
    gsacc[...] = jnp.zeros_like(gsacc)

    def feed_chunk(i):
        c = nc - 1 - i
        landed(0, c, sy1, ry1)
        base = c * TB + core * TH

        def rows(t):
            r = rows_at(t * RT, RT)
            g = rows_at(base + t * RT, RT)
            br = total(c, r, sy1, ry1)
            xb = tokv[g, :]
            x = xb.astype(F32)
            ha = br * mean_sq(br, D)
            mix = x + alv[0:1, :] * (ha - x)
            tokv[g, :] = (mix * mean_sq(mix, D)).astype(BF)

        rows_then_share(0, c, rows, tokv)
        shared(0, c, tokv)
        r = rows_at(c * TB, TB)

        def units(n):
            cu, cv = rows_at(n * 256, 256), rows_at(F + n * 256, 256)
            x = tokv[r, :]
            u = nn(x, wgv[:, cu])
            v = nn(x, wgv[:, cv])
            gu[r, cu] = u.astype(BF)
            gu[r, cv] = v.astype(BF)
            us = u * sml[0:1, cu]
            vs = v * sml[1:2, cu]
            act[r, cu] = (us * vs * jax.nn.sigmoid(vs)).astype(BF)

        loop(F // 256, units)

        @pl.when(i == 0)
        def _():
            w_next(3, 0, 2)
            for st in range(B):
                w_next(4, st, 2, False)

        @pl.when(i == 1)
        def _():
            w_next(3, 0, 3)
            for st in range(B):
                w_next(4, st, 3, False)
            w_ready(3)
            w_local(4).wait()

        @pl.when(i > 0)
        def _():
            down_chunk(i - 1)

    def down_chunk(i):
        c = nc - 1 - i
        exchange(1, c, lambda rr, cols: nt(act[rr, :], wdv[cols, :]), sy2, ry2)

    loop(nc, feed_chunk)
    down_chunk(nc - 1)
    go_local.wait()
    for cp in go_copies:
        cp.wait()

    def grad_rows(c):
        return local(goh.at[c], gst, lsem.at[12])

    grad_rows(nc - 1).start()

    def back_chunk(i):
        c = nc - 1 - i
        landed(1, c, sy2, ry2)
        grad_rows(c).wait()
        base = c * TB + core * TH

        def rows(t):
            r = rows_at(t * RT, RT)
            g = rows_at(base + t * RT, RT)
            am = alv[1:2, :]
            bm = total(c, r, sy2, ry2)
            h = tokv[g, :].astype(F32)
            rm = mean_sq(bm, D)
            hm = bm * rm
            diff = hm - h
            mix = h + am * diff
            r2 = mean_sq(mix, D)
            fin = mix * r2
            fst[r, :] = fin.astype(BF)
            go = gst[r, :].astype(F32)
            gm = r2 * (go - fin * (jnp.sum(go * fin, axis=1, keepdims=True) * (1.0 / D)))
            gacc[8:16, :] += fold(gm * diff)
            gh = am * gm
            ghid[c, r, :] = (gm - gh).astype(BF)
            gb = rm * (gh - hm * (jnp.sum(gh * hm, axis=1, keepdims=True) * (1.0 / D)))
            gml[g, :] = gb.astype(BF)

        rows_then_share(1, c, rows, gml)

        @pl.when(c > 0)
        def _():
            grad_rows(jnp.maximum(c - 1, 0)).start()

        og = rows_at(base, TH)
        o_here = local(fst.at[:, mine], out.at[og], lsem.at[6])
        o_here.start()
        o_there = remote(
            fst.at[:, feat(y * 2 + mate)], out.at[og], out_s.at[c], out_r.at[c], peer
        )
        o_there.start()
        shared(1, c, gml)
        r = rows_at(c * TB, TB)

        def units(n):
            cu, cv = rows_at(n * 256, 256), rows_at(F + n * 256, 256)
            ga = nn(gml[r, :], wdv[:, cu])
            u = gu[r, cu].astype(F32)
            v = gu[r, cv].astype(F32)
            su, sv = sml[0:1, cu], sml[1:2, cu]
            us, vs = u * su, v * sv
            sg = jax.nn.sigmoid(vs)
            si = vs * sg
            g_u = ga * si
            g_v = ga * us * (sg + si - si * sg)
            gsacc[0:8, cu] += fold(g_u * u)
            gsacc[8:16, cu] += fold(g_v * v)
            gu[r, cu] = (g_u * su).astype(BF)
            gu[r, cv] = (g_v * sv).astype(BF)

        loop(F // 256, units)
        exchange(2, c, lambda rr, cols: nt(gu[rr, :], wgv[cols, :]), sy2, ry3)
        o_here.wait()
        o_there.wait()

    loop(nc, back_chunk)

    RA, AR, w = D // A, A * R, F // 2
    pieces = []
    for src, r1, r2, cuts in (
        (gwd_h, r1d_h, r2d_h, (0, w, 2 * w)),
        (gwg_h, r1g_h, r2g_h, (0, w, 2 * w, 3 * w, 4 * w)),
        (gqo_h, r1q_h, r2q_h, (0, 2 * C, 3 * C, 4 * C)),
    ):
        for n in range(len(cuts) - 1):
            pieces.append((src, r1, r2, slice(cuts[n], cuts[n + 1])))
    lanes_of = (0, 1, 3, 0, 1, 3, 1, 3, 0)

    def px_copy(p, k):
        src, r1, _, cols = pieces[p]
        return remote(
            src.at[(b + k) % B, :, cols], r1.at[k - 1, :, cols], p_s.at[p, k - 1], p_r.at[p, k - 1], xpeer(k)
        )

    def rs_start(p):
        for k in range(1, B):
            px_copy(p, k).start()

    def slot(p):
        cols = pieces[p][3]
        return slice(lanes_of[p] * w, lanes_of[p] * w + cols.stop - cols.start)

    def sums(p, aa):
        return gu.at[pl.ds(pl.multiple_of(D + aa * R, R), R), slot(p)]

    def pz_copy(p, k):
        _, _, r2, cols = pieces[p]
        return remote(
            sums(p, (a + k) % A), r2.at[k - 1, :, cols], q_s.at[p, k - 1], q_r.at[p, k - 1], zpeer(k)
        )

    def own_load(p):
        src, _, _, cols = pieces[p]
        return local(src.at[b, :, cols], gu.at[0:AR, slot(p)], rsem.at[lanes_of[p], 0])

    def first_load(p, k):
        _, r1, _, cols = pieces[p]
        return local(
            r1.at[k - 1, :, cols], gu.at[k * AR : (k + 1) * AR, slot(p)], rsem.at[lanes_of[p], k]
        )

    def rs_load(p):
        own_load(p).start()
        for k in range(1, B):
            px_copy(p, k).wait()
            first_load(p, k).start()

    def rs_add(p):
        own_load(p).wait()
        for k in range(1, B):
            first_load(p, k).wait()
        for k in list(range(1, A)) + [0]:
            aa = (a + k) % A
            t = gu[rows_at(aa * R, R), slot(p)].astype(F32)
            for kk in range(1, B):
                t = t + gu[pl.ds(pl.multiple_of(kk * AR + aa * R, R), R), slot(p)].astype(F32)
            gu[pl.ds(pl.multiple_of(D + aa * R, R), R), slot(p)] = t.astype(BF)
            if k:
                pz_copy(p, k).start()

    def second_load(p, k):
        _, _, r2, cols = pieces[p]
        return local(
            r2.at[k - 1, :, cols], gu.at[D + AR + (k - 1) * R : D + AR + k * R, slot(p)], rsem.at[lanes_of[p], B + k]
        )

    def end_load(p):
        for k in range(1, A):
            pz_copy(p, k).wait()
            second_load(p, k).start()

    def rs_end(p, res):
        for k in range(1, A):
            second_load(p, k).wait()
        width = pieces[p][3].stop - pieces[p][3].start
        t = gu[pl.ds(pl.multiple_of(D + a * R, R), R), slot(p)].astype(F32)
        for k in range(1, A):
            t = t + gu[D + AR + (k - 1) * R : D + AR + k * R, slot(p)].astype(F32)
        fstage[:, 0:width] = t
        cp = local(fstage.at[:, 0:width], res, lsem.at[0])
        cp.start()
        cp.wait()

    def rs_finish(p):
        if p < 2:
            res = owd.at[:, p * w : p * w + w]
        elif p < 6:
            res = owg.at[:, (p - 2) * w : (p - 1) * w]
        elif p == 6:
            res = owq.at[:, 0 : 2 * C]
        elif p == 7:
            res = owq.at[:, 2 * C : 3 * C]
        else:
            res = owo
        rs_end(p, res)

    def tile_out(half, dst, t):
        src = wst.at[:, :, half * F : half * F + F]
        return local(src, dst.at[:, rows_at(t * R, R), half * F : half * F + F], lsem.at[1 + half])

    def down_out(half, t):
        src = wst.at[:, :, half * F : half * F + F]
        return local(src, gwd_h.at[:, rows_at(t * R, R)], lsem.at[1 + half])

    def down_tile(t):
        for half in range(2):
            tt = 2 * t + half

            @pl.when(t > 0)
            def _():
                down_out(half, tt).wait()

            cols = rows_at(tt * RA, RA)
            wst[:, :, half * F : half * F + F] = tdot(gml[:, cols], act[...]).astype(BF).reshape(B, R, F)
            down_out(half, tt).start()

    lt_first = local(tokf.at[rows_at((nc - 1) * TB + core * TH, TH)], gst, lsem.at[6])
    lt_first.start()
    loop(A // 2, down_tile)
    for half in range(2):
        down_out(half, 0).wait()
    rs_start(0)

    def up_tile(t):
        cols = rows_at(t * RA, RA)
        lhs = tokv[:, cols]
        for half in range(2):

            @pl.when(t > 0)
            def _():
                tile_out(half, gwg_h, t).wait()

            wst[:, :, half * F : half * F + F] = (
                tdot(lhs, gu[:, half * F : half * F + F]).astype(BF).reshape(B, R, F)
            )
            tile_out(half, gwg_h, t).start()

        @pl.when(t == A // 2)
        def _():
            rs_start(1)

    loop(A, up_tile)
    for half in range(2):
        tile_out(half, gwg_h, 0).wait()
    rs_start(2)
    rs_start(3)
    rs_load(0)
    qv, kv, vv = gml.at[:, 0:C], gml.at[:, C : 2 * C], gml.at[:, 2 * C : 3 * C]
    gv = gml.at[:, 3 * C : 4 * C]
    rot0 = 2 * w
    loads = [
        local(qkv_h, gml.at[:, 0 : 3 * C], lsem.at[7]),
        local(rot_h, gu.at[:, rot0 : rot0 + 2 * C], lsem.at[8]),
        local(tokf, tokv, lsem.at[9]),
    ]
    for cp in loads:
        cp.start()
    dk[...] = jnp.zeros_like(dk)
    dv[...] = jnp.zeros_like(dv)
    gsq[...] = jnp.zeros_like(gsq)
    heads = lax.broadcasted_iota(jnp.int32, (8, C), 0)
    lanes = lax.broadcasted_iota(jnp.int32, (8, C), 1) // DK
    pick = jnp.where(heads == lanes, 1.0, 0.0).astype(BF)
    for cp in loads[:2]:
        cp.wait()
    NY = ny * CF

    def gin_copy(c, hs):
        return remote(
            sc.at[hs * TH : (hs + 1) * TH, 0:NY], rc.at[c, :, hs * NY : (hs + 1) * NY], c_s.at[c, hs],
            c_r.at[c, hs], peer,
        )

    def gin_y(c, k, hs):
        src = slice((hs * (ny - 1) + k - 1) * CF, (hs * (ny - 1) + k) * CF)
        dst = slice(hs * CF, hs * CF + CF)
        return remote(
            sy2.at[c, :, src], ry2.at[k - 1, c, :, dst], yg_s.at[c, k - 1, hs], yg_r.at[c, k - 1, hs],
            ypeer(k, core),
        )

    n128 = CF // 128

    def gin_take(c):
        for hs in range(2):
            gin_copy(c, hs).wait()
            for k in range(ny):
                for q in range(n128):
                    col = hs * NY + k * CF + q * 128
                    t = acc[k * n128 + q, hs * TH : (hs + 1) * TH, :] + rc[c, :, col : col + 128].astype(F32)
                    if k == 0:
                        dk[rows_at(c * TB + hs * TH, TH), q * 128 : q * 128 + 128] = t
                    else:
                        col = (hs * (ny - 1) + k - 1) * CF + q * 128
                        sy2[c, :, col : col + 128] = t.astype(BF)
            for k in range(1, ny):
                gin_y(c, k, hs).start()

    def out_tiles():
        def o_tile(t):
            cols = rows_at(t * RA, RA)
            wst[:, :, 0:C] = tdot(gba[:, cols], attn[...]).astype(BF).reshape(B, R, C)
            cp = local(wst.at[:, :, 0:C], gqo_h.at[:, rows_at(t * R, R), 3 * C : 4 * C], lsem.at[1])
            cp.start()
            cp.wait()

        loop(A, o_tile)

    def kept_rows(c):
        return local(tokf.at[rows_at(c * TB + core * TH, TH)], gst, lsem.at[6])

    def branch_rows(c):
        base = c * TB + core * TH
        landed(2, c, sy2, ry3)
        kept_rows(c).wait()

        def rows(t):
            r = rows_at(t * RT, RT)
            g = rows_at(base + t * RT, RT)
            aa = alv[0:1, :]
            br = total(c, r, sy1, ry1)
            x = gst[r, :].astype(F32)
            ra = mean_sq(br, D)
            ha = br * ra
            diff = ha - x
            mix = x + aa * diff
            r1 = mean_sq(mix, D)
            hid = mix * r1
            gh = ghid[c, r, :].astype(F32) + total(c, r, sy2, ry3)
            gm = r1 * (gh - hid * (jnp.sum(gh * hid, axis=1, keepdims=True) * (1.0 / D)))
            gacc[0:8, :] += fold(gm * diff)
            gt = aa * gm
            ghid[c, r, :] = (gm - gt).astype(BF)
            gb = ra * (gt - ha * (jnp.sum(gt * ha, axis=1, keepdims=True) * (1.0 / D)))
            gba[g, :] = gb.astype(BF)

        rows_then_share(2, c, rows, gba)

        @pl.when(c > 0)
        def _():
            kept_rows(jnp.maximum(c - 1, 0)).start()

    branch_rows(nc - 1)
    rs_add(0)

    def attn_grad_chunk(i):
        c = nc - 1 - i
        shared(2, c, gba)

        @pl.when(c > 0)
        def _():
            branch_rows(jnp.maximum(c - 1, 0))

        r = rows_at(c * TB, TB)
        g = nn(gba[r, :], wqov[:, 3 * C : 4 * C]).astype(BF)
        gv[r, :] = g
        prod = g.astype(F32) * attn[r, :].astype(F32)
        ph = prod.astype(BF)
        dl[:, r] = nt(pick, ph) + nt(pick, (prod - ph.astype(F32)).astype(BF))
        attn_bwd_block(c, TB, H, qv, kv, vv, gv, ll, dl, off_bias, dq, dk, dv)

        @pl.when(i == 0)
        def _():
            rs_load(1)
            rs_start(4)

        @pl.when(i == 1)
        def _():
            rs_add(2)
            rs_load(3)
            end_load(0)

        @pl.when(i == 2)
        def _():
            rs_load(4)
            end_load(1)

        @pl.when(i == nc - 1)
        def _():
            rs_load(5)
            end_load(2)
            out_tiles()
            rs_start(8)

        cs, sn = angles_of(r)
        for part in range(2):
            gh = (dq[...] if part == 0 else dk[r, :]) * 8.0
            t = gu[r, rot0 + part * C : rot0 + part * C + C].astype(F32)
            inv = lax.rsqrt(split_dot(t * t, ones) + epsilon)
            un = t * inv
            gsq[...] += fold(gh * un)
            gh = gh * sq[...]
            gr = inv * (gh - un * split_dot(gh * un, ones))
            act[r, part * C : part * C + C] = turn(gr, cs, sn, -1.0).astype(BF)
        act[r, 2 * C : 3 * C] = dv[r, :].astype(BF)

        def product(hsel, k, cc):
            rr = rows_at(c * TB + hsel * TH, TH)
            cols = feat(((y + k) % ny) * 2 + cc)
            t = nt(act[rr, 0 : 3 * C], wqov[cols, 0 : 3 * C])
            if k == 0:
                t = t + jnp.where(hsel == core, 1.0, 0.0) * ghid[c, :, cols].astype(F32)
            return t

        @pl.when(i > 0)
        def _():
            gin_take(jnp.minimum(c + 1, nc - 1))

        for hs in range(2):
            for k in range(ny):
                sc[hs * TH : (hs + 1) * TH, k * CF : (k + 1) * CF] = product(hs, k, mate).astype(BF)
            gin_copy(c, hs).start()
        for hs in range(2):
            for k in range(ny):
                t = product(hs, k, core)
                for q in range(n128):
                    acc[k * n128 + q, hs * TH : (hs + 1) * TH, :] = t[:, q * 128 : q * 128 + 128]

        @pl.when(i == 0)
        def _():
            rs_add(1)
            rs_start(5)
            rs_load(2)

        @pl.when(i == 1)
        def _():
            rs_finish(0)
            rs_add(3)

        @pl.when(i == 2)
        def _():
            rs_finish(1)
            rs_add(4)

        @pl.when(i == nc - 1)
        def _():
            rs_finish(2)
            rs_add(5)
            end_load(3)

    loop(nc, attn_grad_chunk)
    ga_there = remote(gacc.at[:, feat(y * 2 + mate)], gar, m_s.at[0], m_r.at[0], peer)
    ga_there.start()
    loads[2].wait()

    def q_out(half, t):
        src = wst.at[:, :, half * F : half * F + 2 * C]
        return local(src, gqo_h.at[:, rows_at(t * R, R), 0 : 2 * C], lsem.at[1 + half])

    def q_tile(t):
        for half in range(2):
            tt = 2 * t + half

            @pl.when(t > 0)
            def _():
                q_out(half, tt).wait()

            g = tdot(tokv[:, rows_at(tt * RA, RA)], act[:, 0 : 2 * C]).astype(BF)
            wst[:, :, half * F : half * F + 2 * C] = g.reshape(B, R, 2 * C)
            q_out(half, tt).start()

    loop(A // 2, q_tile)
    for half in range(2):
        q_out(half, 0).wait()
    rs_start(6)

    def v_out(half, t):
        src = wst.at[:, :, half * F : half * F + C]
        return local(src, gqo_h.at[:, rows_at(t * R, R), 2 * C : 3 * C], lsem.at[1 + half])

    def v_tile(t):
        for half in range(2):
            tt = 2 * t + half

            @pl.when(t > 0)
            def _():
                v_out(half, tt).wait()

            g = tdot(tokv[:, rows_at(tt * RA, RA)], act[:, 2 * C : 3 * C]).astype(BF)
            wst[:, :, half * F : half * F + C] = g.reshape(B, R, C)
            v_out(half, tt).start()

    loop(A // 2, v_tile)
    for half in range(2):
        v_out(half, 0).wait()
    rs_start(7)
    gin_take(0)
    rs_finish(3)
    rs_load(8)
    ga_there.wait()
    vec[...] = jnp.zeros_like(vec)
    gt = gacc[:, mine] + gar[...]
    vec[0:1, 0:F] = jnp.sum(gsacc[0:8, :], axis=0, keepdims=True)
    vec[1:2, 0:F] = jnp.sum(gsacc[8:16, :], axis=0, keepdims=True)
    vec[2:3, 0:CF] = jnp.sum(gt[0:8], axis=0, keepdims=True)
    vec[3:4, 0:CF] = jnp.sum(gt[8:16], axis=0, keepdims=True)
    vec[4:5, 0:C] = jnp.sum(gsq[...], axis=0, keepdims=True)
    vx = [remote(vec, rv1.at[k - 1], m_s.at[k], m_r.at[k], xpeer(k)) for k in range(1, B)]
    for cp in vx:
        cp.start()
    rs_add(8)
    end_load(4)
    for cp in vx:
        cp.wait()
    t = vec[...]
    for k in range(B - 1):
        t = t + rv1[k]
    vec[...] = t
    vz = [
        remote(vec, rv2.at[k - 1], m_s.at[B - 1 + k], m_r.at[B - 1 + k], zpeer(k)) for k in range(1, A)
    ]
    for cp in vz:
        cp.start()

    rs_finish(4)
    end_load(5)

    def gin_end(i):
        c = nc - 1 - i
        for hs in range(2):
            rr = rows_at(c * TB + hs * TH, TH)
            for k in range(1, ny):
                gin_y(c, k, hs).wait()
                dk[rr, :] += ry2[k - 1, c, :, hs * CF : hs * CF + CF].astype(F32)

    loop(nc, gin_end)
    ends = [local(dk, gin_o, lsem.at[10])]
    ends[-1].start()
    rs_load(6)
    rs_add(6)
    rs_finish(5)
    rs_load(7)
    rs_add(7)
    end_load(8)
    for cp in vz:
        cp.wait()
    t = vec[...]
    for k in range(A - 1):
        t = t + rv2[k]
    vec[...] = t
    ends.append(local(vec, vec_o, lsem.at[11]))
    ends[-1].start()
    for p in range(5):
        w_sent(p, p != 4)
    rs_finish(8)
    end_load(6)
    rs_finish(6)
    end_load(7)
    rs_finish(7)
    for cp in ends:
        cp.wait()


def run_layer(z, live, tokens, gout, wqo, wg, wd, alpha, table, sq, sml):
    T, C, CF, F, D, H = z.T, z.C, z.CF, z.F, z.D, z.H
    nc, TB, TH, R, A, B, ny, mp = z.nc, z.TB, z.TH, z.R, z.A, z.B, z.ny, z.mp
    S = jax.ShapeDtypeStruct
    hbm = pl.BlockSpec(memory_space=pltpu.HBM)
    vm = pl.BlockSpec(memory_space=pltpu.VMEM)
    W = max(F, CF, C)
    AR = A * R
    outs = [
        S((T, CF), BF), S((T, CF), F32), S((R, 3 * C), F32), S((R, C), F32), S((R, 2 * F), F32), S((R, F), F32),
        S((8, W), F32),
        S((T, 3 * C), BF), S((T, 2 * C), BF), S((T, D), BF), S((nc, TH, D), BF),
    ]
    widths = (F, 2 * F, 4 * C)
    outs += [S((B, AR, n), BF) for n in widths]
    outs += [S((max(B - 1, 1), AR, n), BF) for n in widths]
    outs += [S((max(A - 1, 1), R, n), BF) for n in widths]
    V = pltpu.VMEM
    scratch = [
        V((T, D), BF), V((D, 4 * C), BF), V((D, 2 * F), BF), V((D, F), BF),
        V((T, D), BF), V((T, F), BF), V((T, 2 * F), BF), V((T, D), BF),
        V((T, C), BF), V((8, T), F32), V((8, T), F32), V((max(H, ny * CF // 128), TB, 128), F32),
        V((T, C), F32), V((T, C), F32), V((TB, C), F32), V((R, F // 2), F32),
    ]
    for _ in range(2):
        scratch += [V((nc, TH, D), BF), V((ny - 1, nc, TH, D), BF)]
    scratch += [
        V((ny - 1, nc, TH, D), BF), V((nc, TH, D), BF), V((TB, D), BF), V((nc, TH, D), BF), V((TH, D), BF), V((TH, D), BF),
        V((B, R, 2 * F), BF), V((8, D), F32), V((16, D), F32), V((16, F), F32), V((8, C), F32), V((16, CF), F32),
        V((8, W), F32), V((max(B - 1, 1), 8, W), F32), V((max(A - 1, 1), 8, W), F32),
    ]
    sem = pltpu.SemaphoreType.DMA
    for shape in (
        (nc, 2 * ny - 1), (5, B, 2, max(A - 1, 1)), (5, A, max(B - 1, 1)), (mp - 1,), (mp - 1,), (3, nc, 2),
        (3, nc, ny - 1, 2), (3, nc, 2), (nc,), (9, max(B - 1, 1)), (9, max(A - 1, 1)), (nc, 2), (nc, ny - 1, 2),
        (A + B - 1,),
    ):
        scratch += [sem(shape), sem(shape)]
    scratch += [sem((21,)), sem((4, A + B))]
    return pl.pallas_call(
        functools.partial(layer, z),
        out_shape=outs,
        in_specs=[pl.BlockSpec(memory_space=pltpu.SMEM)] + [hbm] * 6 + [vm] * 3,
        out_specs=[hbm] * len(outs),
        scratch_shapes=scratch,
        compiler_params=pltpu.CompilerParams(
            collective_id=0, has_side_effects=True, vmem_limit_bytes=64 * 2**20 - 2**19
        ),
        name="layer",
    )(live, tokens, gout.reshape(nc, 2, TH, CF), wqo, wg, wd, alpha, table, sq, sml)


def tables(T):
    half = DK // 2
    frequency = np.float32(theta_base) ** (np.float32(-2.0 / DK) * np.arange(half, dtype=np.float32))
    grid = np.arange(T, dtype=np.float32)[:, None] * frequency[None, :].astype(np.float32)
    cos, sin = np.cos(grid, dtype=np.float32), np.sin(grid, dtype=np.float32)
    return np.concatenate([cos, cos, sin, sin], axis=1)


def on_device(
    sizes,
    tokens,
    w_qkv,
    w_out,
    w_gate_up,
    w_down,
    s_qk,
    alpha_attn,
    alpha_mlp,
    s_mlp,
    doc_lengths,
    grad_out,
):
    T, CF = tokens.shape
    H = s_qk.shape[1]
    C = H * DK
    F = w_down.shape[1]
    z = Sizes(sizes, T, C, CF, F, doc_lengths.shape[1])
    D, R = z.D, z.R
    table = jnp.asarray(tables(T))
    scale = s_qk.T.reshape(1, C)
    sml = s_mlp.transpose(1, 2, 0).reshape(2, F)
    alpha = jnp.pad(
        jnp.stack([alpha_attn.T.reshape(-1), alpha_mlp.T.reshape(-1)]), ((0, 6), (0, 0))
    )
    whole = doc_lengths[0, 0] == T
    live = whole.astype(F32).reshape(1)
    (out, grad_in, gw_qkv, gw_out, gw_gu, gw_down, vec) = run_layer(
        z, live, tokens, grad_out, jnp.concatenate([w_qkv.reshape(R, 3 * C), w_out], axis=1),
        w_gate_up.reshape(R, 2 * F), w_down, alpha, table, scale, sml,
    )[:7]
    d, m = place()

    def channel_rows(v, per_head):
        n = per_head // z.dp
        return lax.dynamic_slice_in_dim(v.reshape(H, per_head).T, d * n, n, 0)

    gs = jnp.stack([channel_rows(vec[i, 0:F], F // H) for i in range(2)], axis=1)
    return (
        out,
        grad_in,
        gw_qkv.reshape(R, 3, C),
        gw_out,
        gw_gu.reshape(R, 2, F),
        gw_down,
        channel_rows(vec[4, 0:C], DK),
        channel_rows(vec[2, 0:CF], DK),
        channel_rows(vec[3, 0:CF], DK),
        gs,
    )


def solution(mesh):
    placed = (
        P("dp", "mp"),
        P("dp", None, "mp"),
        P("dp", "mp"),
        P("dp", None, "mp"),
        P("dp", "mp"),
        P(None, "mp"),
        P(None, "mp"),
        P(None, "mp"),
        P(None, None, "mp"),
        P("dp", None),
        P("dp", "mp"),
    )
    return jax.shard_map(
        functools.partial(on_device, dict(mesh.shape)),
        mesh=mesh,
        in_specs=placed,
        out_specs=(
            P("dp", "mp"),
            P("dp", "mp"),
            P("dp", None, "mp"),
            P("dp", "mp"),
            P("dp", None, "mp"),
            P("dp", "mp"),
            P("dp", "mp"),
            P("dp", "mp"),
            P("dp", "mp"),
            P("dp", None, "mp"),
        ),
        check_vma=False,
    )
```

```python
import functools
import math

import jax
import jax.numpy as jnp
import numpy as np
from jax import lax
from jax.experimental import pallas as pl
from jax.experimental.pallas import tpu as pltpu
from jax.sharding import PartitionSpec as P

DK = 64
epsilon = 1e-06
theta_base = 10000.0


LC=math.sqrt(DK)*math.log2(math.e)
NEG=-1e30
def nt(a,b): return lax.dot_general(a,b,(((1,),(1,)),((),())),preferred_element_type=jnp.float32)
def nn(a,b): return jnp.dot(a,b,preferred_element_type=jnp.float32)
def head_mask(x,h):
    lane=lax.broadcasted_iota(jnp.int32,x.shape,1)
    return jnp.where((lane//DK)==(h%2), x, jnp.zeros_like(x))
def attn_fwd_block(i, TB, H, ref, C, live, acc):
    hb=TB//2
    qs=pl.ds(pl.multiple_of(i*TB,TB),TB)
    def vx(h,ks):
        v=ref[ks,pl.ds(2*C+(h//2)*128,128)]
        lane=lax.broadcasted_iota(jnp.int32,v.shape,1)
        return jnp.where((lane//DK)==(h%2),v,jnp.ones_like(v))
    def tile(h,qsl,ks,tri):
        p2=pl.ds((h//2)*128,128)
        x=nt(ref[qsl,p2],head_mask(ref[ks,pl.ds(C+(h//2)*128,128)],h))
        if tri:
            r=lax.broadcasted_iota(jnp.int32,x.shape,0); c=lax.broadcasted_iota(jnp.int32,x.shape,1)
            x=jnp.where(c<=r,x,NEG)
        p=jnp.exp2(x*LC).astype(jnp.bfloat16)
        return nn(p,vx(h,ks))
    k0=pl.ds(pl.multiple_of(i*TB,hb),hb); k1=pl.ds(pl.multiple_of(i*TB+hb,hb),hb)
    for h in range(H):
        a0=tile(h,qs,k0,True)
        a1=tile(h,k1,k1,True)
        acc[h,0:hb]=a0[0:hb]; acc[h,hb:TB]=a0[hb:TB]+a1
    def body(j,_):
        ks=pl.ds(pl.multiple_of(j*TB,TB),TB)
        for h in range(H):
            acc[h]+=live*tile(h,qs,ks,False)
        return 0
    lax.fori_loop(0,i,body,0)
def tdot(a,b): return lax.dot_general(a,b,(((0,),(0,)),((),())),preferred_element_type=jnp.float32)
def attn_bwd_block(i, TB, H, q_ref, k_ref, v_ref, g_ref, ll_ref, dl_ref, ob, dq, dk, dv, between):
    qs=pl.ds(pl.multiple_of(i*TB,TB),TB); hb=TB//2
    qz=[head_mask(q_ref[qs,pl.ds((h//2)*128,128)],h) for h in range(H)]
    gz=[head_mask(g_ref[qs,pl.ds((h//2)*128,128)],h) for h in range(H)]
    lr=[ll_ref[pl.ds(h,1),qs] for h in range(H)]
    dr=[dl_ref[pl.ds(h,1),qs] for h in range(H)]
    def tile(h,ks,qv,gv,lb,dd,tri):
        p2=pl.ds((h//2)*128,128)
        x=nt(k_ref[ks,p2],qv)*LC-lb
        dp=nt(v_ref[ks,p2],gv)
        if tri:
            r=lax.broadcasted_iota(jnp.int32,x.shape,0); c=lax.broadcasted_iota(jnp.int32,x.shape,1)
            x=jnp.where(r<=c,x,NEG)
        p=jnp.exp2(x)
        ds=(p*(dp-dd)).astype(jnp.bfloat16)
        dvp=nn(p.astype(jnp.bfloat16),gv)
        dkp=nn(ds,qv)
        dqp=tdot(ds,head_mask(k_ref[ks,p2],h))
        return dqp,dkp,dvp
    k0=pl.ds(pl.multiple_of(i*TB,hb),hb); k1=pl.ds(pl.multiple_of(i*TB+hb,hb),hb)
    for pr in range((H+1)//2):
        p2=pl.ds(pr*128,128)
        dk0=dv0=dk1=dv1=0; q0=q1=0
        for h in range(2*pr,min(2*pr+2,H)):
            a,b,c=tile(h,k0,qz[h],gz[h],lr[h],dr[h],True)
            a1,b1,c1=tile(h,k1,qz[h][hb:],gz[h][hb:],lr[h][:,hb:],dr[h][:,hb:],True)
            q0+=a[0:hb]; q1+=a[hb:]+a1
            dk0+=b; dv0+=c; dk1+=b1; dv1+=c1
        dq[0:hb,p2]=q0; dq[hb:TB,p2]=q1
        dk[k0,p2]+=dk0; dv[k0,p2]+=dv0; dk[k1,p2]+=dk1; dv[k1,p2]+=dv1
    between()
    lo=[l-ob for l in lr]
    def body(j,_):
        ks=pl.ds(pl.multiple_of(j*TB,TB),TB)
        for pr in range((H+1)//2):
            p2=pl.ds(pr*128,128)
            dka=dva=dqa=0
            for h in range(2*pr,min(2*pr+2,H)):
                a,b,c=tile(h,ks,qz[h],gz[h],lo[h],dr[h],False)
                dqa+=a; dka+=b; dva+=c
            dq[:,p2]+=dqa
            dk[ks,p2]+=dka; dv[ks,p2]+=dva
        return 0
    lax.fori_loop(0,i,body,0)


MESH = pl.DeviceIdType.MESH
F32, BF = jnp.float32, jnp.bfloat16


class Sizes:
    def __init__(self, mesh_shape, T, C, CF, F, pieces):
        self.mp, self.dp = mesh_shape["mp"], mesh_shape["dp"]
        self.ny = self.mp // 2
        self.A = 4 if self.dp % 4 == 0 else 1
        self.B = self.dp // self.A
        self.T, self.C, self.CF, self.F = T, C, CF, F
        self.D = CF * self.mp
        self.H = C // DK
        self.nc = pieces
        self.TB = T // pieces
        self.TH = self.TB // 2
        self.R = self.D // self.dp


def place():
    return lax.axis_index("dp"), lax.axis_index("mp")


def remote(src, dst, ss, rs, dev):
    return pltpu.make_async_remote_copy(
        src, dst, send_sem=ss, recv_sem=rs, device_id=dev, device_id_type=MESH
    )


def local(src, dst, sem):
    return pltpu.make_async_copy(src, dst, sem)


def rows_at(start, size):
    return pl.ds(pl.multiple_of(start, size), size)


def loop(n, fn):
    def body(i, carry):
        fn(i)
        return carry

    lax.fori_loop(0, n, body, 0)


def fold(x):
    return jnp.sum(x.reshape(x.shape[0] // 8, 8, x.shape[1]), axis=0)


def mean_sq(x, D):
    return lax.rsqrt(jnp.sum(x * x, axis=1, keepdims=True) * (1.0 / D) + epsilon)


def split_dot(x, ones):
    hi = x.astype(BF)
    return nn(hi, ones) + nn((x - hi.astype(F32)).astype(BF), ones)


def head_ones(width):
    i = lax.broadcasted_iota(jnp.int32, (width, width), 0) // DK
    j = lax.broadcasted_iota(jnp.int32, (width, width), 1) // DK
    return jnp.where(i == j, 1.0, 0.0).astype(BF)


def turn(x, cosine, sine, sign):
    lane = lax.broadcasted_iota(jnp.int32, x.shape, 1)
    first = (lane % DK) < DK // 2
    other = jnp.where(first, -pltpu.roll(x, x.shape[1] - DK // 2, 1), pltpu.roll(x, DK // 2, 1))
    return x * cosine + sign * other * sine


def layer(
    z,
    live_ref, tokens, gout, wqo, wg, wd, alpha, table, sq, sml,
    out, gin_o, owq, owo, owg, owd, vec_o,
    qkv_h, rot_h, tokf, goh, gwd_h, gwg_h, gqo_h, r1d_h, r1g_h, r1q_h, r2d_h, r2g_h, r2q_h,
    tokv, wqov, wgv, wdv, gml, act, gu, gba, attn, ll, dl, acc, dk, dv, dq, fstage,
    sy1, ry1, sy2, ry2, ry3, rc, sc, ghid, gst, fst, wst, alv, gacc, gsacc, gsq, gar, vec, rv1, rv2,
    tok_s, tok_r, w_s, w_r, x_s, x_r, al_s, al_r, go_s, go_r, ex_s, ex_r, y_s, y_r, hc_s, hc_r, out_s, out_r,
    p_s, p_r, q_s, q_r, c_s, c_r, yg_s, yg_r, m_s, m_r, lsem, rsem,
):
    T, C, CF, F, D, H = z.T, z.C, z.CF, z.F, z.D, z.H
    nc, TB, TH, R, A, B, ny, mp = z.nc, z.TB, z.TH, z.R, z.A, z.B, z.ny, z.mp
    d, m = place()
    a, b = d // B, d % B
    y, core = m // 2, m % 2
    mate = 1 - core
    peer = (d, y * 2 + mate)

    def ypeer(k, cc):
        return (d, ((y + k) % ny) * 2 + cc)

    zpeer = lambda k: (((a + k) % A) * B + b, m)
    xpeer = lambda k: (a * B + (b + k) % B, m)
    others = [peer] + [ypeer(k, cc) for k in range(1, ny) for cc in (core, mate)]
    everyone = others + [zpeer(k) for k in range(1, A)] + [xpeer(k) for k in range(1, B)]
    bar = pltpu.get_barrier_semaphore()
    for dev in everyone:
        pl.semaphore_signal(bar, 1, device_id=dev, device_id_type=MESH)
    pl.semaphore_wait(bar, len(everyone))

    live = live_ref[0]
    off_bias = jnp.where(live > 0.5, 0.0, NEG)
    feat = lambda mm: pl.ds(pl.multiple_of(mm * CF, CF), CF)
    mine = feat(m)


    def tok_own(c, i, dev):
        r = rows_at(c * TB, TB)
        return remote(tokens.at[r], tokv.at[r, mine], tok_s.at[c, i], tok_r.at[c, i], dev)

    def tok_got(c, i, mm):
        r = rows_at(c * TB, TB)
        return remote(tokv.at[r, feat(mm)], tokv.at[r, feat(mm)], tok_s.at[c, i], tok_r.at[c, i], peer)

    def start_tok(i):
        c = nc - 1 - i
        for k in range(1, ny):
            tok_own(c, k, ypeer(k, core)).start()
        tok_own(c, 0, peer).start()

    lo, hi = slice(0, F), slice(F, 2 * F)
    dlo, dhi = slice(0, F // 2), slice(F // 2, F)
    weights = [
        (wqo.at[:, 0 : 2 * C], wqov.at[:, 0 : 2 * C]),
        (wg.at[:, lo], wgv.at[:, lo]),
        (wg.at[:, hi], wgv.at[:, hi]),
        (wd.at[:, dlo], wdv.at[:, dlo]),
        (wd.at[:, dhi], wdv.at[:, dhi]),
        (wqo.at[:, 2 * C : 4 * C], wqov.at[:, 2 * C : 4 * C]),
    ]

    def shard(aa, bb):
        return rows_at((aa * B + bb) * R, R)

    def column(st):
        return (b - st + B) % B

    def z_moves(w, st, h):
        src, dst = weights[w]
        moves = []
        for way, step in ((0, 1), (1, -1)):
            aa = a - step * (h - 1)
            ok = (a + step >= 0) & (a + step < A) & (aa >= 0) & (aa < A)
            moves.append((way, step, jnp.clip(aa, 0, A - 1), ok))
        return src, dst, moves

    def z_copy(w, st, h, way, step, aa):
        src, dst = weights[w]
        r = shard(aa, column(st))
        source = src if (h == 1 and st == 0) else dst.at[r]
        to = jnp.clip(a + step, 0, A - 1) * B + b
        return remote(source, dst.at[r], w_s.at[w, st, way, h - 1], w_r.at[w, st, way, h - 1], (to, m))

    def z_hop(w, st, h):
        if h >= A:
            return
        for way, step, aa, ok in z_moves(w, st, h)[2]:

            @pl.when(ok)
            def _():
                z_copy(w, st, h, way, step, aa).start()

    def z_sent(w, st, h):
        for way, step, aa, ok in z_moves(w, st, h)[2]:

            @pl.when(ok)
            def _():
                z_copy(w, st, h, way, step, aa).wait_send()

    def z_wait(w, st, h, forward=False):
        if h >= A:
            return
        for way, step in ((0, 1), (1, -1)):
            aa = a - step * h

            @pl.when((aa >= 0) & (aa < A))
            def _():
                z_copy(w, st, h, way, step, jnp.clip(aa, 0, A - 1)).wait_recv()
                if forward:
                    x_send(w, aa)

    def x_copy(w, aa, k, own=False):
        src, dst = weights[w]
        r = shard(aa, b)
        return remote(
            src if own else dst.at[r], dst.at[r], x_s.at[w, aa, k - 1], x_r.at[w, aa, k - 1], xpeer(k)
        )

    def x_send(w, aa, own=False):
        for k in range(1, B):
            x_copy(w, aa, k, own).start()

    def x_wait(w, aa):
        src, dst = weights[w]
        for k in range(1, B):
            r = shard(aa, (b - k + B) % B)
            remote(src, dst.at[r], x_s.at[w, aa, k - 1], x_r.at[w, aa, k - 1], xpeer(k)).wait_recv()

    def w_local(w):
        src, dst = weights[w]
        return local(src, dst.at[shard(a, b)], lsem.at[16 + w])

    def w_start(w):
        z_hop(w, 0, 1)
        x_send(w, a, own=True)
        w_local(w).start()

    def w_next(w, st, h, forward=True):
        z_wait(w, st, h, forward)
        z_hop(w, st, h + 1)

    def w_ready(w):
        for aa in range(A):
            x_wait(w, aa)
        w_local(w).wait()

    def w_sent(w, forward):
        for st in range(1 if forward else B):
            for h in range(1, A):
                z_sent(w, st, h)
        for k in range(1, B):
            for aa in range(A) if forward else [a]:
                x_copy(w, aa, k).wait_send()

    w_start(0)
    w_start(5)
    loop(nc, start_tok)
    x_send(4, a, own=True)
    w_local(4).start()
    tok_local = local(tokens, tokv.at[:, mine], lsem.at[4])
    tok_local.start()
    al_local = local(alpha, alv.at[:, mine], lsem.at[5])
    al_local.start()
    al_copies = [
        remote(alpha, alv.at[:, mine], al_s.at[i], al_r.at[i], dev) for i, dev in enumerate(others)
    ]
    for cp in al_copies:
        cp.start()

    def pass_tok(i):
        c = nc - 1 - i
        for k in range(1, ny):
            src = ((y - k + ny) % ny) * 2 + core
            tok_got(c, k, src).wait_recv()
            tok_got(c, ny + k - 1, src).start()

    w_next(0, 0, 1)
    w_next(5, 0, 1)
    w_next(0, 0, 2)
    pass_tok(0)
    w_next(5, 0, 2)
    w_next(0, 0, 3)
    pass_tok(1)
    w_next(5, 0, 3)
    w_start(1)
    w_start(2)
    loop(nc - 2, lambda i: pass_tok(i + 2))

    go4 = gout

    def go_copy(i, dev, cc):
        return remote(go4.at[:, cc], goh.at[:, :, mine], go_s.at[i], go_r.at[i], dev)

    go_copies = [go_copy(0, peer, mate)]
    i = 1
    for k in range(1, ny):
        for cc in (core, mate):
            go_copies.append(go_copy(i, ypeer(k, cc), cc))
            i += 1
    go_local = local(go4.at[:, core], goh.at[:, :, mine], lsem.at[6])
    go_local.start()
    for cp in go_copies:
        cp.start()

    def end_tok(i):
        c = nc - 1 - i
        tok_got(c, 0, y * 2 + mate).wait_recv()
        for k in range(1, ny):
            src = ((y - k + ny) % ny) * 2 + mate
            tok_got(c, ny + k - 1, src).wait_recv()

    loop(nc, end_tok)

    def tok_sent(i):
        c = nc - 1 - i
        tok_own(c, 0, peer).wait_send()
        for k in range(1, ny):
            tok_own(c, k, ypeer(k, core)).wait_send()
            tok_got(c, ny + k - 1, ((y - k + ny) % ny) * 2 + core).wait_send()

    loop(nc, tok_sent)
    tok_local.wait()
    w_ready(0)
    w_ready(5)

    ones = head_ones(C)
    qkvv = gml

    def angles_of(r):
        t = jnp.where(live > 0.5, table[r, :], table[0:TB, :])
        u = pltpu.roll(t, DK, 1)
        first = lax.broadcasted_iota(jnp.int32, t.shape, 1) < DK
        cs, sn = jnp.where(first, t, u), jnp.where(first, u, t)
        return jnp.concatenate([cs] * (C // 128), axis=1), jnp.concatenate([sn] * (C // 128), axis=1)

    def project_rows(i):
        r = rows_at(i * TB, TB)
        x = tokv[r, :]
        cs, sn = angles_of(r)
        for part in range(2):
            cols = slice(part * C, part * C + C)
            t = turn(nn(x, wqov[:, cols]), cs, sn, 1.0)
            act[r, cols] = t.astype(BF)
            inv = lax.rsqrt(split_dot(t * t, ones) + epsilon)
            qkvv[r, cols] = (t * inv * sq[...]).astype(BF)
        qkvv[r, 2 * C : 3 * C] = nn(x, wqov[:, 2 * C : 3 * C]).astype(BF)

        @pl.when(i == 1)
        def _():
            w_next(1, 0, 1)
            w_next(2, 0, 1)

    loop(nc, project_rows)
    save_tok = local(tokv, tokf, lsem.at[4])
    save_tok.start()
    saves = [
        local(qkvv.at[:, 0 : 3 * C], qkv_h, lsem.at[7]),
        local(act.at[:, 0 : 2 * C], rot_h, lsem.at[8]),
    ]
    for cp in saves:
        cp.start()

    RT = 64
    NG = 2
    GW = D // NG

    def y_copy(e, c, k, n, sy, ry):
        cols = slice(n * GW, n * GW + GW)
        return remote(
            sy.at[c, :, cols], ry.at[k - 1, c, :, cols], y_s.at[e, c, k - 1, n], y_r.at[e, c, k - 1, n],
            ypeer(k, core),
        )

    def exchange(e, c, part, sy, ry):
        r = rows_at(c * TB, TB)
        theirs, ours = rows_at(mate * TH, TH), rows_at(core * TH, TH)
        copies = []
        for n in range(NG):
            cols = slice(n * GW, n * GW + GW)
            sc[:, cols] = part(r, cols).astype(BF)
            cp = remote(
                sc.at[theirs, cols], rc.at[c, :, cols], ex_s.at[e, c, n], ex_r.at[e, c, n], peer
            )
            cp.start()
            copies.append(cp)
        for n in range(NG):
            cols = slice(n * GW, n * GW + GW)
            copies[n].wait()
            sy[c, :, cols] = (sc[ours, cols].astype(F32) + rc[c, :, cols].astype(F32)).astype(BF)
            for k in range(1, ny):
                y_copy(e, c, k, n, sy, ry).start()

    def landed(e, c, sy, ry):
        for k in range(1, ny):
            for n in range(NG):
                y_copy(e, c, k, n, sy, ry).wait()

    def total(c, r, sy, ry):
        t = sy[c, r, :].astype(F32)
        for k in range(ny - 1):
            t = t + ry[k, c, r, :].astype(F32)
        return t

    NS = 2
    SH = TH // NS

    def share(e, c, n, buf):
        r = rows_at(c * TB + core * TH + n * SH, SH)
        return remote(buf.at[r], buf.at[r], hc_s.at[e, c, n], hc_r.at[e, c, n], peer)

    def rows_then_share(e, c, rows, buf):
        for n in range(NS):
            loop(SH // RT, lambda t: rows(n * (SH // RT) + t))
            share(e, c, n, buf).start()

    def shared(e, c, buf):
        for n in range(NS):
            share(e, c, n, buf).wait()

    def attend_chunk(i):
        c = nc - 1 - i
        attn_fwd_block(c, TB, H, qkvv, C, live, acc)
        r = rows_at(c * TB, TB)
        for pr in range(C // 128):
            both = []
            for h in (2 * pr, 2 * pr + 1):
                t = acc[h]
                both.append(t / pltpu.roll(t, DK, 1))
                row = DK if h % 2 == 0 else 0
                ll[pl.ds(h, 1), r] = jnp.log2(t).T[row : row + 1]
            lane = lax.broadcasted_iota(jnp.int32, (TB, 128), 1)
            attn[r, pr * 128 : pr * 128 + 128] = jnp.where(lane < DK, both[0], both[1]).astype(BF)

        def part(rr, cols):
            return nt(attn[rr, :], wqov[cols, 3 * C : 4 * C])

        @pl.when(i == 0)
        def _():
            save_tok.wait()

        exchange(0, c, part, sy1, ry1)

        @pl.when(i == 0)
        def _():
            w_next(1, 0, 2)
            w_next(2, 0, 2)
            w_start(3)
            z_hop(4, 0, 1)
            x_wait(4, a)
            for st in range(1, B):
                z_hop(4, st, 1)

        @pl.when(i == 2)
        def _():
            w_next(1, 0, 3)
            w_next(2, 0, 3)

        @pl.when(i == 3)
        def _():
            w_next(3, 0, 1)
            for st in range(B):
                w_next(4, st, 1, False)

    ll[...] = jnp.zeros_like(ll)
    loop(nc, attend_chunk)
    for cp in saves:
        cp.wait()
    al_local.wait()
    for cp in al_copies:
        cp.wait()
    w_ready(1)
    w_ready(2)

    gacc[...] = jnp.zeros_like(gacc)
    gsacc[...] = jnp.zeros_like(gsacc)

    def feed_chunk(i):
        c = nc - 1 - i
        landed(0, c, sy1, ry1)
        base = c * TB + core * TH

        def rows(t):
            r = rows_at(t * RT, RT)
            g = rows_at(base + t * RT, RT)
            br = total(c, r, sy1, ry1)
            xb = tokv[g, :]
            x = xb.astype(F32)
            ha = br * mean_sq(br, D)
            mix = x + alv[0:1, :] * (ha - x)
            tokv[g, :] = (mix * mean_sq(mix, D)).astype(BF)

        rows_then_share(0, c, rows, tokv)
        shared(0, c, tokv)
        r = rows_at(c * TB, TB)

        def units(n):
            cu, cv = rows_at(n * 256, 256), rows_at(F + n * 256, 256)
            x = tokv[r, :]
            u = nn(x, wgv[:, cu])
            v = nn(x, wgv[:, cv])
            gu[r, cu] = u.astype(BF)
            gu[r, cv] = v.astype(BF)
            us = u * sml[0:1, cu]
            vs = v * sml[1:2, cu]
            act[r, cu] = (us * vs * jax.nn.sigmoid(vs)).astype(BF)

        loop(F // 256, units)

        @pl.when(i == 0)
        def _():
            w_next(3, 0, 2)
            for st in range(B):
                w_next(4, st, 2, False)

        @pl.when(i == 1)
        def _():
            w_next(3, 0, 3)
            for st in range(B):
                w_next(4, st, 3, False)
            w_ready(3)
            w_local(4).wait()

        @pl.when(i > 0)
        def _():
            down_chunk(i - 1)

    def down_chunk(i):
        c = nc - 1 - i
        exchange(1, c, lambda rr, cols: nt(act[rr, :], wdv[cols, :]), sy2, ry2)

    loop(nc, feed_chunk)
    down_chunk(nc - 1)
    go_local.wait()
    for cp in go_copies:
        cp.wait()

    def grad_rows(c):
        return local(goh.at[c], gst, lsem.at[12])

    grad_rows(nc - 1).start()

    def back_chunk(i):
        c = nc - 1 - i
        landed(1, c, sy2, ry2)
        grad_rows(c).wait()
        base = c * TB + core * TH

        def rows(t):
            r = rows_at(t * RT, RT)
            g = rows_at(base + t * RT, RT)
            am = alv[1:2, :]
            bm = total(c, r, sy2, ry2)
            h = tokv[g, :].astype(F32)
            rm = mean_sq(bm, D)
            hm = bm * rm
            diff = hm - h
            mix = h + am * diff
            r2 = mean_sq(mix, D)
            fin = mix * r2
            fst[r, :] = fin.astype(BF)
            go = gst[r, :].astype(F32)
            gm = r2 * (go - fin * (jnp.sum(go * fin, axis=1, keepdims=True) * (1.0 / D)))
            gacc[8:16, :] += fold(gm * diff)
            gh = am * gm
            ghid[c, r, :] = (gm - gh).astype(BF)
            gb = rm * (gh - hm * (jnp.sum(gh * hm, axis=1, keepdims=True) * (1.0 / D)))
            gml[g, :] = gb.astype(BF)

        rows_then_share(1, c, rows, gml)

        @pl.when(c > 0)
        def _():
            grad_rows(jnp.maximum(c - 1, 0)).start()

        og = rows_at(base, TH)
        o_here = local(fst.at[:, mine], out.at[og], lsem.at[6])
        o_here.start()
        o_there = remote(
            fst.at[:, feat(y * 2 + mate)], out.at[og], out_s.at[c], out_r.at[c], peer
        )
        o_there.start()
        shared(1, c, gml)
        r = rows_at(c * TB, TB)

        def units(n):
            cu, cv = rows_at(n * 256, 256), rows_at(F + n * 256, 256)
            ga = nn(gml[r, :], wdv[:, cu])
            u = gu[r, cu].astype(F32)
            v = gu[r, cv].astype(F32)
            su, sv = sml[0:1, cu], sml[1:2, cu]
            us, vs = u * su, v * sv
            sg = jax.nn.sigmoid(vs)
            si = vs * sg
            g_u = ga * si
            g_v = ga * us * (sg + si - si * sg)
            gsacc[0:8, cu] += fold(g_u * u)
            gsacc[8:16, cu] += fold(g_v * v)
            gu[r, cu] = (g_u * su).astype(BF)
            gu[r, cv] = (g_v * sv).astype(BF)

        loop(F // 256, units)
        exchange(2, c, lambda rr, cols: nt(gu[rr, :], wgv[cols, :]), sy2, ry3)
        o_here.wait()
        o_there.wait()

    loop(nc, back_chunk)

    RA, AR, w = D // A, A * R, F // 2
    pieces = []
    for src, r1, r2, cuts in (
        (gwd_h, r1d_h, r2d_h, (0, w, 2 * w)),
        (gwg_h, r1g_h, r2g_h, (0, w, 2 * w, 3 * w, 4 * w)),
        (gqo_h, r1q_h, r2q_h, (0, 2 * C, 3 * C, 4 * C)),
    ):
        for n in range(len(cuts) - 1):
            pieces.append((src, r1, r2, slice(cuts[n], cuts[n + 1])))
    lanes_of = (0, 1, 3, 0, 1, 3, 1, 3, 0)

    def px_copy(p, k):
        src, r1, _, cols = pieces[p]
        return remote(
            src.at[(b + k) % B, :, cols], r1.at[k - 1, :, cols], p_s.at[p, k - 1], p_r.at[p, k - 1], xpeer(k)
        )

    def rs_start(p):
        for k in range(1, B):
            px_copy(p, k).start()

    def slot(p):
        cols = pieces[p][3]
        return slice(lanes_of[p] * w, lanes_of[p] * w + cols.stop - cols.start)

    def sums(p, aa):
        return gu.at[pl.ds(pl.multiple_of(D + aa * R, R), R), slot(p)]

    def pz_copy(p, k):
        _, _, r2, cols = pieces[p]
        return remote(
            sums(p, (a + k) % A), r2.at[k - 1, :, cols], q_s.at[p, k - 1], q_r.at[p, k - 1], zpeer(k)
        )

    def own_load(p):
        src, _, _, cols = pieces[p]
        return local(src.at[b, :, cols], gu.at[0:AR, slot(p)], rsem.at[lanes_of[p], 0])

    def first_load(p, k):
        _, r1, _, cols = pieces[p]
        return local(
            r1.at[k - 1, :, cols], gu.at[k * AR : (k + 1) * AR, slot(p)], rsem.at[lanes_of[p], k]
        )

    def rs_load(p):
        own_load(p).start()
        for k in range(1, B):
            px_copy(p, k).wait()
            first_load(p, k).start()

    def rs_add(p):
        own_load(p).wait()
        for k in range(1, B):
            first_load(p, k).wait()
        for k in list(range(1, A)) + [0]:
            aa = (a + k) % A
            t = gu[rows_at(aa * R, R), slot(p)].astype(F32)
            for kk in range(1, B):
                t = t + gu[pl.ds(pl.multiple_of(kk * AR + aa * R, R), R), slot(p)].astype(F32)
            gu[pl.ds(pl.multiple_of(D + aa * R, R), R), slot(p)] = t.astype(BF)
            if k:
                pz_copy(p, k).start()

    def second_load(p, k):
        _, _, r2, cols = pieces[p]
        return local(
            r2.at[k - 1, :, cols], gu.at[D + AR + (k - 1) * R : D + AR + k * R, slot(p)], rsem.at[lanes_of[p], B + k]
        )

    def end_load(p):
        for k in range(1, A):
            pz_copy(p, k).wait()
            second_load(p, k).start()

    def rs_end(p, res):
        for k in range(1, A):
            second_load(p, k).wait()
        width = pieces[p][3].stop - pieces[p][3].start
        t = gu[pl.ds(pl.multiple_of(D + a * R, R), R), slot(p)].astype(F32)
        for k in range(1, A):
            t = t + gu[D + AR + (k - 1) * R : D + AR + k * R, slot(p)].astype(F32)
        fstage[:, 0:width] = t
        cp = local(fstage.at[:, 0:width], res, lsem.at[0])
        cp.start()
        cp.wait()

    def rs_finish(p):
        if p < 2:
            res = owd.at[:, p * w : p * w + w]
        elif p < 6:
            res = owg.at[:, (p - 2) * w : (p - 1) * w]
        elif p == 6:
            res = owq.at[:, 0 : 2 * C]
        elif p == 7:
            res = owq.at[:, 2 * C : 3 * C]
        else:
            res = owo
        rs_end(p, res)

    def tile_out(half, dst, t):
        src = wst.at[:, :, half * F : half * F + F]
        return local(src, dst.at[:, rows_at(t * R, R), half * F : half * F + F], lsem.at[1 + half])

    def down_out(half, t):
        src = wst.at[:, :, half * F : half * F + F]
        return local(src, gwd_h.at[:, rows_at(t * R, R)], lsem.at[1 + half])

    def down_tile(t):
        for half in range(2):
            tt = 2 * t + half

            @pl.when(t > 0)
            def _():
                down_out(half, tt).wait()

            cols = rows_at(tt * RA, RA)
            wst[:, :, half * F : half * F + F] = tdot(gml[:, cols], act[...]).astype(BF).reshape(B, R, F)
            down_out(half, tt).start()

    lt_first = local(tokf.at[rows_at((nc - 1) * TB + core * TH, TH)], gst, lsem.at[6])
    lt_first.start()
    loop(A // 2, down_tile)
    for half in range(2):
        down_out(half, 0).wait()
    rs_start(0)

    def up_tile(t):
        cols = rows_at(t * RA, RA)
        lhs = tokv[:, cols]
        for half in range(2):

            @pl.when(t > 0)
            def _():
                tile_out(half, gwg_h, t).wait()

            wst[:, :, half * F : half * F + F] = (
                tdot(lhs, gu[:, half * F : half * F + F]).astype(BF).reshape(B, R, F)
            )
            tile_out(half, gwg_h, t).start()

        @pl.when(t == A // 2)
        def _():
            rs_start(1)

    loop(A, up_tile)
    for half in range(2):
        tile_out(half, gwg_h, 0).wait()
    rs_start(2)
    rs_start(3)
    rs_load(0)
    qv, kv, vv = gml.at[:, 0:C], gml.at[:, C : 2 * C], gml.at[:, 2 * C : 3 * C]
    gv = gml.at[:, 3 * C : 4 * C]
    rot0 = 2 * w
    loads = [
        local(qkv_h, gml.at[:, 0 : 3 * C], lsem.at[7]),
        local(rot_h, gu.at[:, rot0 : rot0 + 2 * C], lsem.at[8]),
        local(tokf, tokv, lsem.at[9]),
    ]
    for cp in loads:
        cp.start()
    dk[...] = jnp.zeros_like(dk)
    dv[...] = jnp.zeros_like(dv)
    gsq[...] = jnp.zeros_like(gsq)
    heads = lax.broadcasted_iota(jnp.int32, (8, C), 0)
    lanes = lax.broadcasted_iota(jnp.int32, (8, C), 1) // DK
    pick = jnp.where(heads == lanes, 1.0, 0.0).astype(BF)
    for cp in loads[:2]:
        cp.wait()
    NY = ny * CF

    def gin_copy(c, hs):
        return remote(
            sc.at[hs * TH : (hs + 1) * TH, 0:NY], rc.at[c, :, hs * NY : (hs + 1) * NY], c_s.at[c, hs],
            c_r.at[c, hs], peer,
        )

    def gin_y(c, k, hs):
        src = slice((hs * (ny - 1) + k - 1) * CF, (hs * (ny - 1) + k) * CF)
        dst = slice(hs * CF, hs * CF + CF)
        return remote(
            sy2.at[c, :, src], ry2.at[k - 1, c, :, dst], yg_s.at[c, k - 1, hs], yg_r.at[c, k - 1, hs],
            ypeer(k, core),
        )

    n128 = CF // 128

    def gin_take(c):
        for hs in range(2):
            gin_copy(c, hs).wait()
            for k in range(ny):
                for q in range(n128):
                    col = hs * NY + k * CF + q * 128
                    t = acc[k * n128 + q, hs * TH : (hs + 1) * TH, :] + rc[c, :, col : col + 128].astype(F32)
                    if k == 0:
                        dk[rows_at(c * TB + hs * TH, TH), q * 128 : q * 128 + 128] = t
                    else:
                        col = (hs * (ny - 1) + k - 1) * CF + q * 128
                        sy2[c, :, col : col + 128] = t.astype(BF)
            for k in range(1, ny):
                gin_y(c, k, hs).start()

    def out_tiles():
        def o_tile(t):
            cols = rows_at(t * RA, RA)
            wst[:, :, 0:C] = tdot(gba[:, cols], attn[...]).astype(BF).reshape(B, R, C)
            cp = local(wst.at[:, :, 0:C], gqo_h.at[:, rows_at(t * R, R), 3 * C : 4 * C], lsem.at[1])
            cp.start()
            cp.wait()

        loop(A, o_tile)

    def kept_rows(c):
        return local(tokf.at[rows_at(c * TB + core * TH, TH)], gst, lsem.at[6])

    def branch_rows(c):
        base = c * TB + core * TH
        landed(2, c, sy2, ry3)
        kept_rows(c).wait()

        def rows(t):
            r = rows_at(t * RT, RT)
            g = rows_at(base + t * RT, RT)
            aa = alv[0:1, :]
            br = total(c, r, sy1, ry1)
            x = gst[r, :].astype(F32)
            ra = mean_sq(br, D)
            ha = br * ra
            diff = ha - x
            mix = x + aa * diff
            r1 = mean_sq(mix, D)
            hid = mix * r1
            gh = ghid[c, r, :].astype(F32) + total(c, r, sy2, ry3)
            gm = r1 * (gh - hid * (jnp.sum(gh * hid, axis=1, keepdims=True) * (1.0 / D)))
            gacc[0:8, :] += fold(gm * diff)
            gt = aa * gm
            ghid[c, r, :] = (gm - gt).astype(BF)
            gb = ra * (gt - ha * (jnp.sum(gt * ha, axis=1, keepdims=True) * (1.0 / D)))
            gba[g, :] = gb.astype(BF)

        rows_then_share(2, c, rows, gba)

        @pl.when(c > 0)
        def _():
            kept_rows(jnp.maximum(c - 1, 0)).start()

    branch_rows(nc - 1)
    rs_add(0)

    def attn_grad_chunk(i):
        c = nc - 1 - i
        shared(2, c, gba)

        @pl.when(c > 0)
        def _():
            branch_rows(jnp.maximum(c - 1, 0))

        r = rows_at(c * TB, TB)
        g = nn(gba[r, :], wqov[:, 3 * C : 4 * C]).astype(BF)
        gv[r, :] = g
        prod = g.astype(F32) * attn[r, :].astype(F32)
        ph = prod.astype(BF)
        dl[:, r] = nt(pick, ph) + nt(pick, (prod - ph.astype(F32)).astype(BF))

        def between():
            @pl.when(i == 0)
            def _():
                rs_load(1)

            @pl.when(i == 1)
            def _():
                rs_add(2)

        attn_bwd_block(c, TB, H, qv, kv, vv, gv, ll, dl, off_bias, dq, dk, dv, between)

        @pl.when(i == 0)
        def _():
            rs_add(1)
            rs_start(4)

        @pl.when(i == 1)
        def _():
            rs_load(3)
            end_load(0)

        @pl.when(i == 2)
        def _():
            rs_load(4)
            end_load(1)

        @pl.when(i == nc - 1)
        def _():
            rs_load(5)
            end_load(2)
            out_tiles()
            rs_start(8)

        cs, sn = angles_of(r)
        for part in range(2):
            gh = (dq[...] if part == 0 else dk[r, :]) * 8.0
            t = gu[r, rot0 + part * C : rot0 + part * C + C].astype(F32)
            inv = lax.rsqrt(split_dot(t * t, ones) + epsilon)
            un = t * inv
            gsq[...] += fold(gh * un)
            gh = gh * sq[...]
            gr = inv * (gh - un * split_dot(gh * un, ones))
            act[r, part * C : part * C + C] = turn(gr, cs, sn, -1.0).astype(BF)
        act[r, 2 * C : 3 * C] = dv[r, :].astype(BF)

        def product(hsel, k, cc):
            rr = rows_at(c * TB + hsel * TH, TH)
            cols = feat(((y + k) % ny) * 2 + cc)
            t = nt(act[rr, 0 : 3 * C], wqov[cols, 0 : 3 * C])
            if k == 0:
                t = t + jnp.where(hsel == core, 1.0, 0.0) * ghid[c, :, cols].astype(F32)
            return t

        @pl.when(i > 0)
        def _():
            gin_take(jnp.minimum(c + 1, nc - 1))

        for hs in range(2):
            for k in range(ny):
                sc[hs * TH : (hs + 1) * TH, k * CF : (k + 1) * CF] = product(hs, k, mate).astype(BF)
            gin_copy(c, hs).start()
        for hs in range(2):
            for k in range(ny):
                t = product(hs, k, core)
                for q in range(n128):
                    acc[k * n128 + q, hs * TH : (hs + 1) * TH, :] = t[:, q * 128 : q * 128 + 128]

        @pl.when(i == 0)
        def _():
            rs_start(5)
            rs_load(2)

        @pl.when(i == 1)
        def _():
            rs_finish(0)
            rs_add(3)

        @pl.when(i == 2)
        def _():
            rs_finish(1)
            rs_add(4)

        @pl.when(i == nc - 1)
        def _():
            rs_finish(2)
            rs_add(5)
            end_load(3)

    loop(nc, attn_grad_chunk)
    ga_there = remote(gacc.at[:, feat(y * 2 + mate)], gar, m_s.at[0], m_r.at[0], peer)
    ga_there.start()
    loads[2].wait()

    def q_out(half, t):
        src = wst.at[:, :, half * F : half * F + 2 * C]
        return local(src, gqo_h.at[:, rows_at(t * R, R), 0 : 2 * C], lsem.at[1 + half])

    def q_tile(t):
        for half in range(2):
            tt = 2 * t + half

            @pl.when(t > 0)
            def _():
                q_out(half, tt).wait()

            g = tdot(tokv[:, rows_at(tt * RA, RA)], act[:, 0 : 2 * C]).astype(BF)
            wst[:, :, half * F : half * F + 2 * C] = g.reshape(B, R, 2 * C)
            q_out(half, tt).start()

    loop(A // 2, q_tile)
    for half in range(2):
        q_out(half, 0).wait()
    rs_start(6)

    def v_out(half, t):
        src = wst.at[:, :, half * F : half * F + C]
        return local(src, gqo_h.at[:, rows_at(t * R, R), 2 * C : 3 * C], lsem.at[1 + half])

    def v_tile(t):
        for half in range(2):
            tt = 2 * t + half

            @pl.when(t > 0)
            def _():
                v_out(half, tt).wait()

            g = tdot(tokv[:, rows_at(tt * RA, RA)], act[:, 2 * C : 3 * C]).astype(BF)
            wst[:, :, half * F : half * F + C] = g.reshape(B, R, C)
            v_out(half, tt).start()

    loop(A // 2, v_tile)
    for half in range(2):
        v_out(half, 0).wait()
    rs_start(7)
    gin_take(0)
    rs_finish(3)
    rs_load(8)
    ga_there.wait()
    vec[...] = jnp.zeros_like(vec)
    gt = gacc[:, mine] + gar[...]
    vec[0:1, 0:F] = jnp.sum(gsacc[0:8, :], axis=0, keepdims=True)
    vec[1:2, 0:F] = jnp.sum(gsacc[8:16, :], axis=0, keepdims=True)
    vec[2:3, 0:CF] = jnp.sum(gt[0:8], axis=0, keepdims=True)
    vec[3:4, 0:CF] = jnp.sum(gt[8:16], axis=0, keepdims=True)
    vec[4:5, 0:C] = jnp.sum(gsq[...], axis=0, keepdims=True)
    vx = [remote(vec, rv1.at[k - 1], m_s.at[k], m_r.at[k], xpeer(k)) for k in range(1, B)]
    for cp in vx:
        cp.start()
    rs_add(8)
    end_load(4)
    for cp in vx:
        cp.wait()
    t = vec[...]
    for k in range(B - 1):
        t = t + rv1[k]
    vec[...] = t
    vz = [
        remote(vec, rv2.at[k - 1], m_s.at[B - 1 + k], m_r.at[B - 1 + k], zpeer(k)) for k in range(1, A)
    ]
    for cp in vz:
        cp.start()

    rs_finish(4)
    end_load(5)

    def gin_end(i):
        c = nc - 1 - i
        for hs in range(2):
            rr = rows_at(c * TB + hs * TH, TH)
            for k in range(1, ny):
                gin_y(c, k, hs).wait()
                dk[rr, :] += ry2[k - 1, c, :, hs * CF : hs * CF + CF].astype(F32)

    loop(nc, gin_end)
    ends = [local(dk, gin_o, lsem.at[10])]
    ends[-1].start()
    rs_load(6)
    rs_add(6)
    rs_finish(5)
    rs_load(7)
    rs_add(7)
    end_load(8)
    for cp in vz:
        cp.wait()
    t = vec[...]
    for k in range(A - 1):
        t = t + rv2[k]
    vec[...] = t
    ends.append(local(vec, vec_o, lsem.at[11]))
    ends[-1].start()
    for p in range(6):
        w_sent(p, p != 4)
    rs_finish(8)
    end_load(6)
    rs_finish(6)
    end_load(7)
    rs_finish(7)
    for cp in ends:
        cp.wait()


def run_layer(z, live, tokens, gout, wqo, wg, wd, alpha, table, sq, sml):
    T, C, CF, F, D, H = z.T, z.C, z.CF, z.F, z.D, z.H
    nc, TB, TH, R, A, B, ny, mp = z.nc, z.TB, z.TH, z.R, z.A, z.B, z.ny, z.mp
    S = jax.ShapeDtypeStruct
    hbm = pl.BlockSpec(memory_space=pltpu.HBM)
    vm = pl.BlockSpec(memory_space=pltpu.VMEM)
    W = max(F, CF, C)
    AR = A * R
    outs = [
        S((T, CF), BF), S((T, CF), F32), S((R, 3 * C), F32), S((R, C), F32), S((R, 2 * F), F32), S((R, F), F32),
        S((8, W), F32),
        S((T, 3 * C), BF), S((T, 2 * C), BF), S((T, D), BF), S((nc, TH, D), BF),
    ]
    widths = (F, 2 * F, 4 * C)
    outs += [S((B, AR, n), BF) for n in widths]
    outs += [S((max(B - 1, 1), AR, n), BF) for n in widths]
    outs += [S((max(A - 1, 1), R, n), BF) for n in widths]
    V = pltpu.VMEM
    scratch = [
        V((T, D), BF), V((D, 4 * C), BF), V((D, 2 * F), BF), V((D, F), BF),
        V((T, D), BF), V((T, F), BF), V((T, 2 * F), BF), V((T, D), BF),
        V((T, C), BF), V((8, T), F32), V((8, T), F32), V((max(H, ny * CF // 128), TB, 128), F32),
        V((T, C), F32), V((T, C), F32), V((TB, C), F32), V((R, F // 2), F32),
    ]
    for _ in range(2):
        scratch += [V((nc, TH, D), BF), V((ny - 1, nc, TH, D), BF)]
    scratch += [
        V((ny - 1, nc, TH, D), BF), V((nc, TH, D), BF), V((TB, D), BF), V((nc, TH, D), BF), V((TH, D), BF), V((TH, D), BF),
        V((B, R, 2 * F), BF), V((8, D), F32), V((16, D), F32), V((16, F), F32), V((8, C), F32), V((16, CF), F32),
        V((8, W), F32), V((max(B - 1, 1), 8, W), F32), V((max(A - 1, 1), 8, W), F32),
    ]
    sem = pltpu.SemaphoreType.DMA
    for shape in (
        (nc, 2 * ny - 1), (6, B, 2, max(A - 1, 1)), (6, A, max(B - 1, 1)), (mp - 1,), (mp - 1,), (3, nc, 2),
        (3, nc, ny - 1, 2), (3, nc, 2), (nc,), (9, max(B - 1, 1)), (9, max(A - 1, 1)), (nc, 2), (nc, ny - 1, 2),
        (A + B - 1,),
    ):
        scratch += [sem(shape), sem(shape)]
    scratch += [sem((22,)), sem((4, A + B))]
    return pl.pallas_call(
        functools.partial(layer, z),
        out_shape=outs,
        in_specs=[pl.BlockSpec(memory_space=pltpu.SMEM)] + [hbm] * 6 + [vm] * 3,
        out_specs=[hbm] * len(outs),
        scratch_shapes=scratch,
        compiler_params=pltpu.CompilerParams(
            collective_id=0, has_side_effects=True, vmem_limit_bytes=64 * 2**20 - 2**19
        ),
        name="layer",
    )(live, tokens, gout.reshape(nc, 2, TH, CF), wqo, wg, wd, alpha, table, sq, sml)


def tables(T):
    half = DK // 2
    frequency = np.float32(theta_base) ** (np.float32(-2.0 / DK) * np.arange(half, dtype=np.float32))
    grid = np.arange(T, dtype=np.float32)[:, None] * frequency[None, :].astype(np.float32)
    cos, sin = np.cos(grid, dtype=np.float32), np.sin(grid, dtype=np.float32)
    return np.concatenate([cos, cos, sin, sin], axis=1)


def on_device(
    sizes,
    tokens,
    w_qkv,
    w_out,
    w_gate_up,
    w_down,
    s_qk,
    alpha_attn,
    alpha_mlp,
    s_mlp,
    doc_lengths,
    grad_out,
):
    T, CF = tokens.shape
    H = s_qk.shape[1]
    C = H * DK
    F = w_down.shape[1]
    z = Sizes(sizes, T, C, CF, F, doc_lengths.shape[1])
    D, R = z.D, z.R
    table = jnp.asarray(tables(T))
    scale = s_qk.T.reshape(1, C)
    sml = s_mlp.transpose(1, 2, 0).reshape(2, F)
    alpha = jnp.pad(
        jnp.stack([alpha_attn.T.reshape(-1), alpha_mlp.T.reshape(-1)]), ((0, 6), (0, 0))
    )
    whole = doc_lengths[0, 0] == T
    live = whole.astype(F32).reshape(1)
    (out, grad_in, gw_qkv, gw_out, gw_gu, gw_down, vec) = run_layer(
        z, live, tokens, grad_out, jnp.concatenate([w_qkv.reshape(R, 3 * C), w_out], axis=1),
        w_gate_up.reshape(R, 2 * F), w_down, alpha, table, scale, sml,
    )[:7]
    d, m = place()

    def channel_rows(v, per_head):
        n = per_head // z.dp
        return lax.dynamic_slice_in_dim(v.reshape(H, per_head).T, d * n, n, 0)

    gs = jnp.stack([channel_rows(vec[i, 0:F], F // H) for i in range(2)], axis=1)
    return (
        out,
        grad_in,
        gw_qkv.reshape(R, 3, C),
        gw_out,
        gw_gu.reshape(R, 2, F),
        gw_down,
        channel_rows(vec[4, 0:C], DK),
        channel_rows(vec[2, 0:CF], DK),
        channel_rows(vec[3, 0:CF], DK),
        gs,
    )


def solution(mesh):
    placed = (
        P("dp", "mp"),
        P("dp", None, "mp"),
        P("dp", "mp"),
        P("dp", None, "mp"),
        P("dp", "mp"),
        P(None, "mp"),
        P(None, "mp"),
        P(None, "mp"),
        P(None, None, "mp"),
        P("dp", None),
        P("dp", "mp"),
    )
    return jax.shard_map(
        functools.partial(on_device, dict(mesh.shape)),
        mesh=mesh,
        in_specs=placed,
        out_specs=(
            P("dp", "mp"),
            P("dp", "mp"),
            P("dp", None, "mp"),
            P("dp", "mp"),
            P("dp", None, "mp"),
            P("dp", "mp"),
            P("dp", "mp"),
            P("dp", "mp"),
            P("dp", "mp"),
            P("dp", None, "mp"),
        ),
        check_vma=False,
    )
```

```python
import functools
import math

import jax
import jax.numpy as jnp
import numpy as np
from jax import lax
from jax.experimental import pallas as pl
from jax.experimental.pallas import tpu as pltpu
from jax.sharding import PartitionSpec as P

DK = 64
epsilon = 1e-06
theta_base = 10000.0


LC=math.sqrt(DK)*math.log2(math.e)
NEG=-1e30
def nt(a,b): return lax.dot_general(a,b,(((1,),(1,)),((),())),preferred_element_type=jnp.float32)
def nn(a,b): return jnp.dot(a,b,preferred_element_type=jnp.float32)
def head_mask(x,h):
    lane=lax.broadcasted_iota(jnp.int32,x.shape,1)
    return jnp.where((lane//DK)==(h%2), x, jnp.zeros_like(x))
def attn_fwd_block(i, TB, H, ref, C, live, acc):
    hb=TB//2
    qs=pl.ds(pl.multiple_of(i*TB,TB),TB)
    def vx(h,ks):
        v=ref[ks,pl.ds(2*C+(h//2)*128,128)]
        lane=lax.broadcasted_iota(jnp.int32,v.shape,1)
        return jnp.where((lane//DK)==(h%2),v,jnp.ones_like(v))
    def tile(h,qsl,ks,tri):
        p2=pl.ds((h//2)*128,128)
        x=nt(ref[qsl,p2],head_mask(ref[ks,pl.ds(C+(h//2)*128,128)],h))
        if tri:
            r=lax.broadcasted_iota(jnp.int32,x.shape,0); c=lax.broadcasted_iota(jnp.int32,x.shape,1)
            x=jnp.where(c<=r,x,NEG)
        p=jnp.exp2(x*LC).astype(jnp.bfloat16)
        return nn(p,vx(h,ks))
    k0=pl.ds(pl.multiple_of(i*TB,hb),hb); k1=pl.ds(pl.multiple_of(i*TB+hb,hb),hb)
    for h in range(H):
        a0=tile(h,qs,k0,True)
        a1=tile(h,k1,k1,True)
        acc[h,0:hb]=a0[0:hb]; acc[h,hb:TB]=a0[hb:TB]+a1
    def body(j,_):
        ks=pl.ds(pl.multiple_of(j*TB,TB),TB)
        for h in range(H):
            acc[h]+=live*tile(h,qs,ks,False)
        return 0
    lax.fori_loop(0,i,body,0)
def tdot(a,b): return lax.dot_general(a,b,(((0,),(0,)),((),())),preferred_element_type=jnp.float32)
def attn_bwd_block(i, TB, H, q_ref, k_ref, v_ref, g_ref, ll_ref, dl_ref, ob, dq, dk, dv, between):
    qs=pl.ds(pl.multiple_of(i*TB,TB),TB); hb=TB//2
    qz=[head_mask(q_ref[qs,pl.ds((h//2)*128,128)],h) for h in range(H)]
    gz=[head_mask(g_ref[qs,pl.ds((h//2)*128,128)],h) for h in range(H)]
    lr=[ll_ref[pl.ds(h,1),qs] for h in range(H)]
    dr=[dl_ref[pl.ds(h,1),qs] for h in range(H)]
    def tile(h,ks,qv,gv,lb,dd,tri):
        p2=pl.ds((h//2)*128,128)
        x=nt(k_ref[ks,p2],qv)*LC-lb
        dp=nt(v_ref[ks,p2],gv)
        if tri:
            r=lax.broadcasted_iota(jnp.int32,x.shape,0); c=lax.broadcasted_iota(jnp.int32,x.shape,1)
            x=jnp.where(r<=c,x,NEG)
        p=jnp.exp2(x)
        ds=(p*(dp-dd)).astype(jnp.bfloat16)
        dvp=nn(p.astype(jnp.bfloat16),gv)
        dkp=nn(ds,qv)
        dqp=tdot(ds,head_mask(k_ref[ks,p2],h))
        return dqp,dkp,dvp
    k0=pl.ds(pl.multiple_of(i*TB,hb),hb); k1=pl.ds(pl.multiple_of(i*TB+hb,hb),hb)
    for pr in range((H+1)//2):
        p2=pl.ds(pr*128,128)
        dk0=dv0=dk1=dv1=0; q0=q1=0
        for h in range(2*pr,min(2*pr+2,H)):
            a,b,c=tile(h,k0,qz[h],gz[h],lr[h],dr[h],True)
            a1,b1,c1=tile(h,k1,qz[h][hb:],gz[h][hb:],lr[h][:,hb:],dr[h][:,hb:],True)
            q0+=a[0:hb]; q1+=a[hb:]+a1
            dk0+=b; dv0+=c; dk1+=b1; dv1+=c1
        dq[0:hb,p2]=q0; dq[hb:TB,p2]=q1
        dk[k0,p2]+=dk0; dv[k0,p2]+=dv0; dk[k1,p2]+=dk1; dv[k1,p2]+=dv1
    between()
    lo=[l-ob for l in lr]
    def body(j,_):
        ks=pl.ds(pl.multiple_of(j*TB,TB),TB)
        for pr in range((H+1)//2):
            p2=pl.ds(pr*128,128)
            dka=dva=dqa=0
            for h in range(2*pr,min(2*pr+2,H)):
                a,b,c=tile(h,ks,qz[h],gz[h],lo[h],dr[h],False)
                dqa+=a; dka+=b; dva+=c
            dq[:,p2]+=dqa
            dk[ks,p2]+=dka; dv[ks,p2]+=dva
        return 0
    lax.fori_loop(0,i,body,0)


MESH = pl.DeviceIdType.MESH
F32, BF = jnp.float32, jnp.bfloat16


class Sizes:
    def __init__(self, mesh_shape, T, C, CF, F, pieces):
        self.mp, self.dp = mesh_shape["mp"], mesh_shape["dp"]
        self.ny = self.mp // 2
        self.A = 4 if self.dp % 4 == 0 else 1
        self.B = self.dp // self.A
        self.T, self.C, self.CF, self.F = T, C, CF, F
        self.D = CF * self.mp
        self.H = C // DK
        self.nc = pieces
        self.TB = T // pieces
        self.TH = self.TB // 2
        self.R = self.D // self.dp


def place():
    return lax.axis_index("dp"), lax.axis_index("mp")


def remote(src, dst, ss, rs, dev):
    return pltpu.make_async_remote_copy(
        src, dst, send_sem=ss, recv_sem=rs, device_id=dev, device_id_type=MESH
    )


def local(src, dst, sem):
    return pltpu.make_async_copy(src, dst, sem)


def rows_at(start, size):
    return pl.ds(pl.multiple_of(start, size), size)


def loop(n, fn):
    def body(i, carry):
        fn(i)
        return carry

    lax.fori_loop(0, n, body, 0)


def fold(x):
    return jnp.sum(x.reshape(x.shape[0] // 8, 8, x.shape[1]), axis=0)


def mean_sq(x, D):
    return lax.rsqrt(jnp.sum(x * x, axis=1, keepdims=True) * (1.0 / D) + epsilon)


def split_dot(x, ones):
    hi = x.astype(BF)
    return nn(hi, ones) + nn((x - hi.astype(F32)).astype(BF), ones)


def head_ones(width):
    i = lax.broadcasted_iota(jnp.int32, (width, width), 0) // DK
    j = lax.broadcasted_iota(jnp.int32, (width, width), 1) // DK
    return jnp.where(i == j, 1.0, 0.0).astype(BF)


def turn(x, cosine, sine, sign):
    lane = lax.broadcasted_iota(jnp.int32, x.shape, 1)
    first = (lane % DK) < DK // 2
    other = jnp.where(first, -pltpu.roll(x, x.shape[1] - DK // 2, 1), pltpu.roll(x, DK // 2, 1))
    return x * cosine + sign * other * sine


def layer(
    z,
    live_ref, tokens, gout, wqo, wg, wd, alpha, table, sq, sml,
    out, gin_o, owq, owo, owg, owd, vec_o,
    qkv_h, rot_h, tokf, goh, gwd_h, gwg_h, gqo_h, r1d_h, r1g_h, r1q_h, r2d_h, r2g_h, r2q_h,
    tokv, wqov, wgv, wdv, gml, act, gu, gba, attn, ll, dl, acc, dk, dv, dq, fstage,
    sy1, ry1, sy2, ry2, ry3, rc, sc, ghid, gst, fst, wst, alv, gacc, gsacc, gsq, gar, vec, rv1, rv2,
    tok_s, tok_r, w_s, w_r, x_s, x_r, al_s, al_r, go_s, go_r, ex_s, ex_r, y_s, y_r, hc_s, hc_r, out_s, out_r,
    p_s, p_r, q_s, q_r, c_s, c_r, yg_s, yg_r, m_s, m_r, lsem, rsem,
):
    T, C, CF, F, D, H = z.T, z.C, z.CF, z.F, z.D, z.H
    nc, TB, TH, R, A, B, ny, mp = z.nc, z.TB, z.TH, z.R, z.A, z.B, z.ny, z.mp
    d, m = place()
    a, b = d // B, d % B
    y, core = m // 2, m % 2
    mate = 1 - core
    peer = (d, y * 2 + mate)

    def ypeer(k, cc):
        return (d, ((y + k) % ny) * 2 + cc)

    zpeer = lambda k: (((a + k) % A) * B + b, m)
    xpeer = lambda k: (a * B + (b + k) % B, m)
    others = [peer] + [ypeer(k, cc) for k in range(1, ny) for cc in (core, mate)]
    everyone = others + [zpeer(k) for k in range(1, A)] + [xpeer(k) for k in range(1, B)]
    bar = pltpu.get_barrier_semaphore()
    for dev in everyone:
        pl.semaphore_signal(bar, 1, device_id=dev, device_id_type=MESH)
    pl.semaphore_wait(bar, len(everyone))

    live = live_ref[0]
    off_bias = jnp.where(live > 0.5, 0.0, NEG)
    feat = lambda mm: pl.ds(pl.multiple_of(mm * CF, CF), CF)
    mine = feat(m)


    def tok_own(c, i, dev):
        r = rows_at(c * TB, TB)
        return remote(tokens.at[r], tokv.at[r, mine], tok_s.at[c, i], tok_r.at[c, i], dev)

    def tok_got(c, i, mm):
        r = rows_at(c * TB, TB)
        return remote(tokv.at[r, feat(mm)], tokv.at[r, feat(mm)], tok_s.at[c, i], tok_r.at[c, i], peer)

    def start_tok(i):
        c = nc - 1 - i
        for k in range(1, ny):
            tok_own(c, k, ypeer(k, core)).start()
        tok_own(c, 0, peer).start()

    lo, hi = slice(0, F), slice(F, 2 * F)
    dlo, dhi = slice(0, F // 2), slice(F // 2, F)
    weights = [
        (wqo.at[:, 0 : 2 * C], wqov.at[:, 0 : 2 * C]),
        (wg.at[:, lo], wgv.at[:, lo]),
        (wg.at[:, hi], wgv.at[:, hi]),
        (wd.at[:, dlo], wdv.at[:, dlo]),
        (wd.at[:, dhi], wdv.at[:, dhi]),
        (wqo.at[:, 2 * C : 4 * C], wqov.at[:, 2 * C : 4 * C]),
    ]

    def shard(aa, bb):
        return rows_at((aa * B + bb) * R, R)

    def column(st):
        return (b - st + B) % B

    def z_moves(w, st, h):
        src, dst = weights[w]
        moves = []
        for way, step in ((0, 1), (1, -1)):
            aa = a - step * (h - 1)
            ok = (a + step >= 0) & (a + step < A) & (aa >= 0) & (aa < A)
            moves.append((way, step, jnp.clip(aa, 0, A - 1), ok))
        return src, dst, moves

    def z_copy(w, st, h, way, step, aa):
        src, dst = weights[w]
        r = shard(aa, column(st))
        source = src if (h == 1 and st == 0) else dst.at[r]
        to = jnp.clip(a + step, 0, A - 1) * B + b
        return remote(source, dst.at[r], w_s.at[w, st, way, h - 1], w_r.at[w, st, way, h - 1], (to, m))

    def z_hop(w, st, h):
        if h >= A:
            return
        for way, step, aa, ok in z_moves(w, st, h)[2]:

            @pl.when(ok)
            def _():
                z_copy(w, st, h, way, step, aa).start()

    def z_sent(w, st, h):
        for way, step, aa, ok in z_moves(w, st, h)[2]:

            @pl.when(ok)
            def _():
                z_copy(w, st, h, way, step, aa).wait_send()

    def z_wait(w, st, h, forward=False):
        if h >= A:
            return
        for way, step in ((0, 1), (1, -1)):
            aa = a - step * h

            @pl.when((aa >= 0) & (aa < A))
            def _():
                z_copy(w, st, h, way, step, jnp.clip(aa, 0, A - 1)).wait_recv()
                if forward:
                    x_send(w, aa)

    def x_copy(w, aa, k, own=False):
        src, dst = weights[w]
        r = shard(aa, b)
        return remote(
            src if own else dst.at[r], dst.at[r], x_s.at[w, aa, k - 1], x_r.at[w, aa, k - 1], xpeer(k)
        )

    def x_send(w, aa, own=False):
        for k in range(1, B):
            x_copy(w, aa, k, own).start()

    def x_wait(w, aa):
        src, dst = weights[w]
        for k in range(1, B):
            r = shard(aa, (b - k + B) % B)
            remote(src, dst.at[r], x_s.at[w, aa, k - 1], x_r.at[w, aa, k - 1], xpeer(k)).wait_recv()

    def w_local(w):
        src, dst = weights[w]
        return local(src, dst.at[shard(a, b)], lsem.at[16 + w])

    def w_start(w):
        z_hop(w, 0, 1)
        x_send(w, a, own=True)
        w_local(w).start()

    def w_next(w, st, h, forward=True):
        z_wait(w, st, h, forward)
        z_hop(w, st, h + 1)

    def w_ready(w):
        for aa in range(A):
            x_wait(w, aa)
        w_local(w).wait()

    def w_sent(w, forward):
        for st in range(1 if forward else B):
            for h in range(1, A):
                z_sent(w, st, h)
        for k in range(1, B):
            for aa in range(A) if forward else [a]:
                x_copy(w, aa, k).wait_send()

    w_start(0)
    w_start(5)
    loop(nc, start_tok)
    x_send(4, a, own=True)
    w_local(4).start()
    tok_local = local(tokens, tokv.at[:, mine], lsem.at[4])
    tok_local.start()
    al_local = local(alpha, alv.at[:, mine], lsem.at[5])
    al_local.start()
    al_copies = [
        remote(alpha, alv.at[:, mine], al_s.at[i], al_r.at[i], dev) for i, dev in enumerate(others)
    ]
    for cp in al_copies:
        cp.start()

    def pass_tok(i):
        c = nc - 1 - i
        for k in range(1, ny):
            src = ((y - k + ny) % ny) * 2 + core
            tok_got(c, k, src).wait_recv()
            tok_got(c, ny + k - 1, src).start()

    w_next(0, 0, 1)
    w_next(5, 0, 1)
    w_next(0, 0, 2)
    pass_tok(0)
    w_next(5, 0, 2)
    w_next(0, 0, 3)
    pass_tok(1)
    w_next(5, 0, 3)
    w_start(1)
    w_start(2)
    loop(nc - 2, lambda i: pass_tok(i + 2))

    go4 = gout

    def go_copy(i, dev, cc):
        return remote(go4.at[:, cc], goh.at[:, :, mine], go_s.at[i], go_r.at[i], dev)

    go_copies = [go_copy(0, peer, mate)]
    i = 1
    for k in range(1, ny):
        for cc in (core, mate):
            go_copies.append(go_copy(i, ypeer(k, cc), cc))
            i += 1
    go_local = local(go4.at[:, core], goh.at[:, :, mine], lsem.at[6])
    go_local.start()
    for cp in go_copies:
        cp.start()

    def end_tok(i):
        c = nc - 1 - i
        tok_got(c, 0, y * 2 + mate).wait_recv()
        for k in range(1, ny):
            src = ((y - k + ny) % ny) * 2 + mate
            tok_got(c, ny + k - 1, src).wait_recv()

    loop(nc, end_tok)

    def tok_sent(i):
        c = nc - 1 - i
        tok_own(c, 0, peer).wait_send()
        for k in range(1, ny):
            tok_own(c, k, ypeer(k, core)).wait_send()
            tok_got(c, ny + k - 1, ((y - k + ny) % ny) * 2 + core).wait_send()

    loop(nc, tok_sent)
    tok_local.wait()
    w_ready(0)
    w_ready(5)

    ones = head_ones(C)
    qkvv = gml

    def angles_of(r):
        t = jnp.where(live > 0.5, table[r, :], table[0:TB, :])
        u = pltpu.roll(t, DK, 1)
        first = lax.broadcasted_iota(jnp.int32, t.shape, 1) < DK
        cs, sn = jnp.where(first, t, u), jnp.where(first, u, t)
        return jnp.concatenate([cs] * (C // 128), axis=1), jnp.concatenate([sn] * (C // 128), axis=1)

    def project_rows(i):
        r = rows_at(i * TB, TB)
        x = tokv[r, :]
        cs, sn = angles_of(r)
        for part in range(2):
            cols = slice(part * C, part * C + C)
            t = turn(nn(x, wqov[:, cols]), cs, sn, 1.0)
            act[r, cols] = t.astype(BF)
            inv = lax.rsqrt(split_dot(t * t, ones) + epsilon)
            qkvv[r, cols] = (t * inv * sq[...]).astype(BF)
        qkvv[r, 2 * C : 3 * C] = nn(x, wqov[:, 2 * C : 3 * C]).astype(BF)

        @pl.when(i == 1)
        def _():
            w_next(1, 0, 1)
            w_next(2, 0, 1)

    loop(nc, project_rows)
    save_tok = local(tokv, tokf, lsem.at[4])
    save_tok.start()
    saves = [
        local(qkvv.at[:, 0 : 3 * C], qkv_h, lsem.at[7]),
        local(act.at[:, 0 : 2 * C], rot_h, lsem.at[8]),
    ]
    for cp in saves:
        cp.start()

    RT = 64
    NG = 2
    GW = D // NG

    def y_copy(e, c, k, n, sy, ry):
        cols = slice(n * GW, n * GW + GW)
        return remote(
            sy.at[c, :, cols], ry.at[k - 1, c, :, cols], y_s.at[e, c, k - 1, n], y_r.at[e, c, k - 1, n],
            ypeer(k, core),
        )

    def exchange(e, c, part, sy, ry):
        r = rows_at(c * TB, TB)
        theirs, ours = rows_at(mate * TH, TH), rows_at(core * TH, TH)
        copies = []
        for n in range(NG):
            cols = slice(n * GW, n * GW + GW)
            sc[:, cols] = part(r, cols).astype(BF)
            cp = remote(
                sc.at[theirs, cols], rc.at[c, :, cols], ex_s.at[e, c, n], ex_r.at[e, c, n], peer
            )
            cp.start()
            copies.append(cp)
        for n in range(NG):
            cols = slice(n * GW, n * GW + GW)
            copies[n].wait()
            sy[c, :, cols] = (sc[ours, cols].astype(F32) + rc[c, :, cols].astype(F32)).astype(BF)
            for k in range(1, ny):
                y_copy(e, c, k, n, sy, ry).start()

    def landed(e, c, sy, ry):
        for k in range(1, ny):
            for n in range(NG):
                y_copy(e, c, k, n, sy, ry).wait()

    def total(c, r, sy, ry):
        t = sy[c, r, :].astype(F32)
        for k in range(ny - 1):
            t = t + ry[k, c, r, :].astype(F32)
        return t

    NS = 2
    SH = TH // NS

    def share(e, c, n, buf):
        r = rows_at(c * TB + core * TH + n * SH, SH)
        return remote(buf.at[r], buf.at[r], hc_s.at[e, c, n], hc_r.at[e, c, n], peer)

    def rows_then_share(e, c, rows, buf):
        for n in range(NS):
            loop(SH // RT, lambda t: rows(n * (SH // RT) + t))
            share(e, c, n, buf).start()

    def shared(e, c, buf):
        for n in range(NS):
            share(e, c, n, buf).wait()

    def attend_chunk(i):
        c = nc - 1 - i
        attn_fwd_block(c, TB, H, qkvv, C, live, acc)
        r = rows_at(c * TB, TB)
        for pr in range(C // 128):
            both = []
            for h in (2 * pr, 2 * pr + 1):
                t = acc[h]
                both.append(t / pltpu.roll(t, DK, 1))
                row = DK if h % 2 == 0 else 0
                ll[pl.ds(h, 1), r] = jnp.log2(t).T[row : row + 1]
            lane = lax.broadcasted_iota(jnp.int32, (TB, 128), 1)
            attn[r, pr * 128 : pr * 128 + 128] = jnp.where(lane < DK, both[0], both[1]).astype(BF)

        def part(rr, cols):
            return nt(attn[rr, :], wqov[cols, 3 * C : 4 * C])

        @pl.when(i == 0)
        def _():
            save_tok.wait()

        exchange(0, c, part, sy1, ry1)

        @pl.when(i == 0)
        def _():
            w_next(1, 0, 2)
            w_next(2, 0, 2)
            w_start(3)
            z_hop(4, 0, 1)
            x_wait(4, a)
            for st in range(1, B):
                z_hop(4, st, 1)

        @pl.when(i == 2)
        def _():
            w_next(1, 0, 3)
            w_next(2, 0, 3)

        @pl.when(i == 3)
        def _():
            w_next(3, 0, 1)
            for st in range(B):
                w_next(4, st, 1, False)

    ll[...] = jnp.zeros_like(ll)
    loop(nc, attend_chunk)
    for cp in saves:
        cp.wait()
    al_local.wait()
    for cp in al_copies:
        cp.wait()
    w_ready(1)
    w_ready(2)

    gacc[...] = jnp.zeros_like(gacc)
    gsacc[...] = jnp.zeros_like(gsacc)

    def feed_chunk(i):
        c = nc - 1 - i
        landed(0, c, sy1, ry1)
        base = c * TB + core * TH

        def rows(t):
            r = rows_at(t * RT, RT)
            g = rows_at(base + t * RT, RT)
            br = total(c, r, sy1, ry1)
            xb = tokv[g, :]
            x = xb.astype(F32)
            ha = br * mean_sq(br, D)
            mix = x + alv[0:1, :] * (ha - x)
            tokv[g, :] = (mix * mean_sq(mix, D)).astype(BF)

        rows_then_share(0, c, rows, tokv)
        shared(0, c, tokv)
        r = rows_at(c * TB, TB)

        def units(n):
            cu, cv = rows_at(n * 256, 256), rows_at(F + n * 256, 256)
            x = tokv[r, :]
            u = nn(x, wgv[:, cu])
            v = nn(x, wgv[:, cv])
            gu[r, cu] = u.astype(BF)
            gu[r, cv] = v.astype(BF)
            us = u * sml[0:1, cu]
            vs = v * sml[1:2, cu]
            act[r, cu] = (us * vs * jax.nn.sigmoid(vs)).astype(BF)

        loop(F // 256, units)

        @pl.when(i == 0)
        def _():
            w_next(3, 0, 3)
            for st in range(B):
                w_next(4, st, 3, False)

        @pl.when(i == 1)
        def _():
            w_ready(3)
            w_local(4).wait()

        @pl.when(i > 0)
        def _():
            down_chunk(i - 1)

    def down_chunk(i):
        c = nc - 1 - i
        exchange(1, c, lambda rr, cols: nt(act[rr, :], wdv[cols, :]), sy2, ry2)

    w_next(3, 0, 2)
    for st in range(B):
        w_next(4, st, 2, False)
    loop(nc, feed_chunk)
    down_chunk(nc - 1)
    go_local.wait()
    for cp in go_copies:
        cp.wait()

    def grad_rows(c):
        return local(goh.at[c], gst, lsem.at[12])

    grad_rows(nc - 1).start()

    def back_chunk(i):
        c = nc - 1 - i
        landed(1, c, sy2, ry2)
        grad_rows(c).wait()
        base = c * TB + core * TH

        def rows(t):
            r = rows_at(t * RT, RT)
            g = rows_at(base + t * RT, RT)
            am = alv[1:2, :]
            bm = total(c, r, sy2, ry2)
            h = tokv[g, :].astype(F32)
            rm = mean_sq(bm, D)
            hm = bm * rm
            diff = hm - h
            mix = h + am * diff
            r2 = mean_sq(mix, D)
            fin = mix * r2
            fst[r, :] = fin.astype(BF)
            go = gst[r, :].astype(F32)
            gm = r2 * (go - fin * (jnp.sum(go * fin, axis=1, keepdims=True) * (1.0 / D)))
            gacc[8:16, :] += fold(gm * diff)
            gh = am * gm
            ghid[c, r, :] = (gm - gh).astype(BF)
            gb = rm * (gh - hm * (jnp.sum(gh * hm, axis=1, keepdims=True) * (1.0 / D)))
            gml[g, :] = gb.astype(BF)

        rows_then_share(1, c, rows, gml)

        @pl.when(c > 0)
        def _():
            grad_rows(jnp.maximum(c - 1, 0)).start()

        og = rows_at(base, TH)
        o_here = local(fst.at[:, mine], out.at[og], lsem.at[6])
        o_here.start()
        o_there = remote(
            fst.at[:, feat(y * 2 + mate)], out.at[og], out_s.at[c], out_r.at[c], peer
        )
        o_there.start()
        shared(1, c, gml)
        r = rows_at(c * TB, TB)

        def units(n):
            cu, cv = rows_at(n * 256, 256), rows_at(F + n * 256, 256)
            ga = nn(gml[r, :], wdv[:, cu])
            u = gu[r, cu].astype(F32)
            v = gu[r, cv].astype(F32)
            su, sv = sml[0:1, cu], sml[1:2, cu]
            us, vs = u * su, v * sv
            sg = jax.nn.sigmoid(vs)
            si = vs * sg
            g_u = ga * si
            g_v = ga * us * (sg + si - si * sg)
            gsacc[0:8, cu] += fold(g_u * u)
            gsacc[8:16, cu] += fold(g_v * v)
            gu[r, cu] = (g_u * su).astype(BF)
            gu[r, cv] = (g_v * sv).astype(BF)

        loop(F // 256, units)
        exchange(2, c, lambda rr, cols: nt(gu[rr, :], wgv[cols, :]), sy2, ry3)
        o_here.wait()
        o_there.wait()

    loop(nc, back_chunk)

    RA, AR, w = D // A, A * R, F // 2
    pieces = []
    for src, r1, r2, cuts in (
        (gwd_h, r1d_h, r2d_h, (0, w, 2 * w)),
        (gwg_h, r1g_h, r2g_h, (0, w, 2 * w, 3 * w, 4 * w)),
        (gqo_h, r1q_h, r2q_h, (0, 2 * C, 3 * C, 4 * C)),
    ):
        for n in range(len(cuts) - 1):
            pieces.append((src, r1, r2, slice(cuts[n], cuts[n + 1])))
    lanes_of = (0, 1, 3, 0, 1, 3, 1, 3, 0)

    def px_copy(p, k):
        src, r1, _, cols = pieces[p]
        return remote(
            src.at[(b + k) % B, :, cols], r1.at[k - 1, :, cols], p_s.at[p, k - 1], p_r.at[p, k - 1], xpeer(k)
        )

    def rs_start(p):
        for k in range(1, B):
            px_copy(p, k).start()

    def slot(p):
        cols = pieces[p][3]
        return slice(lanes_of[p] * w, lanes_of[p] * w + cols.stop - cols.start)

    def sums(p, aa):
        return gu.at[pl.ds(pl.multiple_of(D + aa * R, R), R), slot(p)]

    def pz_copy(p, k):
        _, _, r2, cols = pieces[p]
        return remote(
            sums(p, (a + k) % A), r2.at[k - 1, :, cols], q_s.at[p, k - 1], q_r.at[p, k - 1], zpeer(k)
        )

    def own_load(p):
        src, _, _, cols = pieces[p]
        return local(src.at[b, :, cols], gu.at[0:AR, slot(p)], rsem.at[lanes_of[p], 0])

    def first_load(p, k):
        _, r1, _, cols = pieces[p]
        return local(
            r1.at[k - 1, :, cols], gu.at[k * AR : (k + 1) * AR, slot(p)], rsem.at[lanes_of[p], k]
        )

    def rs_load(p):
        own_load(p).start()
        for k in range(1, B):
            px_copy(p, k).wait()
            first_load(p, k).start()

    def rs_add(p):
        own_load(p).wait()
        for k in range(1, B):
            first_load(p, k).wait()
        for k in list(range(1, A)) + [0]:
            aa = (a + k) % A
            t = gu[rows_at(aa * R, R), slot(p)].astype(F32)
            for kk in range(1, B):
                t = t + gu[pl.ds(pl.multiple_of(kk * AR + aa * R, R), R), slot(p)].astype(F32)
            gu[pl.ds(pl.multiple_of(D + aa * R, R), R), slot(p)] = t.astype(BF)
            if k:
                pz_copy(p, k).start()

    def second_load(p, k):
        _, _, r2, cols = pieces[p]
        return local(
            r2.at[k - 1, :, cols], gu.at[D + AR + (k - 1) * R : D + AR + k * R, slot(p)], rsem.at[lanes_of[p], B + k]
        )

    def end_load(p):
        for k in range(1, A):
            pz_copy(p, k).wait()
            second_load(p, k).start()

    def rs_end(p, res):
        for k in range(1, A):
            second_load(p, k).wait()
        width = pieces[p][3].stop - pieces[p][3].start
        t = gu[pl.ds(pl.multiple_of(D + a * R, R), R), slot(p)].astype(F32)
        for k in range(1, A):
            t = t + gu[D + AR + (k - 1) * R : D + AR + k * R, slot(p)].astype(F32)
        fstage[:, 0:width] = t
        cp = local(fstage.at[:, 0:width], res, lsem.at[0])
        cp.start()
        cp.wait()

    def rs_finish(p):
        if p < 2:
            res = owd.at[:, p * w : p * w + w]
        elif p < 6:
            res = owg.at[:, (p - 2) * w : (p - 1) * w]
        elif p == 6:
            res = owq.at[:, 0 : 2 * C]
        elif p == 7:
            res = owq.at[:, 2 * C : 3 * C]
        else:
            res = owo
        rs_end(p, res)

    def tile_out(half, dst, t):
        src = wst.at[:, :, half * F : half * F + F]
        return local(src, dst.at[:, rows_at(t * R, R), half * F : half * F + F], lsem.at[1 + half])

    def down_out(half, t):
        src = wst.at[:, :, half * F : half * F + F]
        return local(src, gwd_h.at[:, rows_at(t * R, R)], lsem.at[1 + half])

    def down_tile(t):
        for half in range(2):
            tt = 2 * t + half

            @pl.when(t > 0)
            def _():
                down_out(half, tt).wait()

            cols = rows_at(tt * RA, RA)
            wst[:, :, half * F : half * F + F] = tdot(gml[:, cols], act[...]).astype(BF).reshape(B, R, F)
            down_out(half, tt).start()

    lt_first = local(tokf.at[rows_at((nc - 1) * TB + core * TH, TH)], gst, lsem.at[6])
    lt_first.start()
    loop(A // 2, down_tile)
    for half in range(2):
        down_out(half, 0).wait()
    rs_start(0)

    def up_tile(t):
        cols = rows_at(t * RA, RA)
        lhs = tokv[:, cols]
        for half in range(2):

            @pl.when(t > 0)
            def _():
                tile_out(half, gwg_h, t).wait()

            wst[:, :, half * F : half * F + F] = (
                tdot(lhs, gu[:, half * F : half * F + F]).astype(BF).reshape(B, R, F)
            )
            tile_out(half, gwg_h, t).start()

        @pl.when(t == A // 2)
        def _():
            rs_start(1)

    loop(A, up_tile)
    for half in range(2):
        tile_out(half, gwg_h, 0).wait()
    rs_start(2)
    rs_start(3)
    rs_load(0)
    qv, kv, vv = gml.at[:, 0:C], gml.at[:, C : 2 * C], gml.at[:, 2 * C : 3 * C]
    gv = gml.at[:, 3 * C : 4 * C]
    rot0 = 2 * w
    loads = [
        local(qkv_h, gml.at[:, 0 : 3 * C], lsem.at[7]),
        local(rot_h, gu.at[:, rot0 : rot0 + 2 * C], lsem.at[8]),
        local(tokf, tokv, lsem.at[9]),
    ]
    for cp in loads:
        cp.start()
    dk[...] = jnp.zeros_like(dk)
    dv[...] = jnp.zeros_like(dv)
    gsq[...] = jnp.zeros_like(gsq)
    heads = lax.broadcasted_iota(jnp.int32, (8, C), 0)
    lanes = lax.broadcasted_iota(jnp.int32, (8, C), 1) // DK
    pick = jnp.where(heads == lanes, 1.0, 0.0).astype(BF)
    for cp in loads[:2]:
        cp.wait()
    NY = ny * CF

    def gin_copy(c, hs):
        return remote(
            sc.at[hs * TH : (hs + 1) * TH, 0:NY], rc.at[c, :, hs * NY : (hs + 1) * NY], c_s.at[c, hs],
            c_r.at[c, hs], peer,
        )

    def gin_y(c, k, hs):
        src = slice((hs * (ny - 1) + k - 1) * CF, (hs * (ny - 1) + k) * CF)
        dst = slice(hs * CF, hs * CF + CF)
        return remote(
            sy2.at[c, :, src], ry2.at[k - 1, c, :, dst], yg_s.at[c, k - 1, hs], yg_r.at[c, k - 1, hs],
            ypeer(k, core),
        )

    n128 = CF // 128

    def gin_take(c):
        for hs in range(2):
            gin_copy(c, hs).wait()
            for k in range(ny):
                for q in range(n128):
                    col = hs * NY + k * CF + q * 128
                    t = acc[k * n128 + q, hs * TH : (hs + 1) * TH, :] + rc[c, :, col : col + 128].astype(F32)
                    if k == 0:
                        dk[rows_at(c * TB + hs * TH, TH), q * 128 : q * 128 + 128] = t
                    else:
                        col = (hs * (ny - 1) + k - 1) * CF + q * 128
                        sy2[c, :, col : col + 128] = t.astype(BF)
            for k in range(1, ny):
                gin_y(c, k, hs).start()

    def out_tiles():
        def o_tile(t):
            cols = rows_at(t * RA, RA)
            wst[:, :, 0:C] = tdot(gba[:, cols], attn[...]).astype(BF).reshape(B, R, C)
            cp = local(wst.at[:, :, 0:C], gqo_h.at[:, rows_at(t * R, R), 3 * C : 4 * C], lsem.at[1])
            cp.start()
            cp.wait()

        loop(A, o_tile)

    def kept_rows(c):
        return local(tokf.at[rows_at(c * TB + core * TH, TH)], gst, lsem.at[6])

    def branch_rows(c):
        base = c * TB + core * TH
        landed(2, c, sy2, ry3)
        kept_rows(c).wait()

        def rows(t):
            r = rows_at(t * RT, RT)
            g = rows_at(base + t * RT, RT)
            aa = alv[0:1, :]
            br = total(c, r, sy1, ry1)
            x = gst[r, :].astype(F32)
            ra = mean_sq(br, D)
            ha = br * ra
            diff = ha - x
            mix = x + aa * diff
            r1 = mean_sq(mix, D)
            hid = mix * r1
            gh = ghid[c, r, :].astype(F32) + total(c, r, sy2, ry3)
            gm = r1 * (gh - hid * (jnp.sum(gh * hid, axis=1, keepdims=True) * (1.0 / D)))
            gacc[0:8, :] += fold(gm * diff)
            gt = aa * gm
            ghid[c, r, :] = (gm - gt).astype(BF)
            gb = ra * (gt - ha * (jnp.sum(gt * ha, axis=1, keepdims=True) * (1.0 / D)))
            gba[g, :] = gb.astype(BF)

        rows_then_share(2, c, rows, gba)

        @pl.when(c > 0)
        def _():
            kept_rows(jnp.maximum(c - 1, 0)).start()

    branch_rows(nc - 1)
    rs_add(0)

    def attn_grad_chunk(i):
        c = nc - 1 - i
        shared(2, c, gba)

        @pl.when(c > 0)
        def _():
            branch_rows(jnp.maximum(c - 1, 0))

        r = rows_at(c * TB, TB)
        g = nn(gba[r, :], wqov[:, 3 * C : 4 * C]).astype(BF)
        gv[r, :] = g
        prod = g.astype(F32) * attn[r, :].astype(F32)
        ph = prod.astype(BF)
        dl[:, r] = nt(pick, ph) + nt(pick, (prod - ph.astype(F32)).astype(BF))

        def between():
            @pl.when(i == 0)
            def _():
                rs_load(1)

            @pl.when(i == 1)
            def _():
                rs_add(2)

        attn_bwd_block(c, TB, H, qv, kv, vv, gv, ll, dl, off_bias, dq, dk, dv, between)

        @pl.when(i == 0)
        def _():
            rs_add(1)
            rs_start(4)

        @pl.when(i == 1)
        def _():
            rs_load(3)
            end_load(0)

        @pl.when(i == 2)
        def _():
            rs_load(4)
            end_load(1)

        @pl.when(i == nc - 1)
        def _():
            rs_load(5)
            end_load(2)
            out_tiles()
            rs_start(8)

        cs, sn = angles_of(r)
        for part in range(2):
            gh = (dq[...] if part == 0 else dk[r, :]) * 8.0
            t = gu[r, rot0 + part * C : rot0 + part * C + C].astype(F32)
            inv = lax.rsqrt(split_dot(t * t, ones) + epsilon)
            un = t * inv
            gsq[...] += fold(gh * un)
            gh = gh * sq[...]
            gr = inv * (gh - un * split_dot(gh * un, ones))
            act[r, part * C : part * C + C] = turn(gr, cs, sn, -1.0).astype(BF)
        act[r, 2 * C : 3 * C] = dv[r, :].astype(BF)

        def product(hsel, k, cc):
            rr = rows_at(c * TB + hsel * TH, TH)
            cols = feat(((y + k) % ny) * 2 + cc)
            t = nt(act[rr, 0 : 3 * C], wqov[cols, 0 : 3 * C])
            if k == 0:
                t = t + jnp.where(hsel == core, 1.0, 0.0) * ghid[c, :, cols].astype(F32)
            return t

        @pl.when(i > 0)
        def _():
            gin_take(jnp.minimum(c + 1, nc - 1))

        for hs in range(2):
            for k in range(ny):
                sc[hs * TH : (hs + 1) * TH, k * CF : (k + 1) * CF] = product(hs, k, mate).astype(BF)
            gin_copy(c, hs).start()
        for hs in range(2):
            for k in range(ny):
                t = product(hs, k, core)
                for q in range(n128):
                    acc[k * n128 + q, hs * TH : (hs + 1) * TH, :] = t[:, q * 128 : q * 128 + 128]

        @pl.when(i == 0)
        def _():
            rs_start(5)
            rs_load(2)

        @pl.when(i == 1)
        def _():
            rs_finish(0)
            rs_add(3)

        @pl.when(i == 2)
        def _():
            rs_finish(1)
            rs_add(4)

        @pl.when(i == nc - 1)
        def _():
            rs_finish(2)
            rs_add(5)
            end_load(3)

    loop(nc, attn_grad_chunk)
    ga_there = remote(gacc.at[:, feat(y * 2 + mate)], gar, m_s.at[0], m_r.at[0], peer)
    ga_there.start()
    loads[2].wait()

    def q_out(half, t):
        src = wst.at[:, :, half * F : half * F + 2 * C]
        return local(src, gqo_h.at[:, rows_at(t * R, R), 0 : 2 * C], lsem.at[1 + half])

    def q_tile(t):
        for half in range(2):
            tt = 2 * t + half

            @pl.when(t > 0)
            def _():
                q_out(half, tt).wait()

            g = tdot(tokv[:, rows_at(tt * RA, RA)], act[:, 0 : 2 * C]).astype(BF)
            wst[:, :, half * F : half * F + 2 * C] = g.reshape(B, R, 2 * C)
            q_out(half, tt).start()

    loop(A // 2, q_tile)
    for half in range(2):
        q_out(half, 0).wait()
    rs_start(6)

    def v_out(half, t):
        src = wst.at[:, :, half * F : half * F + C]
        return local(src, gqo_h.at[:, rows_at(t * R, R), 2 * C : 3 * C], lsem.at[1 + half])

    def v_tile(t):
        for half in range(2):
            tt = 2 * t + half

            @pl.when(t > 0)
            def _():
                v_out(half, tt).wait()

            g = tdot(tokv[:, rows_at(tt * RA, RA)], act[:, 2 * C : 3 * C]).astype(BF)
            wst[:, :, half * F : half * F + C] = g.reshape(B, R, C)
            v_out(half, tt).start()

    loop(A // 2, v_tile)
    for half in range(2):
        v_out(half, 0).wait()
    rs_start(7)
    gin_take(0)
    rs_finish(3)
    rs_load(8)
    ga_there.wait()
    vec[...] = jnp.zeros_like(vec)
    gt = gacc[:, mine] + gar[...]
    vec[0:1, 0:F] = jnp.sum(gsacc[0:8, :], axis=0, keepdims=True)
    vec[1:2, 0:F] = jnp.sum(gsacc[8:16, :], axis=0, keepdims=True)
    vec[2:3, 0:CF] = jnp.sum(gt[0:8], axis=0, keepdims=True)
    vec[3:4, 0:CF] = jnp.sum(gt[8:16], axis=0, keepdims=True)
    vec[4:5, 0:C] = jnp.sum(gsq[...], axis=0, keepdims=True)
    vx = [remote(vec, rv1.at[k - 1], m_s.at[k], m_r.at[k], xpeer(k)) for k in range(1, B)]
    for cp in vx:
        cp.start()
    rs_add(8)
    end_load(4)
    for cp in vx:
        cp.wait()
    t = vec[...]
    for k in range(B - 1):
        t = t + rv1[k]
    vec[...] = t
    vz = [
        remote(vec, rv2.at[k - 1], m_s.at[B - 1 + k], m_r.at[B - 1 + k], zpeer(k)) for k in range(1, A)
    ]
    for cp in vz:
        cp.start()

    rs_finish(4)
    end_load(5)

    def gin_end(i):
        c = nc - 1 - i
        for hs in range(2):
            rr = rows_at(c * TB + hs * TH, TH)
            for k in range(1, ny):
                gin_y(c, k, hs).wait()
                dk[rr, :] += ry2[k - 1, c, :, hs * CF : hs * CF + CF].astype(F32)

    loop(nc, gin_end)
    ends = [local(dk, gin_o, lsem.at[10])]
    ends[-1].start()
    rs_load(6)
    rs_add(6)
    rs_finish(5)
    rs_load(7)
    rs_add(7)
    end_load(8)
    for cp in vz:
        cp.wait()
    t = vec[...]
    for k in range(A - 1):
        t = t + rv2[k]
    vec[...] = t
    ends.append(local(vec, vec_o, lsem.at[11]))
    ends[-1].start()
    for p in range(6):
        w_sent(p, p != 4)
    rs_finish(8)
    end_load(6)
    rs_finish(6)
    end_load(7)
    rs_finish(7)
    for cp in ends:
        cp.wait()


def run_layer(z, live, tokens, gout, wqo, wg, wd, alpha, table, sq, sml):
    T, C, CF, F, D, H = z.T, z.C, z.CF, z.F, z.D, z.H
    nc, TB, TH, R, A, B, ny, mp = z.nc, z.TB, z.TH, z.R, z.A, z.B, z.ny, z.mp
    S = jax.ShapeDtypeStruct
    hbm = pl.BlockSpec(memory_space=pltpu.HBM)
    vm = pl.BlockSpec(memory_space=pltpu.VMEM)
    W = max(F, CF, C)
    AR = A * R
    outs = [
        S((T, CF), BF), S((T, CF), F32), S((R, 3 * C), F32), S((R, C), F32), S((R, 2 * F), F32), S((R, F), F32),
        S((8, W), F32),
        S((T, 3 * C), BF), S((T, 2 * C), BF), S((T, D), BF), S((nc, TH, D), BF),
    ]
    widths = (F, 2 * F, 4 * C)
    outs += [S((B, AR, n), BF) for n in widths]
    outs += [S((max(B - 1, 1), AR, n), BF) for n in widths]
    outs += [S((max(A - 1, 1), R, n), BF) for n in widths]
    V = pltpu.VMEM
    scratch = [
        V((T, D), BF), V((D, 4 * C), BF), V((D, 2 * F), BF), V((D, F), BF),
        V((T, D), BF), V((T, F), BF), V((T, 2 * F), BF), V((T, D), BF),
        V((T, C), BF), V((8, T), F32), V((8, T), F32), V((max(H, ny * CF // 128), TB, 128), F32),
        V((T, C), F32), V((T, C), F32), V((TB, C), F32), V((R, F // 2), F32),
    ]
    for _ in range(2):
        scratch += [V((nc, TH, D), BF), V((ny - 1, nc, TH, D), BF)]
    scratch += [
        V((ny - 1, nc, TH, D), BF), V((nc, TH, D), BF), V((TB, D), BF), V((nc, TH, D), BF), V((TH, D), BF), V((TH, D), BF),
        V((B, R, 2 * F), BF), V((8, D), F32), V((16, D), F32), V((16, F), F32), V((8, C), F32), V((16, CF), F32),
        V((8, W), F32), V((max(B - 1, 1), 8, W), F32), V((max(A - 1, 1), 8, W), F32),
    ]
    sem = pltpu.SemaphoreType.DMA
    for shape in (
        (nc, 2 * ny - 1), (6, B, 2, max(A - 1, 1)), (6, A, max(B - 1, 1)), (mp - 1,), (mp - 1,), (3, nc, 2),
        (3, nc, ny - 1, 2), (3, nc, 2), (nc,), (9, max(B - 1, 1)), (9, max(A - 1, 1)), (nc, 2), (nc, ny - 1, 2),
        (A + B - 1,),
    ):
        scratch += [sem(shape), sem(shape)]
    scratch += [sem((22,)), sem((4, A + B))]
    return pl.pallas_call(
        functools.partial(layer, z),
        out_shape=outs,
        in_specs=[pl.BlockSpec(memory_space=pltpu.SMEM)] + [hbm] * 6 + [vm] * 3,
        out_specs=[hbm] * len(outs),
        scratch_shapes=scratch,
        compiler_params=pltpu.CompilerParams(
            collective_id=0, has_side_effects=True, vmem_limit_bytes=64 * 2**20 - 2**19
        ),
        name="layer",
    )(live, tokens, gout.reshape(nc, 2, TH, CF), wqo, wg, wd, alpha, table, sq, sml)


def tables(T):
    half = DK // 2
    frequency = np.float32(theta_base) ** (np.float32(-2.0 / DK) * np.arange(half, dtype=np.float32))
    grid = np.arange(T, dtype=np.float32)[:, None] * frequency[None, :].astype(np.float32)
    cos, sin = np.cos(grid, dtype=np.float32), np.sin(grid, dtype=np.float32)
    return np.concatenate([cos, cos, sin, sin], axis=1)


def on_device(
    sizes,
    tokens,
    w_qkv,
    w_out,
    w_gate_up,
    w_down,
    s_qk,
    alpha_attn,
    alpha_mlp,
    s_mlp,
    doc_lengths,
    grad_out,
):
    T, CF = tokens.shape
    H = s_qk.shape[1]
    C = H * DK
    F = w_down.shape[1]
    z = Sizes(sizes, T, C, CF, F, doc_lengths.shape[1])
    D, R = z.D, z.R
    table = jnp.asarray(tables(T))
    scale = s_qk.T.reshape(1, C)
    sml = s_mlp.transpose(1, 2, 0).reshape(2, F)
    alpha = jnp.pad(
        jnp.stack([alpha_attn.T.reshape(-1), alpha_mlp.T.reshape(-1)]), ((0, 6), (0, 0))
    )
    whole = doc_lengths[0, 0] == T
    live = whole.astype(F32).reshape(1)
    (out, grad_in, gw_qkv, gw_out, gw_gu, gw_down, vec) = run_layer(
        z, live, tokens, grad_out, jnp.concatenate([w_qkv.reshape(R, 3 * C), w_out], axis=1),
        w_gate_up.reshape(R, 2 * F), w_down, alpha, table, scale, sml,
    )[:7]
    d, m = place()

    def channel_rows(v, per_head):
        n = per_head // z.dp
        return lax.dynamic_slice_in_dim(v.reshape(H, per_head).T, d * n, n, 0)

    gs = jnp.stack([channel_rows(vec[i, 0:F], F // H) for i in range(2)], axis=1)
    return (
        out,
        grad_in,
        gw_qkv.reshape(R, 3, C),
        gw_out,
        gw_gu.reshape(R, 2, F),
        gw_down,
        channel_rows(vec[4, 0:C], DK),
        channel_rows(vec[2, 0:CF], DK),
        channel_rows(vec[3, 0:CF], DK),
        gs,
    )


def solution(mesh):
    placed = (
        P("dp", "mp"),
        P("dp", None, "mp"),
        P("dp", "mp"),
        P("dp", None, "mp"),
        P("dp", "mp"),
        P(None, "mp"),
        P(None, "mp"),
        P(None, "mp"),
        P(None, None, "mp"),
        P("dp", None),
        P("dp", "mp"),
    )
    return jax.shard_map(
        functools.partial(on_device, dict(mesh.shape)),
        mesh=mesh,
        in_specs=placed,
        out_specs=(
            P("dp", "mp"),
            P("dp", "mp"),
            P("dp", None, "mp"),
            P("dp", "mp"),
            P("dp", None, "mp"),
            P("dp", "mp"),
            P("dp", "mp"),
            P("dp", "mp"),
            P("dp", "mp"),
            P("dp", None, "mp"),
        ),
        check_vma=False,
    )
```

```python
import functools
import math

import jax
import jax.numpy as jnp
import numpy as np
from jax import lax
from jax.experimental import pallas as pl
from jax.experimental.pallas import tpu as pltpu
from jax.sharding import PartitionSpec as P

DK = 64
epsilon = 1e-06
theta_base = 10000.0


LC=math.sqrt(DK)*math.log2(math.e)
NEG=-1e30
def nt(a,b): return lax.dot_general(a,b,(((1,),(1,)),((),())),preferred_element_type=jnp.float32)
def nn(a,b): return jnp.dot(a,b,preferred_element_type=jnp.float32)
def head_mask(x,h):
    lane=lax.broadcasted_iota(jnp.int32,x.shape,1)
    return jnp.where((lane//DK)==(h%2), x, jnp.zeros_like(x))
def attn_fwd_block(i, TB, H, ref, C, live, acc):
    hb=TB//2
    qs=pl.ds(pl.multiple_of(i*TB,TB),TB)
    def vx(h,ks):
        v=ref[ks,pl.ds(2*C+(h//2)*128,128)]
        lane=lax.broadcasted_iota(jnp.int32,v.shape,1)
        return jnp.where((lane//DK)==(h%2),v,jnp.ones_like(v))
    def tile(h,qsl,ks,tri):
        p2=pl.ds((h//2)*128,128)
        x=nt(ref[qsl,p2],head_mask(ref[ks,pl.ds(C+(h//2)*128,128)],h))
        if tri:
            r=lax.broadcasted_iota(jnp.int32,x.shape,0); c=lax.broadcasted_iota(jnp.int32,x.shape,1)
            x=jnp.where(c<=r,x,NEG)
        p=jnp.exp2(x*LC).astype(jnp.bfloat16)
        return nn(p,vx(h,ks))
    k0=pl.ds(pl.multiple_of(i*TB,hb),hb); k1=pl.ds(pl.multiple_of(i*TB+hb,hb),hb)
    for h in range(H):
        a0=tile(h,qs,k0,True)
        a1=tile(h,k1,k1,True)
        acc[h,0:hb]=a0[0:hb]; acc[h,hb:TB]=a0[hb:TB]+a1
    def body(j,_):
        ks=pl.ds(pl.multiple_of(j*TB,TB),TB)
        for h in range(H):
            acc[h]+=live*tile(h,qs,ks,False)
        return 0
    lax.fori_loop(0,i,body,0)
def tdot(a,b): return lax.dot_general(a,b,(((0,),(0,)),((),())),preferred_element_type=jnp.float32)
def attn_bwd_block(i, TB, H, q_ref, k_ref, v_ref, g_ref, ll_ref, dl_ref, ob, dq, dk, dv, between):
    qs=pl.ds(pl.multiple_of(i*TB,TB),TB); hb=TB//2
    qz=[head_mask(q_ref[qs,pl.ds((h//2)*128,128)],h) for h in range(H)]
    gz=[head_mask(g_ref[qs,pl.ds((h//2)*128,128)],h) for h in range(H)]
    lr=[ll_ref[pl.ds(h,1),qs] for h in range(H)]
    dr=[dl_ref[pl.ds(h,1),qs] for h in range(H)]
    def tile(h,ks,qv,gv,lb,dd,tri):
        p2=pl.ds((h//2)*128,128)
        x=nt(k_ref[ks,p2],qv)*LC-lb
        dp=nt(v_ref[ks,p2],gv)
        if tri:
            r=lax.broadcasted_iota(jnp.int32,x.shape,0); c=lax.broadcasted_iota(jnp.int32,x.shape,1)
            x=jnp.where(r<=c,x,NEG)
        p=jnp.exp2(x)
        ds=(p*(dp-dd)).astype(jnp.bfloat16)
        dvp=nn(p.astype(jnp.bfloat16),gv)
        dkp=nn(ds,qv)
        dqp=tdot(ds,head_mask(k_ref[ks,p2],h))
        return dqp,dkp,dvp
    k0=pl.ds(pl.multiple_of(i*TB,hb),hb); k1=pl.ds(pl.multiple_of(i*TB+hb,hb),hb)
    for pr in range((H+1)//2):
        p2=pl.ds(pr*128,128)
        dk0=dv0=dk1=dv1=0; q0=q1=0
        for h in range(2*pr,min(2*pr+2,H)):
            a,b,c=tile(h,k0,qz[h],gz[h],lr[h],dr[h],True)
            a1,b1,c1=tile(h,k1,qz[h][hb:],gz[h][hb:],lr[h][:,hb:],dr[h][:,hb:],True)
            q0+=a[0:hb]; q1+=a[hb:]+a1
            dk0+=b; dv0+=c; dk1+=b1; dv1+=c1
        dq[0:hb,p2]=q0; dq[hb:TB,p2]=q1
        dk[k0,p2]+=dk0; dv[k0,p2]+=dv0; dk[k1,p2]+=dk1; dv[k1,p2]+=dv1
    between()
    lo=[l-ob for l in lr]
    def body(j,_):
        ks=pl.ds(pl.multiple_of(j*TB,TB),TB)
        for pr in range((H+1)//2):
            p2=pl.ds(pr*128,128)
            dka=dva=dqa=0
            for h in range(2*pr,min(2*pr+2,H)):
                a,b,c=tile(h,ks,qz[h],gz[h],lo[h],dr[h],False)
                dqa+=a; dka+=b; dva+=c
            dq[:,p2]+=dqa
            dk[ks,p2]+=dka; dv[ks,p2]+=dva
        return 0
    lax.fori_loop(0,i,body,0)


MESH = pl.DeviceIdType.MESH
F32, BF = jnp.float32, jnp.bfloat16


class Sizes:
    def __init__(self, mesh_shape, T, C, CF, F, pieces):
        self.mp, self.dp = mesh_shape["mp"], mesh_shape["dp"]
        self.ny = self.mp // 2
        self.A = 4 if self.dp % 4 == 0 else 1
        self.B = self.dp // self.A
        self.T, self.C, self.CF, self.F = T, C, CF, F
        self.D = CF * self.mp
        self.H = C // DK
        self.nc = pieces
        self.TB = T // pieces
        self.TH = self.TB // 2
        self.R = self.D // self.dp


def place():
    return lax.axis_index("dp"), lax.axis_index("mp")


def remote(src, dst, ss, rs, dev):
    return pltpu.make_async_remote_copy(
        src, dst, send_sem=ss, recv_sem=rs, device_id=dev, device_id_type=MESH
    )


def local(src, dst, sem):
    return pltpu.make_async_copy(src, dst, sem)


def rows_at(start, size):
    return pl.ds(pl.multiple_of(start, size), size)


def loop(n, fn):
    def body(i, carry):
        fn(i)
        return carry

    lax.fori_loop(0, n, body, 0)


def fold(x):
    return jnp.sum(x.reshape(x.shape[0] // 8, 8, x.shape[1]), axis=0)


def mean_sq(x, D):
    return lax.rsqrt(jnp.sum(x * x, axis=1, keepdims=True) * (1.0 / D) + epsilon)


def split_dot(x, ones):
    hi = x.astype(BF)
    return nn(hi, ones) + nn((x - hi.astype(F32)).astype(BF), ones)


def head_ones(width):
    i = lax.broadcasted_iota(jnp.int32, (width, width), 0) // DK
    j = lax.broadcasted_iota(jnp.int32, (width, width), 1) // DK
    return jnp.where(i == j, 1.0, 0.0).astype(BF)


def turn(x, cosine, sine, sign):
    lane = lax.broadcasted_iota(jnp.int32, x.shape, 1)
    first = (lane % DK) < DK // 2
    other = jnp.where(first, -pltpu.roll(x, x.shape[1] - DK // 2, 1), pltpu.roll(x, DK // 2, 1))
    return x * cosine + sign * other * sine


def layer(
    z,
    live_ref, tokens, gout, wqo, wg, wd, alpha, table, sq, sml,
    out, gin_o, owq, owo, owg, owd, vec_o,
    qkv_h, rot_h, tokf, goh, gwd_h, gwg_h, gqo_h, r1d_h, r1g_h, r1q_h, r2d_h, r2g_h, r2q_h,
    tokv, wqov, wgv, wdv, gml, act, gu, gba, attn, ll, dl, acc, dk, dv, dq, fstage,
    sy1, ry1, sy2, ry2, ry3, rc, sc, ghid, gst, fst, wst, alv, gacc, gsacc, gsq, gar, vec, rv1, rv2,
    tok_s, tok_r, w_s, w_r, x_s, x_r, al_s, al_r, go_s, go_r, ex_s, ex_r, y_s, y_r, hc_s, hc_r, out_s, out_r,
    p_s, p_r, q_s, q_r, c_s, c_r, yg_s, yg_r, m_s, m_r, lsem, rsem,
):
    T, C, CF, F, D, H = z.T, z.C, z.CF, z.F, z.D, z.H
    nc, TB, TH, R, A, B, ny, mp = z.nc, z.TB, z.TH, z.R, z.A, z.B, z.ny, z.mp
    d, m = place()
    a, b = d // B, d % B
    y, core = m // 2, m % 2
    mate = 1 - core
    peer = (d, y * 2 + mate)

    def ypeer(k, cc):
        return (d, ((y + k) % ny) * 2 + cc)

    zpeer = lambda k: (((a + k) % A) * B + b, m)
    xpeer = lambda k: (a * B + (b + k) % B, m)
    others = [peer] + [ypeer(k, cc) for k in range(1, ny) for cc in (core, mate)]
    everyone = others + [zpeer(k) for k in range(1, A)] + [xpeer(k) for k in range(1, B)]
    bar = pltpu.get_barrier_semaphore()
    for dev in everyone:
        pl.semaphore_signal(bar, 1, device_id=dev, device_id_type=MESH)
    pl.semaphore_wait(bar, len(everyone))

    live = live_ref[0]
    off_bias = jnp.where(live > 0.5, 0.0, NEG)
    feat = lambda mm: pl.ds(pl.multiple_of(mm * CF, CF), CF)
    mine = feat(m)


    def tok_own(c, i, dev):
        r = rows_at(c * TB, TB)
        return remote(tokens.at[r], tokv.at[r, mine], tok_s.at[c, i], tok_r.at[c, i], dev)

    def tok_got(c, i, mm):
        r = rows_at(c * TB, TB)
        return remote(tokv.at[r, feat(mm)], tokv.at[r, feat(mm)], tok_s.at[c, i], tok_r.at[c, i], peer)

    def start_tok(i):
        c = nc - 1 - i
        for k in range(1, ny):
            tok_own(c, k, ypeer(k, core)).start()
        tok_own(c, 0, peer).start()

    lo, hi = slice(0, F), slice(F, 2 * F)
    dlo, dhi = slice(0, F // 2), slice(F // 2, F)
    weights = [
        (wqo.at[:, 0 : 2 * C], wqov.at[:, 0 : 2 * C]),
        (wg.at[:, lo], wgv.at[:, lo]),
        (wg.at[:, hi], wgv.at[:, hi]),
        (wd.at[:, dlo], wdv.at[:, dlo]),
        (wd.at[:, dhi], wdv.at[:, dhi]),
        (wqo.at[:, 2 * C : 4 * C], wqov.at[:, 2 * C : 4 * C]),
    ]

    def shard(aa, bb):
        return rows_at((aa * B + bb) * R, R)

    def column(st):
        return (b - st + B) % B

    def z_moves(w, st, h):
        src, dst = weights[w]
        moves = []
        for way, step in ((0, 1), (1, -1)):
            aa = a - step * (h - 1)
            ok = (a + step >= 0) & (a + step < A) & (aa >= 0) & (aa < A)
            moves.append((way, step, jnp.clip(aa, 0, A - 1), ok))
        return src, dst, moves

    def z_copy(w, st, h, way, step, aa):
        src, dst = weights[w]
        r = shard(aa, column(st))
        source = src if (h == 1 and st == 0) else dst.at[r]
        to = jnp.clip(a + step, 0, A - 1) * B + b
        return remote(source, dst.at[r], w_s.at[w, st, way, h - 1], w_r.at[w, st, way, h - 1], (to, m))

    def z_hop(w, st, h):
        if h >= A:
            return
        for way, step, aa, ok in z_moves(w, st, h)[2]:

            @pl.when(ok)
            def _():
                z_copy(w, st, h, way, step, aa).start()

    def z_sent(w, st, h):
        for way, step, aa, ok in z_moves(w, st, h)[2]:

            @pl.when(ok)
            def _():
                z_copy(w, st, h, way, step, aa).wait_send()

    def z_wait(w, st, h, forward=False):
        if h >= A:
            return
        for way, step in ((0, 1), (1, -1)):
            aa = a - step * h

            @pl.when((aa >= 0) & (aa < A))
            def _():
                z_copy(w, st, h, way, step, jnp.clip(aa, 0, A - 1)).wait_recv()
                if forward:
                    x_send(w, aa)

    def x_copy(w, aa, k, own=False):
        src, dst = weights[w]
        r = shard(aa, b)
        return remote(
            src if own else dst.at[r], dst.at[r], x_s.at[w, aa, k - 1], x_r.at[w, aa, k - 1], xpeer(k)
        )

    def x_send(w, aa, own=False):
        for k in range(1, B):
            x_copy(w, aa, k, own).start()

    def x_wait(w, aa):
        src, dst = weights[w]
        for k in range(1, B):
            r = shard(aa, (b - k + B) % B)
            remote(src, dst.at[r], x_s.at[w, aa, k - 1], x_r.at[w, aa, k - 1], xpeer(k)).wait_recv()

    def w_local(w):
        src, dst = weights[w]
        return local(src, dst.at[shard(a, b)], lsem.at[16 + w])

    def w_start(w):
        z_hop(w, 0, 1)
        x_send(w, a, own=True)
        w_local(w).start()

    def w_next(w, st, h, forward=True):
        z_wait(w, st, h, forward)
        z_hop(w, st, h + 1)

    def w_ready(w):
        for aa in range(A):
            x_wait(w, aa)
        w_local(w).wait()

    def w_sent(w, forward):
        for st in range(1 if forward else B):
            for h in range(1, A):
                z_sent(w, st, h)
        for k in range(1, B):
            for aa in range(A) if forward else [a]:
                x_copy(w, aa, k).wait_send()

    w_start(0)
    w_start(5)
    loop(nc, start_tok)
    x_send(4, a, own=True)
    w_local(4).start()
    tok_local = local(tokens, tokv.at[:, mine], lsem.at[4])
    tok_local.start()
    al_local = local(alpha, alv.at[:, mine], lsem.at[5])
    al_local.start()
    al_copies = [
        remote(alpha, alv.at[:, mine], al_s.at[i], al_r.at[i], dev) for i, dev in enumerate(others)
    ]
    for cp in al_copies:
        cp.start()

    def pass_tok(i):
        c = nc - 1 - i
        for k in range(1, ny):
            src = ((y - k + ny) % ny) * 2 + core
            tok_got(c, k, src).wait_recv()
            tok_got(c, ny + k - 1, src).start()

    w_next(0, 0, 1)
    w_next(5, 0, 1)
    w_next(0, 0, 2)
    pass_tok(0)
    w_next(5, 0, 2)
    w_next(0, 0, 3)
    pass_tok(1)
    w_next(5, 0, 3)
    w_start(1)
    w_start(2)
    loop(nc - 2, lambda i: pass_tok(i + 2))

    go4 = gout

    def go_copy(i, dev, cc):
        return remote(go4.at[:, cc], goh.at[:, :, mine], go_s.at[i], go_r.at[i], dev)

    go_copies = [go_copy(0, peer, mate)]
    i = 1
    for k in range(1, ny):
        for cc in (core, mate):
            go_copies.append(go_copy(i, ypeer(k, cc), cc))
            i += 1
    go_local = local(go4.at[:, core], goh.at[:, :, mine], lsem.at[6])
    go_local.start()
    for cp in go_copies:
        cp.start()

    def end_tok(i):
        c = nc - 1 - i
        tok_got(c, 0, y * 2 + mate).wait_recv()
        for k in range(1, ny):
            src = ((y - k + ny) % ny) * 2 + mate
            tok_got(c, ny + k - 1, src).wait_recv()

    loop(nc, end_tok)

    def tok_sent(i):
        c = nc - 1 - i
        tok_own(c, 0, peer).wait_send()
        for k in range(1, ny):
            tok_own(c, k, ypeer(k, core)).wait_send()
            tok_got(c, ny + k - 1, ((y - k + ny) % ny) * 2 + core).wait_send()

    loop(nc, tok_sent)
    tok_local.wait()
    w_ready(0)
    w_ready(5)

    ones = head_ones(C)
    qkvv = gml

    def angles_of(r):
        t = jnp.where(live > 0.5, table[r, :], table[0:TB, :])
        u = pltpu.roll(t, DK, 1)
        first = lax.broadcasted_iota(jnp.int32, t.shape, 1) < DK
        cs, sn = jnp.where(first, t, u), jnp.where(first, u, t)
        return jnp.concatenate([cs] * (C // 128), axis=1), jnp.concatenate([sn] * (C // 128), axis=1)

    def project_rows(i):
        r = rows_at(i * TB, TB)
        x = tokv[r, :]
        cs, sn = angles_of(r)
        for part in range(2):
            cols = slice(part * C, part * C + C)
            t = turn(nn(x, wqov[:, cols]), cs, sn, 1.0)
            act[r, cols] = t.astype(BF)
            inv = lax.rsqrt(split_dot(t * t, ones) + epsilon)
            qkvv[r, cols] = (t * inv * sq[...]).astype(BF)
        qkvv[r, 2 * C : 3 * C] = nn(x, wqov[:, 2 * C : 3 * C]).astype(BF)

        @pl.when(i == 1)
        def _():
            w_next(1, 0, 1)
            w_next(2, 0, 1)

    loop(nc, project_rows)
    save_tok = local(tokv, tokf, lsem.at[4])
    save_tok.start()
    saves = [
        local(qkvv.at[:, 0 : 3 * C], qkv_h, lsem.at[7]),
        local(act.at[:, 0 : 2 * C], rot_h, lsem.at[8]),
    ]
    for cp in saves:
        cp.start()

    RT = 64
    NG = 2
    GW = D // NG

    def y_copy(e, c, k, n, sy, ry):
        cols = slice(n * GW, n * GW + GW)
        return remote(
            sy.at[c, :, cols], ry.at[k - 1, c, :, cols], y_s.at[e, c, k - 1, n], y_r.at[e, c, k - 1, n],
            ypeer(k, core),
        )

    def exchange(e, c, part, sy, ry):
        r = rows_at(c * TB, TB)
        theirs, ours = rows_at(mate * TH, TH), rows_at(core * TH, TH)
        copies = []
        for n in range(NG):
            cols = slice(n * GW, n * GW + GW)
            sc[:, cols] = part(r, cols).astype(BF)
            cp = remote(
                sc.at[theirs, cols], rc.at[c, :, cols], ex_s.at[e, c, n], ex_r.at[e, c, n], peer
            )
            cp.start()
            copies.append(cp)
        for n in range(NG):
            cols = slice(n * GW, n * GW + GW)
            copies[n].wait()
            sy[c, :, cols] = (sc[ours, cols].astype(F32) + rc[c, :, cols].astype(F32)).astype(BF)
            for k in range(1, ny):
                y_copy(e, c, k, n, sy, ry).start()

    def landed(e, c, sy, ry):
        for k in range(1, ny):
            for n in range(NG):
                y_copy(e, c, k, n, sy, ry).wait()

    def total(c, r, sy, ry):
        t = sy[c, r, :].astype(F32)
        for k in range(ny - 1):
            t = t + ry[k, c, r, :].astype(F32)
        return t

    NS = 2
    SH = TH // NS

    def share(e, c, n, buf):
        r = rows_at(c * TB + core * TH + n * SH, SH)
        return remote(buf.at[r], buf.at[r], hc_s.at[e, c, n], hc_r.at[e, c, n], peer)

    def rows_then_share(e, c, rows, buf):
        for n in range(NS):
            loop(SH // RT, lambda t: rows(n * (SH // RT) + t))
            share(e, c, n, buf).start()

    def shared(e, c, buf):
        for n in range(NS):
            share(e, c, n, buf).wait()

    def attend_chunk(i):
        c = nc - 1 - i
        attn_fwd_block(c, TB, H, qkvv, C, live, acc)
        r = rows_at(c * TB, TB)
        for pr in range(C // 128):
            both = []
            for h in (2 * pr, 2 * pr + 1):
                t = acc[h]
                both.append(t / pltpu.roll(t, DK, 1))
                row = DK if h % 2 == 0 else 0
                ll[pl.ds(h, 1), r] = jnp.log2(t).T[row : row + 1]
            lane = lax.broadcasted_iota(jnp.int32, (TB, 128), 1)
            attn[r, pr * 128 : pr * 128 + 128] = jnp.where(lane < DK, both[0], both[1]).astype(BF)

        def part(rr, cols):
            return nt(attn[rr, :], wqov[cols, 3 * C : 4 * C])

        @pl.when(i == 0)
        def _():
            save_tok.wait()

        exchange(0, c, part, sy1, ry1)

        @pl.when(i == 0)
        def _():
            w_next(1, 0, 2)
            w_next(2, 0, 2)
            w_start(3)
            z_hop(4, 0, 1)
            x_wait(4, a)
            for st in range(1, B):
                z_hop(4, st, 1)

        @pl.when(i == 2)
        def _():
            w_next(1, 0, 3)
            w_next(2, 0, 3)

        @pl.when(i == 3)
        def _():
            w_next(3, 0, 1)
            for st in range(B):
                w_next(4, st, 1, False)

    ll[...] = jnp.zeros_like(ll)
    loop(nc, attend_chunk)
    for cp in saves:
        cp.wait()
    al_local.wait()
    for cp in al_copies:
        cp.wait()
    w_ready(1)
    w_ready(2)

    gacc[...] = jnp.zeros_like(gacc)
    gsacc[...] = jnp.zeros_like(gsacc)

    def feed_chunk(i):
        c = nc - 1 - i
        landed(0, c, sy1, ry1)
        base = c * TB + core * TH

        def rows(t):
            r = rows_at(t * RT, RT)
            g = rows_at(base + t * RT, RT)
            br = total(c, r, sy1, ry1)
            xb = tokv[g, :]
            x = xb.astype(F32)
            ha = br * mean_sq(br, D)
            mix = x + alv[0:1, :] * (ha - x)
            tokv[g, :] = (mix * mean_sq(mix, D)).astype(BF)

        rows_then_share(0, c, rows, tokv)
        shared(0, c, tokv)
        r = rows_at(c * TB, TB)

        def units(n):
            cu, cv = rows_at(n * 256, 256), rows_at(F + n * 256, 256)
            x = tokv[r, :]
            u = nn(x, wgv[:, cu])
            v = nn(x, wgv[:, cv])
            gu[r, cu] = u.astype(BF)
            gu[r, cv] = v.astype(BF)
            us = u * sml[0:1, cu]
            vs = v * sml[1:2, cu]
            act[r, cu] = (us * vs * jax.nn.sigmoid(vs)).astype(BF)

        loop(F // 256, units)

        @pl.when(i == 0)
        def _():
            w_next(3, 0, 2)
            for st in range(B):
                w_next(4, st, 2, False)

        @pl.when(i == 1)
        def _():
            w_next(3, 0, 3)
            for st in range(B):
                w_next(4, st, 3, False)
            w_ready(3)
            w_local(4).wait()

        @pl.when(i > 0)
        def _():
            down_chunk(i - 1)

    def down_chunk(i):
        c = nc - 1 - i
        exchange(1, c, lambda rr, cols: nt(act[rr, :], wdv[cols, :]), sy2, ry2)

    loop(nc, feed_chunk)
    down_chunk(nc - 1)
    go_local.wait()
    for cp in go_copies:
        cp.wait()

    def grad_rows(c):
        return local(goh.at[c], gst, lsem.at[12])

    grad_rows(nc - 1).start()

    def back_chunk(i):
        c = nc - 1 - i
        landed(1, c, sy2, ry2)
        grad_rows(c).wait()
        base = c * TB + core * TH

        def rows(t):
            r = rows_at(t * RT, RT)
            g = rows_at(base + t * RT, RT)
            am = alv[1:2, :]
            bm = total(c, r, sy2, ry2)
            h = tokv[g, :].astype(F32)
            rm = mean_sq(bm, D)
            hm = bm * rm
            diff = hm - h
            mix = h + am * diff
            r2 = mean_sq(mix, D)
            fin = mix * r2
            fst[r, :] = fin.astype(BF)
            go = gst[r, :].astype(F32)
            gm = r2 * (go - fin * (jnp.sum(go * fin, axis=1, keepdims=True) * (1.0 / D)))
            gacc[8:16, :] += fold(gm * diff)
            gh = am * gm
            ghid[c, r, :] = (gm - gh).astype(BF)
            gb = rm * (gh - hm * (jnp.sum(gh * hm, axis=1, keepdims=True) * (1.0 / D)))
            gml[g, :] = gb.astype(BF)

        rows_then_share(1, c, rows, gml)

        @pl.when(c > 0)
        def _():
            grad_rows(jnp.maximum(c - 1, 0)).start()

        og = rows_at(base, TH)
        o_here = local(fst.at[:, mine], out.at[og], lsem.at[6])
        o_here.start()
        o_there = remote(
            fst.at[:, feat(y * 2 + mate)], out.at[og], out_s.at[c], out_r.at[c], peer
        )
        o_there.start()
        shared(1, c, gml)
        r = rows_at(c * TB, TB)

        def units(n):
            cu, cv = rows_at(n * 256, 256), rows_at(F + n * 256, 256)
            ga = nn(gml[r, :], wdv[:, cu])
            u = gu[r, cu].astype(F32)
            v = gu[r, cv].astype(F32)
            su, sv = sml[0:1, cu], sml[1:2, cu]
            us, vs = u * su, v * sv
            sg = jax.nn.sigmoid(vs)
            si = vs * sg
            g_u = ga * si
            g_v = ga * us * (sg + si - si * sg)
            gsacc[0:8, cu] += fold(g_u * u)
            gsacc[8:16, cu] += fold(g_v * v)
            gu[r, cu] = (g_u * su).astype(BF)
            gu[r, cv] = (g_v * sv).astype(BF)

        loop(F // 256, units)
        exchange(2, c, lambda rr, cols: nt(gu[rr, :], wgv[cols, :]), sy2, ry3)
        o_here.wait()
        o_there.wait()

    loop(nc, back_chunk)

    RA, AR, w = D // A, A * R, F // 2
    pieces = []
    for src, r1, r2, cuts in (
        (gwd_h, r1d_h, r2d_h, (0, w, 2 * w)),
        (gwg_h, r1g_h, r2g_h, (0, w, 2 * w, 3 * w, 4 * w)),
        (gqo_h, r1q_h, r2q_h, (0, 2 * C, 3 * C, 4 * C)),
    ):
        for n in range(len(cuts) - 1):
            pieces.append((src, r1, r2, slice(cuts[n], cuts[n + 1])))
    lanes_of = (0, 1, 3, 0, 1, 3, 1, 3, 0)

    def px_copy(p, k):
        src, r1, _, cols = pieces[p]
        return remote(
            src.at[(b + k) % B, :, cols], r1.at[k - 1, :, cols], p_s.at[p, k - 1], p_r.at[p, k - 1], xpeer(k)
        )

    def rs_start(p):
        for k in range(1, B):
            px_copy(p, k).start()

    def slot(p):
        cols = pieces[p][3]
        return slice(lanes_of[p] * w, lanes_of[p] * w + cols.stop - cols.start)

    def sums(p, aa):
        return gu.at[pl.ds(pl.multiple_of(D + aa * R, R), R), slot(p)]

    def pz_copy(p, k):
        _, _, r2, cols = pieces[p]
        return remote(
            sums(p, (a + k) % A), r2.at[k - 1, :, cols], q_s.at[p, k - 1], q_r.at[p, k - 1], zpeer(k)
        )

    def own_load(p):
        src, _, _, cols = pieces[p]
        return local(src.at[b, :, cols], gu.at[0:AR, slot(p)], rsem.at[lanes_of[p], 0])

    def first_load(p, k):
        _, r1, _, cols = pieces[p]
        return local(
            r1.at[k - 1, :, cols], gu.at[k * AR : (k + 1) * AR, slot(p)], rsem.at[lanes_of[p], k]
        )

    def rs_load(p):
        own_load(p).start()
        for k in range(1, B):
            px_copy(p, k).wait()
            first_load(p, k).start()

    def rs_add(p):
        own_load(p).wait()
        for k in range(1, B):
            first_load(p, k).wait()
        for k in list(range(1, A)) + [0]:
            aa = (a + k) % A
            t = gu[rows_at(aa * R, R), slot(p)].astype(F32)
            for kk in range(1, B):
                t = t + gu[pl.ds(pl.multiple_of(kk * AR + aa * R, R), R), slot(p)].astype(F32)
            gu[pl.ds(pl.multiple_of(D + aa * R, R), R), slot(p)] = t.astype(BF)
            if k:
                pz_copy(p, k).start()

    def second_load(p, k):
        _, _, r2, cols = pieces[p]
        return local(
            r2.at[k - 1, :, cols], gu.at[D + AR + (k - 1) * R : D + AR + k * R, slot(p)], rsem.at[lanes_of[p], B + k]
        )

    def end_load(p):
        for k in range(1, A):
            pz_copy(p, k).wait()
            second_load(p, k).start()

    def rs_end(p, res):
        for k in range(1, A):
            second_load(p, k).wait()
        width = pieces[p][3].stop - pieces[p][3].start
        t = gu[pl.ds(pl.multiple_of(D + a * R, R), R), slot(p)].astype(F32)
        for k in range(1, A):
            t = t + gu[D + AR + (k - 1) * R : D + AR + k * R, slot(p)].astype(F32)
        fstage[:, 0:width] = t
        for col, n, dst in res:
            cp = local(fstage.at[:, col : col + n], dst, lsem.at[0])
            cp.start()
            cp.wait()

    def rs_finish(p):
        if p < 2:
            res = [(0, w, owd.at[:, p * w : p * w + w])]
        elif p < 6:
            first = ((p - 2) % 2) * w
            res = [(0, w, owg.at[(p - 2) // 2, :, first : first + w])]
        elif p == 6:
            res = [(0, C, owq.at[0]), (C, C, owq.at[1])]
        elif p == 7:
            res = [(0, C, owq.at[2])]
        else:
            res = [(0, C, owo)]
        rs_end(p, res)

    def tile_out(half, dst, t):
        src = wst.at[:, :, half * F : half * F + F]
        return local(src, dst.at[:, rows_at(t * R, R), half * F : half * F + F], lsem.at[1 + half])

    def down_out(half, t):
        src = wst.at[:, :, half * F : half * F + F]
        return local(src, gwd_h.at[:, rows_at(t * R, R)], lsem.at[1 + half])

    def down_tile(t):
        for half in range(2):
            tt = 2 * t + half

            @pl.when(t > 0)
            def _():
                down_out(half, tt).wait()

            cols = rows_at(tt * RA, RA)
            wst[:, :, half * F : half * F + F] = tdot(gml[:, cols], act[...]).astype(BF).reshape(B, R, F)
            down_out(half, tt).start()

    lt_first = local(tokf.at[rows_at((nc - 1) * TB + core * TH, TH)], gst, lsem.at[6])
    lt_first.start()
    loop(A // 2, down_tile)
    for half in range(2):
        down_out(half, 0).wait()
    rs_start(0)

    def up_tile(t):
        cols = rows_at(t * RA, RA)
        lhs = tokv[:, cols]
        for half in range(2):

            @pl.when(t > 0)
            def _():
                tile_out(half, gwg_h, t).wait()

            wst[:, :, half * F : half * F + F] = (
                tdot(lhs, gu[:, half * F : half * F + F]).astype(BF).reshape(B, R, F)
            )
            tile_out(half, gwg_h, t).start()

        @pl.when(t == A // 2)
        def _():
            rs_start(1)

    loop(A, up_tile)
    for half in range(2):
        tile_out(half, gwg_h, 0).wait()
    rs_start(2)
    rs_start(3)
    rs_load(0)
    qv, kv, vv = gml.at[:, 0:C], gml.at[:, C : 2 * C], gml.at[:, 2 * C : 3 * C]
    gv = gml.at[:, 3 * C : 4 * C]
    rot0 = 2 * w
    loads = [
        local(qkv_h, gml.at[:, 0 : 3 * C], lsem.at[7]),
        local(rot_h, gu.at[:, rot0 : rot0 + 2 * C], lsem.at[8]),
        local(tokf, tokv, lsem.at[9]),
    ]
    for cp in loads:
        cp.start()
    dk[...] = jnp.zeros_like(dk)
    dv[...] = jnp.zeros_like(dv)
    gsq[...] = jnp.zeros_like(gsq)
    heads = lax.broadcasted_iota(jnp.int32, (8, C), 0)
    lanes = lax.broadcasted_iota(jnp.int32, (8, C), 1) // DK
    pick = jnp.where(heads == lanes, 1.0, 0.0).astype(BF)
    for cp in loads[:2]:
        cp.wait()
    NY = ny * CF

    def gin_copy(c, hs):
        return remote(
            sc.at[hs * TH : (hs + 1) * TH, 0:NY], rc.at[c, :, hs * NY : (hs + 1) * NY], c_s.at[c, hs],
            c_r.at[c, hs], peer,
        )

    def gin_y(c, k, hs):
        src = slice((hs * (ny - 1) + k - 1) * CF, (hs * (ny - 1) + k) * CF)
        dst = slice(hs * CF, hs * CF + CF)
        return remote(
            sy2.at[c, :, src], ry2.at[k - 1, c, :, dst], yg_s.at[c, k - 1, hs], yg_r.at[c, k - 1, hs],
            ypeer(k, core),
        )

    n128 = CF // 128

    def gin_take(c):
        for hs in range(2):
            gin_copy(c, hs).wait()
            for k in range(ny):
                for q in range(n128):
                    col = hs * NY + k * CF + q * 128
                    t = acc[k * n128 + q, hs * TH : (hs + 1) * TH, :] + rc[c, :, col : col + 128].astype(F32)
                    if k == 0:
                        dk[rows_at(c * TB + hs * TH, TH), q * 128 : q * 128 + 128] = t
                    else:
                        col = (hs * (ny - 1) + k - 1) * CF + q * 128
                        sy2[c, :, col : col + 128] = t.astype(BF)
            for k in range(1, ny):
                gin_y(c, k, hs).start()

    def out_tiles():
        def o_tile(t):
            cols = rows_at(t * RA, RA)
            wst[:, :, 0:C] = tdot(gba[:, cols], attn[...]).astype(BF).reshape(B, R, C)
            cp = local(wst.at[:, :, 0:C], gqo_h.at[:, rows_at(t * R, R), 3 * C : 4 * C], lsem.at[1])
            cp.start()
            cp.wait()

        loop(A, o_tile)

    def kept_rows(c):
        return local(tokf.at[rows_at(c * TB + core * TH, TH)], gst, lsem.at[6])

    def branch_rows(c):
        base = c * TB + core * TH
        landed(2, c, sy2, ry3)
        kept_rows(c).wait()

        def rows(t):
            r = rows_at(t * RT, RT)
            g = rows_at(base + t * RT, RT)
            aa = alv[0:1, :]
            br = total(c, r, sy1, ry1)
            x = gst[r, :].astype(F32)
            ra = mean_sq(br, D)
            ha = br * ra
            diff = ha - x
            mix = x + aa * diff
            r1 = mean_sq(mix, D)
            hid = mix * r1
            gh = ghid[c, r, :].astype(F32) + total(c, r, sy2, ry3)
            gm = r1 * (gh - hid * (jnp.sum(gh * hid, axis=1, keepdims=True) * (1.0 / D)))
            gacc[0:8, :] += fold(gm * diff)
            gt = aa * gm
            ghid[c, r, :] = (gm - gt).astype(BF)
            gb = ra * (gt - ha * (jnp.sum(gt * ha, axis=1, keepdims=True) * (1.0 / D)))
            gba[g, :] = gb.astype(BF)

        rows_then_share(2, c, rows, gba)

        @pl.when(c > 0)
        def _():
            kept_rows(jnp.maximum(c - 1, 0)).start()

    branch_rows(nc - 1)
    rs_add(0)

    def attn_grad_chunk(i):
        c = nc - 1 - i
        shared(2, c, gba)

        @pl.when(c > 0)
        def _():
            branch_rows(jnp.maximum(c - 1, 0))

        r = rows_at(c * TB, TB)
        g = nn(gba[r, :], wqov[:, 3 * C : 4 * C]).astype(BF)
        gv[r, :] = g
        prod = g.astype(F32) * attn[r, :].astype(F32)
        ph = prod.astype(BF)
        dl[:, r] = nt(pick, ph) + nt(pick, (prod - ph.astype(F32)).astype(BF))

        def between():
            @pl.when(i == 0)
            def _():
                rs_load(1)

            @pl.when(i == 1)
            def _():
                rs_add(2)

        attn_bwd_block(c, TB, H, qv, kv, vv, gv, ll, dl, off_bias, dq, dk, dv, between)

        @pl.when(i == 0)
        def _():
            rs_add(1)
            rs_start(4)

        @pl.when(i == 1)
        def _():
            rs_load(3)
            end_load(0)

        @pl.when(i == 2)
        def _():
            rs_load(4)
            end_load(1)

        @pl.when(i == nc - 1)
        def _():
            rs_load(5)
            end_load(2)
            out_tiles()
            rs_start(8)

        cs, sn = angles_of(r)
        for part in range(2):
            gh = (dq[...] if part == 0 else dk[r, :]) * 8.0
            t = gu[r, rot0 + part * C : rot0 + part * C + C].astype(F32)
            inv = lax.rsqrt(split_dot(t * t, ones) + epsilon)
            un = t * inv
            gsq[...] += fold(gh * un)
            gh = gh * sq[...]
            gr = inv * (gh - un * split_dot(gh * un, ones))
            act[r, part * C : part * C + C] = turn(gr, cs, sn, -1.0).astype(BF)
        act[r, 2 * C : 3 * C] = dv[r, :].astype(BF)

        def product(hsel, k, cc):
            rr = rows_at(c * TB + hsel * TH, TH)
            cols = feat(((y + k) % ny) * 2 + cc)
            t = nt(act[rr, 0 : 3 * C], wqov[cols, 0 : 3 * C])
            if k == 0:
                t = t + jnp.where(hsel == core, 1.0, 0.0) * ghid[c, :, cols].astype(F32)
            return t

        @pl.when(i > 0)
        def _():
            gin_take(jnp.minimum(c + 1, nc - 1))

        for hs in range(2):
            for k in range(ny):
                sc[hs * TH : (hs + 1) * TH, k * CF : (k + 1) * CF] = product(hs, k, mate).astype(BF)
            gin_copy(c, hs).start()
        for hs in range(2):
            for k in range(ny):
                t = product(hs, k, core)
                for q in range(n128):
                    acc[k * n128 + q, hs * TH : (hs + 1) * TH, :] = t[:, q * 128 : q * 128 + 128]

        @pl.when(i == 0)
        def _():
            rs_start(5)
            rs_load(2)

        @pl.when(i == 1)
        def _():
            rs_finish(0)
            rs_add(3)

        @pl.when(i == 2)
        def _():
            rs_finish(1)
            rs_add(4)

        @pl.when(i == nc - 1)
        def _():
            rs_finish(2)
            rs_add(5)
            end_load(3)

    loop(nc, attn_grad_chunk)
    ga_there = remote(gacc.at[:, feat(y * 2 + mate)], gar, m_s.at[0], m_r.at[0], peer)
    ga_there.start()
    loads[2].wait()

    def q_out(half, t):
        src = wst.at[:, :, half * F : half * F + 2 * C]
        return local(src, gqo_h.at[:, rows_at(t * R, R), 0 : 2 * C], lsem.at[1 + half])

    def q_tile(t):
        for half in range(2):
            tt = 2 * t + half

            @pl.when(t > 0)
            def _():
                q_out(half, tt).wait()

            g = tdot(tokv[:, rows_at(tt * RA, RA)], act[:, 0 : 2 * C]).astype(BF)
            wst[:, :, half * F : half * F + 2 * C] = g.reshape(B, R, 2 * C)
            q_out(half, tt).start()

    loop(A // 2, q_tile)
    for half in range(2):
        q_out(half, 0).wait()
    rs_start(6)

    def v_out(half, t):
        src = wst.at[:, :, half * F : half * F + C]
        return local(src, gqo_h.at[:, rows_at(t * R, R), 2 * C : 3 * C], lsem.at[1 + half])

    def v_tile(t):
        for half in range(2):
            tt = 2 * t + half

            @pl.when(t > 0)
            def _():
                v_out(half, tt).wait()

            g = tdot(tokv[:, rows_at(tt * RA, RA)], act[:, 2 * C : 3 * C]).astype(BF)
            wst[:, :, half * F : half * F + C] = g.reshape(B, R, C)
            v_out(half, tt).start()

    loop(A // 2, v_tile)
    for half in range(2):
        v_out(half, 0).wait()
    rs_start(7)
    gin_take(0)
    rs_finish(3)
    rs_load(8)
    ga_there.wait()
    vec[...] = jnp.zeros_like(vec)
    gt = gacc[:, mine] + gar[...]
    vec[0:1, 0:F] = jnp.sum(gsacc[0:8, :], axis=0, keepdims=True)
    vec[1:2, 0:F] = jnp.sum(gsacc[8:16, :], axis=0, keepdims=True)
    vec[2:3, 0:CF] = jnp.sum(gt[0:8], axis=0, keepdims=True)
    vec[3:4, 0:CF] = jnp.sum(gt[8:16], axis=0, keepdims=True)
    vec[4:5, 0:C] = jnp.sum(gsq[...], axis=0, keepdims=True)
    vx = [remote(vec, rv1.at[k - 1], m_s.at[k], m_r.at[k], xpeer(k)) for k in range(1, B)]
    for cp in vx:
        cp.start()
    rs_add(8)
    end_load(4)
    for cp in vx:
        cp.wait()
    t = vec[...]
    for k in range(B - 1):
        t = t + rv1[k]
    vec[...] = t
    vz = [
        remote(vec, rv2.at[k - 1], m_s.at[B - 1 + k], m_r.at[B - 1 + k], zpeer(k)) for k in range(1, A)
    ]
    for cp in vz:
        cp.start()

    rs_finish(4)
    end_load(5)

    def gin_end(i):
        c = nc - 1 - i
        for hs in range(2):
            rr = rows_at(c * TB + hs * TH, TH)
            for k in range(1, ny):
                gin_y(c, k, hs).wait()
                dk[rr, :] += ry2[k - 1, c, :, hs * CF : hs * CF + CF].astype(F32)

    loop(nc, gin_end)
    ends = [local(dk, gin_o, lsem.at[10])]
    ends[-1].start()
    rs_load(6)
    rs_add(6)
    rs_finish(5)
    rs_load(7)
    rs_add(7)
    end_load(8)
    for cp in vz:
        cp.wait()
    t = vec[...]
    for k in range(A - 1):
        t = t + rv2[k]
    vec[...] = t
    ends.append(local(vec, vec_o, lsem.at[11]))
    ends[-1].start()
    for p in range(6):
        w_sent(p, p != 4)
    rs_finish(8)
    end_load(6)
    rs_finish(6)
    end_load(7)
    rs_finish(7)
    for cp in ends:
        cp.wait()


def run_layer(z, live, tokens, gout, wqo, wg, wd, alpha, table, sq, sml):
    T, C, CF, F, D, H = z.T, z.C, z.CF, z.F, z.D, z.H
    nc, TB, TH, R, A, B, ny, mp = z.nc, z.TB, z.TH, z.R, z.A, z.B, z.ny, z.mp
    S = jax.ShapeDtypeStruct
    hbm = pl.BlockSpec(memory_space=pltpu.HBM)
    vm = pl.BlockSpec(memory_space=pltpu.VMEM)
    W = max(F, CF, C)
    AR = A * R
    outs = [
        S((T, CF), BF), S((T, CF), F32), S((3, R, C), F32), S((R, C), F32), S((2, R, F), F32), S((R, F), F32),
        S((8, W), F32),
        S((T, 3 * C), BF), S((T, 2 * C), BF), S((T, D), BF), S((nc, TH, D), BF),
    ]
    widths = (F, 2 * F, 4 * C)
    outs += [S((B, AR, n), BF) for n in widths]
    outs += [S((max(B - 1, 1), AR, n), BF) for n in widths]
    outs += [S((max(A - 1, 1), R, n), BF) for n in widths]
    V = pltpu.VMEM
    scratch = [
        V((T, D), BF), V((D, 4 * C), BF), V((D, 2 * F), BF), V((D, F), BF),
        V((T, D), BF), V((T, F), BF), V((T, 2 * F), BF), V((T, D), BF),
        V((T, C), BF), V((8, T), F32), V((8, T), F32), V((max(H, ny * CF // 128), TB, 128), F32),
        V((T, C), F32), V((T, C), F32), V((TB, C), F32), V((R, F // 2), F32),
    ]
    for _ in range(2):
        scratch += [V((nc, TH, D), BF), V((ny - 1, nc, TH, D), BF)]
    scratch += [
        V((ny - 1, nc, TH, D), BF), V((nc, TH, D), BF), V((TB, D), BF), V((nc, TH, D), BF), V((TH, D), BF), V((TH, D), BF),
        V((B, R, 2 * F), BF), V((8, D), F32), V((16, D), F32), V((16, F), F32), V((8, C), F32), V((16, CF), F32),
        V((8, W), F32), V((max(B - 1, 1), 8, W), F32), V((max(A - 1, 1), 8, W), F32),
    ]
    sem = pltpu.SemaphoreType.DMA
    for shape in (
        (nc, 2 * ny - 1), (6, B, 2, max(A - 1, 1)), (6, A, max(B - 1, 1)), (mp - 1,), (mp - 1,), (3, nc, 2),
        (3, nc, ny - 1, 2), (3, nc, 2), (nc,), (9, max(B - 1, 1)), (9, max(A - 1, 1)), (nc, 2), (nc, ny - 1, 2),
        (A + B - 1,),
    ):
        scratch += [sem(shape), sem(shape)]
    scratch += [sem((22,)), sem((4, A + B))]
    return pl.pallas_call(
        functools.partial(layer, z),
        out_shape=outs,
        in_specs=[pl.BlockSpec(memory_space=pltpu.SMEM)] + [hbm] * 6 + [vm] * 3,
        out_specs=[hbm] * len(outs),
        scratch_shapes=scratch,
        compiler_params=pltpu.CompilerParams(
            collective_id=0, has_side_effects=True, vmem_limit_bytes=64 * 2**20 - 2**19
        ),
        name="layer",
    )(live, tokens, gout.reshape(nc, 2, TH, CF), wqo, wg, wd, alpha, table, sq, sml)


def tables(T):
    half = DK // 2
    frequency = np.float32(theta_base) ** (np.float32(-2.0 / DK) * np.arange(half, dtype=np.float32))
    grid = np.arange(T, dtype=np.float32)[:, None] * frequency[None, :].astype(np.float32)
    cos, sin = np.cos(grid, dtype=np.float32), np.sin(grid, dtype=np.float32)
    return np.concatenate([cos, cos, sin, sin], axis=1)


def on_device(
    sizes,
    tokens,
    w_qkv,
    w_out,
    w_gate_up,
    w_down,
    s_qk,
    alpha_attn,
    alpha_mlp,
    s_mlp,
    doc_lengths,
    grad_out,
):
    T, CF = tokens.shape
    H = s_qk.shape[1]
    C = H * DK
    F = w_down.shape[1]
    z = Sizes(sizes, T, C, CF, F, doc_lengths.shape[1])
    D, R = z.D, z.R
    table = jnp.asarray(tables(T))
    scale = s_qk.T.reshape(1, C)
    sml = s_mlp.transpose(1, 2, 0).reshape(2, F)
    alpha = jnp.pad(
        jnp.stack([alpha_attn.T.reshape(-1), alpha_mlp.T.reshape(-1)]), ((0, 6), (0, 0))
    )
    whole = doc_lengths[0, 0] == T
    live = whole.astype(F32).reshape(1)
    (out, grad_in, gw_qkv, gw_out, gw_gu, gw_down, vec) = run_layer(
        z, live, tokens, grad_out, jnp.concatenate([w_qkv.reshape(R, 3 * C), w_out], axis=1),
        w_gate_up.reshape(R, 2 * F), w_down, alpha, table, scale, sml,
    )[:7]
    d, m = place()

    def channel_rows(v, per_head):
        n = per_head // z.dp
        return lax.dynamic_slice_in_dim(v.reshape(H, per_head).T, d * n, n, 0)

    gs = jnp.stack([channel_rows(vec[i, 0:F], F // H) for i in range(2)], axis=1)
    return (
        out,
        grad_in,
        gw_qkv.transpose(1, 0, 2),
        gw_out,
        gw_gu.transpose(1, 0, 2),
        gw_down,
        channel_rows(vec[4, 0:C], DK),
        channel_rows(vec[2, 0:CF], DK),
        channel_rows(vec[3, 0:CF], DK),
        gs,
    )


def solution(mesh):
    placed = (
        P("dp", "mp"),
        P("dp", None, "mp"),
        P("dp", "mp"),
        P("dp", None, "mp"),
        P("dp", "mp"),
        P(None, "mp"),
        P(None, "mp"),
        P(None, "mp"),
        P(None, None, "mp"),
        P("dp", None),
        P("dp", "mp"),
    )
    return jax.shard_map(
        functools.partial(on_device, dict(mesh.shape)),
        mesh=mesh,
        in_specs=placed,
        out_specs=(
            P("dp", "mp"),
            P("dp", "mp"),
            P("dp", None, "mp"),
            P("dp", "mp"),
            P("dp", None, "mp"),
            P("dp", "mp"),
            P("dp", "mp"),
            P("dp", "mp"),
            P("dp", "mp"),
            P("dp", None, "mp"),
        ),
        check_vma=False,
    )
```
